32 devices in a mesh: dp: 2 (over core), mp: 16 (over z, y, x).
Axes of the slice: x: 2, y: 2, z: 4, core: 2. Of those that a mesh axis runs over, the one named last changes fastest.
Arguments:
- tokens: bfloat16 [512, 8192], P('mp', 'dp'), may hold values from -48 to 48
- lengths: int32 [2], P('dp'), may hold values from 512 to 4096, as said below
- norm_gain: float32 [512], P('mp'), may hold values from 0.5 to 1.5
- norm_bias: float32 [512], P('mp'), may hold values from -1.5 to 1.5
- log_step: float32 [512], P('mp'), may hold values from -4.6 to -2.3
- decay_log: float32 [512, 32], P('mp'), may hold values from -2.3 to 0
- frequency: float32 [512, 32], P('mp'), may hold values from 0.1 to 10
- readout: float32 [512, 64], P('mp'), may hold values from -2 to 2
- liquid_readout: float32 [512, 64], P('mp'), may hold values from -2 to 2
- skip_gain: float32 [512], P('mp'), may hold values from -1 to 1
- value_weight: bfloat16 [512, 512], P(None, 'mp'), may hold values from -0.25 to 0.25
- gate_weight: bfloat16 [512, 512], P(None, 'mp'), may hold values from -0.25 to 0.25
- value_bias: bfloat16 [512], P('mp'), may hold values from -1.5 to 1.5
- gate_bias: bfloat16 [512], P('mp'), may hold values from -1.5 to 1.5
- grad_out: bfloat16 [512, 8192], P('mp', 'dp'), may hold values from -6 to 6
Outputs:
- layer_out: bfloat16 [512, 8192], P('mp', 'dp')
- grad_tokens: float32 [512, 8192], P('mp', 'dp')
- gain_grad: float32 [512], P('mp')
- bias_grad: float32 [512], P('mp')
- step_grad: float32 [512], P('mp')
- decay_grad: float32 [512, 32], P('mp')
- frequency_grad: float32 [512, 32], P('mp')
- readout_grad: float32 [512, 64], P('mp')
- liquid_grad: float32 [512, 64], P('mp')
- skip_grad: float32 [512], P('mp')
- value_grad: float32 [512, 512], P(None, 'mp')
- gate_grad: float32 [512, 512], P(None, 'mp')
- value_bias_grad: float32 [512], P('mp')
- gate_bias_grad: float32 [512], P('mp')
The draws below stay inside these ranges and needn't reach their ends.
Inputs may be any that keep to these rules, and one draw needn't show every extreme that they name: `lengths`: A document's valid length; some document is full and some has 512 valid positions.
All inputs are finite; a program needn't handle non-finite values.
Results may differ from the reference program's by a relative error of at most 0.002.
The reference program's roundings to bfloat16 on the way (of `mixed`) count: a program that leaves them out, or rounds other values in their place, can miss the bound.
Values may be sent and summed in bfloat16 or wider, within the bound.
No kernel may reach another device: no remote copies, remote signals or barrier semaphores. Data moves between devices by JAX's collectives and lax.ppermute only.
A program may use at most 128 MiB of HBM per device.

```python
import math
import jax
import jax.numpy as jnp
from jax import lax

H = 512
STATE = 64
MODES = 32
LEN = 4096
DOCS = 2
TOKENS = 8192


def draw_lengths(key, part):
    first_key, second_key = jax.random.split(key)
    drawn = jax.random.randint(first_key, (DOCS,), LEN // 8, LEN + 1)
    order = jax.random.permutation(second_key, DOCS)
    drawn = drawn.at[order[0]].set(LEN)
    drawn = drawn.at[order[1]].set(LEN // 8)
    return drawn.astype(jnp.int32)


def draw_tokens(key, part):
    value_key = jax.random.fold_in(key, 11)
    row_key = jax.random.fold_in(key, 12)
    channel_pos = jnp.arange(H).astype(jnp.float32) / (H - 1)
    rising = 0.5 * (1.0 + 2.0 * channel_pos)
    row_scale = jnp.exp(jax.random.uniform(row_key, (TOKENS, 1), minval=0.0, maxval=1.098612))
    values = jnp.clip(jax.random.normal(value_key, (TOKENS, H)), -4.0, 4.0)
    return (values * rising[None, :] * row_scale).T.astype(jnp.bfloat16)


def block_scale(key, shape, cuts, least, top_value):
    def one(axis_at, shards_of):
        steps = jax.random.uniform(jax.random.fold_in(jax.random.fold_in(key, 6), axis_at), (shards_of,), jnp.float32, least / len(cuts), top_value / len(cuts))
        return jnp.repeat(jnp.exp(steps), shape[axis_at] // shards_of).reshape((-1,) + (1,) * (len(shape) - axis_at - 1))

    loudness = one(*cuts[0])
    for cut in cuts[1:]:
        loudness = loudness * one(*cut)
    return loudness


def normal_values(rng, dims, scale, limit, pieces=(), kind=jnp.bfloat16):
    gain = block_scale(rng, dims, pieces, -0.22, 0.18) if pieces else 1.0
    entries = jax.random.normal(rng, dims, jnp.float32) * scale * gain
    return jnp.minimum(jnp.maximum(entries, -limit), limit).astype(kind)


def setup_inputs(seed: int = 0) -> dict:
    key_of = jax.random.split(jax.random.key(seed), 16)
    return {
        "tokens": draw_tokens(jax.random.fold_in(key_of[15], 71), 0),
        "lengths": draw_lengths(jax.random.fold_in(key_of[15], 71), 0),
        "norm_gain": jnp.clip(1.0 + 0.1 * jax.random.normal(key_of[2], (H,), jnp.float32), 0.5, 1.5),
        "norm_bias": normal_values(key_of[3], (H,), 0.3, 1.5, ((0, 16),), jnp.float32),
        "log_step": jnp.clip(-4.6 + 2.3 * jax.random.uniform(key_of[4], (H,), jnp.float32) ** block_scale(key_of[4], (H,), ((0, 16),), -0.2, 0.2), -4.6, -2.3),
        "decay_log": jnp.clip(-2.3 + 2.3 * jax.random.uniform(key_of[5], (H, MODES), jnp.float32) ** block_scale(key_of[5], (H, MODES), ((0, 16),), -0.2, 0.2), -2.3, 0.0),
        "frequency": jnp.clip(jnp.exp(math.log(10.0) - 4.6051702 * jax.random.uniform(key_of[6], (H, MODES), jnp.float32) ** block_scale(key_of[6], (H, MODES), ((0, 16),), -0.2, 0.2)), 0.1, 10.0),
        "readout": normal_values(key_of[7], (H, STATE), 0.35, 2.0, ((0, 16),), jnp.float32),
        "liquid_readout": normal_values(key_of[8], (H, STATE), 0.35, 2.0, ((0, 16),), jnp.float32),
        "skip_gain": jnp.clip(jax.random.uniform(key_of[9], (H,), jnp.float32, -1.0, 1.0) * block_scale(key_of[9], (H,), ((0, 16),), -0.4, 0.0), -1.0, 1.0),
        "value_weight": normal_values(key_of[10], (H, H), H ** -0.5, 0.25, ((1, 16),)),
        "gate_weight": normal_values(key_of[11], (H, H), H ** -0.5, 0.25, ((1, 16),)),
        "value_bias": normal_values(key_of[12], (H,), 0.3, 1.5, ((0, 16),)),
        "gate_bias": normal_values(key_of[13], (H,), 0.3, 1.5, ((0, 16),)),
        "grad_out": normal_values(key_of[14], (H, TOKENS), 1.0, 6.0, ((0, 16), (1, 2))),
    }


@jax.custom_vjp
def low(v):
    return lax.optimization_barrier(v.astype(jnp.bfloat16)).astype(jnp.float32)

@jax.custom_vjp
def low_back(v):
    return v

def low_keep(v):
    return (low(v), None)

def low_pass(kept, grad):
    return (grad,)

def back_keep(v):
    return (v, None)

def back_low(kept, grad):
    return (low(grad),)
low.defvjp(low_keep, low_pass)
low_back.defvjp(back_keep, back_low)

def kernels(log_step, decay_log, frequency, readout, liquid_readout, seq_len):
    mode_count = decay_log.shape[1]
    step_size = jnp.exp(log_step)[:, None]
    real_rate = -jnp.exp(decay_log)
    real_step = step_size * real_rate
    imag_step = step_size * frequency
    growth = jnp.exp(real_step)
    num_real = growth * jnp.cos(imag_step) - 1.0
    num_imag = growth * jnp.sin(imag_step)
    denominator = real_rate * real_rate + frequency * frequency
    in_real = (num_real * real_rate + num_imag * frequency) / denominator
    in_imag = (num_imag * real_rate - num_real * frequency) / denominator
    places = jnp.arange(seq_len).astype(jnp.float32)
    envelope = jnp.exp(real_step[:, :, None] * places)
    phases = imag_step[:, :, None] * places
    wave_real = envelope * jnp.cos(phases)
    wave_imag = envelope * jnp.sin(phases)

    def combine(coeffs):
        coef_real = coeffs[:, :mode_count]
        coef_imag = coeffs[:, mode_count:]
        prod_real = coef_real * in_real - coef_imag * in_imag
        prod_imag = coef_real * in_imag + coef_imag * in_real
        first = jnp.einsum('hm,hml->hl', prod_real, wave_real, precision=lax.Precision.HIGHEST)
        second = jnp.einsum('hm,hml->hl', prod_imag, wave_imag, precision=lax.Precision.HIGHEST)
        return 2.0 * (first - second)
    return (combine(readout), combine(liquid_readout))

def forward(valid_mask, tokens, norm_gain, norm_bias, log_step, decay_log, frequency, readout, liquid_readout, skip_gain, value_weight, gate_weight, value_bias, gate_bias):

    def block_kernels(params):
        return kernels(params[0], params[1], params[2], params[3], params[4], LEN)
    stacked = tuple((member.reshape((H // 8, 8) + member.shape[1:]) for member in (log_step, decay_log, frequency, readout, liquid_readout)))
    main_blocks, liquid_blocks = lax.map(jax.checkpoint(block_kernels), stacked)
    kernel_main = main_blocks.reshape(H, LEN)
    kernel_liquid = liquid_blocks.reshape(H, LEN)
    fft_len = 2 * LEN
    main_spectrum = jnp.fft.rfft(kernel_main, n=fft_len, axis=1)
    liquid_spectrum = jnp.fft.rfft(kernel_liquid, n=fft_len, axis=1)

    def one_doc(state_carry, doc_item):
        doc_tokens, doc_mask = doc_item
        row_mean = lax.optimization_barrier(jnp.mean(doc_tokens, axis=1, keepdims=True))
        centered = doc_tokens - row_mean
        variance = lax.optimization_barrier(jnp.mean(centered * centered, axis=1, keepdims=True))
        normed = centered * lax.rsqrt(variance + 1e-05)
        signal = (normed * norm_gain + norm_bias) * doc_mask[:, None]
        earlier = jnp.concatenate([jnp.zeros((1, H), jnp.float32), signal[:-1]], axis=0)
        liquid_in = signal * earlier
        both = jnp.fft.rfft(signal.T, n=fft_len, axis=1) * main_spectrum + jnp.fft.rfft(liquid_in.T, n=fft_len, axis=1) * liquid_spectrum
        mixer_pre = jnp.fft.irfft(both, n=fft_len, axis=1)[:, :LEN].T + skip_gain * signal
        mixed = low(doc_mask[:, None] * jax.nn.gelu(mixer_pre, approximate=True))
        value_pre = low_back(jnp.dot(mixed, value_weight, precision=lax.Precision.HIGHEST) + value_bias)
        gate_pre = low_back(jnp.dot(mixed, gate_weight, precision=lax.Precision.HIGHEST) + gate_bias)
        return (state_carry, doc_tokens + value_pre * jax.nn.sigmoid(gate_pre))
    doc_tokens = tokens.T.reshape(DOCS, LEN, H)
    state_carry, outputs = lax.scan(jax.checkpoint(one_doc), jnp.zeros((), jnp.float32), (doc_tokens, valid_mask))
    return outputs.reshape(TOKENS, H).T

def reference(tokens, lengths, norm_gain, norm_bias, log_step, decay_log, frequency, readout, liquid_readout, skip_gain, value_weight, gate_weight, value_bias, gate_bias, grad_out):
    positions = jnp.arange(LEN).astype(jnp.int32)
    valid_mask = (positions[None, :] < lengths.astype(jnp.int32)[:, None]).astype(jnp.float32)
    primals = (tokens.astype(jnp.float32), norm_gain, norm_bias, log_step, decay_log, frequency, readout, liquid_readout, skip_gain, value_weight.astype(jnp.float32), gate_weight.astype(jnp.float32), value_bias.astype(jnp.float32), gate_bias.astype(jnp.float32))

    def closed(*inputs):
        return forward(valid_mask, *inputs)
    layer_out, pullback = jax.vjp(closed, *primals)
    grads = pullback(grad_out.astype(jnp.float32))
    return (layer_out.astype(jnp.bfloat16), grads[0], grads[1], grads[2], grads[3], grads[4], grads[5], grads[6], grads[7], grads[8], grads[9], grads[10], grads[11], grads[12])
```

```python
from functools import partial

import jax
import jax.numpy as jnp
import numpy as np
from jax import lax
from jax.experimental import pallas as pl
from jax.experimental.pallas import tpu as pltpu
from jax.sharding import PartitionSpec as P

B = 128
G = 4
F32 = jnp.float32
BF16 = jnp.bfloat16
NN = (((1,), (0,)), ((), ()))
NT = (((1,), (1,)), ((), ()))
TN = (((0,), (0,)), ((), ()))
EPS = 1e-05
VMEM = pl.BlockSpec(memory_space=pltpu.VMEM)
SMEM = pl.BlockSpec(memory_space=pltpu.SMEM)


def params(mb=48):
    return pltpu.CompilerParams(vmem_limit_bytes=mb * 1024 * 1024)


def cost(us):
    return pl.CostEstimate(flops=int(us * 1e9), bytes_accessed=int(us * 1e6), transcendentals=0)


def dot(a, b, dims=NN):
    return lax.dot_general(a, b, dims, preferred_element_type=F32)


def split(v):
    hi = v.astype(BF16)
    return hi, (v - hi.astype(F32)).astype(BF16)


def sincos(x):
    k = jnp.floor(x * 0.6366197723675814 + 0.5)
    y = ((x - k * 1.5703125) - k * 4.837512969970703e-4) - k * 7.54978995489188e-8
    y2 = y * y
    s = y + y * y2 * (-1.6666654611e-1 + y2 * (8.3321608736e-3 - y2 * 1.9515295891e-4))
    c = 1.0 - 0.5 * y2 + y2 * y2 * (4.166664568298827e-2 + y2 * (-1.388731625493765e-3 + y2 * 2.443315711809948e-5))
    q = k.astype(jnp.int32)
    odd = (q & 1) == 1
    sin = jnp.where(odd, c, s)
    cos = jnp.where(odd, s, c)
    sin = jnp.where((q & 2) == 2, -sin, sin)
    cos = jnp.where(((q + 1) & 2) == 2, -cos, cos)
    return sin, cos


def row_iota(shape):
    return lax.broadcasted_iota(jnp.int32, shape, 0)


def lane_iota(shape):
    return lax.broadcasted_iota(jnp.int32, shape, 1)


def shift_rows(x, k):
    n = x.shape[0]
    if abs(k) % 8 == 0:
        zero = jnp.zeros((abs(k), x.shape[1]), x.dtype)
        if k > 0:
            return jnp.concatenate([zero, x[: n - k]], axis=0)
        return jnp.concatenate([x[-k:], zero], axis=0)
    rows = row_iota(x.shape)
    keep = rows >= k if k > 0 else rows < n + k
    return jnp.where(keep, pltpu.roll(x, k % n, 0), 0.0)


def shift_token(x, k):
    n = x.shape[0]
    lanes = lane_iota(x.shape)
    rows = row_iota(x.shape)
    turned = pltpu.roll(x, k % B, 1)
    wrapped = pltpu.roll(turned, k % n, 0)
    if k > 0:
        wrapped = jnp.where(rows >= 1, wrapped, 0.0)
        return jnp.where(lanes == 0, wrapped, turned)
    wrapped = jnp.where(rows < n - 1, wrapped, 0.0)
    return jnp.where(lanes == B - 1, wrapped, turned)


def swap_halves(x):
    return pltpu.roll(x, B // 2, 1)


def scan_rows(x, jump_ref, ci, direction):
    x = shift_rows(x, direction)
    step = 0
    while (1 << step) < x.shape[0]:
        moved = shift_rows(x, direction * (1 << step))
        x = x + moved * jump_ref[2 * step, pl.ds(ci, 1), :] + swap_halves(moved) * jump_ref[2 * step + 1, pl.ds(ci, 1), :]
        step += 1
    return x


def start_kernel(half_ref, x_ref, g_ref, w_ref, bias_ref, stat_ref, pay_ref):
    C, L = x_ref.shape
    mp, _, nt = pay_ref.shape
    kh = w_ref.shape[2] // nt
    for n in range(L // B):
        x = x_ref[:, n * B : (n + 1) * B].astype(F32)
        mean = jnp.sum(x, axis=0, keepdims=True) * (1.0 / C)
        dev = x - mean
        stat_ref[0, n : n + 1, :] = mean
        stat_ref[1, n : n + 1, :] = jnp.sum(dev * dev, axis=0, keepdims=True)
    wt = w_ref[half_ref[0]]
    bias = bias_ref[...]
    for j in range(mp):
        pay_ref[j, 0:C, :] = x_ref[:, j * nt : (j + 1) * nt]
        pay_ref[j, C : 2 * C, :] = g_ref[:, j * nt : (j + 1) * nt]
        for q in range(kh):
            pay_ref[j, (2 + q) * C : (3 + q) * C, :] = wt[:, q * nt : (q + 1) * nt]
        pay_ref[j, (2 + kh) * C :, :] = bias


def table_kernel(
    rates_ref, coef_ref, f_ref, w_ref, t_ref, wb_ref, near_ref, jump_ref, wout_ref, cols, *, C, M
):
    i = pl.program_id(0)

    @pl.when(i == 0)
    def _():
        log_step = rates_ref[0]
        decay = rates_ref[1]
        freq = rates_ref[2]
        step_size = jnp.exp(log_step)
        real_rate = -jnp.exp(decay)
        re = step_size * real_rate
        im = step_size * freq
        growth = jnp.exp(re)
        sin, cos = sincos(im)
        num_re = growth * cos - 1.0
        num_im = growth * sin
        den = real_rate * real_rate + freq * freq
        in_re = (num_re * real_rate + num_im * freq) / den
        in_im = (num_im * real_rate - num_re * freq) / den
        coef = coef_ref[...]
        first = lane_iota(coef.shape) < B // 2
        w = coef * in_re + swap_halves(coef) * jnp.where(first, -in_im, in_im)
        wout_ref[...] = w
        sin, cos = sincos(im * float(B))
        mag = jnp.exp(re * float(B))
        a_re, a_im = mag * cos, mag * sin
        for k in range(jump_ref.shape[0] // 2):
            jump_ref[2 * k] = a_re
            jump_ref[2 * k + 1] = jnp.where(first, -a_im, a_im)
            a_re, a_im = a_re * a_re - a_im * a_im, 2.0 * a_re * a_im
        pad = jnp.zeros((B - C, B), F32)
        cols[0] = jnp.concatenate([re, pad], axis=0).T
        cols[1] = jnp.concatenate([im, pad], axis=0).T
        cols[2] = jnp.concatenate([w, pad], axis=0).T

    back = (B - i * G) % B
    al = pltpu.roll(cols[0, 0:M, :], back, 1)
    om = pltpu.roll(cols[1, 0:M, :], back, 1)
    ww = pltpu.roll(cols[2], back, 1)
    place = lane_iota((M, B)).astype(F32)
    ahead = float(B) - place
    rows = row_iota((B, B))
    lanes = lane_iota((B, B))
    zero = jnp.zeros((M, B), BF16)
    for j in range(G):
        a = jnp.broadcast_to(al[:, j : j + 1], (M, B))
        o = jnp.broadcast_to(om[:, j : j + 1], (M, B))
        w = [jnp.broadcast_to(ww[q * M : (q + 1) * M, j : j + 1], (M, B)) for q in range(4)]
        sin, cos = sincos(o * place)
        mag = jnp.exp(a * place)
        n_re, n_im = mag * cos, mag * sin
        sin, cos = sincos(o * ahead)
        mag = jnp.exp(a * ahead)
        f_re, f_im = mag * cos, mag * sin
        for q, part in enumerate(split(n_re)):
            near_ref[j, q * B : q * B + M, :] = part
            near_ref[j, q * B + M : q * B + 2 * M, :] = part
        for q, part in enumerate(split(n_im)):
            near_ref[j, q * B + 2 * M : q * B + 3 * M, :] = part
            near_ref[j, q * B + 3 * M : q * B + 4 * M, :] = part
        for q, (re_part, im_part) in enumerate(zip(split(f_re), split(f_im))):
            f_ref[j, q * B : q * B + M, 0:B] = re_part
            f_ref[j, q * B : q * B + M, B:] = zero
            f_ref[j, q * B + M : q * B + 2 * M, 0:B] = zero
            f_ref[j, q * B + M : q * B + 2 * M, B:] = re_part
            f_ref[j, q * B + 2 * M : q * B + 3 * M, 0:B] = im_part
            f_ref[j, q * B + 2 * M : q * B + 3 * M, B:] = zero
            f_ref[j, q * B + 3 * M : q * B + 4 * M, 0:B] = zero
            f_ref[j, q * B + 3 * M : q * B + 4 * M, B:] = im_part
        for h in range(2):
            w_re, w_im = 2.0 * w[h], 2.0 * w[2 + h]
            e_re = w_re * n_re - w_im * n_im
            e_im = -(w_re * n_im + w_im * n_re)
            for q, part in enumerate(split(e_re)):
                w_ref[j, h * M : (h + 1) * M, q * B : (q + 1) * B] = part
            for q, part in enumerate(split(e_im)):
                w_ref[j, (2 + h) * M : (3 + h) * M, q * B : (q + 1) * B] = part
            kern = jnp.broadcast_to(jnp.sum(e_re, axis=0, keepdims=True), (B, B))
            toe = jnp.where(lanes >= rows, pltpu.roll(kern, 0, 1, stride=1, stride_axis=0), 0.0)
            for q, part in enumerate(split(toe)):
                t_ref[j, h * B : (h + 1) * B, q * B : (q + 1) * B] = part
            b_re = w_re * f_re - w_im * f_im
            b_im = -(w_re * f_im + w_im * f_re)
            for q, part in enumerate(split(b_re)):
                wb_ref[j, 0:M, (2 * q + h) * B : (2 * q + h + 1) * B] = part
                wb_ref[j, M : 2 * M, (2 * q + h) * B : (2 * q + h + 1) * B] = zero
            for q, part in enumerate(split(b_im)):
                wb_ref[j, 2 * M : 3 * M, (2 * q + h) * B : (2 * q + h + 1) * B] = part
                wb_ref[j, 3 * M : 4 * M, (2 * q + h) * B : (2 * q + h + 1) * B] = zero


def token_stats(stat_ref, length, count):
    mean = stat_ref[0]
    inv = lax.rsqrt(stat_ref[1] * (1.0 / count) + EPS)
    place = row_iota(mean.shape) * B + lane_iota(mean.shape)
    return mean, inv, (place < length).astype(F32)


def mixer_kernel(
    len_ref, vec_ref, x_ref, stat_ref, f_ref, w_ref, t_ref, jump_ref,
    mixed_ref, slope_ref, state_ref, lift_ref, xs, ms, tok, *, count,
):
    i = pl.program_id(0)
    C, L = x_ref.shape
    N = L // B
    nt = mixed_ref.shape[2]

    @pl.when(i == 0)
    def _():
        for n in range(N):
            xs[n * C : (n + 1) * C, :] = x_ref[:, n * B : (n + 1) * B].astype(F32)
        mean, inv, mask = token_stats(stat_ref, len_ref[0], count)
        tok[0] = mean
        tok[1] = inv
        tok[2] = mask

    ahead = float(B) - lane_iota((N, B)).astype(F32)
    for j in range(G):
        ci = i * G + j
        mask = tok[2]
        normed = (xs[pl.ds(ci, N, stride=C), :] - tok[0]) * tok[1]
        sig = mask * (normed * vec_ref[0, ci] + vec_ref[1, ci])
        liq = sig * shift_token(sig, 1)
        u = jnp.concatenate([sig, liq], axis=1)
        u2 = jnp.concatenate([sig * ahead, liq * ahead], axis=1)
        u_hi, u_lo = split(u)
        u2_hi, u2_lo = split(u2)
        up = dot(jnp.concatenate([u_hi, u_lo, u2_hi, u2_lo], axis=0), f_ref[j], NT)
        lift = up[2 * N : 3 * N, :B] + (up[2 * N : 3 * N, B:] + up[3 * N :, :B])
        state = scan_rows(up[:N, :B] + (up[:N, B:] + up[N : 2 * N, :B]), jump_ref, ci, 1)
        s_hi, s_lo = split(state)
        out = dot(jnp.concatenate([u_hi, u_lo], axis=0), t_ref[j]) + dot(
            jnp.concatenate([s_hi, s_lo], axis=0), w_ref[j]
        )
        y = out[:N, :B] + (out[:N, B:] + out[N:, :B]) + vec_ref[2, ci] * sig
        y2 = y * y
        th = jnp.tanh(0.7978845608028654 * (y + 0.044715 * (y * y2)))
        half = 0.5 * (1.0 + th)
        ms[pl.ds(pl.multiple_of(ci * N, N), N), :] = mask * (y * half)
        slope_ref[j] = mask * (half + 0.5 * y * (1.0 - th * th) * (0.7978845608028654 * (1.0 + 0.134145 * y2)))
        state_ref[j] = state
        lift_ref[j] = lift

    @pl.when(i == pl.num_programs(0) - 1)
    def _():
        per = nt // B
        for n in range(N):
            mixed_ref[n // per, :, (n % per) * B : (n % per + 1) * B] = ms[pl.ds(n, C, stride=N), :].astype(BF16)


def glu_kernel(half_ref, mixed_ref, first_ref, other_ref, lay_ref, gm_ref, keep_ref, send_ref, gp, wt, *, C):
    mp, _, nt = mixed_ref.shape
    H = mp * C
    kh = H // nt
    own = half_ref[0]
    mixed = mixed_ref[...].reshape(H, nt)
    for q in range(kh):
        at = slice(q * nt, (q + 1) * nt)
        wt[own, :, at] = first_ref[:, (2 + q) * C : (3 + q) * C, :].reshape(H, nt)
        wt[1 - own, :, at] = other_ref[:, q * C : (q + 1) * C, :].reshape(H, nt)
    step = B
    per = step // C
    at = (2 + kh) * C
    bias = first_ref[:, at : at + 16, 0:B].astype(F32)[:, 0, :]
    bias = jnp.concatenate([bias, jnp.zeros((B - mp, B), F32)], axis=0).T
    for s in range(mp // per):
        lo = s * step
        col_v = jnp.concatenate([bias[0:C, k : k + 1] for k in range(s * per, (s + 1) * per)], axis=0)
        col_g = jnp.concatenate([bias[C : 2 * C, k : k + 1] for k in range(s * per, (s + 1) * per)], axis=0)
        value = dot(wt[0, lo : lo + step, :], mixed) + col_v
        gate = dot(wt[1, lo : lo + step, :], mixed) + col_g
        sig = jax.nn.sigmoid(gate)
        x = first_ref[s * per : (s + 1) * per, 0:C, :].reshape(step, nt).astype(F32)
        g = first_ref[s * per : (s + 1) * per, C : 2 * C, :].reshape(step, nt).astype(F32)
        lay_ref[s * per : (s + 1) * per] = (x + value * sig).astype(BF16).reshape(per, C, nt)
        gv = g * sig
        gp[0, lo : lo + step, :] = gv.astype(BF16)
        gp[1, lo : lo + step, :] = (gv * value * (1.0 - sig)).astype(BF16)
    for s in range(mp // per):
        at = slice(s * step, (s + 1) * step)
        gm = dot(wt[0, :, at], gp[0], TN) + dot(wt[1, :, at], gp[1], TN)
        hi, lo = split(gm)
        gm_ref[s * per : (s + 1) * per, 0:C, :] = hi.reshape(per, C, nt)
        gm_ref[s * per : (s + 1) * per, C:, :] = lo.reshape(per, C, nt)
    keep_ref[...] = gp[own]
    send_ref[...] = gp[1 - own]


def weight_kernel(keep_ref, got_ref, mixed_ref, theirs_ref, lay_ref, pay_ref):
    mp, C, nt = mixed_ref.shape
    H = mp * C
    kh = H // nt
    step = B
    per = step // C
    pay_ref[:, 0:C, :] = lay_ref[...]
    mixed = mixed_ref[...].reshape(H, nt)
    theirs = theirs_ref[...].reshape(H, nt)
    ones = jnp.ones((16, nt), BF16)
    rows = row_iota((16, B))
    at = (1 + 2 * kh) * C
    for s in range(mp // per):
        mine, other = keep_ref[s * step : (s + 1) * step, :], got_ref[s * step : (s + 1) * step, :]
        parts = split(dot(mine, mixed, NT) + dot(other, theirs, NT))
        for q in range(kh):
            for h, part in enumerate(parts):
                lo = (1 + 2 * q + h) * C
                pay_ref[s * per : (s + 1) * per, lo : lo + C, :] = part[:, q * nt : (q + 1) * nt].reshape(per, C, nt)
        hi, lo = split(dot(ones, mine, NT) + dot(ones, other, NT))
        put = jnp.where(rows == 0, hi.astype(F32), jnp.where(rows == 1, lo.astype(F32), 0.0)).astype(BF16)
        for k in range(per):
            pay_ref[s * per + k, at : at + 16, 0:B] = put
            if nt > B:
                pay_ref[s * per + k, at : at + 16, B:] = jnp.zeros((16, nt - B), BF16)


def back_kernel(
    len_ref, vec_ref, x_ref, stat_ref, gm_ref, slope_ref, state_ref, lift_ref,
    t_ref, wb_ref, near_ref, jump_ref,
    gn_ref, sum_ref, row_ref, xs, gs, ns, tok, *, count,
):
    i = pl.program_id(0)
    C, L = x_ref.shape
    N = L // B
    nt = gm_ref.shape[2]
    per = nt // B

    @pl.when(i == 0)
    def _():
        for n in range(N):
            xs[n * C : (n + 1) * C, :] = x_ref[:, n * B : (n + 1) * B].astype(F32)
            at = slice((n % per) * B, (n % per + 1) * B)
            gs[n * C : (n + 1) * C, :] = gm_ref[n // per, 0:C, at].astype(F32) + gm_ref[n // per, C:, at].astype(F32)
        mean, inv, mask = token_stats(stat_ref, len_ref[0], count)
        tok[0] = mean
        tok[1] = inv
        tok[2] = mask
        sum_ref[...] = jnp.zeros_like(sum_ref)

    place = lane_iota((N, B)).astype(F32)
    lag = lane_iota((8, B)).astype(F32)
    rows2 = row_iota((B, B))
    lanes2 = lane_iota((B, B))
    flip = (lanes2 + rows2 == B - 1).astype(BF16)
    rows16 = row_iota((16, B))
    for j in range(G):
        ci = i * G + j
        mask = tok[2]
        normed = (xs[pl.ds(ci, N, stride=C), :] - tok[0]) * tok[1]
        sig = mask * (normed * vec_ref[0, ci] + vec_ref[1, ci])
        prev = shift_token(sig, 1)
        liq = sig * prev
        u_hi, u_lo = split(jnp.concatenate([sig, liq], axis=1))
        g = gs[pl.ds(ci, N, stride=C), :] * slope_ref[j]
        g_hi, g_lo = split(g)
        g3 = jnp.concatenate([g_hi, g_hi, g_lo], axis=0)
        sums = []
        for q in range(2):
            at = slice(q * B, (q + 1) * B)
            turned = dot(flip, jnp.concatenate([u_hi[:, at], u_lo[:, at], u_hi[:, at]], axis=0), NT).astype(BF16)
            corr = jnp.where(lanes2 + rows2 >= B - 1, dot(turned, g3), 0.0)
            sums.append(jnp.sum(pltpu.roll(corr, 1, 1, stride=1, stride_axis=0), axis=0, keepdims=True))
        main, liquid = sums
        lags = jnp.where(rows16 == 0, main, jnp.where(rows16 == 1, liquid, 0.0))
        lags = jnp.where(rows16 == 2, main * lag[0:1], jnp.where(rows16 == 3, liquid * lag[0:1], lags))
        left_hi, left_lo = split(jnp.concatenate([g, g * place, lags], axis=0))
        R = 2 * N + 16
        z = dot(jnp.concatenate([left_hi, left_lo], axis=0), near_ref[j], NT)
        z = z[:R, :B] + (z[:R, B:] + z[R:, :B])
        p, p_place, inner = z[:N], z[N : 2 * N], z[2 * N :]
        r = scan_rows(p, jump_ref, ci, -1)
        r_hi, r_lo = split(r)
        lhs_g = jnp.concatenate([g_hi, g_lo], axis=0)
        big = dot(jnp.concatenate([r_hi, r_lo], axis=0), wb_ref[j])
        one = dot(lhs_g, t_ref[j, :, :B], NT)
        two = dot(g_hi, t_ref[j, :, B:], NT)
        both = one[:N] + (one[N:] + two) + (big[:N, : 2 * B] + (big[:N, 2 * B :] + big[N:, : 2 * B]))
        gl = both[:, B:]
        grad = both[:, :B] + vec_ref[2, ci] * g + gl * prev + shift_token(gl * sig, -1)
        masked = mask * grad
        gn = masked * vec_ref[0, ci]
        sum_ref[0] += gn
        sum_ref[1] += gn * normed
        ns[pl.ds(pl.multiple_of(ci * N, N), N), :] = gn
        state, lift = state_ref[j], lift_ref[j]
        state_x, r_x = swap_halves(state), swap_halves(r)
        carry = p_place + float(B) * (r * jump_ref[0, pl.ds(ci, 1), :] + r_x * jump_ref[1, pl.ds(ci, 1), :])
        total = [
            p * state, p * state_x,
            carry * state + lift * r, carry * state_x + lift * r_x,
            masked * normed, masked, g * sig,
        ]
        put = jnp.where(rows16 >= 8, pltpu.roll(inner, 8, 0), 0.0)
        for q, v in enumerate(total):
            put = jnp.where(rows16 == q, jnp.sum(v, axis=0, keepdims=True), put)
        row_ref[j] = put

    @pl.when(i == pl.num_programs(0) - 1)
    def _():
        for n in range(N):
            gn_ref[:, n * B : (n + 1) * B] = ns[pl.ds(n, C, stride=N), :]


def last_kernel(x_ref, g_ref, gn_ref, stat_ref, sum_ref, out_ref, *, count):
    C, L = x_ref.shape
    for n in range(L // B):
        at = slice(n * B, (n + 1) * B)
        mean = stat_ref[0, n : n + 1, :]
        inv = lax.rsqrt(stat_ref[1, n : n + 1, :] * (1.0 / count) + EPS)
        first = sum_ref[0, n : n + 1, :] * (1.0 / count)
        second = sum_ref[1, n : n + 1, :] * (1.0 / count)
        normed = (x_ref[:, at].astype(F32) - mean) * inv
        out_ref[:, at] = inv * (gn_ref[:, at] - first - normed * second) + g_ref[:, at].astype(F32)


def gather_kernel(pay_ref, out_ref, sum_ref):
    mp, _, nt = pay_ref.shape
    C = out_ref.shape[0]
    kh = sum_ref.shape[1] // nt
    for s in range(mp):
        out_ref[:, s * nt : (s + 1) * nt] = pay_ref[s, 0:C, :]
    for q in range(kh):
        at = slice((1 + 2 * q) * C, (3 + 2 * q) * C)
        total = jnp.sum(pay_ref[:, at, :].astype(F32), axis=0)
        sum_ref[0:C, q * nt : (q + 1) * nt] = total[:C] + total[C:]
    tail = jnp.sum(pay_ref[:, (1 + 2 * kh) * C :, 0:B].astype(F32), axis=0)
    sum_ref[C:, 0:B] = jnp.broadcast_to(tail[0:1] + tail[1:2], (8, B))
    sum_ref[C:, B:] = jnp.zeros((8, sum_ref.shape[1] - B), F32)


def rounds_of(size):
    rounds, bit = [], 1
    while bit < size:
        if bit * 2 < size:
            rounds.append((bit, 2 * bit, 3 * bit))
            bit *= 4
        else:
            rounds.append((bit,))
            bit *= 2
    return rounds


def exchange(v, axis, size, off):
    return lax.ppermute(v, axis, [(k, k ^ off) for k in range(size)])


def all_stats(stat, size, local):
    count = float(local)
    for offs in rounds_of(size):
        parts = [stat] + [exchange(stat, "mp", size, o) for o in offs]
        mean = sum(p[0] for p in parts) * (1.0 / len(parts))
        spread = sum(p[1] for p in parts) + count * sum((p[0] - mean) * (p[0] - mean) for p in parts)
        stat = jnp.stack([mean, spread])
        count *= len(parts)
    return stat


def all_sums(v, size):
    for offs in rounds_of(size):
        v = sum([exchange(v, "mp", size, o) for o in offs], v)
    return v


def sum_docs(v, size, stride):
    total = v
    for k in range(stride, size, stride):
        total = total + lax.ppermute(v, "dp", [(q, (q + k) % size) for q in range(size)])
    return total


def partner(v, size):
    return lax.ppermute(v, "dp", [(q, q ^ 1) for q in range(size)])


def mode_terms(log_step, decay_log, frequency, readout, liquid_readout):
    M = decay_log.shape[1]
    step_size = jnp.exp(log_step)[:, None]
    real_rate = -jnp.exp(decay_log)
    real_step = step_size * real_rate
    imag_step = step_size * frequency
    growth = jnp.exp(real_step)
    num_real = growth * jnp.cos(imag_step) - 1.0
    num_imag = growth * jnp.sin(imag_step)
    denominator = real_rate * real_rate + frequency * frequency
    in_real = (num_real * real_rate + num_imag * frequency) / denominator
    in_imag = (num_imag * real_rate - num_real * frequency) / denominator

    def mix(coeffs):
        re, im = coeffs[:, :M], coeffs[:, M:]
        return re * in_real - im * in_imag, re * in_imag + im * in_real

    return mix(readout) + mix(liquid_readout) + (real_step, imag_step)


def per_device(
    mp, dp,
    tokens, lengths, norm_gain, norm_bias, log_step, decay_log, frequency, readout, liquid_readout,
    skip_gain, value_weight, gate_weight, value_bias, gate_bias, grad_out,
):
    C, L = tokens.shape
    H = value_weight.shape[0]
    M = decay_log.shape[1]
    N = L // B
    nt = L // mp
    kh = H // nt
    steps = max(1, (N - 1).bit_length())
    shape = jax.ShapeDtypeStruct

    half = lax.rem(lax.axis_index("dp"), 2).astype(jnp.int32)
    halves = half.reshape(1)
    bias = jnp.pad(jnp.concatenate([value_bias, gate_bias])[None], ((0, 15), (0, nt - 2 * C)))
    weights = jnp.stack([value_weight.T, gate_weight.T])
    stat, pay = pl.pallas_call(
        start_kernel,
        out_shape=(shape((2, N, B), F32), shape((mp, (2 + kh) * C + 16, nt), BF16)),
        in_specs=[SMEM] + [VMEM] * 4,
        out_specs=(VMEM, VMEM),
        compiler_params=params(),
        cost_estimate=cost(2),
    )(halves, tokens, grad_out, weights, bias)
    first = lax.all_to_all(pay, "mp", split_axis=0, concat_axis=0, tiled=True)
    other = partner(first[:, 2 * C : (2 + kh) * C, :], dp)

    rates = jnp.stack(
        [jnp.broadcast_to(log_step[:, None], (C, 4 * M)), jnp.tile(decay_log, (1, 4)), jnp.tile(frequency, (1, 4))]
    )
    coef = jnp.concatenate([readout[:, :M], liquid_readout[:, :M], readout[:, M:], liquid_readout[:, M:]], axis=1)

    def whole(*dims):
        return pl.BlockSpec(dims, lambda i: (0,) * len(dims))

    def chan(*dims):
        return pl.BlockSpec((G,) + dims, lambda i: (i,) + (0,) * len(dims))

    f_tab, w_tab, t_tab, wb_tab, near_tab, jump, w_all = pl.pallas_call(
        partial(table_kernel, C=C, M=M),
        grid=(C // G,),
        out_shape=(
            shape((C, 2 * B, 2 * B), BF16),
            shape((C, B, 2 * B), BF16),
            shape((C, 2 * B, 2 * B), BF16),
            shape((C, B, 4 * B), BF16),
            shape((C, 2 * B, B), BF16),
            shape((2 * steps, C, B), F32),
            shape((C, B), F32),
        ),
        in_specs=[whole(3, C, B), whole(C, B)],
        out_specs=(
            chan(2 * B, 2 * B), chan(B, 2 * B), chan(2 * B, 2 * B), chan(B, 4 * B), chan(2 * B, B),
            whole(2 * steps, C, B), whole(C, B),
        ),
        scratch_shapes=[pltpu.VMEM((3, B, B), F32)],
        compiler_params=params(),
        cost_estimate=cost(8),
    )(rates, coef)

    stat = all_stats(stat, mp, C)
    vecs = jnp.stack([norm_gain, norm_bias, skip_gain])
    mixed, slope, state, lift = pl.pallas_call(
        partial(mixer_kernel, count=H),
        grid=(C // G,),
        out_shape=(
            shape((mp, C, nt), BF16), shape((C, N, B), F32), shape((C, N, B), F32), shape((C, N, B), F32),
        ),
        in_specs=[
            SMEM, SMEM, whole(C, L), whole(2, N, B), chan(2 * B, 2 * B), chan(B, 2 * B), chan(2 * B, 2 * B),
            whole(2 * steps, C, B),
        ],
        out_specs=(whole(mp, C, nt), chan(N, B), chan(N, B), chan(N, B)),
        scratch_shapes=[pltpu.VMEM((N * C, B), F32), pltpu.VMEM((N * C, B), F32), pltpu.VMEM((3, N, B), F32)],
        compiler_params=params(),
        cost_estimate=cost(18),
    )(lengths, vecs, tokens, stat, f_tab, w_tab, t_tab, jump)

    mixed, first, other = lax.optimization_barrier((mixed, first, other))
    mixed_tok = lax.all_to_all(mixed, "mp", split_axis=0, concat_axis=0, tiled=True)
    theirs = partner(mixed_tok, dp)
    lay, gm, keep, send = pl.pallas_call(
        partial(glu_kernel, C=C),
        out_shape=(
            shape((mp, C, nt), BF16), shape((mp, 2 * C, nt), BF16), shape((H, nt), BF16), shape((H, nt), BF16),
        ),
        in_specs=[SMEM] + [VMEM] * 3,
        out_specs=(VMEM,) * 4,
        scratch_shapes=[pltpu.VMEM((2, H, nt), BF16), pltpu.VMEM((2, H, H), BF16)],
        compiler_params=params(),
        cost_estimate=cost(3),
    )(halves, mixed_tok, first, other)
    gm = lax.all_to_all(gm, "mp", split_axis=0, concat_axis=0, tiled=True)
    pay = pl.pallas_call(
        weight_kernel,
        out_shape=shape((mp, (1 + 2 * kh) * C + 16, nt), BF16),
        in_specs=[VMEM] * 5,
        out_specs=VMEM,
        compiler_params=params(),
        cost_estimate=cost(2),
    )(keep, partner(send, dp), mixed_tok, theirs, lay)
    pay, gm = lax.optimization_barrier((pay, gm))
    third = lax.all_to_all(pay, "mp", split_axis=0, concat_axis=0, tiled=True)

    gn, sums, rows = pl.pallas_call(
        partial(back_kernel, count=H),
        grid=(C // G,),
        out_shape=(shape((C, L), F32), shape((2, N, B), F32), shape((C, 16, B), F32)),
        in_specs=[
            SMEM, SMEM, whole(C, L), whole(2, N, B), whole(mp, 2 * C, nt), chan(N, B), chan(N, B), chan(N, B),
            chan(2 * B, 2 * B), chan(B, 4 * B), chan(2 * B, B), whole(2 * steps, C, B),
        ],
        out_specs=(whole(C, L), whole(2, N, B), chan(16, B)),
        scratch_shapes=[
            pltpu.VMEM((N * C, B), F32), pltpu.VMEM((N * C, B), F32), pltpu.VMEM((N * C, B), F32),
            pltpu.VMEM((3, N, B), F32),
        ],
        compiler_params=params(),
        cost_estimate=cost(32),
    )(lengths, vecs, tokens, stat, gm, slope, state, lift, t_tab, wb_tab, near_tab, jump)

    sums, third = lax.optimization_barrier((sums, third))
    sums = all_sums(sums, mp)
    grad_tokens = pl.pallas_call(
        partial(last_kernel, count=H),
        out_shape=shape((C, L), F32),
        in_specs=[VMEM] * 5,
        out_specs=VMEM,
        compiler_params=params(),
        cost_estimate=cost(1),
    )(tokens, grad_out, gn, stat, sums)

    layer_out, wsum = pl.pallas_call(
        gather_kernel,
        out_shape=(shape((C, L), BF16), shape((C + 8, H), F32)),
        in_specs=[VMEM],
        out_specs=(VMEM, VMEM),
        compiler_params=params(),
        cost_estimate=cost(1),
    )(third)
    wsum = sum_docs(wsum, dp, 2)
    rows = sum_docs(rows, dp, 1)
    across = partner(wsum, dp)
    value_all = jnp.where(half == 0, wsum, across)
    gate_all = jnp.where(half == 0, across, wsum)
    value_wgrad, gate_wgrad = value_all[:C].T, gate_all[:C].T
    at = (lax.axis_index("mp") % (B // C)) * C
    value_bgrad = lax.dynamic_slice(value_all[C], (at,), (C,))
    gate_bgrad = lax.dynamic_slice(gate_all[C], (at,), (C,))

    half = B // 2

    def complex_rows(a, b):
        return rows[:, a, :half] - rows[:, a, half:], rows[:, b, :half] + rows[:, b, half:]

    g_re, g_im = complex_rows(0, 1)
    d_re, d_im = complex_rows(2, 3)
    main, liquid = slice(0, M), slice(M, 2 * M)

    def inner(a, part):
        lo = half if part else 0
        return jnp.concatenate([rows[:, a, lo : lo + M], rows[:, a + 1, lo + M : lo + 2 * M]], axis=1)

    g_re, g_im = g_re + inner(8, 0), g_im + inner(8, 1)
    d_re, d_im = d_re + inner(10, 0), d_im + inner(10, 1)
    w_re, w_im = w_all[:, :half], w_all[:, half:]
    l_re = w_re * d_re - w_im * d_im
    l_im = w_re * d_im + w_im * d_re
    cot = (
        2.0 * g_re[:, main], -2.0 * g_im[:, main], 2.0 * g_re[:, liquid], -2.0 * g_im[:, liquid],
        2.0 * (l_re[:, main] + l_re[:, liquid]), -2.0 * (l_im[:, main] + l_im[:, liquid]),
    )
    _, back = jax.vjp(mode_terms, log_step, decay_log, frequency, readout, liquid_readout)
    step_grad, decay_grad, frequency_grad, readout_grad, liquid_grad = back(cot)
    plain = jnp.sum(rows[:, 4:7, :], axis=2)
    return (
        layer_out, grad_tokens, plain[:, 0], plain[:, 1], step_grad, decay_grad, frequency_grad, readout_grad,
        liquid_grad, plain[:, 2], value_wgrad, gate_wgrad, value_bgrad, gate_bgrad,
    )


def solution(mesh):
    row, col, act = P("mp"), P(None, "mp"), P("mp", "dp")
    wide = P("mp", None)
    in_specs = (act, P("dp"), row, row, row, wide, wide, wide, wide, row, col, col, row, row, act)
    out_specs = (act, act, row, row, row, wide, wide, wide, wide, row, col, col, row, row)
    return jax.shard_map(
        partial(per_device, mesh.shape["mp"], mesh.shape["dp"]),
        mesh=mesh, in_specs=in_specs, out_specs=out_specs, check_vma=False,
    )
```

```python
from functools import partial

import jax
import jax.numpy as jnp
import numpy as np
from jax import lax
from jax.experimental import pallas as pl
from jax.experimental.pallas import tpu as pltpu
from jax.sharding import PartitionSpec as P

B = 128
G = 8
F32 = jnp.float32
BF16 = jnp.bfloat16
NN = (((1,), (0,)), ((), ()))
NT = (((1,), (1,)), ((), ()))
TN = (((0,), (0,)), ((), ()))
EPS = 1e-05
VMEM = pl.BlockSpec(memory_space=pltpu.VMEM)
SMEM = pl.BlockSpec(memory_space=pltpu.SMEM)


def params(mb):
    return pltpu.CompilerParams(vmem_limit_bytes=mb * 1024 * 1024)


def cost(us):
    return pl.CostEstimate(flops=int(us * 1e9), bytes_accessed=int(us * 1e6), transcendentals=0)


def dot(a, b, dims=NN):
    return lax.dot_general(a, b, dims, preferred_element_type=F32)


def split(v):
    hi = v.astype(BF16)
    return hi, (v - hi.astype(F32)).astype(BF16)


def sincos(x):
    k = jnp.floor(x * 0.6366197723675814 + 0.5)
    y = ((x - k * 1.5703125) - k * 4.837512969970703e-4) - k * 7.54978995489188e-8
    y2 = y * y
    s = y + y * y2 * (-1.6666654611e-1 + y2 * (8.3321608736e-3 - y2 * 1.9515295891e-4))
    c = 1.0 - 0.5 * y2 + y2 * y2 * (4.166664568298827e-2 + y2 * (-1.388731625493765e-3 + y2 * 2.443315711809948e-5))
    q = k.astype(jnp.int32)
    odd = (q & 1) == 1
    sin = jnp.where(odd, c, s)
    cos = jnp.where(odd, s, c)
    sin = jnp.where((q & 2) == 2, -sin, sin)
    cos = jnp.where(((q + 1) & 2) == 2, -cos, cos)
    return sin, cos


def row_iota(shape):
    return lax.broadcasted_iota(jnp.int32, shape, 0)


def lane_iota(shape):
    return lax.broadcasted_iota(jnp.int32, shape, 1)


def shift_token(x, k):
    n = x.shape[0]
    lanes = lane_iota(x.shape)
    rows = row_iota(x.shape)
    turned = pltpu.roll(x, k % B, 1)
    wrapped = pltpu.roll(turned, k % n, 0)
    if k > 0:
        wrapped = jnp.where(rows >= 1, wrapped, 0.0)
        return jnp.where(lanes == 0, wrapped, turned)
    wrapped = jnp.where(rows < n - 1, wrapped, 0.0)
    return jnp.where(lanes == B - 1, wrapped, turned)


def swap_halves(x):
    return pltpu.roll(x, B // 2, 1)


def scan_blocks(v_ref, out_ref, turned_ref, jump, N, backward):
    a_re, a_im = jump
    s = jnp.zeros((G, B), F32)
    t = s
    for k in range(N):
        n = N - 1 - k if backward else k
        out_ref[pl.ds(n, G, stride=N), :] = s
        turned_ref[pl.ds(n, G, stride=N), :] = t
        v = v_ref[pl.ds(n, G, stride=N), :]
        s, t = a_re * s + (a_im * t + v), a_re * t + (swap_halves(v) - a_im * s)


def start_kernel(place_ref, bias_ref, x_hbm, g_hbm, v_hbm, w_hbm, stat_ref, pay_ref, x_ref, g_ref, wt_ref, sems):
    C, L = x_ref.shape
    N = L // B
    mp, rows, nt = pay_ref.shape
    kh = rows // C - 2
    moves = [pltpu.make_async_copy(x_hbm, x_ref, sems.at[0]), pltpu.make_async_copy(g_hbm, g_ref, sems.at[1])]
    for move in moves:
        move.start()
    for half, ref in enumerate((v_hbm, w_hbm)):

        @pl.when(place_ref[0] == half)
        def _():
            pltpu.make_async_copy(ref, wt_ref, sems.at[2]).start()

    moves[0].wait()
    for n in range(N):
        x = x_ref[:, n * B : (n + 1) * B].astype(F32)
        mean = jnp.sum(x, axis=0, keepdims=True) * (1.0 / C)
        dev = x - mean
        stat_ref[n : n + 1, :] = mean
        stat_ref[N + n : N + n + 1, :] = jnp.sum(dev * dev, axis=0, keepdims=True)
    own = row_iota((mp, B))
    stat_ref[2 * N :, :] = jnp.where(own == place_ref[1], bias_ref[...], 0.0)
    for j in range(mp):
        pay_ref[j, kh * C : (kh + 1) * C, :] = x_ref[:, j * nt : (j + 1) * nt]
    moves[1].wait()
    for j in range(mp):
        pay_ref[j, (kh + 1) * C :, :] = g_ref[:, j * nt : (j + 1) * nt]
    pltpu.make_async_copy(v_hbm, wt_ref, sems.at[2]).wait()
    for j in range(mp):
        for q in range(kh):
            pay_ref[j, q * C : (q + 1) * C, :] = wt_ref[:, q * nt : (q + 1) * nt]


def join_stats(parts, N, count):
    mean = sum(p[:N] for p in parts) * (1.0 / len(parts))
    spread = sum(p[N : 2 * N] for p in parts) + count * sum((p[:N] - mean) * (p[:N] - mean) for p in parts)
    return mean, spread, sum(p[2 * N :] for p in parts)


def columns(arrays, cols, C):
    pad = jnp.zeros((B - C, B), F32)
    for q, v in enumerate(arrays):
        cols[q] = jnp.concatenate([v, pad], axis=0).T


def channel_waves(cols, i, M):
    back = (B - i * G) % B
    al = pltpu.roll(cols[0, 0:M, :], back, 1)
    om = pltpu.roll(cols[1, 0:M, :], back, 1)
    ww = 2.0 * pltpu.roll(cols[2], back, 1)
    place = lane_iota((M, B)).astype(F32)
    ahead = float(B) - place
    out = []
    for j in range(G):
        a = jnp.broadcast_to(al[:, j : j + 1], (M, B))
        o = jnp.broadcast_to(om[:, j : j + 1], (M, B))
        w = [jnp.broadcast_to(ww[q * M : (q + 1) * M, j : j + 1], (M, B)) for q in range(4)]
        sin, cos = sincos(o * place)
        mag = jnp.exp(a * place)
        near = mag * cos, mag * sin
        sin, cos = sincos(o * ahead)
        mag = jnp.exp(a * ahead)
        out.append((near, (mag * cos, mag * sin), w))
    return out


def toeplitz_rows(kern, start):
    return pltpu.roll(jnp.broadcast_to(kern, (B, B)), start, 1, stride=1, stride_axis=0)


def table_kernel(rates_ref, coef_ref, f_ref, again_ref, t_ref, jump_ref, wout_ref, cols, *, C, M):
    i = pl.program_id(0)

    @pl.when(i == 0)
    def _():
        step_size = jnp.exp(rates_ref[0])
        real_rate = -jnp.exp(rates_ref[1])
        freq = rates_ref[2]
        re = step_size * real_rate
        im = step_size * freq
        growth = jnp.exp(re)
        sin, cos = sincos(im)
        num_re = growth * cos - 1.0
        num_im = growth * sin
        den = real_rate * real_rate + freq * freq
        in_re = (num_re * real_rate + num_im * freq) / den
        in_im = (num_im * real_rate - num_re * freq) / den
        coef = coef_ref[...]
        first = lane_iota(coef.shape) < B // 2
        w = coef * in_re + swap_halves(coef) * jnp.where(first, -in_im, in_im)
        wout_ref[...] = w
        sin, cos = sincos(im * float(B))
        mag = jnp.exp(re * float(B))
        jump_ref[0] = mag * cos
        jump_ref[1] = mag * jnp.where(first, -sin, sin)
        columns((re, im, w), cols, C)

    rows = row_iota((B, B))
    lanes = lane_iota((B, B))
    odd = (lanes & M) == M
    every = range(G)
    waves = channel_waves(cols, i, M)
    feeds = [jnp.concatenate([f_re, f_re, f_im, f_im], axis=0).T for _, (f_re, f_im), _ in waves]
    kerns = []
    for j in every:
        (n_re, n_im), _, w = waves[j]
        for h in range(2):
            w_re, w_im = w[h], w[2 + h]
            e_re = w_re * n_re - w_im * n_im
            e_im = -(w_re * n_im + w_im * n_re)
            kerns.append(jnp.sum(e_re, axis=0, keepdims=True))
            for q, v in enumerate(split(e_re)):
                t_ref[j, 2 * B + h * M : 2 * B + (h + 1) * M, q * B : (q + 1) * B] = v
            for q, v in enumerate(split(e_im)):
                t_ref[j, 2 * B + (2 + h) * M : 2 * B + (3 + h) * M, q * B : (q + 1) * B] = v
    rolled = [toeplitz_rows(kern, 0) for kern in kerns]
    for j in every:
        for h in range(2):
            part = jnp.where(odd if h == 1 else ~odd, feeds[j], 0.0)
            for q, v in enumerate(split(part)):
                f_ref[j, h * B : (h + 1) * B, q * B : (q + 1) * B] = v
                again_ref[j, h * B : (h + 1) * B, q * B : (q + 1) * B] = v
            toe = jnp.where(lanes >= rows, rolled[2 * j + h], 0.0)
            for q, v in enumerate(split(toe)):
                t_ref[j, h * B : (h + 1) * B, q * B : (q + 1) * B] = v


def back_table_kernel(rates_ref, w_ref, t_ref, near_ref, cols, *, C, M):
    i = pl.program_id(0)

    @pl.when(i == 0)
    def _():
        step_size = jnp.exp(rates_ref[0])
        columns((step_size * -jnp.exp(rates_ref[1]), step_size * rates_ref[2], w_ref[...]), cols, C)

    rows = row_iota((B, B))
    lanes = lane_iota((B, B))
    zero = jnp.zeros((M, B), BF16)
    every = range(G)
    waves = channel_waves(cols, i, M)
    turned = [jnp.concatenate([n_re, n_re, n_im, n_im], axis=0).T for (n_re, n_im), _, _ in waves]
    kerns, starts = [], []
    for j in every:
        (n_re, n_im), (f_re, f_im), w = waves[j]
        for h in range(2):
            w_re, w_im = w[h], w[2 + h]
            b_re = w_re * f_re - w_im * f_im
            b_im = -(w_re * f_im + w_im * f_re)
            kerns.append(jnp.sum(b_re, axis=0, keepdims=True))
            starts.append(jnp.sum(w_re * n_re - w_im * n_im, axis=0, keepdims=True)[:, 0:1])
            for part, v2 in ((0, b_re), (2, b_im)):
                for q, v in enumerate(split(v2)):
                    at = slice((2 * q + h) * B, (2 * q + h + 1) * B)
                    t_ref[j, B + part * M : B + (part + 1) * M, at] = v
                    t_ref[j, B + (part + 1) * M : B + (part + 2) * M, at] = zero
    rolled = [toeplitz_rows(kern, 0) for kern in kerns]
    for j in every:
        for q, v in enumerate(split(turned[j])):
            near_ref[j, :, q * B : (q + 1) * B] = v
        for h in range(2):
            start = jnp.broadcast_to(starts[2 * j + h], (B, B))
            toe = jnp.where(lanes < rows, rolled[2 * j + h], jnp.where(lanes == rows, start, 0.0))
            for q, v in enumerate(split(toe)):
                t_ref[j, 0:B, (2 * q + h) * B : (2 * q + h + 1) * B] = v


def token_stats(stat_ref, length, count):
    mean = stat_ref[0]
    inv = lax.rsqrt(stat_ref[1] * (1.0 / count) + EPS)
    place = row_iota(mean.shape) * B + lane_iota(mean.shape)
    return mean, inv, (place < length).astype(F32)


def mixer_kernel(len_ref, vec_ref, x_ref, *refs, count, parts):
    part_refs, refs = refs[:parts], refs[parts:]
    f_ref, t_ref, jump_ref = refs[:3]
    mixed_ref, slope_ref, state_ref, other_ref, stat_ref, bias_ref = refs[3:9]
    xs, ms, tok, us, ups, sts, ots = refs[9:]
    i = pl.program_id(0)
    C, L = x_ref.shape
    N = L // B
    nt = mixed_ref.shape[2]

    @pl.when(i == 0)
    def _():
        for n in range(N):
            xs[n * C : (n + 1) * C, :] = x_ref[:, n * B : (n + 1) * B].astype(F32)
        stat_ref[0], stat_ref[1], bias_ref[...] = join_stats([r[...] for r in part_refs], N, count / parts)
        mean, inv, mask = token_stats(stat_ref, len_ref[0], count)
        tok[0] = mean
        tok[1] = inv
        tok[2] = mask

    for j in range(G):
        ci = i * G + j
        normed = (xs[pl.ds(ci, N, stride=C), :] - tok[0]) * tok[1]
        sig = tok[2] * (normed * vec_ref[0, ci] + vec_ref[1, ci])
        liq = sig * shift_token(sig, 1)
        for q, v in enumerate((sig, liq)):
            hi, lo = split(v)
            us[j, 0:N, q * B : (q + 1) * B] = hi
            us[j, N:, q * B : (q + 1) * B] = lo
        slope_ref[j] = sig
    ups_all = [dot(us[j], f_ref[j]) for j in range(G)]
    for j, up in enumerate(ups_all):
        ups[j * N : (j + 1) * N, :] = up[:N, :B] + (up[:N, B:] + up[N:, :B])
    at = pl.ds(pl.multiple_of(i * G, G), G)
    scan_blocks(ups, sts, ots, (jump_ref[0, at, :], jump_ref[1, at, :]), N, False)
    left = []
    for j in range(G):
        state = sts[j * N : (j + 1) * N, :]
        state_ref[j] = state
        other_ref[j] = ots[j * N : (j + 1) * N, :]
        left.append(jnp.concatenate([us[j], jnp.concatenate(split(state), axis=0)], axis=1))
    outs = [dot(left[j], t_ref[j]) for j in range(G)]
    for j, out in enumerate(outs):
        ci = i * G + j
        mask = tok[2]
        y = out[:N, :B] + (out[:N, B:] + out[N:, :B]) + vec_ref[2, ci] * slope_ref[j]
        y2 = y * y
        th = jnp.tanh(0.7978845608028654 * (y + 0.044715 * (y * y2)))
        half = 0.5 * (1.0 + th)
        ms[pl.ds(pl.multiple_of(ci * N, N), N), :] = mask * (y * half)
        slope_ref[j] = mask * (half + 0.5 * y * (1.0 - th * th) * (0.7978845608028654 * (1.0 + 0.134145 * y2)))

    @pl.when(i == pl.num_programs(0) - 1)
    def _():
        per = nt // B
        for n in range(N):
            mixed_ref[n // per, :, (n % per) * B : (n % per + 1) * B] = ms[pl.ds(n, C, stride=N), :].astype(BF16)


def glu_kernel(half_ref, in_ref, first_ref, other_ref, bias_ref, gm_ref, keep_ref, send_ref, gp, wt):
    mp, C, nt = in_ref.shape
    H = mp * C
    kh = H // nt
    own = half_ref[0]
    mixed = in_ref[...].reshape(H, nt)
    for q in range(kh):
        at = slice(q * nt, (q + 1) * nt)
        wt[own, :, at] = first_ref[:, q * C : (q + 1) * C, :].reshape(H, nt)
        wt[1 - own, :, at] = other_ref[:, q * C : (q + 1) * C, :].reshape(H, nt)
    step = B
    per = step // C
    bias = jnp.concatenate([bias_ref[...], jnp.zeros((B - mp, B), F32)], axis=0).T
    for s in range(mp // per):
        lo = s * step
        col_v = jnp.concatenate([bias[0:C, k : k + 1] for k in range(s * per, (s + 1) * per)], axis=0)
        col_g = jnp.concatenate([bias[C : 2 * C, k : k + 1] for k in range(s * per, (s + 1) * per)], axis=0)
        value = dot(wt[0, lo : lo + step, :], mixed) + col_v
        gate = dot(wt[1, lo : lo + step, :], mixed) + col_g
        sig = jax.nn.sigmoid(gate)
        x = first_ref[s * per : (s + 1) * per, kh * C : (kh + 1) * C, :].reshape(step, nt).astype(F32)
        g = first_ref[s * per : (s + 1) * per, (kh + 1) * C :, :].reshape(step, nt).astype(F32)
        gm_ref[s * per : (s + 1) * per, 2 * C :, :] = (x + value * sig).astype(BF16).reshape(per, C, nt)
        gv = g * sig
        gp[0, lo : lo + step, :] = gv.astype(BF16)
        gp[1, lo : lo + step, :] = (gv * value * (1.0 - sig)).astype(BF16)
    for s in range(mp // per):
        at = slice(s * step, (s + 1) * step)
        gm = dot(wt[0, :, at], gp[0], TN) + dot(wt[1, :, at], gp[1], TN)
        hi, lo = split(gm)
        gm_ref[s * per : (s + 1) * per, 0:C, :] = hi.reshape(per, C, nt)
        gm_ref[s * per : (s + 1) * per, C : 2 * C, :] = lo.reshape(per, C, nt)
    keep_ref[...] = gp[own]
    send_ref[...] = gp[1 - own]


def weight_kernel(place_ref, keep_ref, got_ref, mixed_ref, theirs_ref, *refs, C, mp):
    outs, wg = refs[:-1], refs[-1]
    nt = mixed_ref.shape[1]
    ways = len(outs)
    per = mp // ways
    total = dot(keep_ref[...], mixed_ref[...], NT) + dot(got_ref[...], theirs_ref[...], NT)
    for m in range(mp):
        at = (m // ways) * C
        wg[m % ways, at : at + C, :] = total[m * C : (m + 1) * C]
    ones = jnp.ones((8, nt), BF16)
    tail = dot(ones, keep_ref[...], NT) + dot(ones, got_ref[...], NT)
    for q in range(ways):
        wg[q, per * C :, :] = tail
    for k in range(ways):
        outs[k][...] = wg[lax.rem(place_ref[1], ways) ^ k]


def fold_kernel(place_ref, *refs, ways, got, C, seen):
    parts, outs, acc = refs[:got], refs[got:-1], refs[-1]
    total = parts[0][...]
    for p in parts[1:]:
        total = total + p[...]
    blocks = (total.shape[0] - 8) // C
    for z in range(blocks):
        at = (z // ways) * C
        acc[z % ways, at : at + C, :] = total[z * C : (z + 1) * C]
    for q in range(ways):
        acc[q, (blocks // ways) * C :, :] = total[blocks * C :]
    for k in range(ways):
        outs[k][...] = acc[lax.rem(lax.div(place_ref[1], seen), ways) ^ k]


def back_kernel(
    len_ref, vec_ref, x_ref, stat_ref, gm_ref, slope_ref, t_ref, near_ref, jump_ref,
    gn_ref, sum_ref, row_ref, g_ref, p_ref, r_ref, turned_ref, xs, gs, ns, tok, hs, ps, rs, rts, tab, sem, *, count,
):
    i = pl.program_id(0)
    C, L = x_ref.shape
    N = L // B
    nt = gm_ref.shape[2]
    per = nt // B

    def fetch(k):
        at = pl.ds(k * G, G)
        return pltpu.make_async_copy(t_ref.at[at], tab.at[at], sem.at[k])

    @pl.when(i == 0)
    def _():
        for k in range(C // G):
            fetch(k).start()
        for n in range(N):
            xs[n * C : (n + 1) * C, :] = x_ref[:, n * B : (n + 1) * B].astype(F32)
            at = slice((n % per) * B, (n % per + 1) * B)
            gs[n * C : (n + 1) * C, :] = gm_ref[n // per, 0:C, at].astype(F32) + gm_ref[n // per, C : 2 * C, at].astype(F32)
        mean, inv, mask = token_stats(stat_ref, len_ref[0], count)
        tok[0] = mean
        tok[1] = inv
        tok[2] = mask
        sum_ref[...] = jnp.zeros_like(sum_ref)

    for j in range(G):
        ci = i * G + j
        g = gs[pl.ds(ci, N, stride=C), :] * slope_ref[j]
        g_ref[j] = g
        hi, lo = split(g)
        hs[j, 0:N, :] = hi
        hs[j, N:, :] = lo
    z_all = [dot(hs[j], near_ref[j]) for j in range(G)]
    for j, z in enumerate(z_all):
        p = z[:N, :B] + (z[:N, B:] + z[N:, :B])
        p_ref[j] = p
        ps[j * N : (j + 1) * N, :] = p
    at = pl.ds(pl.multiple_of(i * G, G), G)
    scan_blocks(ps, rs, rts, (jump_ref[0, at, :], jump_ref[1, at, :]), N, True)
    left = []
    for j in range(G):
        r = rs[j * N : (j + 1) * N, :]
        r_ref[j] = r
        turned_ref[j] = rts[j * N : (j + 1) * N, :]
        left.append(jnp.concatenate([hs[j], jnp.concatenate(split(r), axis=0)], axis=1))
    fetch(i).wait()
    both_all = [dot(left[j], tab[i * G + j]) for j in range(G)]
    for j, both in enumerate(both_all):
        ci = i * G + j
        mask = tok[2]
        normed = (xs[pl.ds(ci, N, stride=C), :] - tok[0]) * tok[1]
        sig = mask * (normed * vec_ref[0, ci] + vec_ref[1, ci])
        both = both[:N, : 2 * B] + (both[:N, 2 * B :] + both[N:, : 2 * B])
        gl = both[:, B:]
        grad = both[:, :B] + vec_ref[2, ci] * g_ref[j] + gl * shift_token(sig, 1) + shift_token(gl * sig, -1)
        masked = mask * grad
        gn = masked * vec_ref[0, ci]
        sum_ref[0] += gn
        sum_ref[1] += gn * normed
        ns[pl.ds(pl.multiple_of(ci * N, N), N), :] = gn
        for q, v in enumerate((g_ref[j] * sig, masked * normed, masked)):
            row_ref[j, q * 8 : (q + 1) * 8, :] = sum(v[8 * k : 8 * k + 8] for k in range(N // 8))

    @pl.when(i == pl.num_programs(0) - 1)
    def _():
        for n in range(N):
            gn_ref[:, n * B : (n + 1) * B] = ns[pl.ds(n, C, stride=N), :]


def lift_kernel(len_ref, vec_ref, x_ref, stat_ref, f_ref, u_ref, lift_ref, xs, tok, *, count):
    i = pl.program_id(0)
    C, L = x_ref.shape
    N = L // B

    @pl.when(i == 0)
    def _():
        for n in range(N):
            xs[n * C : (n + 1) * C, :] = x_ref[:, n * B : (n + 1) * B].astype(F32)
        tok[0], tok[1], tok[2] = token_stats(stat_ref, len_ref[0], count)

    ahead = float(B) - lane_iota((N, B)).astype(F32)
    flip = (lane_iota((B, B)) + row_iota((B, B)) == B - 1).astype(BF16)
    flat, left = [], []
    for j in range(G):
        ci = i * G + j
        normed = (xs[pl.ds(ci, N, stride=C), :] - tok[0]) * tok[1]
        sig = tok[2] * (normed * vec_ref[0, ci] + vec_ref[1, ci])
        liq = sig * shift_token(sig, 1)
        flat.append(jnp.concatenate(split(sig) + split(liq), axis=0))
        left.append(jnp.concatenate(split(jnp.concatenate([sig * ahead, liq * ahead], axis=1)), axis=0))
    turned_all = [dot(v, flip).astype(BF16) for v in flat]
    lifts = [dot(left[j], f_ref[j]) for j in range(G)]
    for j in range(G):
        turned, lift = turned_all[j], lifts[j]
        for q in range(2):
            at = slice(q * B, (q + 1) * B)
            u_ref[j, 0 : 2 * N, at] = turned[2 * q * N : (2 * q + 2) * N]
            u_ref[j, 2 * N :, at] = turned[2 * q * N : (2 * q + 1) * N]
        lift_ref[j] = lift[:N, :B] + (lift[:N, B:] + lift[N:, :B])


def sums_kernel(u_ref, lift_ref, g_ref, p_ref, r_ref, rx_ref, state_ref, sx_ref, near_ref, jump_ref, row_ref):
    i = pl.program_id(0)
    _, N, _ = g_ref.shape
    place = lane_iota((N, B)).astype(F32)
    rows2, lanes2 = row_iota((B, B)), lane_iota((B, B))
    inside = lanes2 + rows2 >= B - 1
    rows16 = row_iota((16, B))
    lag = lane_iota((16, B)).astype(F32)
    R = N + 16
    every = range(G)
    turned = []
    for j in every:
        g_hi, g_lo = split(g_ref[j])
        turned.append(jnp.concatenate([g_hi, g_hi, g_lo], axis=0).T)
    corr = [dot(turned[j], u_ref[j]) for j in every]
    left = []
    for j in every:
        lags = []
        for q in range(2):
            part = jnp.where(inside, corr[j][:, q * B : (q + 1) * B], 0.0)
            lags.append(jnp.sum(pltpu.roll(part, 1, 1, stride=1, stride_axis=0), axis=0, keepdims=True))
        pair = jnp.where((rows16 & 1) == 0, lags[0], lags[1])
        pair = jnp.where(rows16 < 2, pair, jnp.where(rows16 < 4, pair * lag, 0.0))
        left.append(jnp.concatenate(split(jnp.concatenate([g_ref[j] * place, pair], axis=0)), axis=0))
    both = [dot(left[j], near_ref[j]) for j in every]
    for j in every:
        ci = i * G + j
        z = both[j][:R, :B] + (both[j][:R, B:] + both[j][R:, :B])
        row_ref[j, 0:8, :] = z[N : N + 8]
        p, r, state, lift = p_ref[j], r_ref[j], state_ref[j], lift_ref[j]
        state_x, r_x = sx_ref[j], rx_ref[j]
        carry = z[:N] + float(B) * (r * jump_ref[0, pl.ds(ci, 1), :] + r_x * jump_ref[1, pl.ds(ci, 1), :])
        total = [p * state, p * state_x, carry * state + lift * r, carry * state_x + lift * r_x]
        for q, v in enumerate(total):
            row_ref[j, 8 + 8 * q : 16 + 8 * q, :] = sum(v[8 * k : 8 * k + 8] for k in range(N // 8))


def join_kernel(plain_ref, ref, out_ref):
    odd = (lane_iota((out_ref.shape[1], B)) & (B // 4)) != 0
    for q in range(2):
        out_ref[q] = jnp.where(odd, ref[:, 2 * q + 1, :], ref[:, 2 * q, :])
    for q in range(4):
        out_ref[2 + q] = jnp.sum(ref[:, 8 + 8 * q : 16 + 8 * q, :], axis=1)
    for q in range(3):
        out_ref[6 + q] = jnp.sum(plain_ref[:, 8 * q : 8 * q + 8, :], axis=1)


def finish_kernel(
    place_ref, mine_ref, theirs_ref, w_ref, step_ref, decay_ref, freq_ref, read_ref, liquid_ref, wsum_ref, across_ref,
    value_ref, gate_ref, vbias_ref, gbias_ref, step_out, decay_out, freq_out, read_out, liquid_out,
    skip_out, gain_out, bias_out, *, M,
):
    C = decay_ref.shape[0]
    half = B // 2

    def emit(first, second):
        value_ref[...] = first[0:C, :]
        gate_ref[...] = second[0:C, :]
        per = B // C
        group = place_ref[1] // per
        back = (B - (place_ref[1] % per) * C) % B
        for out, v in ((vbias_ref, first), (gbias_ref, second)):
            lanes = v[C : C + 8, pl.ds(pl.multiple_of(group * B, B), B)]
            out[...] = pltpu.roll(lanes, back, 1)[0:1, 0:C]

    @pl.when(place_ref[0] == 0)
    def _():
        emit(wsum_ref, across_ref)

    @pl.when(place_ref[0] == 1)
    def _():
        emit(across_ref, wsum_ref)

    rows = [mine_ref[q] + theirs_ref[q] for q in range(9)]

    def parts(a, b, c):
        return a[:, :half] - a[:, half:] + c[:, :half], b[:, :half] + b[:, half:] + c[:, half:]

    g_re, g_im = parts(rows[2], rows[3], rows[0])
    d_re, d_im = parts(rows[4], rows[5], rows[1])
    w = w_ref[...]
    w_re, w_im = w[:, :half], w[:, half:]
    l_re = w_re * d_re - w_im * d_im
    l_im = w_re * d_im + w_im * d_re
    cot = (
        2.0 * g_re[:, :M], -2.0 * g_im[:, :M], 2.0 * g_re[:, M:], -2.0 * g_im[:, M:],
        2.0 * (l_re[:, :M] + l_re[:, M:]), -2.0 * (l_im[:, :M] + l_im[:, M:]),
    )
    step = jnp.sum(jnp.where(row_iota((C, C)) == lane_iota((C, C)), step_ref[...], 0.0), axis=1, keepdims=True)
    _, back = jax.vjp(mode_terms, step, decay_ref[...], freq_ref[...], read_ref[...], liquid_ref[...])
    step_grad, decay_out[...], freq_out[...], read_out[...], liquid_out[...] = back(cot)
    lanes = lane_iota((B, B))
    pad = jnp.zeros((B - C, 1), F32)
    plain = jnp.zeros((B, B), F32)
    for q, v in enumerate([step_grad] + [jnp.sum(rows[6 + q], axis=1, keepdims=True) for q in range(3)]):
        plain = jnp.where(lanes == q, jnp.concatenate([v, pad], axis=0), plain)
    plain = plain.T
    for q, out in enumerate((step_out, skip_out, gain_out, bias_out)):
        out[...] = plain[q : q + 1, 0:C]


def last_kernel(x_ref, g_ref, gn_ref, stat_ref, sum_ref, out_ref, *, count):
    C, L = x_ref.shape
    for n in range(L // B):
        at = slice(n * B, (n + 1) * B)
        mean = stat_ref[0, n : n + 1, :]
        inv = lax.rsqrt(stat_ref[1, n : n + 1, :] * (1.0 / count) + EPS)
        first = sum_ref[0, n : n + 1, :] * (1.0 / count)
        second = sum_ref[1, n : n + 1, :] * (1.0 / count)
        normed = (x_ref[:, at].astype(F32) - mean) * inv
        out_ref[:, at] = inv * (gn_ref[:, at] - first - normed * second) + g_ref[:, at].astype(F32)


def gather_kernel(pay_ref, out_ref):
    mp, _, nt = pay_ref.shape
    C = out_ref.shape[0]
    for s in range(mp):
        out_ref[:, s * nt : (s + 1) * nt] = pay_ref[s, 2 * C :, :]


def total_kernel(*refs):
    total = refs[0][...]
    for p in refs[1:-1]:
        total = total + p[...]
    refs[-1][...] = total


def rounds_of(size):
    rounds, bit = [], 1
    while bit < size:
        if bit * 2 < size:
            rounds.append((bit, 2 * bit, 3 * bit))
            bit *= 4
        else:
            rounds.append((bit,))
            bit *= 2
    return rounds


def exchange(v, axis, size, off):
    return lax.ppermute(v, axis, [(k, k ^ off) for k in range(size)])


def all_sums(v, size):
    for offs in rounds_of(size):
        v = sum([exchange(v, "mp", size, o) for o in offs], v)
    return v


def sum_docs(v, size, stride):
    total = v
    for k in range(stride, size, stride):
        total = total + lax.ppermute(v, "dp", [(q, (q + k) % size) for q in range(size)])
    return total


def partner(v, size):
    return lax.ppermute(v, "dp", [(q, q ^ 1) for q in range(size)])


def mode_terms(log_step, decay_log, frequency, readout, liquid_readout):
    M = decay_log.shape[1]
    step_size = jnp.exp(log_step)
    real_rate = -jnp.exp(decay_log)
    real_step = step_size * real_rate
    imag_step = step_size * frequency
    growth = jnp.exp(real_step)
    num_real = growth * jnp.cos(imag_step) - 1.0
    num_imag = growth * jnp.sin(imag_step)
    denominator = real_rate * real_rate + frequency * frequency
    in_real = (num_real * real_rate + num_imag * frequency) / denominator
    in_imag = (num_imag * real_rate - num_real * frequency) / denominator

    def mix(coeffs):
        re, im = coeffs[:, :M], coeffs[:, M:]
        return re * in_real - im * in_imag, re * in_imag + im * in_real

    return mix(readout) + mix(liquid_readout) + (real_step, imag_step)


def per_device(
    mp, dp,
    tokens, lengths, norm_gain, norm_bias, log_step, decay_log, frequency, readout, liquid_readout,
    skip_gain, value_weight, gate_weight, value_bias, gate_bias, grad_out,
):
    C, L = tokens.shape
    H = value_weight.shape[0]
    M = decay_log.shape[1]
    N = L // B
    nt = L // mp
    kh = H // nt
    shape = jax.ShapeDtypeStruct

    place = jnp.stack([lax.axis_index("dp") & 1, lax.axis_index("mp")]).astype(jnp.int32)
    rounds = rounds_of(mp)
    small, large = 16, 28

    def pin(v):
        return pltpu.with_memory_space_constraint(v, pltpu.HBM)

    def call(kernel, out, n_in, smem=0, us=1, scratch=(), mb=small):
        return pl.pallas_call(
            kernel,
            out_shape=out,
            in_specs=[SMEM] * smem + [VMEM] * (n_in - smem),
            out_specs=jax.tree.map(lambda _: VMEM, out),
            scratch_shapes=list(scratch),
            compiler_params=params(mb),
            cost_estimate=cost(us),
        )

    def whole(*dims):
        return pl.BlockSpec(dims, lambda i: (0,) * len(dims))

    def chan(*dims, at=0):
        return pl.BlockSpec((G,) + dims, lambda i: (i + at,) + (0,) * len(dims))

    def by_channel(kernel, out, in_specs, out_specs, us, scratch, mb=small, channels=C):
        return pl.pallas_call(
            kernel,
            grid=(channels // G,),
            out_shape=out,
            in_specs=in_specs,
            out_specs=out_specs,
            scratch_shapes=scratch,
            compiler_params=params(mb),
            cost_estimate=cost(us),
        )

    vm = pltpu.VMEM
    blocks = shape((C, N, B), F32)
    far = pltpu.HBM
    far_blocks = far((C, N, B), F32)
    def pin(v):
        return pltpu.with_memory_space_constraint(v, far)

    bias = jnp.pad(jnp.concatenate([value_bias, gate_bias]).astype(F32)[None], ((0, 0), (0, B - 2 * C)))
    hbm = pl.BlockSpec(memory_space=pltpu.HBM)
    stat, pay = pl.pallas_call(
        start_kernel,
        out_shape=(shape((2 * N + mp, B), F32), shape((mp, (2 + kh) * C, nt), BF16)),
        in_specs=[SMEM, VMEM, hbm, hbm, hbm, hbm],
        out_specs=(VMEM, VMEM),
        scratch_shapes=[
            pltpu.VMEM((C, L), BF16), pltpu.VMEM((C, L), BF16), pltpu.VMEM((C, H), BF16), pltpu.SemaphoreType.DMA((3,)),
        ],
        compiler_params=params(small),
        cost_estimate=cost(3),
    )(place, bias, pin(tokens), pin(grad_out), pin(value_weight.T), pin(gate_weight.T))
    first = lax.all_to_all(pay, "mp", split_axis=0, concat_axis=0, tiled=True)

    rates = jnp.stack(
        [jnp.broadcast_to(log_step[:, None], (C, 4 * M)), jnp.tile(decay_log, (1, 4)), jnp.tile(frequency, (1, 4))]
    )
    coef = jnp.concatenate([readout[:, :M], liquid_readout[:, :M], readout[:, M:], liquid_readout[:, M:]], axis=1)
    f_near, f_tab, t_tab, jump, w_all = by_channel(
        partial(table_kernel, C=C, M=M),
        (
            shape((C, 2 * B, 2 * B), BF16), far((C, 2 * B, 2 * B), BF16), shape((C, 3 * B, 2 * B), BF16),
            shape((2, C, B), F32), shape((C, B), F32),
        ),
        [whole(3, C, B), whole(C, B)],
        (chan(2 * B, 2 * B), chan(2 * B, 2 * B), chan(3 * B, 2 * B), whole(2, C, B), whole(C, B)),
        6,
        [vm((3, B, B), F32)],
    )(rates, coef)

    count = C
    for k, offs in enumerate(rounds[::-1]):
        parts = [stat] + [exchange(stat, "mp", mp, o) for o in offs]
        if k == 0:
            parts[1], parts[-1], t_tab = lax.optimization_barrier((parts[1], parts[-1], t_tab))
        if k < len(rounds) - 1:
            stat = jnp.concatenate(join_stats(parts, N, float(count)), axis=0)
            count *= len(parts)

    vecs = jnp.stack([norm_gain, norm_bias, skip_gain])
    mixed, slope, state, state_x, stat, bias = by_channel(
        partial(mixer_kernel, count=H, parts=len(parts)),
        (shape((mp, C, nt), BF16), far_blocks, far_blocks, far_blocks, shape((2, N, B), F32), shape((mp, B), F32)),
        [SMEM, SMEM, whole(C, L)] + [whole(2 * N + mp, B)] * len(parts)
        + [chan(2 * B, 2 * B), chan(3 * B, 2 * B), whole(2, C, B)],
        (whole(mp, C, nt), chan(N, B), chan(N, B), chan(N, B), whole(2, N, B), whole(mp, B)),
        6,
        [
            vm((N * C, B), F32), vm((N * C, B), F32), vm((3, N, B), F32), vm((G, 2 * N, 2 * B), BF16),
            vm((G * N, B), F32), vm((G * N, B), F32), vm((G * N, B), F32),
        ],
    )(lengths, vecs, tokens, *parts, f_near, t_tab, jump)

    mixed, first, rates = lax.optimization_barrier((mixed, first, rates))
    other_w = partner(first[:, : kh * C, :], dp)
    mixed_tok = lax.all_to_all(mixed, "mp", split_axis=0, concat_axis=0, tiled=True)
    back_tab, near_tab = by_channel(
        partial(back_table_kernel, C=C, M=M),
        (far((C, 2 * B, 4 * B), BF16), far((C, B, 2 * B), BF16)),
        [whole(3, C, B), whole(C, B)],
        (chan(2 * B, 4 * B), chan(B, 2 * B)),
        7,
        [vm((3, B, B), F32)],
    )(rates, w_all)
    mixed_tok, back_tab = lax.optimization_barrier((mixed_tok, back_tab))
    gm, keep, send = call(
        glu_kernel,
        (shape((mp, 3 * C, nt), BF16),) + (shape((H, nt), BF16),) * 2,
        5, 1, 2, [vm((2, H, nt), BF16), vm((2, H, H), BF16)],
    )(place, mixed_tok, first, other_w, bias)
    mixed_tok = mixed_tok.reshape(H, nt)
    gm, f_tab = lax.optimization_barrier((gm, f_tab))
    gm = lax.all_to_all(gm, "mp", split_axis=0, concat_axis=0, tiled=True)
    u_rev, lift = by_channel(
        partial(lift_kernel, count=H),
        (far((C, 3 * N, 2 * B), BF16), far_blocks),
        [SMEM, SMEM, whole(C, L), whole(2, N, B), chan(2 * B, 2 * B)],
        (chan(3 * N, 2 * B), chan(N, B)),
        3,
        [vm((N * C, B), F32), vm((3, N, B), F32)],
        56,
    )(lengths, vecs, tokens, stat, pin(f_tab))
    gm, lift = lax.optimization_barrier((gm, lift))

    ways = len(rounds[0]) + 1
    rows_left = mp // ways
    outs = call(
        partial(weight_kernel, C=C, mp=mp), (shape((rows_left * C + 8, H), F32),) * ways, 5, 1, 2,
        [vm((ways, rows_left * C + 8, H), F32)],
    )(place, keep, partner(send, dp), mixed_tok, partner(mixed_tok, dp))
    terms = [outs[0]] + [exchange(v, "mp", mp, o) for v, o in zip(outs[1:], rounds[0])]

    gn, sums, plain, g_pre, p_blk, r_blk, rx_blk = by_channel(
        partial(back_kernel, count=H),
        (shape((C, L), F32), shape((2, N, B), F32), shape((C, 24, B), F32)) + (blocks,) * 4,
        [
            SMEM, SMEM, whole(C, L), whole(2, N, B), whole(mp, 3 * C, nt), chan(N, B),
            pl.BlockSpec(memory_space=pltpu.HBM), chan(B, 2 * B), whole(2, C, B),
        ],
        (whole(C, L), whole(2, N, B), chan(24, B)) + (chan(N, B),) * 4,
        7,
        [
            vm((N * C, B), F32), vm((N * C, B), F32), vm((N * C, B), F32), vm((3, N, B), F32),
            vm((G, 2 * N, B), BF16), vm((G * N, B), F32), vm((G * N, B), F32), vm((G * N, B), F32),
            vm((C, 2 * B, 4 * B), BF16), pltpu.SemaphoreType.DMA((C // G,)),
        ],
        large,
    )(lengths, vecs, tokens, stat, gm, pin(slope), pin(back_tab), pin(near_tab), jump)

    for k, offs in enumerate(rounds[::-1]):
        got = [exchange(sums, "mp", mp, o) for o in offs]
        if k == len(rounds) - 1:
            g_pre, sums = lax.optimization_barrier((g_pre, sums))
            rows = by_channel(
                sums_kernel,
                shape((C, 40, B), F32),
                [chan(3 * N, 2 * B)] + [chan(N, B)] * 7 + [chan(B, 2 * B), whole(2, C, B)],
                chan(40, B),
                20,
                [],
            )(pin(u_rev), pin(lift), g_pre, p_blk, r_blk, rx_blk, pin(state), pin(state_x), pin(near_tab), jump)
            *got, rows = lax.optimization_barrier((*got, rows))
        sums = sum(got, sums)
    grad_tokens = call(partial(last_kernel, count=H), shape((C, L), F32), 5)(tokens, grad_out, gn, stat, sums)
    layer_out = call(gather_kernel, shape((C, L), BF16), 1)(gm)
    rows = call(join_kernel, shape((9, C, B), F32), 2)(plain, rows)
    others = sum_docs(rows, dp, 1) - rows if dp > 2 else partner(rows, dp)

    seen = ways
    terms[0], plain = lax.optimization_barrier((terms[0], plain))
    for offs in rounds[1:]:
        ways = len(offs) + 1
        rows_left //= ways
        outs = call(
            partial(fold_kernel, ways=ways, got=len(terms), C=C, seen=seen),
            (shape((rows_left * C + 8, H), F32),) * ways,
            1 + len(terms), 1, 1, [vm((ways, rows_left * C + 8, H), F32)],
        )(place, *terms)
        terms = [outs[0]] + [exchange(v, "mp", mp, o) for v, o in zip(outs[1:], offs)]
        seen *= ways
    wsum = call(total_kernel, shape((C + 8, H), F32), len(terms))(*terms)
    wsum = sum_docs(wsum, dp, 2)
    across = partner(wsum, dp)
    thin, wide = shape((C, M), F32), shape((C, 2 * M), F32)
    line = shape((1, C), F32)
    (
        value_wgrad, gate_wgrad, vb, gb, step_grad, decay_grad, frequency_grad, readout_grad, liquid_grad,
        skip_grad, gain_grad, bias_grad,
    ) = call(
        partial(finish_kernel, M=M),
        (shape((C, H), F32), shape((C, H), F32), line, line, line, thin, thin, wide, wide, line, line, line),
        11, 1,
    )(
        place, rows, others, w_all, log_step[None], decay_log, frequency, readout, liquid_readout, wsum, across,
    )
    return (
        layer_out, grad_tokens, gain_grad[0], bias_grad[0], step_grad[0], decay_grad, frequency_grad, readout_grad,
        liquid_grad, skip_grad[0], value_wgrad.T, gate_wgrad.T, vb[0], gb[0],
    )


def solution(mesh):
    row, col, act = P("mp"), P(None, "mp"), P("mp", "dp")
    wide = P("mp", None)
    in_specs = (act, P("dp"), row, row, row, wide, wide, wide, wide, row, col, col, row, row, act)
    out_specs = (act, act, row, row, row, wide, wide, wide, wide, row, col, col, row, row)
    return jax.shard_map(
        partial(per_device, mesh.shape["mp"], mesh.shape["dp"]),
        mesh=mesh, in_specs=in_specs, out_specs=out_specs, check_vma=False,
    )
```

```python
from functools import partial

import jax
import jax.numpy as jnp
import numpy as np
from jax import lax
from jax.experimental import pallas as pl
from jax.experimental.pallas import tpu as pltpu
from jax.sharding import PartitionSpec as P

B = 128
TABLE_GROUP = 8
MIXER_GROUP = 16
F32 = jnp.float32
BF16 = jnp.bfloat16
NN = (((1,), (0,)), ((), ()))
NT = (((1,), (1,)), ((), ()))
TN = (((0,), (0,)), ((), ()))
EPS = 1e-05
VMEM = pl.BlockSpec(memory_space=pltpu.VMEM)
SMEM = pl.BlockSpec(memory_space=pltpu.SMEM)


def params(mb):
    return pltpu.CompilerParams(vmem_limit_bytes=mb * 1024 * 1024)


def cost(us):
    return pl.CostEstimate(flops=int(us * 1e9), bytes_accessed=int(us * 1e6), transcendentals=0)


def dot(a, b, dims=NN):
    return lax.dot_general(a, b, dims, preferred_element_type=F32)


def split(v):
    hi = v.astype(BF16)
    return hi, (v - hi.astype(F32)).astype(BF16)


def sincos(x):
    k = jnp.floor(x * 0.6366197723675814 + 0.5)
    y = ((x - k * 1.5703125) - k * 4.837512969970703e-4) - k * 7.54978995489188e-8
    y2 = y * y
    s = y + y * y2 * (-1.6666654611e-1 + y2 * (8.3321608736e-3 - y2 * 1.9515295891e-4))
    c = 1.0 - 0.5 * y2 + y2 * y2 * (4.166664568298827e-2 + y2 * (-1.388731625493765e-3 + y2 * 2.443315711809948e-5))
    q = k.astype(jnp.int32)
    odd = (q & 1) == 1
    sin = jnp.where(odd, c, s)
    cos = jnp.where(odd, s, c)
    sin = jnp.where((q & 2) == 2, -sin, sin)
    cos = jnp.where(((q + 1) & 2) == 2, -cos, cos)
    return sin, cos


def row_iota(shape):
    return lax.broadcasted_iota(jnp.int32, shape, 0)


def lane_iota(shape):
    return lax.broadcasted_iota(jnp.int32, shape, 1)


def shift_token(x, k):
    n = x.shape[0]
    lanes = lane_iota(x.shape)
    rows = row_iota(x.shape)
    turned = pltpu.roll(x, k % B, 1)
    wrapped = pltpu.roll(turned, k % n, 0)
    if k > 0:
        wrapped = jnp.where(rows >= 1, wrapped, 0.0)
        return jnp.where(lanes == 0, wrapped, turned)
    wrapped = jnp.where(rows < n - 1, wrapped, 0.0)
    return jnp.where(lanes == B - 1, wrapped, turned)


def swap_halves(x):
    return pltpu.roll(x, B // 2, 1)


def scan_blocks(v_ref, out_ref, turned_ref, jump, N, backward):
    a_re, a_im = jump
    G = v_ref.shape[0] // N
    s = jnp.zeros((G, B), F32)
    t = s
    for k in range(N):
        n = N - 1 - k if backward else k
        out_ref[pl.ds(n, G, stride=N), :] = s
        turned_ref[pl.ds(n, G, stride=N), :] = t
        v = v_ref[pl.ds(n, G, stride=N), :]
        s, t = a_re * s + (a_im * t + v), a_re * t + (swap_halves(v) - a_im * s)


def start_kernel(
    place_ref, x_hbm, g_hbm, v_hbm, w_hbm, vb_hbm, gb_hbm, stat_ref, pay_ref, x_ref, g_ref, wt_ref, vb_ref, gb_ref, sems,
):
    C, L = x_ref.shape
    N = L // B
    mp, rows, nt = pay_ref.shape
    kh = rows // C - 2
    pairs = ((x_hbm, x_ref), (g_hbm, g_ref), (vb_hbm, vb_ref), (gb_hbm, gb_ref))
    moves = [pltpu.make_async_copy(src, dst, sems.at[1 + k]) for k, (src, dst) in enumerate(pairs)]
    for move in moves:
        move.start()
    for half, ref in enumerate((v_hbm, w_hbm)):

        @pl.when(place_ref[0] == half)
        def _():
            pltpu.make_async_copy(ref, wt_ref, sems.at[0]).start()

    moves[0].wait()
    for n in range(N):
        x = x_ref[:, n * B : (n + 1) * B].astype(F32)
        mean = jnp.sum(x, axis=0, keepdims=True) * (1.0 / C)
        dev = x - mean
        stat_ref[n : n + 1, :] = mean
        stat_ref[N + n : N + n + 1, :] = jnp.sum(dev * dev, axis=0, keepdims=True)
    own = row_iota((mp, B))
    moves[2].wait()
    moves[3].wait()
    bias = jnp.concatenate([vb_ref[...].astype(F32), gb_ref[...].astype(F32), jnp.zeros((1, B - 2 * C), F32)], axis=1)
    stat_ref[2 * N :, :] = jnp.where(own == place_ref[1], bias, 0.0)
    for j in range(mp):
        pay_ref[j, kh * C : (kh + 1) * C, :] = x_ref[:, j * nt : (j + 1) * nt]
    moves[1].wait()
    for j in range(mp):
        pay_ref[j, (kh + 1) * C :, :] = g_ref[:, j * nt : (j + 1) * nt]
    pltpu.make_async_copy(v_hbm, wt_ref, sems.at[0]).wait()
    for j in range(mp):
        for q in range(kh):
            pay_ref[j, q * C : (q + 1) * C, :] = wt_ref[:, q * nt : (q + 1) * nt]


def join_stats(parts, N, count):
    mean = sum(p[:N] for p in parts) * (1.0 / len(parts))
    spread = sum(p[N : 2 * N] for p in parts) + count * sum((p[:N] - mean) * (p[:N] - mean) for p in parts)
    return mean, spread, sum(p[2 * N :] for p in parts)


def columns(arrays, cols, C):
    pad = jnp.zeros((B - C, B), F32)
    for q, v in enumerate(arrays):
        cols[q] = jnp.concatenate([v, pad], axis=0).T


def channel_waves(cols, i, M, G):
    back = (B - i * G) % B
    al = pltpu.roll(cols[0, 0:M, :], back, 1)
    om = pltpu.roll(cols[1, 0:M, :], back, 1)
    ww = 2.0 * pltpu.roll(cols[2], back, 1)
    place = lane_iota((M, B)).astype(F32)
    ahead = float(B) - place
    out = []
    for j in range(G):
        a = jnp.broadcast_to(al[:, j : j + 1], (M, B))
        o = jnp.broadcast_to(om[:, j : j + 1], (M, B))
        w = [jnp.broadcast_to(ww[q * M : (q + 1) * M, j : j + 1], (M, B)) for q in range(4)]
        sin, cos = sincos(o * place)
        mag = jnp.exp(a * place)
        near = mag * cos, mag * sin
        sin, cos = sincos(o * ahead)
        mag = jnp.exp(a * ahead)
        out.append((near, (mag * cos, mag * sin), w))
    return out


def toeplitz_rows(kern, start):
    return pltpu.roll(jnp.broadcast_to(kern, (B, B)), start, 1, stride=1, stride_axis=0)


def table_kernel(rates_ref, coef_ref, f_ref, again_ref, t_ref, jump_ref, wout_ref, cols, *, C, M):
    i = pl.program_id(0)
    G = f_ref.shape[0]

    @pl.when(i == 0)
    def _():
        step_size = jnp.exp(rates_ref[0])
        real_rate = -jnp.exp(rates_ref[1])
        freq = rates_ref[2]
        re = step_size * real_rate
        im = step_size * freq
        growth = jnp.exp(re)
        sin, cos = sincos(im)
        num_re = growth * cos - 1.0
        num_im = growth * sin
        den = real_rate * real_rate + freq * freq
        in_re = (num_re * real_rate + num_im * freq) / den
        in_im = (num_im * real_rate - num_re * freq) / den
        coef = coef_ref[...]
        first = lane_iota(coef.shape) < B // 2
        w = coef * in_re + swap_halves(coef) * jnp.where(first, -in_im, in_im)
        wout_ref[...] = w
        sin, cos = sincos(im * float(B))
        mag = jnp.exp(re * float(B))
        jump_ref[0] = mag * cos
        jump_ref[1] = mag * jnp.where(first, -sin, sin)
        columns((re, im, w), cols, C)

    rows = row_iota((B, B))
    lanes = lane_iota((B, B))
    odd = (lanes & M) == M
    every = range(G)
    waves = channel_waves(cols, i, M, G)
    feeds = [jnp.concatenate([f_re, f_re, f_im, f_im], axis=0).T for _, (f_re, f_im), _ in waves]
    kerns = []
    for j in every:
        (n_re, n_im), _, w = waves[j]
        for h in range(2):
            w_re, w_im = w[h], w[2 + h]
            e_re = w_re * n_re - w_im * n_im
            e_im = -(w_re * n_im + w_im * n_re)
            kerns.append(jnp.sum(e_re, axis=0, keepdims=True))
            for q, v in enumerate(split(e_re)):
                t_ref[j, 2 * B + h * M : 2 * B + (h + 1) * M, q * B : (q + 1) * B] = v
            for q, v in enumerate(split(e_im)):
                t_ref[j, 2 * B + (2 + h) * M : 2 * B + (3 + h) * M, q * B : (q + 1) * B] = v
    rolled = [toeplitz_rows(kern, 0) for kern in kerns]
    for j in every:
        for h in range(2):
            part = jnp.where(odd if h == 1 else ~odd, feeds[j], 0.0)
            for q, v in enumerate(split(part)):
                f_ref[j, h * B : (h + 1) * B, q * B : (q + 1) * B] = v
                again_ref[j, h * B : (h + 1) * B, q * B : (q + 1) * B] = v
            toe = jnp.where(lanes >= rows, rolled[2 * j + h], 0.0)
            for q, v in enumerate(split(toe)):
                t_ref[j, h * B : (h + 1) * B, q * B : (q + 1) * B] = v


def back_table_kernel(rates_ref, w_ref, t_ref, near_ref, cols, *, C, M):
    i = pl.program_id(0)
    G = t_ref.shape[0]

    @pl.when(i == 0)
    def _():
        step_size = jnp.exp(rates_ref[0])
        columns((step_size * -jnp.exp(rates_ref[1]), step_size * rates_ref[2], w_ref[...]), cols, C)

    rows = row_iota((B, B))
    lanes = lane_iota((B, B))
    zero = jnp.zeros((M, B), BF16)
    every = range(G)
    waves = channel_waves(cols, i, M, G)
    turned = [jnp.concatenate([n_re, n_re, n_im, n_im], axis=0).T for (n_re, n_im), _, _ in waves]
    kerns, starts = [], []
    for j in every:
        (n_re, n_im), (f_re, f_im), w = waves[j]
        for h in range(2):
            w_re, w_im = w[h], w[2 + h]
            b_re = w_re * f_re - w_im * f_im
            b_im = -(w_re * f_im + w_im * f_re)
            kerns.append(jnp.sum(b_re, axis=0, keepdims=True))
            starts.append(jnp.sum(w_re * n_re - w_im * n_im, axis=0, keepdims=True)[:, 0:1])
            for part, v2 in ((0, b_re), (2, b_im)):
                for q, v in enumerate(split(v2)):
                    at = slice((2 * q + h) * B, (2 * q + h + 1) * B)
                    t_ref[j, B + part * M : B + (part + 1) * M, at] = v
                    t_ref[j, B + (part + 1) * M : B + (part + 2) * M, at] = zero
    rolled = [toeplitz_rows(kern, 0) for kern in kerns]
    for j in every:
        for q, v in enumerate(split(turned[j])):
            near_ref[j, :, q * B : (q + 1) * B] = v
        for h in range(2):
            start = jnp.broadcast_to(starts[2 * j + h], (B, B))
            toe = jnp.where(lanes < rows, rolled[2 * j + h], jnp.where(lanes == rows, start, 0.0))
            for q, v in enumerate(split(toe)):
                t_ref[j, 0:B, (2 * q + h) * B : (2 * q + h + 1) * B] = v


def token_stats(stat_ref, length, count):
    mean = stat_ref[0]
    inv = lax.rsqrt(stat_ref[1] * (1.0 / count) + EPS)
    place = row_iota(mean.shape) * B + lane_iota(mean.shape)
    return mean, inv, (place < length).astype(F32)


def mixer_kernel(len_ref, vec_ref, x_ref, *refs, count, parts):
    part_refs, refs = refs[:parts], refs[parts:]
    f_ref, t_ref, jump_ref = refs[:3]
    mixed_ref, slope_ref, state_ref, other_ref, stat_ref, bias_ref = refs[3:9]
    xs, ms, tok, us, ups, sts, ots = refs[9:]
    i = pl.program_id(0)
    G = f_ref.shape[0]
    C, L = x_ref.shape
    N = L // B
    nt = mixed_ref.shape[2]

    @pl.when(i == 0)
    def _():
        for n in range(N):
            xs[n * C : (n + 1) * C, :] = x_ref[:, n * B : (n + 1) * B].astype(F32)
        stat_ref[0], stat_ref[1], bias_ref[...] = join_stats([r[...] for r in part_refs], N, count / parts)
        mean, inv, mask = token_stats(stat_ref, len_ref[0], count)
        tok[0] = mean
        tok[1] = inv
        tok[2] = mask

    for j in range(G):
        ci = i * G + j
        normed = (xs[pl.ds(ci, N, stride=C), :] - tok[0]) * tok[1]
        sig = tok[2] * (normed * vec_ref[0, ci] + vec_ref[1, ci])
        liq = sig * shift_token(sig, 1)
        for q, v in enumerate((sig, liq)):
            hi, lo = split(v)
            us[j, 0:N, q * B : (q + 1) * B] = hi
            us[j, N:, q * B : (q + 1) * B] = lo
        slope_ref[j] = sig
    ups_all = [dot(us[j], f_ref[j]) for j in range(G)]
    for j, up in enumerate(ups_all):
        ups[j * N : (j + 1) * N, :] = up[:N, :B] + (up[:N, B:] + up[N:, :B])
    at = pl.ds(pl.multiple_of(i * G, G), G)
    scan_blocks(ups, sts, ots, (jump_ref[0, at, :], jump_ref[1, at, :]), N, False)
    left = []
    for j in range(G):
        state = sts[j * N : (j + 1) * N, :]
        state_ref[j] = state
        other_ref[j] = ots[j * N : (j + 1) * N, :]
        left.append(jnp.concatenate([us[j], jnp.concatenate(split(state), axis=0)], axis=1))
    outs = [dot(left[j], t_ref[j]) for j in range(G)]
    for j, out in enumerate(outs):
        ci = i * G + j
        mask = tok[2]
        y = out[:N, :B] + (out[:N, B:] + out[N:, :B]) + vec_ref[2, ci] * slope_ref[j]
        y2 = y * y
        th = jnp.tanh(0.7978845608028654 * (y + 0.044715 * (y * y2)))
        half = 0.5 * (1.0 + th)
        ms[pl.ds(pl.multiple_of(ci * N, N), N), :] = mask * (y * half)
        slope_ref[j] = mask * (half + 0.5 * y * (1.0 - th * th) * (0.7978845608028654 * (1.0 + 0.134145 * y2)))

    @pl.when(i == pl.num_programs(0) - 1)
    def _():
        per = nt // B
        for n in range(N):
            mixed_ref[n // per, :, (n % per) * B : (n % per + 1) * B] = ms[pl.ds(n, C, stride=N), :].astype(BF16)


def glu_kernel(half_ref, in_ref, first_ref, other_ref, bias_ref, gm_ref, keep_ref, send_ref, gp, wt):
    mp, C, nt = in_ref.shape
    H = mp * C
    kh = H // nt
    own = half_ref[0]
    mixed = in_ref[...].reshape(H, nt)
    for q in range(kh):
        at = slice(q * nt, (q + 1) * nt)
        wt[own, :, at] = first_ref[:, q * C : (q + 1) * C, :].reshape(H, nt)
        wt[1 - own, :, at] = other_ref[:, q * C : (q + 1) * C, :].reshape(H, nt)
    step = B
    per = step // C
    bias = jnp.concatenate([bias_ref[...], jnp.zeros((B - mp, B), F32)], axis=0).T
    for s in range(mp // per):
        lo = s * step
        col_v = jnp.concatenate([bias[0:C, k : k + 1] for k in range(s * per, (s + 1) * per)], axis=0)
        col_g = jnp.concatenate([bias[C : 2 * C, k : k + 1] for k in range(s * per, (s + 1) * per)], axis=0)
        value = dot(wt[0, lo : lo + step, :], mixed) + col_v
        gate = dot(wt[1, lo : lo + step, :], mixed) + col_g
        sig = jax.nn.sigmoid(gate)
        x = first_ref[s * per : (s + 1) * per, kh * C : (kh + 1) * C, :].reshape(step, nt).astype(F32)
        g = first_ref[s * per : (s + 1) * per, (kh + 1) * C :, :].reshape(step, nt).astype(F32)
        gm_ref[s * per : (s + 1) * per, 2 * C :, :] = (x + value * sig).astype(BF16).reshape(per, C, nt)
        gv = g * sig
        gp[0, lo : lo + step, :] = gv.astype(BF16)
        gp[1, lo : lo + step, :] = (gv * value * (1.0 - sig)).astype(BF16)
    for s in range(mp // per):
        at = slice(s * step, (s + 1) * step)
        gm = dot(wt[0, :, at], gp[0], TN) + dot(wt[1, :, at], gp[1], TN)
        hi, lo = split(gm)
        gm_ref[s * per : (s + 1) * per, 0:C, :] = hi.reshape(per, C, nt)
        gm_ref[s * per : (s + 1) * per, C : 2 * C, :] = lo.reshape(per, C, nt)
    keep_ref[...] = gp[own]
    send_ref[...] = gp[1 - own]


def weight_kernel(place_ref, keep_ref, got_ref, mixed_ref, theirs_ref, *refs, C, mp):
    outs, wg = refs[:-1], refs[-1]
    nt = mixed_ref.shape[1]
    ways = len(outs)
    per = mp // ways
    total = dot(keep_ref[...], mixed_ref[...], NT) + dot(got_ref[...], theirs_ref[...], NT)
    for m in range(mp):
        at = (m // ways) * C
        wg[m % ways, at : at + C, :] = total[m * C : (m + 1) * C]
    ones = jnp.ones((8, nt), BF16)
    tail = dot(ones, keep_ref[...], NT) + dot(ones, got_ref[...], NT)
    for q in range(ways):
        wg[q, per * C :, :] = tail
    for k in range(ways):
        outs[k][...] = wg[lax.rem(place_ref[1], ways) ^ k]


def fold_kernel(place_ref, *refs, ways, got, C, seen):
    parts, outs, acc = refs[:got], refs[got:-1], refs[-1]
    total = parts[0][...]
    for p in parts[1:]:
        total = total + p[...]
    blocks = (total.shape[0] - 8) // C
    for z in range(blocks):
        at = (z // ways) * C
        acc[z % ways, at : at + C, :] = total[z * C : (z + 1) * C]
    for q in range(ways):
        acc[q, (blocks // ways) * C :, :] = total[blocks * C :]
    for k in range(ways):
        outs[k][...] = acc[lax.rem(lax.div(place_ref[1], seen), ways) ^ k]


def back_kernel(
    len_ref, vec_ref, x_ref, stat_ref, gm_ref, slope_hbm, t_ref, near_hbm, jump_ref,
    layer_ref, gn_ref, sum_ref, row_ref, g_ref, p_ref, r_ref, turned_ref, xs, gs, ns, tok, hs, ps, rs, rts, tab, near_ref, slope_ref, sem, *, count,
):
    i = pl.program_id(0)
    G = g_ref.shape[0]
    C, L = x_ref.shape
    N = L // B
    nt = gm_ref.shape[2]
    per = nt // B

    def fetch(q, k):
        src, dst = ((slope_hbm, slope_ref), (near_hbm, near_ref), (t_ref, tab))[q]
        at = pl.ds(k * G, G)
        return pltpu.make_async_copy(src.at[at], dst.at[at], sem.at[q, k])

    @pl.when(i == 0)
    def _():
        for k in range(C // G):
            for q in range(3):
                fetch(q, k).start()
        for n in range(N):
            xs[n * C : (n + 1) * C, :] = x_ref[:, n * B : (n + 1) * B].astype(F32)
            at = slice((n % per) * B, (n % per + 1) * B)
            gs[n * C : (n + 1) * C, :] = gm_ref[n // per, 0:C, at].astype(F32) + gm_ref[n // per, C : 2 * C, at].astype(F32)
        mean, inv, mask = token_stats(stat_ref, len_ref[0], count)
        tok[0] = mean
        tok[1] = inv
        tok[2] = mask
        sum_ref[...] = jnp.zeros_like(sum_ref)
        for m in range(gm_ref.shape[0]):
            layer_ref[:, m * nt : (m + 1) * nt] = gm_ref[m, 2 * C :, :]

    fetch(0, i).wait()
    for j in range(G):
        ci = i * G + j
        g = gs[pl.ds(ci, N, stride=C), :] * slope_ref[ci]
        g_ref[j] = g
        hi, lo = split(g)
        hs[j, 0:N, :] = hi
        hs[j, N:, :] = lo
    fetch(1, i).wait()
    z_all = [dot(hs[j], near_ref[i * G + j]) for j in range(G)]
    for j, z in enumerate(z_all):
        p = z[:N, :B] + (z[:N, B:] + z[N:, :B])
        p_ref[j] = p
        ps[j * N : (j + 1) * N, :] = p
    at = pl.ds(pl.multiple_of(i * G, G), G)
    scan_blocks(ps, rs, rts, (jump_ref[0, at, :], jump_ref[1, at, :]), N, True)
    left = []
    for j in range(G):
        r = rs[j * N : (j + 1) * N, :]
        r_ref[j] = r
        turned_ref[j] = rts[j * N : (j + 1) * N, :]
        left.append(jnp.concatenate([hs[j], jnp.concatenate(split(r), axis=0)], axis=1))
    fetch(2, i).wait()
    both_all = [dot(left[j], tab[i * G + j]) for j in range(G)]
    for j, both in enumerate(both_all):
        ci = i * G + j
        mask = tok[2]
        normed = (xs[pl.ds(ci, N, stride=C), :] - tok[0]) * tok[1]
        sig = mask * (normed * vec_ref[0, ci] + vec_ref[1, ci])
        both = both[:N, : 2 * B] + (both[:N, 2 * B :] + both[N:, : 2 * B])
        gl = both[:, B:]
        grad = both[:, :B] + vec_ref[2, ci] * g_ref[j] + gl * shift_token(sig, 1) + shift_token(gl * sig, -1)
        masked = mask * grad
        gn = masked * vec_ref[0, ci]
        sum_ref[0] += gn
        sum_ref[1] += gn * normed
        ns[pl.ds(pl.multiple_of(ci * N, N), N), :] = gn
        for q, v in enumerate((g_ref[j] * sig, masked * normed, masked)):
            row_ref[j, q * 8 : (q + 1) * 8, :] = sum(v[8 * k : 8 * k + 8] for k in range(N // 8))

    @pl.when(i == pl.num_programs(0) - 1)
    def _():
        for n in range(N):
            gn_ref[:, n * B : (n + 1) * B] = ns[pl.ds(n, C, stride=N), :]


def lift_kernel(len_ref, vec_ref, x_ref, stat_ref, f_ref, u_ref, lift_ref, xs, tok, *, count):
    i = pl.program_id(0)
    G = f_ref.shape[0]
    C, L = x_ref.shape
    N = L // B

    @pl.when(i == 0)
    def _():
        for n in range(N):
            xs[n * C : (n + 1) * C, :] = x_ref[:, n * B : (n + 1) * B].astype(F32)
        tok[0], tok[1], tok[2] = token_stats(stat_ref, len_ref[0], count)

    ahead = float(B) - lane_iota((N, B)).astype(F32)
    flip = (lane_iota((B, B)) + row_iota((B, B)) == B - 1).astype(BF16)
    flat, left = [], []
    for j in range(G):
        ci = i * G + j
        normed = (xs[pl.ds(ci, N, stride=C), :] - tok[0]) * tok[1]
        sig = tok[2] * (normed * vec_ref[0, ci] + vec_ref[1, ci])
        liq = sig * shift_token(sig, 1)
        flat.append(jnp.concatenate(split(sig) + split(liq), axis=0))
        left.append(jnp.concatenate(split(jnp.concatenate([sig * ahead, liq * ahead], axis=1)), axis=0))
    turned_all = [dot(v, flip).astype(BF16) for v in flat]
    lifts = [dot(left[j], f_ref[j]) for j in range(G)]
    for j in range(G):
        turned, lift = turned_all[j], lifts[j]
        for q in range(2):
            at = slice(q * B, (q + 1) * B)
            u_ref[j, 0 : 2 * N, at] = turned[2 * q * N : (2 * q + 2) * N]
            u_ref[j, 2 * N :, at] = turned[2 * q * N : (2 * q + 1) * N]
        lift_ref[j] = lift[:N, :B] + (lift[:N, B:] + lift[N:, :B])


def sums_kernel(u_ref, lift_ref, g_ref, p_ref, r_ref, rx_ref, state_ref, sx_ref, near_ref, jump_ref, row_ref):
    i = pl.program_id(0)
    G = g_ref.shape[0]
    _, N, _ = g_ref.shape
    place = lane_iota((N, B)).astype(F32)
    rows2, lanes2 = row_iota((B, B)), lane_iota((B, B))
    inside = lanes2 + rows2 >= B - 1
    rows16 = row_iota((16, B))
    lag = lane_iota((16, B)).astype(F32)
    R = N + 16
    every = range(G)
    turned = []
    for j in every:
        g_hi, g_lo = split(g_ref[j])
        turned.append(jnp.concatenate([g_hi, g_hi, g_lo], axis=0).T)
    corr = [dot(turned[j], u_ref[j]) for j in every]
    left = []
    for j in every:
        lags = []
        for q in range(2):
            part = jnp.where(inside, corr[j][:, q * B : (q + 1) * B], 0.0)
            lags.append(jnp.sum(pltpu.roll(part, 1, 1, stride=1, stride_axis=0), axis=0, keepdims=True))
        pair = jnp.where((rows16 & 1) == 0, lags[0], lags[1])
        pair = jnp.where(rows16 < 2, pair, jnp.where(rows16 < 4, pair * lag, 0.0))
        left.append(jnp.concatenate(split(jnp.concatenate([g_ref[j] * place, pair], axis=0)), axis=0))
    both = [dot(left[j], near_ref[j]) for j in every]
    for j in every:
        ci = i * G + j
        z = both[j][:R, :B] + (both[j][:R, B:] + both[j][R:, :B])
        row_ref[j, 0:8, :] = z[N : N + 8]
        p, r, state, lift = p_ref[j], r_ref[j], state_ref[j], lift_ref[j]
        state_x, r_x = sx_ref[j], rx_ref[j]
        carry = z[:N] + float(B) * (r * jump_ref[0, pl.ds(ci, 1), :] + r_x * jump_ref[1, pl.ds(ci, 1), :])
        total = [p * state, p * state_x, carry * state + lift * r, carry * state_x + lift * r_x]
        for q, v in enumerate(total):
            row_ref[j, 8 + 8 * q : 16 + 8 * q, :] = sum(v[8 * k : 8 * k + 8] for k in range(N // 8))


def join_kernel(plain_ref, ref, out_ref):
    odd = (lane_iota((out_ref.shape[1], B)) & (B // 4)) != 0
    for q in range(2):
        out_ref[q] = jnp.where(odd, ref[:, 2 * q + 1, :], ref[:, 2 * q, :])
    for q in range(4):
        out_ref[2 + q] = jnp.sum(ref[:, 8 + 8 * q : 16 + 8 * q, :], axis=1)
    for q in range(3):
        out_ref[6 + q] = jnp.sum(plain_ref[:, 8 * q : 8 * q + 8, :], axis=1)


def finish_kernel(
    place_ref, mine_ref, theirs_ref, w_ref, step_ref, decay_ref, freq_ref, read_ref, liquid_ref, wsum_ref, across_ref,
    value_ref, gate_ref, vbias_ref, gbias_ref, step_out, decay_out, freq_out, read_out, liquid_out,
    skip_out, gain_out, bias_out, *, M,
):
    C = decay_ref.shape[0]
    half = B // 2

    def emit(first, second):
        value_ref[...] = first[0:C, :]
        gate_ref[...] = second[0:C, :]
        per = B // C
        group = place_ref[1] // per
        back = (B - (place_ref[1] % per) * C) % B
        for out, v in ((vbias_ref, first), (gbias_ref, second)):
            lanes = v[C : C + 8, pl.ds(pl.multiple_of(group * B, B), B)]
            out[...] = pltpu.roll(lanes, back, 1)[0:1, 0:C]

    @pl.when(place_ref[0] == 0)
    def _():
        emit(wsum_ref, across_ref)

    @pl.when(place_ref[0] == 1)
    def _():
        emit(across_ref, wsum_ref)

    rows = [mine_ref[q] + theirs_ref[q] for q in range(9)]

    def parts(a, b, c):
        return a[:, :half] - a[:, half:] + c[:, :half], b[:, :half] + b[:, half:] + c[:, half:]

    g_re, g_im = parts(rows[2], rows[3], rows[0])
    d_re, d_im = parts(rows[4], rows[5], rows[1])
    w = w_ref[...]
    w_re, w_im = w[:, :half], w[:, half:]
    l_re = w_re * d_re - w_im * d_im
    l_im = w_re * d_im + w_im * d_re
    cot = (
        2.0 * g_re[:, :M], -2.0 * g_im[:, :M], 2.0 * g_re[:, M:], -2.0 * g_im[:, M:],
        2.0 * (l_re[:, :M] + l_re[:, M:]), -2.0 * (l_im[:, :M] + l_im[:, M:]),
    )
    step = jnp.sum(jnp.where(row_iota((C, C)) == lane_iota((C, C)), step_ref[...], 0.0), axis=1, keepdims=True)
    _, back = jax.vjp(mode_terms, step, decay_ref[...], freq_ref[...], read_ref[...], liquid_ref[...])
    step_grad, decay_out[...], freq_out[...], read_out[...], liquid_out[...] = back(cot)
    lanes = lane_iota((B, B))
    pad = jnp.zeros((B - C, 1), F32)
    plain = jnp.zeros((B, B), F32)
    for q, v in enumerate([step_grad] + [jnp.sum(rows[6 + q], axis=1, keepdims=True) for q in range(3)]):
        plain = jnp.where(lanes == q, jnp.concatenate([v, pad], axis=0), plain)
    plain = plain.T
    for q, out in enumerate((step_out, skip_out, gain_out, bias_out)):
        out[...] = plain[q : q + 1, 0:C]


def last_kernel(x_ref, g_ref, gn_ref, stat_ref, sum_ref, out_ref, *, count):
    C, L = x_ref.shape
    for n in range(L // B):
        at = slice(n * B, (n + 1) * B)
        mean = stat_ref[0, n : n + 1, :]
        inv = lax.rsqrt(stat_ref[1, n : n + 1, :] * (1.0 / count) + EPS)
        first = sum_ref[0, n : n + 1, :] * (1.0 / count)
        second = sum_ref[1, n : n + 1, :] * (1.0 / count)
        normed = (x_ref[:, at].astype(F32) - mean) * inv
        out_ref[:, at] = inv * (gn_ref[:, at] - first - normed * second) + g_ref[:, at].astype(F32)


def total_kernel(*refs):
    total = refs[0][...]
    for p in refs[1:-1]:
        total = total + p[...]
    refs[-1][...] = total


def rounds_of(size):
    rounds, bit = [], 1
    while bit < size:
        if bit * 2 < size:
            rounds.append((bit, 2 * bit, 3 * bit))
            bit *= 4
        else:
            rounds.append((bit,))
            bit *= 2
    return rounds


def exchange(v, axis, size, off):
    return lax.ppermute(v, axis, [(k, k ^ off) for k in range(size)])


def all_sums(v, size):
    for offs in rounds_of(size):
        v = sum([exchange(v, "mp", size, o) for o in offs], v)
    return v


def sum_docs(v, size, stride):
    total = v
    for k in range(stride, size, stride):
        total = total + lax.ppermute(v, "dp", [(q, (q + k) % size) for q in range(size)])
    return total


def partner(v, size):
    return lax.ppermute(v, "dp", [(q, q ^ 1) for q in range(size)])


def mode_terms(log_step, decay_log, frequency, readout, liquid_readout):
    M = decay_log.shape[1]
    step_size = jnp.exp(log_step)
    real_rate = -jnp.exp(decay_log)
    real_step = step_size * real_rate
    imag_step = step_size * frequency
    growth = jnp.exp(real_step)
    num_real = growth * jnp.cos(imag_step) - 1.0
    num_imag = growth * jnp.sin(imag_step)
    denominator = real_rate * real_rate + frequency * frequency
    in_real = (num_real * real_rate + num_imag * frequency) / denominator
    in_imag = (num_imag * real_rate - num_real * frequency) / denominator

    def mix(coeffs):
        re, im = coeffs[:, :M], coeffs[:, M:]
        return re * in_real - im * in_imag, re * in_imag + im * in_real

    return mix(readout) + mix(liquid_readout) + (real_step, imag_step)


def per_device(
    mp, dp,
    tokens, lengths, norm_gain, norm_bias, log_step, decay_log, frequency, readout, liquid_readout,
    skip_gain, value_weight, gate_weight, value_bias, gate_bias, grad_out,
):
    C, L = tokens.shape
    H = value_weight.shape[0]
    M = decay_log.shape[1]
    N = L // B
    nt = L // mp
    kh = H // nt
    shape = jax.ShapeDtypeStruct

    place = jnp.stack([lax.axis_index("dp") & 1, lax.axis_index("mp")]).astype(jnp.int32)
    rounds = rounds_of(mp)
    small, large = 16, 32

    def pin(v):
        return pltpu.with_memory_space_constraint(v, pltpu.HBM)

    def call(kernel, out, n_in, smem=0, us=1, scratch=(), mb=small):
        return pl.pallas_call(
            kernel,
            out_shape=out,
            in_specs=[SMEM] * smem + [VMEM] * (n_in - smem),
            out_specs=jax.tree.map(lambda _: VMEM, out),
            scratch_shapes=list(scratch),
            compiler_params=params(mb),
            cost_estimate=cost(us),
        )

    def whole(*dims):
        return pl.BlockSpec(dims, lambda i: (0,) * len(dims))

    def chan_by(group):
        return lambda *dims: pl.BlockSpec((group,) + dims, lambda i: (i,) + (0,) * len(dims))

    def by_channel(kernel, out, in_specs, out_specs, us, scratch, mb=small, group=TABLE_GROUP):
        return pl.pallas_call(
            kernel,
            grid=(C // group,),
            out_shape=out,
            in_specs=in_specs,
            out_specs=out_specs,
            scratch_shapes=scratch,
            compiler_params=params(mb),
            cost_estimate=cost(us),
        )

    vm = pltpu.VMEM
    G = min(MIXER_GROUP, C)
    chan, few = chan_by(G), chan_by(TABLE_GROUP)
    blocks = shape((C, N, B), F32)
    far = pltpu.HBM
    far_blocks = far((C, N, B), F32)
    def pin(v):
        return pltpu.with_memory_space_constraint(v, far)

    hbm = pl.BlockSpec(memory_space=pltpu.HBM)
    stat, pay = pl.pallas_call(
        start_kernel,
        out_shape=(shape((2 * N + mp, B), F32), shape((mp, (2 + kh) * C, nt), BF16)),
        in_specs=[SMEM] + [hbm] * 6,
        out_specs=(VMEM, VMEM),
        scratch_shapes=[
            pltpu.VMEM((C, L), BF16), pltpu.VMEM((C, L), BF16), pltpu.VMEM((C, H), BF16),
            pltpu.VMEM((1, C), BF16), pltpu.VMEM((1, C), BF16), pltpu.SemaphoreType.DMA((5,)),
        ],
        compiler_params=params(small),
        cost_estimate=cost(3),
    )(
        place, pin(tokens), pin(grad_out), pin(value_weight.T), pin(gate_weight.T), pin(value_bias[None]), pin(gate_bias[None])
    )
    first = lax.all_to_all(pay, "mp", split_axis=0, concat_axis=0, tiled=True)

    rates = jnp.stack(
        [jnp.broadcast_to(log_step[:, None], (C, 4 * M)), jnp.tile(decay_log, (1, 4)), jnp.tile(frequency, (1, 4))]
    )
    coef = jnp.concatenate([readout[:, :M], liquid_readout[:, :M], readout[:, M:], liquid_readout[:, M:]], axis=1)
    f_near, f_tab, t_tab, jump, w_all = by_channel(
        partial(table_kernel, C=C, M=M),
        (
            shape((C, 2 * B, 2 * B), BF16), far((C, 2 * B, 2 * B), BF16), shape((C, 3 * B, 2 * B), BF16),
            shape((2, C, B), F32), shape((C, B), F32),
        ),
        [whole(3, C, B), whole(C, B)],
        (few(2 * B, 2 * B), few(2 * B, 2 * B), few(3 * B, 2 * B), whole(2, C, B), whole(C, B)),
        6,
        [vm((3, B, B), F32)],
    )(rates, coef)

    count = C
    for k, offs in enumerate(rounds[::-1]):
        parts = [stat] + [exchange(stat, "mp", mp, o) for o in offs]
        if k == 0:
            parts[1], parts[-1], t_tab = lax.optimization_barrier((parts[1], parts[-1], t_tab))
        if k < len(rounds) - 1:
            stat = jnp.concatenate(join_stats(parts, N, float(count)), axis=0)
            count *= len(parts)

    vecs = jnp.stack([norm_gain, norm_bias, skip_gain])
    mixed, slope, state, state_x, stat, bias = by_channel(
        partial(mixer_kernel, count=H, parts=len(parts)),
        (shape((mp, C, nt), BF16), far_blocks, far_blocks, far_blocks, shape((2, N, B), F32), shape((mp, B), F32)),
        [SMEM, SMEM, whole(C, L)] + [whole(2 * N + mp, B)] * len(parts)
        + [chan(2 * B, 2 * B), chan(3 * B, 2 * B), whole(2, C, B)],
        (whole(mp, C, nt), chan(N, B), chan(N, B), chan(N, B), whole(2, N, B), whole(mp, B)),
        6,
        [
            vm((N * C, B), F32), vm((N * C, B), F32), vm((3, N, B), F32), vm((G, 2 * N, 2 * B), BF16),
            vm((G * N, B), F32), vm((G * N, B), F32), vm((G * N, B), F32),
        ],
        large,
        G,
    )(lengths, vecs, tokens, *parts, f_near, t_tab, jump)

    mixed, first, rates = lax.optimization_barrier((mixed, first, rates))
    other_w = partner(first[:, : kh * C, :], dp)
    mixed_tok = lax.all_to_all(mixed, "mp", split_axis=0, concat_axis=0, tiled=True)
    back_tab, near_tab = by_channel(
        partial(back_table_kernel, C=C, M=M),
        (far((C, 2 * B, 4 * B), BF16), far((C, B, 2 * B), BF16)),
        [whole(3, C, B), whole(C, B)],
        (few(2 * B, 4 * B), few(B, 2 * B)),
        7,
        [vm((3, B, B), F32)],
    )(rates, w_all)
    mixed_tok, back_tab = lax.optimization_barrier((mixed_tok, back_tab))
    gm, keep, send = call(
        glu_kernel,
        (shape((mp, 3 * C, nt), BF16),) + (shape((H, nt), BF16),) * 2,
        5, 1, 2, [vm((2, H, nt), BF16), vm((2, H, H), BF16)],
    )(place, mixed_tok, first, other_w, bias)
    mixed_tok = mixed_tok.reshape(H, nt)
    gm, f_tab = lax.optimization_barrier((gm, f_tab))
    gm = lax.all_to_all(gm, "mp", split_axis=0, concat_axis=0, tiled=True)
    u_rev, lift = by_channel(
        partial(lift_kernel, count=H),
        (far((C, 3 * N, 2 * B), BF16), far_blocks),
        [SMEM, SMEM, whole(C, L), whole(2, N, B), few(2 * B, 2 * B)],
        (few(3 * N, 2 * B), few(N, B)),
        3,
        [vm((N * C, B), F32), vm((3, N, B), F32)],
        56,
    )(lengths, vecs, tokens, stat, pin(f_tab))
    gm, lift = lax.optimization_barrier((gm, lift))

    ways = len(rounds[0]) + 1
    rows_left = mp // ways
    outs = call(
        partial(weight_kernel, C=C, mp=mp), (shape((rows_left * C + 8, H), F32),) * ways, 5, 1, 2,
        [vm((ways, rows_left * C + 8, H), F32)],
    )(place, keep, partner(send, dp), mixed_tok, partner(mixed_tok, dp))
    terms = [outs[0]] + [exchange(v, "mp", mp, o) for v, o in zip(outs[1:], rounds[0])]

    layer_out, gn, sums, plain, g_pre, p_blk, r_blk, rx_blk = by_channel(
        partial(back_kernel, count=H),
        (shape((C, L), BF16), shape((C, L), F32), shape((2, N, B), F32), shape((C, 24, B), F32)) + (blocks,) * 4,
        [
            SMEM, SMEM, VMEM, VMEM, VMEM, hbm, hbm, hbm, VMEM,
        ],
        (whole(C, L), whole(C, L), whole(2, N, B), chan(24, B)) + (chan(N, B),) * 4,
        7,
        [
            vm((N * C, B), F32), vm((N * C, B), F32), vm((N * C, B), F32), vm((3, N, B), F32),
            vm((G, 2 * N, B), BF16), vm((G * N, B), F32), vm((G * N, B), F32), vm((G * N, B), F32),
            vm((C, 2 * B, 4 * B), BF16), vm((C, B, 2 * B), BF16), vm((C, N, B), F32),
            pltpu.SemaphoreType.DMA((3, C // G)),
        ],
        large,
        G,
    )(lengths, vecs, tokens, stat, gm, pin(slope), pin(back_tab), pin(near_tab), jump)

    seen = ways
    terms[0], plain = lax.optimization_barrier((terms[0], plain))
    while seen < mp:
        ways, offs = 2, (seen,)
        rows_left //= ways
        outs = call(
            partial(fold_kernel, ways=ways, got=len(terms), C=C, seen=seen),
            (shape((rows_left * C + 8, H), F32),) * ways,
            1 + len(terms), 1, 1, [vm((ways, rows_left * C + 8, H), F32)],
        )(place, *terms)
        terms = [outs[0]] + [exchange(v, "mp", mp, o) for v, o in zip(outs[1:], offs)]
        seen *= ways
    for k, offs in enumerate(rounds[::-1]):
        got = [exchange(sums, "mp", mp, o) for o in offs]
        if k == len(rounds) - 1:
            g_pre, sums, terms[0] = lax.optimization_barrier((g_pre, sums, terms[0]))
            rows = by_channel(
                sums_kernel,
                shape((C, 40, B), F32),
                [chan(3 * N, 2 * B)] + [chan(N, B)] * 7 + [chan(B, 2 * B), whole(2, C, B)],
                chan(40, B),
                20,
                [],
                large,
                G,
            )(pin(u_rev), pin(lift), g_pre, p_blk, r_blk, rx_blk, pin(state), pin(state_x), pin(near_tab), jump)
            got, rows, terms = lax.optimization_barrier((got, rows, terms))
        sums = sum(got, sums)
    grad_tokens = call(partial(last_kernel, count=H), shape((C, L), F32), 5)(tokens, grad_out, gn, stat, sums)
    rows = call(join_kernel, shape((9, C, B), F32), 2)(plain, rows)
    others = sum_docs(rows, dp, 1) - rows if dp > 2 else partner(rows, dp)

    wsum = call(total_kernel, shape((C + 8, H), F32), len(terms))(*terms)
    wsum = sum_docs(wsum, dp, 2)
    across = partner(wsum, dp)
    thin, wide = shape((C, M), F32), shape((C, 2 * M), F32)
    line = shape((1, C), F32)
    (
        value_wgrad, gate_wgrad, vb, gb, step_grad, decay_grad, frequency_grad, readout_grad, liquid_grad,
        skip_grad, gain_grad, bias_grad,
    ) = call(
        partial(finish_kernel, M=M),
        (shape((C, H), F32), shape((C, H), F32), line, line, line, thin, thin, wide, wide, line, line, line),
        11, 1,
    )(
        place, rows, others, w_all, log_step[None], decay_log, frequency, readout, liquid_readout, wsum, across,
    )
    return (
        layer_out, grad_tokens, gain_grad[0], bias_grad[0], step_grad[0], decay_grad, frequency_grad, readout_grad,
        liquid_grad, skip_grad[0], value_wgrad.T, gate_wgrad.T, vb[0], gb[0],
    )


def solution(mesh):
    row, col, act = P("mp"), P(None, "mp"), P("mp", "dp")
    wide = P("mp", None)
    in_specs = (act, P("dp"), row, row, row, wide, wide, wide, wide, row, col, col, row, row, act)
    out_specs = (act, act, row, row, row, wide, wide, wide, wide, row, col, col, row, row)
    return jax.shard_map(
        partial(per_device, mesh.shape["mp"], mesh.shape["dp"]),
        mesh=mesh, in_specs=in_specs, out_specs=out_specs, check_vma=False,
    )
```

```python
from functools import partial

import jax
import jax.numpy as jnp
import numpy as np
from jax import lax
from jax.experimental import pallas as pl
from jax.experimental.pallas import tpu as pltpu
from jax.sharding import PartitionSpec as P

B = 128
TABLE_GROUP = 8
MIXER_GROUP = 16
F32 = jnp.float32
BF16 = jnp.bfloat16
NN = (((1,), (0,)), ((), ()))
NT = (((1,), (1,)), ((), ()))
TN = (((0,), (0,)), ((), ()))
EPS = 1e-05
SQUARE_SCALE = 65536.0
VMEM = pl.BlockSpec(memory_space=pltpu.VMEM)
SMEM = pl.BlockSpec(memory_space=pltpu.SMEM)


def params(mb):
    return pltpu.CompilerParams(vmem_limit_bytes=mb * 1024 * 1024)


def cost(us):
    return pl.CostEstimate(flops=int(us * 1e9), bytes_accessed=int(us * 1e6), transcendentals=0)


def dot(a, b, dims=NN):
    return lax.dot_general(a, b, dims, preferred_element_type=F32)


def split(v):
    hi = v.astype(BF16)
    return hi, (v - hi.astype(F32)).astype(BF16)


def sincos(x):
    k = jnp.floor(x * 0.6366197723675814 + 0.5)
    y = ((x - k * 1.5703125) - k * 4.837512969970703e-4) - k * 7.54978995489188e-8
    y2 = y * y
    s = y + y * y2 * (-1.6666654611e-1 + y2 * (8.3321608736e-3 - y2 * 1.9515295891e-4))
    c = 1.0 - 0.5 * y2 + y2 * y2 * (4.166664568298827e-2 + y2 * (-1.388731625493765e-3 + y2 * 2.443315711809948e-5))
    q = k.astype(jnp.int32)
    odd = (q & 1) == 1
    sin = jnp.where(odd, c, s)
    cos = jnp.where(odd, s, c)
    sin = jnp.where((q & 2) == 2, -sin, sin)
    cos = jnp.where(((q + 1) & 2) == 2, -cos, cos)
    return sin, cos


def row_iota(shape):
    return lax.broadcasted_iota(jnp.int32, shape, 0)


def lane_iota(shape):
    return lax.broadcasted_iota(jnp.int32, shape, 1)


def shift_token(x, k):
    n = x.shape[0]
    lanes = lane_iota(x.shape)
    rows = row_iota(x.shape)
    turned = pltpu.roll(x, k % B, 1)
    wrapped = pltpu.roll(turned, k % n, 0)
    if k > 0:
        wrapped = jnp.where(rows >= 1, wrapped, 0.0)
        return jnp.where(lanes == 0, wrapped, turned)
    wrapped = jnp.where(rows < n - 1, wrapped, 0.0)
    return jnp.where(lanes == B - 1, wrapped, turned)


def swap_halves(x):
    return pltpu.roll(x, B // 2, 1)


def scan_blocks(v_ref, out_ref, turned_ref, jump, N, backward):
    a_re, a_im = jump
    G = v_ref.shape[0] // N
    s = jnp.zeros((G, B), F32)
    t = s
    for k in range(N):
        n = N - 1 - k if backward else k
        out_ref[pl.ds(n, G, stride=N), :] = s
        turned_ref[pl.ds(n, G, stride=N), :] = t
        v = v_ref[pl.ds(n, G, stride=N), :]
        s, t = a_re * s + (a_im * t + v), a_re * t + (swap_halves(v) - a_im * s)


def start_kernel(
    place_ref, x_hbm, g_hbm, v_hbm, w_hbm, vb_hbm, gb_hbm, stat_ref, pay_ref, x_ref, g_ref, wt_ref, vb_ref, gb_ref, sems,
):
    C, L = x_ref.shape
    N = L // B
    mp, rows, nt = pay_ref.shape
    kh = rows // C - 2
    pairs = ((x_hbm, x_ref), (g_hbm, g_ref), (vb_hbm, vb_ref), (gb_hbm, gb_ref))
    moves = [pltpu.make_async_copy(src, dst, sems.at[1 + k]) for k, (src, dst) in enumerate(pairs)]
    for move in moves:
        move.start()
    for half, ref in enumerate((v_hbm, w_hbm)):

        @pl.when(place_ref[0] == half)
        def _():
            pltpu.make_async_copy(ref, wt_ref, sems.at[0]).start()

    moves[0].wait()
    for n in range(N):
        x = x_ref[:, n * B : (n + 1) * B].astype(F32)
        mean = jnp.sum(x, axis=0, keepdims=True) * (1.0 / C)
        dev = x - mean
        stat_ref[n : n + 1, :] = mean
        stat_ref[N + n : N + n + 1, :] = jnp.sum(dev * dev, axis=0, keepdims=True)
    own = row_iota((mp, B))
    moves[2].wait()
    moves[3].wait()
    bias = jnp.concatenate([vb_ref[...].astype(F32), gb_ref[...].astype(F32), jnp.zeros((1, B - 2 * C), F32)], axis=1)
    stat_ref[2 * N :, :] = jnp.where(own == place_ref[1], bias, 0.0)
    for j in range(mp):
        pay_ref[j, kh * C : (kh + 1) * C, :] = x_ref[:, j * nt : (j + 1) * nt]
    moves[1].wait()
    for j in range(mp):
        pay_ref[j, (kh + 1) * C :, :] = g_ref[:, j * nt : (j + 1) * nt]
    pltpu.make_async_copy(v_hbm, wt_ref, sems.at[0]).wait()
    for j in range(mp):
        for q in range(kh):
            pay_ref[j, q * C : (q + 1) * C, :] = wt_ref[:, q * nt : (q + 1) * nt]


def join_stats(parts, N, count):
    mean = sum(p[:N] for p in parts) * (1.0 / len(parts))
    spread = sum(p[N : 2 * N] for p in parts) + count * sum((p[:N] - mean) * (p[:N] - mean) for p in parts)
    return mean, spread, sum(p[2 * N :] for p in parts)


def columns(arrays, cols, C):
    pad = jnp.zeros((B - C, B), F32)
    for q, v in enumerate(arrays):
        cols[q] = jnp.concatenate([v, pad], axis=0).T


def channel_waves(cols, i, M, G):
    back = (B - i * G) % B
    al = pltpu.roll(cols[0, 0:M, :], back, 1)
    om = pltpu.roll(cols[1, 0:M, :], back, 1)
    ww = 2.0 * pltpu.roll(cols[2], back, 1)
    place = lane_iota((M, B)).astype(F32)
    ahead = float(B) - place
    out = []
    for j in range(G):
        a = jnp.broadcast_to(al[:, j : j + 1], (M, B))
        o = jnp.broadcast_to(om[:, j : j + 1], (M, B))
        w = [jnp.broadcast_to(ww[q * M : (q + 1) * M, j : j + 1], (M, B)) for q in range(4)]
        sin, cos = sincos(o * place)
        mag = jnp.exp(a * place)
        near = mag * cos, mag * sin
        sin, cos = sincos(o * ahead)
        mag = jnp.exp(a * ahead)
        out.append((near, (mag * cos, mag * sin), w))
    return out


def toeplitz_rows(kern, start):
    return pltpu.roll(jnp.broadcast_to(kern, (B, B)), start, 1, stride=1, stride_axis=0)


def table_kernel(rates_ref, coef_ref, f_ref, again_ref, t_ref, jump_ref, wout_ref, cols, *, C, M):
    i = pl.program_id(0)
    G = f_ref.shape[0]

    @pl.when(i == 0)
    def _():
        step_size = jnp.exp(rates_ref[0])
        real_rate = -jnp.exp(rates_ref[1])
        freq = rates_ref[2]
        re = step_size * real_rate
        im = step_size * freq
        growth = jnp.exp(re)
        sin, cos = sincos(im)
        num_re = growth * cos - 1.0
        num_im = growth * sin
        den = real_rate * real_rate + freq * freq
        in_re = (num_re * real_rate + num_im * freq) / den
        in_im = (num_im * real_rate - num_re * freq) / den
        coef = coef_ref[...]
        first = lane_iota(coef.shape) < B // 2
        w = coef * in_re + swap_halves(coef) * jnp.where(first, -in_im, in_im)
        wout_ref[...] = w
        sin, cos = sincos(im * float(B))
        mag = jnp.exp(re * float(B))
        jump_ref[0] = mag * cos
        jump_ref[1] = mag * jnp.where(first, -sin, sin)
        columns((re, im, w), cols, C)

    rows = row_iota((B, B))
    lanes = lane_iota((B, B))
    odd = (lanes & M) == M
    every = range(G)
    waves = channel_waves(cols, i, M, G)
    feeds = [jnp.concatenate([f_re, f_re, f_im, f_im], axis=0).T for _, (f_re, f_im), _ in waves]
    kerns = []
    for j in every:
        (n_re, n_im), _, w = waves[j]
        for h in range(2):
            w_re, w_im = w[h], w[2 + h]
            e_re = w_re * n_re - w_im * n_im
            e_im = -(w_re * n_im + w_im * n_re)
            kerns.append(jnp.sum(e_re, axis=0, keepdims=True))
            for q, v in enumerate(split(e_re)):
                t_ref[j, 2 * B + h * M : 2 * B + (h + 1) * M, q * B : (q + 1) * B] = v
            for q, v in enumerate(split(e_im)):
                t_ref[j, 2 * B + (2 + h) * M : 2 * B + (3 + h) * M, q * B : (q + 1) * B] = v
    rolled = [toeplitz_rows(kern, 0) for kern in kerns]
    for j in every:
        for h in range(2):
            part = jnp.where(odd if h == 1 else ~odd, feeds[j], 0.0)
            for q, v in enumerate(split(part)):
                f_ref[j, h * B : (h + 1) * B, q * B : (q + 1) * B] = v
                again_ref[j, h * B : (h + 1) * B, q * B : (q + 1) * B] = v
            toe = jnp.where(lanes >= rows, rolled[2 * j + h], 0.0)
            for q, v in enumerate(split(toe)):
                t_ref[j, h * B : (h + 1) * B, q * B : (q + 1) * B] = v


def back_table_kernel(rates_ref, w_ref, t_ref, near_ref, cols, *, C, M):
    i = pl.program_id(0)
    G = t_ref.shape[0]

    @pl.when(i == 0)
    def _():
        step_size = jnp.exp(rates_ref[0])
        columns((step_size * -jnp.exp(rates_ref[1]), step_size * rates_ref[2], w_ref[...]), cols, C)

    rows = row_iota((B, B))
    lanes = lane_iota((B, B))
    zero = jnp.zeros((M, B), BF16)
    every = range(G)
    waves = channel_waves(cols, i, M, G)
    turned = [jnp.concatenate([n_re, n_re, n_im, n_im], axis=0).T for (n_re, n_im), _, _ in waves]
    kerns, starts = [], []
    for j in every:
        (n_re, n_im), (f_re, f_im), w = waves[j]
        for h in range(2):
            w_re, w_im = w[h], w[2 + h]
            b_re = w_re * f_re - w_im * f_im
            b_im = -(w_re * f_im + w_im * f_re)
            kerns.append(jnp.sum(b_re, axis=0, keepdims=True))
            starts.append(jnp.sum(w_re * n_re - w_im * n_im, axis=0, keepdims=True)[:, 0:1])
            for part, v2 in ((0, b_re), (2, b_im)):
                for q, v in enumerate(split(v2)):
                    at = slice((2 * q + h) * B, (2 * q + h + 1) * B)
                    t_ref[j, B + part * M : B + (part + 1) * M, at] = v
                    t_ref[j, B + (part + 1) * M : B + (part + 2) * M, at] = zero
    rolled = [toeplitz_rows(kern, 0) for kern in kerns]
    for j in every:
        for q, v in enumerate(split(turned[j])):
            near_ref[j, :, q * B : (q + 1) * B] = v
        for h in range(2):
            start = jnp.broadcast_to(starts[2 * j + h], (B, B))
            toe = jnp.where(lanes < rows, rolled[2 * j + h], jnp.where(lanes == rows, start, 0.0))
            for q, v in enumerate(split(toe)):
                t_ref[j, 0:B, (2 * q + h) * B : (2 * q + h + 1) * B] = v


def token_stats(stat_ref, length, count):
    mean = stat_ref[0]
    inv = lax.rsqrt(stat_ref[1] * (1.0 / count) + EPS)
    place = row_iota(mean.shape) * B + lane_iota(mean.shape)
    return mean, inv, (place < length).astype(F32)


def mixer_kernel(len_ref, vec_ref, x_ref, *refs, count, parts):
    part_refs, refs = refs[:parts], refs[parts:]
    f_ref, t_ref, jump_ref = refs[:3]
    mixed_ref, slope_ref, state_ref, other_ref, stat_ref, bias_ref = refs[3:9]
    xs, ms, tok, us, ups, sts, ots = refs[9:]
    i = pl.program_id(0)
    G = f_ref.shape[0]
    C, L = x_ref.shape
    N = L // B
    nt = mixed_ref.shape[2]

    @pl.when(i == 0)
    def _():
        for n in range(N):
            xs[n * C : (n + 1) * C, :] = x_ref[:, n * B : (n + 1) * B].astype(F32)
        stat_ref[0], stat_ref[1], bias_ref[...] = join_stats([r[...] for r in part_refs], N, count / parts)
        mean, inv, mask = token_stats(stat_ref, len_ref[0], count)
        tok[0] = mean
        tok[1] = inv
        tok[2] = mask

    for j in range(G):
        ci = i * G + j
        normed = (xs[pl.ds(ci, N, stride=C), :] - tok[0]) * tok[1]
        sig = tok[2] * (normed * vec_ref[0, ci] + vec_ref[1, ci])
        liq = sig * shift_token(sig, 1)
        for q, v in enumerate((sig, liq)):
            hi, lo = split(v)
            us[j, 0:N, q * B : (q + 1) * B] = hi
            us[j, N:, q * B : (q + 1) * B] = lo
        slope_ref[j] = sig
    ups_all = [dot(us[j], f_ref[j]) for j in range(G)]
    for j, up in enumerate(ups_all):
        ups[j * N : (j + 1) * N, :] = up[:N, :B] + (up[:N, B:] + up[N:, :B])
    at = pl.ds(pl.multiple_of(i * G, G), G)
    scan_blocks(ups, sts, ots, (jump_ref[0, at, :], jump_ref[1, at, :]), N, False)
    left = []
    for j in range(G):
        state = sts[j * N : (j + 1) * N, :]
        state_ref[j] = state
        other_ref[j] = ots[j * N : (j + 1) * N, :]
        left.append(jnp.concatenate([us[j], jnp.concatenate(split(state), axis=0)], axis=1))
    outs = [dot(left[j], t_ref[j]) for j in range(G)]
    for j, out in enumerate(outs):
        ci = i * G + j
        mask = tok[2]
        y = out[:N, :B] + (out[:N, B:] + out[N:, :B]) + vec_ref[2, ci] * slope_ref[j]
        y2 = y * y
        th = jnp.tanh(0.7978845608028654 * (y + 0.044715 * (y * y2)))
        half = 0.5 * (1.0 + th)
        ms[pl.ds(pl.multiple_of(ci * N, N), N), :] = mask * (y * half)
        slope_ref[j] = mask * (half + 0.5 * y * (1.0 - th * th) * (0.7978845608028654 * (1.0 + 0.134145 * y2)))

    @pl.when(i == pl.num_programs(0) - 1)
    def _():
        per = nt // B
        for n in range(N):
            mixed_ref[n // per, :, (n % per) * B : (n % per + 1) * B] = ms[pl.ds(n, C, stride=N), :].astype(BF16)


def glu_kernel(half_ref, in_ref, first_ref, other_ref, bias_ref, gm_ref, keep_ref, send_ref, gp, wt):
    mp, C, nt = in_ref.shape
    H = mp * C
    kh = H // nt
    own = half_ref[0]
    mixed = in_ref[...].reshape(H, nt)
    for q in range(kh):
        at = slice(q * nt, (q + 1) * nt)
        wt[own, :, at] = first_ref[:, q * C : (q + 1) * C, :].reshape(H, nt)
        wt[1 - own, :, at] = other_ref[:, q * C : (q + 1) * C, :].reshape(H, nt)
    step = B
    per = step // C
    bias = jnp.concatenate([bias_ref[...], jnp.zeros((B - mp, B), F32)], axis=0).T
    for s in range(mp // per):
        lo = s * step
        col_v = jnp.concatenate([bias[0:C, k : k + 1] for k in range(s * per, (s + 1) * per)], axis=0)
        col_g = jnp.concatenate([bias[C : 2 * C, k : k + 1] for k in range(s * per, (s + 1) * per)], axis=0)
        value = dot(wt[0, lo : lo + step, :], mixed) + col_v
        gate = dot(wt[1, lo : lo + step, :], mixed) + col_g
        sig = jax.nn.sigmoid(gate)
        x = first_ref[s * per : (s + 1) * per, kh * C : (kh + 1) * C, :].reshape(step, nt).astype(F32)
        g = first_ref[s * per : (s + 1) * per, (kh + 1) * C :, :].reshape(step, nt).astype(F32)
        gm_ref[s * per : (s + 1) * per, C:, :] = (x + value * sig).astype(BF16).reshape(per, C, nt)
        gv = g * sig
        gp[0, lo : lo + step, :] = gv.astype(BF16)
        gp[1, lo : lo + step, :] = (gv * value * (1.0 - sig)).astype(BF16)
    for s in range(mp // per):
        at = slice(s * step, (s + 1) * step)
        gm = dot(wt[0, :, at], gp[0], TN) + dot(wt[1, :, at], gp[1], TN)
        wide = gm * SQUARE_SCALE
        gm_ref[s * per : (s + 1) * per, 0:C, :] = (wide * jnp.abs(wide)).astype(BF16).reshape(per, C, nt)
    keep_ref[...] = gp[own]
    send_ref[...] = gp[1 - own]


def weight_kernel(place_ref, keep_ref, got_ref, mixed_ref, theirs_ref, *refs, C, mp):
    outs, wg = refs[:-1], refs[-1]
    nt = mixed_ref.shape[1]
    ways = len(outs)
    per = mp // ways
    total = dot(keep_ref[...], mixed_ref[...], NT) + dot(got_ref[...], theirs_ref[...], NT)
    for m in range(mp):
        at = (m // ways) * C
        wg[m % ways, at : at + C, :] = total[m * C : (m + 1) * C]
    ones = jnp.ones((8, nt), BF16)
    tail = dot(ones, keep_ref[...], NT) + dot(ones, got_ref[...], NT)
    for q in range(ways):
        wg[q, per * C :, :] = tail
    for k in range(ways):
        outs[k][...] = wg[lax.rem(place_ref[1], ways) ^ k]


def fold_kernel(place_ref, *refs, ways, got, C, seen):
    parts, outs, acc = refs[:got], refs[got:-1], refs[-1]
    total = parts[0][...]
    for p in parts[1:]:
        total = total + p[...]
    blocks = (total.shape[0] - 8) // C
    for z in range(blocks):
        at = (z // ways) * C
        acc[z % ways, at : at + C, :] = total[z * C : (z + 1) * C]
    for q in range(ways):
        acc[q, (blocks // ways) * C :, :] = total[blocks * C :]
    for k in range(ways):
        outs[k][...] = acc[lax.rem(lax.div(place_ref[1], seen), ways) ^ k]


def back_kernel(
    len_ref, vec_ref, x_ref, stat_ref, gm_ref, slope_hbm, t_ref, near_hbm, jump_ref,
    layer_ref, gn_ref, sum_ref, row_ref, g_ref, p_ref, r_ref, turned_ref, xs, gs, ns, tok, hs, ps, rs, rts, tab, near_ref, slope_ref, sem, *, count,
):
    i = pl.program_id(0)
    G = g_ref.shape[0]
    C, L = x_ref.shape
    N = L // B
    nt = gm_ref.shape[2]
    per = nt // B

    def fetch(q, k):
        src, dst = ((slope_hbm, slope_ref), (near_hbm, near_ref), (t_ref, tab))[q]
        at = pl.ds(k * G, G)
        return pltpu.make_async_copy(src.at[at], dst.at[at], sem.at[q, k])

    @pl.when(i == 0)
    def _():
        for k in range(C // G):
            for q in range(3):
                fetch(q, k).start()
        for n in range(N):
            xs[n * C : (n + 1) * C, :] = x_ref[:, n * B : (n + 1) * B].astype(F32)
            at = slice((n % per) * B, (n % per + 1) * B)
            square = gm_ref[n // per, 0:C, at].astype(F32)
            gs[n * C : (n + 1) * C, :] = square * (lax.rsqrt(jnp.maximum(jnp.abs(square), 1e-37)) * (1.0 / SQUARE_SCALE))
        mean, inv, mask = token_stats(stat_ref, len_ref[0], count)
        tok[0] = mean
        tok[1] = inv
        tok[2] = mask
        sum_ref[...] = jnp.zeros_like(sum_ref)
        for m in range(gm_ref.shape[0]):
            layer_ref[:, m * nt : (m + 1) * nt] = gm_ref[m, C:, :]

    fetch(0, i).wait()
    for j in range(G):
        ci = i * G + j
        g = gs[pl.ds(ci, N, stride=C), :] * slope_ref[ci]
        g_ref[j] = g
        hi, lo = split(g)
        hs[j, 0:N, :] = hi
        hs[j, N:, :] = lo
    fetch(1, i).wait()
    z_all = [dot(hs[j], near_ref[i * G + j]) for j in range(G)]
    for j, z in enumerate(z_all):
        p = z[:N, :B] + (z[:N, B:] + z[N:, :B])
        p_ref[j] = p
        ps[j * N : (j + 1) * N, :] = p
    at = pl.ds(pl.multiple_of(i * G, G), G)
    scan_blocks(ps, rs, rts, (jump_ref[0, at, :], jump_ref[1, at, :]), N, True)
    left = []
    for j in range(G):
        r = rs[j * N : (j + 1) * N, :]
        r_ref[j] = r
        turned_ref[j] = rts[j * N : (j + 1) * N, :]
        left.append(jnp.concatenate([hs[j], jnp.concatenate(split(r), axis=0)], axis=1))
    fetch(2, i).wait()
    both_all = [dot(left[j], tab[i * G + j]) for j in range(G)]
    for j, both in enumerate(both_all):
        ci = i * G + j
        mask = tok[2]
        normed = (xs[pl.ds(ci, N, stride=C), :] - tok[0]) * tok[1]
        sig = mask * (normed * vec_ref[0, ci] + vec_ref[1, ci])
        both = both[:N, : 2 * B] + (both[:N, 2 * B :] + both[N:, : 2 * B])
        gl = both[:, B:]
        grad = both[:, :B] + vec_ref[2, ci] * g_ref[j] + gl * shift_token(sig, 1) + shift_token(gl * sig, -1)
        masked = mask * grad
        gn = masked * vec_ref[0, ci]
        sum_ref[0] += gn
        sum_ref[1] += gn * normed
        ns[pl.ds(pl.multiple_of(ci * N, N), N), :] = gn
        for q, v in enumerate((g_ref[j] * sig, masked * normed, masked)):
            row_ref[j, q * 8 : (q + 1) * 8, :] = sum(v[8 * k : 8 * k + 8] for k in range(N // 8))

    @pl.when(i == pl.num_programs(0) - 1)
    def _():
        for n in range(N):
            gn_ref[:, n * B : (n + 1) * B] = ns[pl.ds(n, C, stride=N), :]


def lift_kernel(len_ref, vec_ref, x_ref, stat_ref, f_ref, u_ref, lift_ref, xs, tok, *, count):
    i = pl.program_id(0)
    G = f_ref.shape[0]
    C, L = x_ref.shape
    N = L // B

    @pl.when(i == 0)
    def _():
        for n in range(N):
            xs[n * C : (n + 1) * C, :] = x_ref[:, n * B : (n + 1) * B].astype(F32)
        tok[0], tok[1], tok[2] = token_stats(stat_ref, len_ref[0], count)

    ahead = float(B) - lane_iota((N, B)).astype(F32)
    flip = (lane_iota((B, B)) + row_iota((B, B)) == B - 1).astype(BF16)
    flat, left = [], []
    for j in range(G):
        ci = i * G + j
        normed = (xs[pl.ds(ci, N, stride=C), :] - tok[0]) * tok[1]
        sig = tok[2] * (normed * vec_ref[0, ci] + vec_ref[1, ci])
        liq = sig * shift_token(sig, 1)
        flat.append(jnp.concatenate(split(sig) + split(liq), axis=0))
        left.append(jnp.concatenate(split(jnp.concatenate([sig * ahead, liq * ahead], axis=1)), axis=0))
    turned_all = [dot(v, flip).astype(BF16) for v in flat]
    lifts = [dot(left[j], f_ref[j]) for j in range(G)]
    for j in range(G):
        turned, lift = turned_all[j], lifts[j]
        for q in range(2):
            at = slice(q * B, (q + 1) * B)
            u_ref[j, 0 : 2 * N, at] = turned[2 * q * N : (2 * q + 2) * N]
            u_ref[j, 2 * N :, at] = turned[2 * q * N : (2 * q + 1) * N]
        lift_ref[j] = lift[:N, :B] + (lift[:N, B:] + lift[N:, :B])


def sums_kernel(u_ref, lift_ref, g_ref, p_ref, r_ref, rx_ref, state_ref, sx_ref, near_ref, jump_ref, row_ref):
    i = pl.program_id(0)
    G = g_ref.shape[0]
    _, N, _ = g_ref.shape
    place = lane_iota((N, B)).astype(F32)
    rows2, lanes2 = row_iota((B, B)), lane_iota((B, B))
    inside = lanes2 + rows2 >= B - 1
    rows16 = row_iota((16, B))
    lag = lane_iota((16, B)).astype(F32)
    R = N + 16
    every = range(G)
    turned = []
    for j in every:
        g_hi, g_lo = split(g_ref[j])
        turned.append(jnp.concatenate([g_hi, g_hi, g_lo], axis=0).T)
    corr = [dot(turned[j], u_ref[j]) for j in every]
    left = []
    for j in every:
        lags = []
        for q in range(2):
            part = jnp.where(inside, corr[j][:, q * B : (q + 1) * B], 0.0)
            lags.append(jnp.sum(pltpu.roll(part, 1, 1, stride=1, stride_axis=0), axis=0, keepdims=True))
        pair = jnp.where((rows16 & 1) == 0, lags[0], lags[1])
        pair = jnp.where(rows16 < 2, pair, jnp.where(rows16 < 4, pair * lag, 0.0))
        left.append(jnp.concatenate(split(jnp.concatenate([g_ref[j] * place, pair], axis=0)), axis=0))
    both = [dot(left[j], near_ref[j]) for j in every]
    for j in every:
        ci = i * G + j
        z = both[j][:R, :B] + (both[j][:R, B:] + both[j][R:, :B])
        row_ref[j, 0:8, :] = z[N : N + 8]
        p, r, state, lift = p_ref[j], r_ref[j], state_ref[j], lift_ref[j]
        state_x, r_x = sx_ref[j], rx_ref[j]
        carry = z[:N] + float(B) * (r * jump_ref[0, pl.ds(ci, 1), :] + r_x * jump_ref[1, pl.ds(ci, 1), :])
        total = [p * state, p * state_x, carry * state + lift * r, carry * state_x + lift * r_x]
        for q, v in enumerate(total):
            row_ref[j, 8 + 8 * q : 16 + 8 * q, :] = sum(v[8 * k : 8 * k + 8] for k in range(N // 8))


def join_kernel(plain_ref, ref, out_ref):
    odd = (lane_iota((out_ref.shape[1], B)) & (B // 4)) != 0
    for q in range(2):
        out_ref[q] = jnp.where(odd, ref[:, 2 * q + 1, :], ref[:, 2 * q, :])
    for q in range(4):
        out_ref[2 + q] = jnp.sum(ref[:, 8 + 8 * q : 16 + 8 * q, :], axis=1)
    for q in range(3):
        out_ref[6 + q] = jnp.sum(plain_ref[:, 8 * q : 8 * q + 8, :], axis=1)


def finish_kernel(
    place_ref, mine_ref, theirs_ref, w_ref, step_ref, decay_ref, freq_ref, read_ref, liquid_ref, wsum_ref, across_ref,
    value_ref, gate_ref, vbias_ref, gbias_ref, step_out, decay_out, freq_out, read_out, liquid_out,
    skip_out, gain_out, bias_out, *, M,
):
    C = decay_ref.shape[0]
    half = B // 2

    def emit(first, second):
        value_ref[...] = first[0:C, :]
        gate_ref[...] = second[0:C, :]
        per = B // C
        group = place_ref[1] // per
        back = (B - (place_ref[1] % per) * C) % B
        for out, v in ((vbias_ref, first), (gbias_ref, second)):
            lanes = v[C : C + 8, pl.ds(pl.multiple_of(group * B, B), B)]
            out[...] = pltpu.roll(lanes, back, 1)[0:1, 0:C]

    @pl.when(place_ref[0] == 0)
    def _():
        emit(wsum_ref, across_ref)

    @pl.when(place_ref[0] == 1)
    def _():
        emit(across_ref, wsum_ref)

    rows = [mine_ref[q] + theirs_ref[q] for q in range(9)]

    def parts(a, b, c):
        return a[:, :half] - a[:, half:] + c[:, :half], b[:, :half] + b[:, half:] + c[:, half:]

    g_re, g_im = parts(rows[2], rows[3], rows[0])
    d_re, d_im = parts(rows[4], rows[5], rows[1])
    w = w_ref[...]
    w_re, w_im = w[:, :half], w[:, half:]
    l_re = w_re * d_re - w_im * d_im
    l_im = w_re * d_im + w_im * d_re
    cot = (
        2.0 * g_re[:, :M], -2.0 * g_im[:, :M], 2.0 * g_re[:, M:], -2.0 * g_im[:, M:],
        2.0 * (l_re[:, :M] + l_re[:, M:]), -2.0 * (l_im[:, :M] + l_im[:, M:]),
    )
    step = jnp.sum(jnp.where(row_iota((C, C)) == lane_iota((C, C)), step_ref[...], 0.0), axis=1, keepdims=True)
    _, back = jax.vjp(mode_terms, step, decay_ref[...], freq_ref[...], read_ref[...], liquid_ref[...])
    step_grad, decay_out[...], freq_out[...], read_out[...], liquid_out[...] = back(cot)
    lanes = lane_iota((B, B))
    pad = jnp.zeros((B - C, 1), F32)
    plain = jnp.zeros((B, B), F32)
    for q, v in enumerate([step_grad] + [jnp.sum(rows[6 + q], axis=1, keepdims=True) for q in range(3)]):
        plain = jnp.where(lanes == q, jnp.concatenate([v, pad], axis=0), plain)
    plain = plain.T
    for q, out in enumerate((step_out, skip_out, gain_out, bias_out)):
        out[...] = plain[q : q + 1, 0:C]


def last_kernel(x_ref, g_ref, gn_ref, stat_ref, sum_ref, out_ref, *, count):
    C, L = x_ref.shape
    for n in range(L // B):
        at = slice(n * B, (n + 1) * B)
        mean = stat_ref[0, n : n + 1, :]
        inv = lax.rsqrt(stat_ref[1, n : n + 1, :] * (1.0 / count) + EPS)
        first = sum_ref[0, n : n + 1, :] * (1.0 / count)
        second = sum_ref[1, n : n + 1, :] * (1.0 / count)
        normed = (x_ref[:, at].astype(F32) - mean) * inv
        out_ref[:, at] = inv * (gn_ref[:, at] - first - normed * second) + g_ref[:, at].astype(F32)


def total_kernel(*refs):
    total = refs[0][...]
    for p in refs[1:-1]:
        total = total + p[...]
    refs[-1][...] = total


def rounds_of(size):
    rounds, bit = [], 1
    while bit < size:
        if bit * 2 < size:
            rounds.append((bit, 2 * bit, 3 * bit))
            bit *= 4
        else:
            rounds.append((bit,))
            bit *= 2
    return rounds


def exchange(v, axis, size, off):
    return lax.ppermute(v, axis, [(k, k ^ off) for k in range(size)])


def all_sums(v, size):
    for offs in rounds_of(size):
        v = sum([exchange(v, "mp", size, o) for o in offs], v)
    return v


def sum_docs(v, size, stride):
    total = v
    for k in range(stride, size, stride):
        total = total + lax.ppermute(v, "dp", [(q, (q + k) % size) for q in range(size)])
    return total


def partner(v, size):
    return lax.ppermute(v, "dp", [(q, q ^ 1) for q in range(size)])


def mode_terms(log_step, decay_log, frequency, readout, liquid_readout):
    M = decay_log.shape[1]
    step_size = jnp.exp(log_step)
    real_rate = -jnp.exp(decay_log)
    real_step = step_size * real_rate
    imag_step = step_size * frequency
    growth = jnp.exp(real_step)
    num_real = growth * jnp.cos(imag_step) - 1.0
    num_imag = growth * jnp.sin(imag_step)
    denominator = real_rate * real_rate + frequency * frequency
    in_real = (num_real * real_rate + num_imag * frequency) / denominator
    in_imag = (num_imag * real_rate - num_real * frequency) / denominator

    def mix(coeffs):
        re, im = coeffs[:, :M], coeffs[:, M:]
        return re * in_real - im * in_imag, re * in_imag + im * in_real

    return mix(readout) + mix(liquid_readout) + (real_step, imag_step)


def per_device(
    mp, dp,
    tokens, lengths, norm_gain, norm_bias, log_step, decay_log, frequency, readout, liquid_readout,
    skip_gain, value_weight, gate_weight, value_bias, gate_bias, grad_out,
):
    C, L = tokens.shape
    H = value_weight.shape[0]
    M = decay_log.shape[1]
    N = L // B
    nt = L // mp
    kh = H // nt
    shape = jax.ShapeDtypeStruct

    place = jnp.stack([lax.axis_index("dp") & 1, lax.axis_index("mp")]).astype(jnp.int32)
    rounds = rounds_of(mp)
    small, large = 16, 32

    def pin(v):
        return pltpu.with_memory_space_constraint(v, pltpu.HBM)

    def call(kernel, out, n_in, smem=0, us=1, scratch=(), mb=small):
        return pl.pallas_call(
            kernel,
            out_shape=out,
            in_specs=[SMEM] * smem + [VMEM] * (n_in - smem),
            out_specs=jax.tree.map(lambda _: VMEM, out),
            scratch_shapes=list(scratch),
            compiler_params=params(mb),
            cost_estimate=cost(us),
        )

    def whole(*dims):
        return pl.BlockSpec(dims, lambda i: (0,) * len(dims))

    def chan_by(group):
        return lambda *dims: pl.BlockSpec((group,) + dims, lambda i: (i,) + (0,) * len(dims))

    def by_channel(kernel, out, in_specs, out_specs, us, scratch, mb=small, group=TABLE_GROUP):
        return pl.pallas_call(
            kernel,
            grid=(C // group,),
            out_shape=out,
            in_specs=in_specs,
            out_specs=out_specs,
            scratch_shapes=scratch,
            compiler_params=params(mb),
            cost_estimate=cost(us),
        )

    vm = pltpu.VMEM
    G = min(MIXER_GROUP, C)
    chan, few = chan_by(G), chan_by(TABLE_GROUP)
    blocks = shape((C, N, B), F32)
    far = pltpu.HBM
    far_blocks = far((C, N, B), F32)
    def pin(v):
        return pltpu.with_memory_space_constraint(v, far)

    hbm = pl.BlockSpec(memory_space=pltpu.HBM)
    stat, pay = pl.pallas_call(
        start_kernel,
        out_shape=(shape((2 * N + mp, B), F32), shape((mp, (2 + kh) * C, nt), BF16)),
        in_specs=[SMEM] + [hbm] * 6,
        out_specs=(VMEM, VMEM),
        scratch_shapes=[
            pltpu.VMEM((C, L), BF16), pltpu.VMEM((C, L), BF16), pltpu.VMEM((C, H), BF16),
            pltpu.VMEM((1, C), BF16), pltpu.VMEM((1, C), BF16), pltpu.SemaphoreType.DMA((5,)),
        ],
        compiler_params=params(small),
        cost_estimate=cost(3),
    )(
        place, pin(tokens), pin(grad_out), pin(value_weight.T), pin(gate_weight.T), pin(value_bias[None]), pin(gate_bias[None])
    )
    first = lax.all_to_all(pay, "mp", split_axis=0, concat_axis=0, tiled=True)

    rates = jnp.stack(
        [jnp.broadcast_to(log_step[:, None], (C, 4 * M)), jnp.tile(decay_log, (1, 4)), jnp.tile(frequency, (1, 4))]
    )
    coef = jnp.concatenate([readout[:, :M], liquid_readout[:, :M], readout[:, M:], liquid_readout[:, M:]], axis=1)
    f_near, f_tab, t_tab, jump, w_all = by_channel(
        partial(table_kernel, C=C, M=M),
        (
            shape((C, 2 * B, 2 * B), BF16), far((C, 2 * B, 2 * B), BF16), shape((C, 3 * B, 2 * B), BF16),
            shape((2, C, B), F32), shape((C, B), F32),
        ),
        [whole(3, C, B), whole(C, B)],
        (few(2 * B, 2 * B), few(2 * B, 2 * B), few(3 * B, 2 * B), whole(2, C, B), whole(C, B)),
        6,
        [vm((3, B, B), F32)],
    )(rates, coef)

    count = C
    for k, offs in enumerate(rounds[::-1]):
        parts = [stat] + [exchange(stat, "mp", mp, o) for o in offs]
        if k == 0:
            parts[1], parts[-1], t_tab = lax.optimization_barrier((parts[1], parts[-1], t_tab))
        if k < len(rounds) - 1:
            stat = jnp.concatenate(join_stats(parts, N, float(count)), axis=0)
            count *= len(parts)

    vecs = jnp.stack([norm_gain, norm_bias, skip_gain])
    mixed, slope, state, state_x, stat, bias = by_channel(
        partial(mixer_kernel, count=H, parts=len(parts)),
        (shape((mp, C, nt), BF16), far_blocks, far_blocks, far_blocks, shape((2, N, B), F32), shape((mp, B), F32)),
        [SMEM, SMEM, whole(C, L)] + [whole(2 * N + mp, B)] * len(parts)
        + [chan(2 * B, 2 * B), chan(3 * B, 2 * B), whole(2, C, B)],
        (whole(mp, C, nt), chan(N, B), chan(N, B), chan(N, B), whole(2, N, B), whole(mp, B)),
        6,
        [
            vm((N * C, B), F32), vm((N * C, B), F32), vm((3, N, B), F32), vm((G, 2 * N, 2 * B), BF16),
            vm((G * N, B), F32), vm((G * N, B), F32), vm((G * N, B), F32),
        ],
        large,
        G,
    )(lengths, vecs, tokens, *parts, f_near, t_tab, jump)

    mixed, first, rates = lax.optimization_barrier((mixed, first, rates))
    other_w = partner(first[:, : kh * C, :], dp)
    mixed_tok = lax.all_to_all(mixed, "mp", split_axis=0, concat_axis=0, tiled=True)
    back_tab, near_tab = by_channel(
        partial(back_table_kernel, C=C, M=M),
        (far((C, 2 * B, 4 * B), BF16), far((C, B, 2 * B), BF16)),
        [whole(3, C, B), whole(C, B)],
        (few(2 * B, 4 * B), few(B, 2 * B)),
        7,
        [vm((3, B, B), F32)],
    )(rates, w_all)
    mixed_tok, back_tab = lax.optimization_barrier((mixed_tok, back_tab))
    gm, keep, send = call(
        glu_kernel,
        (shape((mp, 2 * C, nt), BF16),) + (shape((H, nt), BF16),) * 2,
        5, 1, 2, [vm((2, H, nt), BF16), vm((2, H, H), BF16)],
    )(place, mixed_tok, first, other_w, bias)
    mixed_tok = mixed_tok.reshape(H, nt)
    gm, f_tab = lax.optimization_barrier((gm, f_tab))
    gm = lax.all_to_all(gm, "mp", split_axis=0, concat_axis=0, tiled=True)
    u_rev, lift = by_channel(
        partial(lift_kernel, count=H),
        (far((C, 3 * N, 2 * B), BF16), far_blocks),
        [SMEM, SMEM, whole(C, L), whole(2, N, B), few(2 * B, 2 * B)],
        (few(3 * N, 2 * B), few(N, B)),
        3,
        [vm((N * C, B), F32), vm((3, N, B), F32)],
        56,
    )(lengths, vecs, tokens, stat, pin(f_tab))
    gm, lift = lax.optimization_barrier((gm, lift))

    ways = len(rounds[0]) + 1
    rows_left = mp // ways
    outs = call(
        partial(weight_kernel, C=C, mp=mp), (shape((rows_left * C + 8, H), F32),) * ways, 5, 1, 2,
        [vm((ways, rows_left * C + 8, H), F32)],
    )(place, keep, partner(send, dp), mixed_tok, partner(mixed_tok, dp))
    terms = [outs[0]] + [exchange(v, "mp", mp, o) for v, o in zip(outs[1:], rounds[0])]

    layer_out, gn, sums, plain, g_pre, p_blk, r_blk, rx_blk = by_channel(
        partial(back_kernel, count=H),
        (shape((C, L), BF16), shape((C, L), F32), shape((2, N, B), F32), shape((C, 24, B), F32)) + (blocks,) * 4,
        [
            SMEM, SMEM, VMEM, VMEM, VMEM, hbm, hbm, hbm, VMEM,
        ],
        (whole(C, L), whole(C, L), whole(2, N, B), chan(24, B)) + (chan(N, B),) * 4,
        7,
        [
            vm((N * C, B), F32), vm((N * C, B), F32), vm((N * C, B), F32), vm((3, N, B), F32),
            vm((G, 2 * N, B), BF16), vm((G * N, B), F32), vm((G * N, B), F32), vm((G * N, B), F32),
            vm((C, 2 * B, 4 * B), BF16), vm((C, B, 2 * B), BF16), vm((C, N, B), F32),
            pltpu.SemaphoreType.DMA((3, C // G)),
        ],
        large,
        G,
    )(lengths, vecs, tokens, stat, gm, pin(slope), pin(back_tab), pin(near_tab), jump)

    seen = ways
    terms[0], plain = lax.optimization_barrier((terms[0], plain))
    while seen < mp:
        ways, offs = 2, (seen,)
        rows_left //= ways
        outs = call(
            partial(fold_kernel, ways=ways, got=len(terms), C=C, seen=seen),
            (shape((rows_left * C + 8, H), F32),) * ways,
            1 + len(terms), 1, 1, [vm((ways, rows_left * C + 8, H), F32)],
        )(place, *terms)
        terms = [outs[0]] + [exchange(v, "mp", mp, o) for v, o in zip(outs[1:], offs)]
        seen *= ways
    for k, offs in enumerate(rounds[::-1]):
        got = [exchange(sums, "mp", mp, o) for o in offs]
        if k == len(rounds) - 1:
            g_pre, sums, terms[0] = lax.optimization_barrier((g_pre, sums, terms[0]))
            rows = by_channel(
                sums_kernel,
                shape((C, 40, B), F32),
                [chan(3 * N, 2 * B)] + [chan(N, B)] * 7 + [chan(B, 2 * B), whole(2, C, B)],
                chan(40, B),
                20,
                [],
                large,
                G,
            )(pin(u_rev), pin(lift), g_pre, p_blk, r_blk, rx_blk, pin(state), pin(state_x), pin(near_tab), jump)
            got, rows, terms = lax.optimization_barrier((got, rows, terms))
        sums = sum(got, sums)
    grad_tokens = call(partial(last_kernel, count=H), shape((C, L), F32), 5)(tokens, grad_out, gn, stat, sums)
    rows = call(join_kernel, shape((9, C, B), F32), 2)(plain, rows)
    others = sum_docs(rows, dp, 1) - rows if dp > 2 else partner(rows, dp)

    wsum = call(total_kernel, shape((C + 8, H), F32), len(terms))(*terms)
    wsum = sum_docs(wsum, dp, 2)
    across = partner(wsum, dp)
    thin, wide = shape((C, M), F32), shape((C, 2 * M), F32)
    line = shape((1, C), F32)
    (
        value_wgrad, gate_wgrad, vb, gb, step_grad, decay_grad, frequency_grad, readout_grad, liquid_grad,
        skip_grad, gain_grad, bias_grad,
    ) = call(
        partial(finish_kernel, M=M),
        (shape((C, H), F32), shape((C, H), F32), line, line, line, thin, thin, wide, wide, line, line, line),
        11, 1,
    )(
        place, rows, others, w_all, log_step[None], decay_log, frequency, readout, liquid_readout, wsum, across,
    )
    return (
        layer_out, grad_tokens, gain_grad[0], bias_grad[0], step_grad[0], decay_grad, frequency_grad, readout_grad,
        liquid_grad, skip_grad[0], value_wgrad.T, gate_wgrad.T, vb[0], gb[0],
    )


def solution(mesh):
    row, col, act = P("mp"), P(None, "mp"), P("mp", "dp")
    wide = P("mp", None)
    in_specs = (act, P("dp"), row, row, row, wide, wide, wide, wide, row, col, col, row, row, act)
    out_specs = (act, act, row, row, row, wide, wide, wide, wide, row, col, col, row, row)
    return jax.shard_map(
        partial(per_device, mesh.shape["mp"], mesh.shape["dp"]),
        mesh=mesh, in_specs=in_specs, out_specs=out_specs, check_vma=False,
    )
```

```python
from functools import partial

import jax
import jax.numpy as jnp
import numpy as np
from jax import lax
from jax.experimental import pallas as pl
from jax.experimental.pallas import tpu as pltpu
from jax.sharding import PartitionSpec as P

B = 128
TABLE_GROUP = 8
MIXER_GROUP = 16
F32 = jnp.float32
BF16 = jnp.bfloat16
NN = (((1,), (0,)), ((), ()))
NT = (((1,), (1,)), ((), ()))
TN = (((0,), (0,)), ((), ()))
EPS = 1e-05
SQUARE_SCALE = 65536.0
VMEM = pl.BlockSpec(memory_space=pltpu.VMEM)
SMEM = pl.BlockSpec(memory_space=pltpu.SMEM)


def params(mb):
    return pltpu.CompilerParams(vmem_limit_bytes=mb * 1024 * 1024)


def cost(us):
    return pl.CostEstimate(flops=int(us * 1e9), bytes_accessed=int(us * 1e6), transcendentals=0)


def dot(a, b, dims=NN):
    return lax.dot_general(a, b, dims, preferred_element_type=F32)


def split(v):
    hi = v.astype(BF16)
    return hi, (v - hi.astype(F32)).astype(BF16)


def sincos(x):
    k = jnp.floor(x * 0.6366197723675814 + 0.5)
    y = ((x - k * 1.5703125) - k * 4.837512969970703e-4) - k * 7.54978995489188e-8
    y2 = y * y
    s = y + y * y2 * (-1.6666654611e-1 + y2 * (8.3321608736e-3 - y2 * 1.9515295891e-4))
    c = 1.0 - 0.5 * y2 + y2 * y2 * (4.166664568298827e-2 + y2 * (-1.388731625493765e-3 + y2 * 2.443315711809948e-5))
    q = k.astype(jnp.int32)
    odd = (q & 1) == 1
    sin = jnp.where(odd, c, s)
    cos = jnp.where(odd, s, c)
    sin = jnp.where((q & 2) == 2, -sin, sin)
    cos = jnp.where(((q + 1) & 2) == 2, -cos, cos)
    return sin, cos


def row_iota(shape):
    return lax.broadcasted_iota(jnp.int32, shape, 0)


def lane_iota(shape):
    return lax.broadcasted_iota(jnp.int32, shape, 1)


def shift_token(x, k):
    n = x.shape[0]
    lanes = lane_iota(x.shape)
    rows = row_iota(x.shape)
    turned = pltpu.roll(x, k % B, 1)
    wrapped = pltpu.roll(turned, k % n, 0)
    if k > 0:
        wrapped = jnp.where(rows >= 1, wrapped, 0.0)
        return jnp.where(lanes == 0, wrapped, turned)
    wrapped = jnp.where(rows < n - 1, wrapped, 0.0)
    return jnp.where(lanes == B - 1, wrapped, turned)


def swap_halves(x):
    return pltpu.roll(x, B // 2, 1)


def scan_blocks(v_ref, out_ref, turned_ref, jump, N, backward):
    a_re, a_im = jump
    G = v_ref.shape[0] // N
    s = jnp.zeros((G, B), F32)
    t = s
    for k in range(N):
        n = N - 1 - k if backward else k
        out_ref[pl.ds(n, G, stride=N), :] = s
        turned_ref[pl.ds(n, G, stride=N), :] = t
        v = v_ref[pl.ds(n, G, stride=N), :]
        s, t = a_re * s + (a_im * t + v), a_re * t + (swap_halves(v) - a_im * s)


def start_kernel(
    place_ref, x_hbm, g_hbm, v_hbm, w_hbm, vb_hbm, gb_hbm, stat_ref, pay_ref, x_ref, g_ref, wt_ref, vb_ref, gb_ref, sems,
):
    C, L = x_ref.shape
    N = L // B
    mp, rows, nt = pay_ref.shape
    few = rows - 2 * C
    pairs = ((x_hbm, x_ref), (g_hbm, g_ref), (vb_hbm, vb_ref), (gb_hbm, gb_ref))
    moves = [pltpu.make_async_copy(src, dst, sems.at[1 + k]) for k, (src, dst) in enumerate(pairs)]
    for move in moves:
        move.start()
    for half, ref in enumerate((v_hbm, w_hbm)):

        @pl.when(place_ref[0] == half)
        def _():
            pltpu.make_async_copy(ref, wt_ref, sems.at[0]).start()

    moves[0].wait()
    for n in range(N):
        x = x_ref[:, n * B : (n + 1) * B].astype(F32)
        mean = jnp.sum(x, axis=0, keepdims=True) * (1.0 / C)
        dev = x - mean
        stat_ref[n : n + 1, :] = mean
        stat_ref[N + n : N + n + 1, :] = jnp.sum(dev * dev, axis=0, keepdims=True)
    own = row_iota((mp, B))
    moves[2].wait()
    moves[3].wait()
    bias = jnp.concatenate([vb_ref[...].astype(F32), gb_ref[...].astype(F32), jnp.zeros((1, B - 2 * C), F32)], axis=1)
    stat_ref[2 * N :, :] = jnp.where(own == place_ref[1], bias, 0.0)
    for j in range(mp):
        pay_ref[j, few : few + C, :] = x_ref[:, j * nt : (j + 1) * nt]
    moves[1].wait()
    for j in range(mp):
        pay_ref[j, few + C :, :] = g_ref[:, j * nt : (j + 1) * nt]
    pltpu.make_async_copy(v_hbm, wt_ref, sems.at[0]).wait()
    parts = wt_ref.shape[1] // B
    for j in range(mp):
        lanes = slice(j % parts * B, (j % parts + 1) * B)
        for q in range(nt // B):
            pay_ref[j, 0:few, q * B : (q + 1) * B] = wt_ref[q * few : (q + 1) * few, lanes]


def join_stats(parts, N, count):
    mean = sum(p[:N] for p in parts) * (1.0 / len(parts))
    spread = sum(p[N : 2 * N] for p in parts) + count * sum((p[:N] - mean) * (p[:N] - mean) for p in parts)
    return mean, spread, sum(p[2 * N :] for p in parts)


def columns(arrays, cols, C):
    pad = jnp.zeros((B - C, B), F32)
    for q, v in enumerate(arrays):
        cols[q] = jnp.concatenate([v, pad], axis=0).T


def channel_waves(cols, i, M, G):
    back = (B - i * G) % B
    al = pltpu.roll(cols[0, 0:M, :], back, 1)
    om = pltpu.roll(cols[1, 0:M, :], back, 1)
    ww = 2.0 * pltpu.roll(cols[2], back, 1)
    place = lane_iota((M, B)).astype(F32)
    ahead = float(B) - place
    out = []
    for j in range(G):
        a = jnp.broadcast_to(al[:, j : j + 1], (M, B))
        o = jnp.broadcast_to(om[:, j : j + 1], (M, B))
        w = [jnp.broadcast_to(ww[q * M : (q + 1) * M, j : j + 1], (M, B)) for q in range(4)]
        sin, cos = sincos(o * place)
        mag = jnp.exp(a * place)
        near = mag * cos, mag * sin
        sin, cos = sincos(o * ahead)
        mag = jnp.exp(a * ahead)
        out.append((near, (mag * cos, mag * sin), w))
    return out


def toeplitz_rows(kern, start):
    return pltpu.roll(jnp.broadcast_to(kern, (B, B)), start, 1, stride=1, stride_axis=0)


def table_kernel(rates_ref, coef_ref, f_ref, again_ref, t_ref, jump_ref, wout_ref, cols, *, C, M):
    i = pl.program_id(0)
    G = f_ref.shape[0]

    @pl.when(i == 0)
    def _():
        step_size = jnp.exp(rates_ref[0])
        real_rate = -jnp.exp(rates_ref[1])
        freq = rates_ref[2]
        re = step_size * real_rate
        im = step_size * freq
        growth = jnp.exp(re)
        sin, cos = sincos(im)
        num_re = growth * cos - 1.0
        num_im = growth * sin
        den = real_rate * real_rate + freq * freq
        in_re = (num_re * real_rate + num_im * freq) / den
        in_im = (num_im * real_rate - num_re * freq) / den
        coef = coef_ref[...]
        first = lane_iota(coef.shape) < B // 2
        w = coef * in_re + swap_halves(coef) * jnp.where(first, -in_im, in_im)
        wout_ref[...] = w
        sin, cos = sincos(im * float(B))
        mag = jnp.exp(re * float(B))
        jump_ref[0] = mag * cos
        jump_ref[1] = mag * jnp.where(first, -sin, sin)
        columns((re, im, w), cols, C)

    rows = row_iota((B, B))
    lanes = lane_iota((B, B))
    odd = (lanes & M) == M
    every = range(G)
    waves = channel_waves(cols, i, M, G)
    feeds = [jnp.concatenate([f_re, f_re, f_im, f_im], axis=0).T for _, (f_re, f_im), _ in waves]
    kerns = []
    for j in every:
        (n_re, n_im), _, w = waves[j]
        for h in range(2):
            w_re, w_im = w[h], w[2 + h]
            e_re = w_re * n_re - w_im * n_im
            e_im = -(w_re * n_im + w_im * n_re)
            kerns.append(jnp.sum(e_re, axis=0, keepdims=True))
            for q, v in enumerate(split(e_re)):
                t_ref[j, 2 * B + h * M : 2 * B + (h + 1) * M, q * B : (q + 1) * B] = v
            for q, v in enumerate(split(e_im)):
                t_ref[j, 2 * B + (2 + h) * M : 2 * B + (3 + h) * M, q * B : (q + 1) * B] = v
    rolled = [toeplitz_rows(kern, 0) for kern in kerns]
    for j in every:
        for h in range(2):
            part = jnp.where(odd if h == 1 else ~odd, feeds[j], 0.0)
            for q, v in enumerate(split(part)):
                f_ref[j, h * B : (h + 1) * B, q * B : (q + 1) * B] = v
                again_ref[j, h * B : (h + 1) * B, q * B : (q + 1) * B] = v
            toe = jnp.where(lanes >= rows, rolled[2 * j + h], 0.0)
            for q, v in enumerate(split(toe)):
                t_ref[j, h * B : (h + 1) * B, q * B : (q + 1) * B] = v


def back_table_kernel(rates_ref, w_ref, *refs, C, M, start):
    t_ref, near_ref, cols = refs[-3:]
    i = pl.program_id(0) + start
    G = t_ref.shape[0]

    @pl.when(i == start)
    def _():
        step_size = jnp.exp(rates_ref[0])
        columns((step_size * -jnp.exp(rates_ref[1]), step_size * rates_ref[2], w_ref[...]), cols, C)

    rows = row_iota((B, B))
    lanes = lane_iota((B, B))
    zero = jnp.zeros((M, B), BF16)
    every = range(G)
    waves = channel_waves(cols, i, M, G)
    turned = [jnp.concatenate([n_re, n_re, n_im, n_im], axis=0).T for (n_re, n_im), _, _ in waves]
    kerns, starts = [], []
    for j in every:
        (n_re, n_im), (f_re, f_im), w = waves[j]
        for h in range(2):
            w_re, w_im = w[h], w[2 + h]
            b_re = w_re * f_re - w_im * f_im
            b_im = -(w_re * f_im + w_im * f_re)
            kerns.append(jnp.sum(b_re, axis=0, keepdims=True))
            starts.append(jnp.sum(w_re * n_re - w_im * n_im, axis=0, keepdims=True)[:, 0:1])
            for part, v2 in ((0, b_re), (2, b_im)):
                for q, v in enumerate(split(v2)):
                    at = slice((2 * q + h) * B, (2 * q + h + 1) * B)
                    t_ref[j, B + part * M : B + (part + 1) * M, at] = v
                    t_ref[j, B + (part + 1) * M : B + (part + 2) * M, at] = zero
    rolled = [toeplitz_rows(kern, 0) for kern in kerns]
    for j in every:
        for q, v in enumerate(split(turned[j])):
            near_ref[j, :, q * B : (q + 1) * B] = v
        for h in range(2):
            start = jnp.broadcast_to(starts[2 * j + h], (B, B))
            toe = jnp.where(lanes < rows, rolled[2 * j + h], jnp.where(lanes == rows, start, 0.0))
            for q, v in enumerate(split(toe)):
                t_ref[j, 0:B, (2 * q + h) * B : (2 * q + h + 1) * B] = v


def token_stats(stat_ref, length, count):
    mean = stat_ref[0]
    inv = lax.rsqrt(stat_ref[1] * (1.0 / count) + EPS)
    place = row_iota(mean.shape) * B + lane_iota(mean.shape)
    return mean, inv, (place < length).astype(F32)


def mixer_kernel(len_ref, vec_ref, x_ref, *refs, count, parts):
    part_refs, refs = refs[:parts], refs[parts:]
    f_ref, t_ref, jump_ref = refs[:3]
    mixed_ref, slope_ref, state_ref, other_ref, stat_ref, bias_ref = refs[3:9]
    xs, ms, tok, us, ups, sts, ots = refs[9:]
    i = pl.program_id(0)
    G = f_ref.shape[0]
    C, L = x_ref.shape
    N = L // B
    nt = mixed_ref.shape[2]

    @pl.when(i == 0)
    def _():
        for n in range(N):
            xs[n * C : (n + 1) * C, :] = x_ref[:, n * B : (n + 1) * B].astype(F32)
        stat_ref[0], stat_ref[1], bias_ref[...] = join_stats([r[...] for r in part_refs], N, count / parts)
        mean, inv, mask = token_stats(stat_ref, len_ref[0], count)
        tok[0] = mean
        tok[1] = inv
        tok[2] = mask

    for j in range(G):
        ci = i * G + j
        normed = (xs[pl.ds(ci, N, stride=C), :] - tok[0]) * tok[1]
        sig = tok[2] * (normed * vec_ref[0, ci] + vec_ref[1, ci])
        liq = sig * shift_token(sig, 1)
        for q, v in enumerate((sig, liq)):
            hi, lo = split(v)
            us[j, 0:N, q * B : (q + 1) * B] = hi
            us[j, N:, q * B : (q + 1) * B] = lo
        slope_ref[j] = sig
    ups_all = [dot(us[j], f_ref[j]) for j in range(G)]
    for j, up in enumerate(ups_all):
        ups[j * N : (j + 1) * N, :] = up[:N, :B] + (up[:N, B:] + up[N:, :B])
    at = pl.ds(pl.multiple_of(i * G, G), G)
    scan_blocks(ups, sts, ots, (jump_ref[0, at, :], jump_ref[1, at, :]), N, False)
    left = []
    for j in range(G):
        state = sts[j * N : (j + 1) * N, :]
        state_ref[j] = state
        other_ref[j] = ots[j * N : (j + 1) * N, :]
        left.append(jnp.concatenate([us[j], jnp.concatenate(split(state), axis=0)], axis=1))
    outs = [dot(left[j], t_ref[j]) for j in range(G)]
    for j, out in enumerate(outs):
        ci = i * G + j
        mask = tok[2]
        y = out[:N, :B] + (out[:N, B:] + out[N:, :B]) + vec_ref[2, ci] * slope_ref[j]
        y2 = y * y
        th = jnp.tanh(0.7978845608028654 * (y + 0.044715 * (y * y2)))
        half = 0.5 * (1.0 + th)
        ms[pl.ds(pl.multiple_of(ci * N, N), N), :] = mask * (y * half)
        slope_ref[j] = mask * (half + 0.5 * y * (1.0 - th * th) * (0.7978845608028654 * (1.0 + 0.134145 * y2)))

    @pl.when(i == pl.num_programs(0) - 1)
    def _():
        per = nt // B
        for n in range(N):
            mixed_ref[n // per, :, (n % per) * B : (n % per + 1) * B] = ms[pl.ds(n, C, stride=N), :].astype(BF16)


def glu_kernel(place_ref, in_ref, first_ref, bias_ref, *refs, parts):
    own_refs, other_refs, refs = refs[:parts], refs[parts : 2 * parts], refs[2 * parts :]
    gm_ref, keep_ref, send_ref, gp, wt = refs
    mp, C, nt = in_ref.shape
    H = mp * C
    few = own_refs[0].shape[1]
    own = place_ref[0]
    mixed = in_ref[...].reshape(H, nt)
    for k in range(parts):
        lanes = pl.ds(pl.multiple_of((lax.rem(place_ref[1], parts) ^ k) * B, B), B)
        for q in range(nt // B):
            at = slice(q * few, (q + 1) * few)
            wt[own, :, at, lanes] = own_refs[k][:, :, q * B : (q + 1) * B]
            wt[1 - own, :, at, lanes] = other_refs[k][:, :, q * B : (q + 1) * B]
    step = B
    per = step // C
    bias = jnp.concatenate([bias_ref[...], jnp.zeros((B - mp, B), F32)], axis=0).T
    for s in range(mp // per):
        lo = s * step
        col_v = jnp.concatenate([bias[0:C, k : k + 1] for k in range(s * per, (s + 1) * per)], axis=0)
        col_g = jnp.concatenate([bias[C : 2 * C, k : k + 1] for k in range(s * per, (s + 1) * per)], axis=0)
        at = slice(s * per, (s + 1) * per)
        value = dot(wt[0, at].reshape(step, H), mixed) + col_v
        gate = dot(wt[1, at].reshape(step, H), mixed) + col_g
        sig = jax.nn.sigmoid(gate)
        x = first_ref[at, few : few + C, :].reshape(step, nt).astype(F32)
        g = first_ref[at, few + C :, :].reshape(step, nt).astype(F32)
        gm_ref[s * per : (s + 1) * per, C:, :] = (x + value * sig).astype(BF16).reshape(per, C, nt)
        gv = g * sig
        gp[0, lo : lo + step, :] = gv.astype(BF16)
        gp[1, lo : lo + step, :] = (gv * value * (1.0 - sig)).astype(BF16)
    for s in range(mp // per):
        at = slice(s * step, (s + 1) * step)
        gm = sum(dot(wt[h, :, :, at].reshape(H, step), gp[h], TN) for h in range(2))
        wide = gm * SQUARE_SCALE
        gm_ref[s * per : (s + 1) * per, 0:C, :] = (wide * jnp.abs(wide)).astype(BF16).reshape(per, C, nt)
    keep_ref[...] = gp[own]
    send_ref[...] = gp[1 - own]


def weight_kernel(place_ref, keep_ref, got_ref, mixed_ref, theirs_ref, *refs, C, mp):
    outs, wg = refs[:-1], refs[-1]
    nt = mixed_ref.shape[1]
    ways = len(outs)
    per = mp // ways
    total = dot(keep_ref[...], mixed_ref[...], NT) + dot(got_ref[...], theirs_ref[...], NT)
    for m in range(mp):
        at = (m // ways) * C
        wg[m % ways, at : at + C, :] = total[m * C : (m + 1) * C]
    ones = jnp.ones((8, nt), BF16)
    tail = dot(ones, keep_ref[...], NT) + dot(ones, got_ref[...], NT)
    for q in range(ways):
        wg[q, per * C :, :] = tail
    for k in range(ways):
        outs[k][...] = wg[lax.rem(place_ref[1], ways) ^ k]


def fold_kernel(place_ref, *refs, ways, got, C, seen):
    parts, outs, acc = refs[:got], refs[got:-1], refs[-1]
    total = parts[0][...]
    for p in parts[1:]:
        total = total + p[...]
    blocks = (total.shape[0] - 8) // C
    for z in range(blocks):
        at = (z // ways) * C
        acc[z % ways, at : at + C, :] = total[z * C : (z + 1) * C]
    for q in range(ways):
        acc[q, (blocks // ways) * C :, :] = total[blocks * C :]
    for k in range(ways):
        outs[k][...] = acc[lax.rem(lax.div(place_ref[1], seen), ways) ^ k]


def back_kernel(
    len_ref, vec_ref, x_ref, stat_ref, gm_ref, slope_hbm, t_ref, near_hbm, jump_ref,
    layer_ref, gn_ref, sum_ref, row_ref, g_ref, p_ref, r_ref, turned_ref, xs, gs, ns, tok, hs, ps, rs, rts, tab, near_ref, slope_ref, sem, *, count,
):
    i = pl.program_id(0)
    G = g_ref.shape[0]
    C, L = x_ref.shape
    N = L // B
    nt = gm_ref.shape[2]
    per = nt // B

    def fetch(q, k):
        src, dst = ((slope_hbm, slope_ref), (near_hbm, near_ref), (t_ref, tab))[q]
        at = pl.ds(k * G, G)
        return pltpu.make_async_copy(src.at[at], dst.at[at], sem.at[q, k])

    @pl.when(i == 0)
    def _():
        for k in range(C // G):
            for q in range(3):
                fetch(q, k).start()
        for n in range(N):
            xs[n * C : (n + 1) * C, :] = x_ref[:, n * B : (n + 1) * B].astype(F32)
            at = slice((n % per) * B, (n % per + 1) * B)
            square = gm_ref[n // per, 0:C, at].astype(F32)
            gs[n * C : (n + 1) * C, :] = square * (lax.rsqrt(jnp.maximum(jnp.abs(square), 1e-37)) * (1.0 / SQUARE_SCALE))
        mean, inv, mask = token_stats(stat_ref, len_ref[0], count)
        tok[0] = mean
        tok[1] = inv
        tok[2] = mask
        sum_ref[...] = jnp.zeros_like(sum_ref)
        for m in range(gm_ref.shape[0]):
            layer_ref[:, m * nt : (m + 1) * nt] = gm_ref[m, C:, :]

    fetch(0, i).wait()
    for j in range(G):
        ci = i * G + j
        g = gs[pl.ds(ci, N, stride=C), :] * slope_ref[ci]
        g_ref[j] = g
        hi, lo = split(g)
        hs[j, 0:N, :] = hi
        hs[j, N:, :] = lo
    fetch(1, i).wait()
    z_all = [dot(hs[j], near_ref[i * G + j]) for j in range(G)]
    for j, z in enumerate(z_all):
        p = z[:N, :B] + (z[:N, B:] + z[N:, :B])
        p_ref[j] = p
        ps[j * N : (j + 1) * N, :] = p
    at = pl.ds(pl.multiple_of(i * G, G), G)
    scan_blocks(ps, rs, rts, (jump_ref[0, at, :], jump_ref[1, at, :]), N, True)
    left = []
    for j in range(G):
        r = rs[j * N : (j + 1) * N, :]
        r_ref[j] = r
        turned_ref[j] = rts[j * N : (j + 1) * N, :]
        left.append(jnp.concatenate([hs[j], jnp.concatenate(split(r), axis=0)], axis=1))
    fetch(2, i).wait()
    both_all = [dot(left[j], tab[i * G + j]) for j in range(G)]
    for j, both in enumerate(both_all):
        ci = i * G + j
        mask = tok[2]
        normed = (xs[pl.ds(ci, N, stride=C), :] - tok[0]) * tok[1]
        sig = mask * (normed * vec_ref[0, ci] + vec_ref[1, ci])
        both = both[:N, : 2 * B] + (both[:N, 2 * B :] + both[N:, : 2 * B])
        gl = both[:, B:]
        grad = both[:, :B] + vec_ref[2, ci] * g_ref[j] + gl * shift_token(sig, 1) + shift_token(gl * sig, -1)
        masked = mask * grad
        gn = masked * vec_ref[0, ci]
        sum_ref[0] += gn
        sum_ref[1] += gn * normed
        ns[pl.ds(pl.multiple_of(ci * N, N), N), :] = gn
        for q, v in enumerate((g_ref[j] * sig, masked * normed, masked)):
            row_ref[j, q * 8 : (q + 1) * 8, :] = sum(v[8 * k : 8 * k + 8] for k in range(N // 8))

    @pl.when(i == pl.num_programs(0) - 1)
    def _():
        for n in range(N):
            gn_ref[:, n * B : (n + 1) * B] = ns[pl.ds(n, C, stride=N), :]


def lift_kernel(len_ref, vec_ref, x_ref, stat_ref, f_ref, u_ref, lift_ref, xs, tok, *, count):
    i = pl.program_id(0)
    G = f_ref.shape[0]
    C, L = x_ref.shape
    N = L // B

    @pl.when(i == 0)
    def _():
        for n in range(N):
            xs[n * C : (n + 1) * C, :] = x_ref[:, n * B : (n + 1) * B].astype(F32)
        tok[0], tok[1], tok[2] = token_stats(stat_ref, len_ref[0], count)

    ahead = float(B) - lane_iota((N, B)).astype(F32)
    flip = (lane_iota((B, B)) + row_iota((B, B)) == B - 1).astype(BF16)
    flat, left = [], []
    for j in range(G):
        ci = i * G + j
        normed = (xs[pl.ds(ci, N, stride=C), :] - tok[0]) * tok[1]
        sig = tok[2] * (normed * vec_ref[0, ci] + vec_ref[1, ci])
        liq = sig * shift_token(sig, 1)
        flat.append(jnp.concatenate(split(sig) + split(liq), axis=0))
        left.append(jnp.concatenate(split(jnp.concatenate([sig * ahead, liq * ahead], axis=1)), axis=0))
    turned_all = [dot(v, flip).astype(BF16) for v in flat]
    lifts = [dot(left[j], f_ref[j]) for j in range(G)]
    for j in range(G):
        turned, lift = turned_all[j], lifts[j]
        for q in range(2):
            at = slice(q * B, (q + 1) * B)
            u_ref[j, 0 : 2 * N, at] = turned[2 * q * N : (2 * q + 2) * N]
            u_ref[j, 2 * N :, at] = turned[2 * q * N : (2 * q + 1) * N]
        lift_ref[j] = lift[:N, :B] + (lift[:N, B:] + lift[N:, :B])


def sums_kernel(u_ref, lift_ref, g_ref, p_ref, r_ref, rx_ref, state_ref, sx_ref, near_ref, jump_ref, row_ref):
    i = pl.program_id(0)
    G = g_ref.shape[0]
    _, N, _ = g_ref.shape
    place = lane_iota((N, B)).astype(F32)
    rows2, lanes2 = row_iota((B, B)), lane_iota((B, B))
    inside = lanes2 + rows2 >= B - 1
    rows16 = row_iota((16, B))
    lag = lane_iota((16, B)).astype(F32)
    R = N + 16
    every = range(G)
    turned = []
    for j in every:
        g_hi, g_lo = split(g_ref[j])
        turned.append(jnp.concatenate([g_hi, g_hi, g_lo], axis=0).T)
    corr = [dot(turned[j], u_ref[j]) for j in every]
    left = []
    for j in every:
        lags = []
        for q in range(2):
            part = jnp.where(inside, corr[j][:, q * B : (q + 1) * B], 0.0)
            lags.append(jnp.sum(pltpu.roll(part, 1, 1, stride=1, stride_axis=0), axis=0, keepdims=True))
        pair = jnp.where((rows16 & 1) == 0, lags[0], lags[1])
        pair = jnp.where(rows16 < 2, pair, jnp.where(rows16 < 4, pair * lag, 0.0))
        left.append(jnp.concatenate(split(jnp.concatenate([g_ref[j] * place, pair], axis=0)), axis=0))
    both = [dot(left[j], near_ref[j]) for j in every]
    for j in every:
        ci = i * G + j
        z = both[j][:R, :B] + (both[j][:R, B:] + both[j][R:, :B])
        row_ref[j, 0:8, :] = z[N : N + 8]
        p, r, state, lift = p_ref[j], r_ref[j], state_ref[j], lift_ref[j]
        state_x, r_x = sx_ref[j], rx_ref[j]
        carry = z[:N] + float(B) * (r * jump_ref[0, pl.ds(ci, 1), :] + r_x * jump_ref[1, pl.ds(ci, 1), :])
        total = [p * state, p * state_x, carry * state + lift * r, carry * state_x + lift * r_x]
        for q, v in enumerate(total):
            row_ref[j, 8 + 8 * q : 16 + 8 * q, :] = sum(v[8 * k : 8 * k + 8] for k in range(N // 8))


def join_kernel(plain_ref, ref, out_ref):
    odd = (lane_iota((out_ref.shape[1], B)) & (B // 4)) != 0
    for q in range(2):
        out_ref[q] = jnp.where(odd, ref[:, 2 * q + 1, :], ref[:, 2 * q, :])
    for q in range(4):
        out_ref[2 + q] = jnp.sum(ref[:, 8 + 8 * q : 16 + 8 * q, :], axis=1)
    for q in range(3):
        out_ref[6 + q] = jnp.sum(plain_ref[:, 8 * q : 8 * q + 8, :], axis=1)


def finish_kernel(
    place_ref, mine_ref, theirs_ref, w_ref, step_ref, decay_ref, freq_ref, read_ref, liquid_ref, wsum_ref, across_ref,
    value_ref, gate_ref, vbias_ref, gbias_ref, step_out, decay_out, freq_out, read_out, liquid_out,
    skip_out, gain_out, bias_out, *, M,
):
    C = decay_ref.shape[0]
    half = B // 2

    def emit(first, second):
        value_ref[...] = first[0:C, :]
        gate_ref[...] = second[0:C, :]
        per = B // C
        group = place_ref[1] // per
        back = (B - (place_ref[1] % per) * C) % B
        for out, v in ((vbias_ref, first), (gbias_ref, second)):
            lanes = v[C : C + 8, pl.ds(pl.multiple_of(group * B, B), B)]
            out[...] = pltpu.roll(lanes, back, 1)[0:1, 0:C]

    @pl.when(place_ref[0] == 0)
    def _():
        emit(wsum_ref, across_ref)

    @pl.when(place_ref[0] == 1)
    def _():
        emit(across_ref, wsum_ref)

    rows = [mine_ref[q] + theirs_ref[q] for q in range(9)]

    def parts(a, b, c):
        return a[:, :half] - a[:, half:] + c[:, :half], b[:, :half] + b[:, half:] + c[:, half:]

    g_re, g_im = parts(rows[2], rows[3], rows[0])
    d_re, d_im = parts(rows[4], rows[5], rows[1])
    w = w_ref[...]
    w_re, w_im = w[:, :half], w[:, half:]
    l_re = w_re * d_re - w_im * d_im
    l_im = w_re * d_im + w_im * d_re
    cot = (
        2.0 * g_re[:, :M], -2.0 * g_im[:, :M], 2.0 * g_re[:, M:], -2.0 * g_im[:, M:],
        2.0 * (l_re[:, :M] + l_re[:, M:]), -2.0 * (l_im[:, :M] + l_im[:, M:]),
    )
    step = jnp.sum(jnp.where(row_iota((C, C)) == lane_iota((C, C)), step_ref[...], 0.0), axis=1, keepdims=True)
    _, back = jax.vjp(mode_terms, step, decay_ref[...], freq_ref[...], read_ref[...], liquid_ref[...])
    step_grad, decay_out[...], freq_out[...], read_out[...], liquid_out[...] = back(cot)
    lanes = lane_iota((B, B))
    pad = jnp.zeros((B - C, 1), F32)
    plain = jnp.zeros((B, B), F32)
    for q, v in enumerate([step_grad] + [jnp.sum(rows[6 + q], axis=1, keepdims=True) for q in range(3)]):
        plain = jnp.where(lanes == q, jnp.concatenate([v, pad], axis=0), plain)
    plain = plain.T
    for q, out in enumerate((step_out, skip_out, gain_out, bias_out)):
        out[...] = plain[q : q + 1, 0:C]


def last_kernel(x_ref, g_ref, gn_ref, stat_ref, sum_ref, out_ref, *, count):
    C, L = x_ref.shape
    for n in range(L // B):
        at = slice(n * B, (n + 1) * B)
        mean = stat_ref[0, n : n + 1, :]
        inv = lax.rsqrt(stat_ref[1, n : n + 1, :] * (1.0 / count) + EPS)
        first = sum_ref[0, n : n + 1, :] * (1.0 / count)
        second = sum_ref[1, n : n + 1, :] * (1.0 / count)
        normed = (x_ref[:, at].astype(F32) - mean) * inv
        out_ref[:, at] = inv * (gn_ref[:, at] - first - normed * second) + g_ref[:, at].astype(F32)


def total_kernel(*refs):
    total = refs[0][...]
    for p in refs[1:-1]:
        total = total + p[...]
    refs[-1][...] = total


def rounds_of(size):
    rounds, bit = [], 1
    while bit < size:
        if bit * 2 < size:
            rounds.append((bit, 2 * bit, 3 * bit))
            bit *= 4
        else:
            rounds.append((bit,))
            bit *= 2
    return rounds


def exchange(v, axis, size, off):
    return lax.ppermute(v, axis, [(k, k ^ off) for k in range(size)])


def all_sums(v, size):
    for offs in rounds_of(size):
        v = sum([exchange(v, "mp", size, o) for o in offs], v)
    return v


def sum_docs(v, size, stride):
    total = v
    for k in range(stride, size, stride):
        total = total + lax.ppermute(v, "dp", [(q, (q + k) % size) for q in range(size)])
    return total


def partner(v, size):
    return lax.ppermute(v, "dp", [(q, q ^ 1) for q in range(size)])


def mode_terms(log_step, decay_log, frequency, readout, liquid_readout):
    M = decay_log.shape[1]
    step_size = jnp.exp(log_step)
    real_rate = -jnp.exp(decay_log)
    real_step = step_size * real_rate
    imag_step = step_size * frequency
    growth = jnp.exp(real_step)
    num_real = growth * jnp.cos(imag_step) - 1.0
    num_imag = growth * jnp.sin(imag_step)
    denominator = real_rate * real_rate + frequency * frequency
    in_real = (num_real * real_rate + num_imag * frequency) / denominator
    in_imag = (num_imag * real_rate - num_real * frequency) / denominator

    def mix(coeffs):
        re, im = coeffs[:, :M], coeffs[:, M:]
        return re * in_real - im * in_imag, re * in_imag + im * in_real

    return mix(readout) + mix(liquid_readout) + (real_step, imag_step)


def per_device(
    mp, dp,
    tokens, lengths, norm_gain, norm_bias, log_step, decay_log, frequency, readout, liquid_readout,
    skip_gain, value_weight, gate_weight, value_bias, gate_bias, grad_out,
):
    C, L = tokens.shape
    H = value_weight.shape[0]
    M = decay_log.shape[1]
    N = L // B
    nt = L // mp
    few_rows = C * B // nt
    shape = jax.ShapeDtypeStruct

    place = jnp.stack([lax.axis_index("dp") & 1, lax.axis_index("mp")]).astype(jnp.int32)
    rounds = rounds_of(mp)
    small, large = 16, 32

    def pin(v):
        return pltpu.with_memory_space_constraint(v, pltpu.HBM)

    def call(kernel, out, n_in, smem=0, us=1, scratch=(), mb=small):
        return pl.pallas_call(
            kernel,
            out_shape=out,
            in_specs=[SMEM] * smem + [VMEM] * (n_in - smem),
            out_specs=jax.tree.map(lambda _: VMEM, out),
            scratch_shapes=list(scratch),
            compiler_params=params(mb),
            cost_estimate=cost(us),
        )

    def whole(*dims):
        return pl.BlockSpec(dims, lambda i: (0,) * len(dims))

    def chan_by(group):
        return lambda *dims: pl.BlockSpec((group,) + dims, lambda i: (i,) + (0,) * len(dims))

    def by_channel(kernel, out, in_specs, out_specs, us, scratch, mb=small, group=TABLE_GROUP):
        return pl.pallas_call(
            kernel,
            grid=(C // group,),
            out_shape=out,
            in_specs=in_specs,
            out_specs=out_specs,
            scratch_shapes=scratch,
            compiler_params=params(mb),
            cost_estimate=cost(us),
        )

    vm = pltpu.VMEM
    G = min(MIXER_GROUP, C)
    chan, few = chan_by(G), chan_by(TABLE_GROUP)
    blocks = shape((C, N, B), F32)
    far = pltpu.HBM
    far_blocks = far((C, N, B), F32)
    def pin(v):
        return pltpu.with_memory_space_constraint(v, far)

    hbm = pl.BlockSpec(memory_space=pltpu.HBM)
    stat, pay = pl.pallas_call(
        start_kernel,
        out_shape=(shape((2 * N + mp, B), F32), shape((mp, few_rows + 2 * C, nt), BF16)),
        in_specs=[SMEM] + [hbm] * 6,
        out_specs=(VMEM, VMEM),
        scratch_shapes=[
            pltpu.VMEM((C, L), BF16), pltpu.VMEM((C, L), BF16), pltpu.VMEM((C, H), BF16),
            pltpu.VMEM((1, C), BF16), pltpu.VMEM((1, C), BF16), pltpu.SemaphoreType.DMA((5,)),
        ],
        compiler_params=params(small),
        cost_estimate=cost(3),
    )(
        place, pin(tokens), pin(grad_out), pin(value_weight.T), pin(gate_weight.T), pin(value_bias[None]), pin(gate_bias[None])
    )
    first = lax.all_to_all(pay, "mp", split_axis=0, concat_axis=0, tiled=True)

    rates = jnp.stack(
        [jnp.broadcast_to(log_step[:, None], (C, 4 * M)), jnp.tile(decay_log, (1, 4)), jnp.tile(frequency, (1, 4))]
    )
    coef = jnp.concatenate([readout[:, :M], liquid_readout[:, :M], readout[:, M:], liquid_readout[:, M:]], axis=1)
    count = C
    for k, offs in enumerate(rounds[::-1]):
        parts = [stat] + [exchange(stat, "mp", mp, o) for o in offs]
        if k < len(rounds) - 1:
            stat = jnp.concatenate(join_stats(parts, N, float(count)), axis=0)
            count *= len(parts)
            stat, rates = lax.optimization_barrier((stat, rates))
    f_near, f_tab, t_tab, jump, w_all = by_channel(
        partial(table_kernel, C=C, M=M),
        (
            shape((C, 2 * B, 2 * B), BF16), far((C, 2 * B, 2 * B), BF16), shape((C, 3 * B, 2 * B), BF16),
            shape((2, C, B), F32), shape((C, B), F32),
        ),
        [whole(3, C, B), whole(C, B)],
        (few(2 * B, 2 * B), few(2 * B, 2 * B), few(3 * B, 2 * B), whole(2, C, B), whole(C, B)),
        6,
        [vm((3, B, B), F32)],
    )(rates, coef)
    parts, t_tab = lax.optimization_barrier((parts, t_tab))

    vecs = jnp.stack([norm_gain, norm_bias, skip_gain])
    mixed, slope, state, state_x, stat, bias = by_channel(
        partial(mixer_kernel, count=H, parts=len(parts)),
        (shape((mp, C, nt), BF16), far_blocks, far_blocks, far_blocks, far((2, N, B), F32), shape((mp, B), F32)),
        [SMEM, SMEM, whole(C, L)] + [whole(2 * N + mp, B)] * len(parts)
        + [chan(2 * B, 2 * B), chan(3 * B, 2 * B), whole(2, C, B)],
        (whole(mp, C, nt), chan(N, B), chan(N, B), chan(N, B), whole(2, N, B), whole(mp, B)),
        6,
        [
            vm((N * C, B), F32), vm((N * C, B), F32), vm((3, N, B), F32), vm((G, 2 * N, 2 * B), BF16),
            vm((G * N, B), F32), vm((G * N, B), F32), vm((G * N, B), F32),
        ],
        large,
        G,
    )(lengths, vecs, tokens, *parts, f_near, t_tab, jump)

    mixed, first, rates = lax.optimization_barrier((mixed, first, rates))
    own_w = [first[:, :few_rows, :]]
    own_w += [exchange(own_w[0], "mp", mp, o) for o in rounds[0]]
    other_w = [partner(v, dp) for v in own_w]
    mixed_tok = lax.all_to_all(mixed, "mp", split_axis=0, concat_axis=0, tiled=True)
    half_steps = C // TABLE_GROUP // 2

    def back_tables(held, start, steps):
        def block(*dims):
            return pl.BlockSpec((TABLE_GROUP,) + dims, lambda i: (i + start,) + (0,) * len(dims))

        return pl.pallas_call(
            partial(back_table_kernel, C=C, M=M, start=start),
            grid=(steps,),
            out_shape=(far((C, 2 * B, 4 * B), BF16), far((C, B, 2 * B), BF16)),
            in_specs=[whole(3, C, B), whole(C, B)] + [hbm] * len(held),
            out_specs=(block(2 * B, 4 * B), block(B, 2 * B)),
            scratch_shapes=[vm((3, B, B), F32)],
            input_output_aliases={2 + k: k for k in range(len(held))},
            compiler_params=params(small),
            cost_estimate=cost(4),
        )(rates, w_all, *[pin(v) for v in held])

    tables = back_tables([], 0, half_steps)
    mixed_tok, tables = lax.optimization_barrier((mixed_tok, tables))
    gm, keep, send = call(
        partial(glu_kernel, parts=len(own_w)),
        (shape((mp, 2 * C, nt), BF16),) + (shape((H, nt), BF16),) * 2,
        4 + 2 * len(own_w), 1, 2, [vm((2, H, nt), BF16), vm((2, mp, C, H), BF16)],
    )(place, mixed_tok, first, bias, *own_w, *other_w)
    mixed_tok = mixed_tok.reshape(H, nt)
    gm, f_tab, rates = lax.optimization_barrier((gm, f_tab, rates))
    gm = lax.all_to_all(gm, "mp", split_axis=0, concat_axis=0, tiled=True)
    u_rev, lift = by_channel(
        partial(lift_kernel, count=H),
        (far((C, 3 * N, 2 * B), BF16), far_blocks),
        [SMEM, SMEM, whole(C, L), whole(2, N, B), few(2 * B, 2 * B)],
        (few(3 * N, 2 * B), few(N, B)),
        3,
        [vm((N * C, B), F32), vm((3, N, B), F32)],
        56,
    )(lengths, vecs, tokens, stat, pin(f_tab))
    back_tab, near_tab = back_tables(tables, half_steps, half_steps)
    gm, lift, back_tab = lax.optimization_barrier((gm, lift, back_tab))

    ways = len(rounds[0]) + 1
    rows_left = mp // ways
    outs = call(
        partial(weight_kernel, C=C, mp=mp), (shape((rows_left * C + 8, H), F32),) * ways, 5, 1, 2,
        [vm((ways, rows_left * C + 8, H), F32)],
    )(place, keep, partner(send, dp), mixed_tok, partner(mixed_tok, dp))
    terms = [outs[0]] + [exchange(v, "mp", mp, o) for v, o in zip(outs[1:], rounds[0])]

    layer_out, gn, sums, plain, g_pre, p_blk, r_blk, rx_blk = by_channel(
        partial(back_kernel, count=H),
        (shape((C, L), BF16), shape((C, L), F32), shape((2, N, B), F32), shape((C, 24, B), F32)) + (blocks,) * 4,
        [
            SMEM, SMEM, VMEM, VMEM, VMEM, hbm, hbm, hbm, VMEM,
        ],
        (whole(C, L), whole(C, L), whole(2, N, B), chan(24, B)) + (chan(N, B),) * 4,
        7,
        [
            vm((N * C, B), F32), vm((N * C, B), F32), vm((N * C, B), F32), vm((3, N, B), F32),
            vm((G, 2 * N, B), BF16), vm((G * N, B), F32), vm((G * N, B), F32), vm((G * N, B), F32),
            vm((C, 2 * B, 4 * B), BF16), vm((C, B, 2 * B), BF16), vm((C, N, B), F32),
            pltpu.SemaphoreType.DMA((3, C // G)),
        ],
        large,
        G,
    )(lengths, vecs, tokens, stat, gm, pin(slope), pin(back_tab), pin(near_tab), jump)

    seen = ways
    terms[0], plain = lax.optimization_barrier((terms[0], plain))
    while seen < mp:
        ways, offs = 2, (seen,)
        rows_left //= ways
        outs = call(
            partial(fold_kernel, ways=ways, got=len(terms), C=C, seen=seen),
            (shape((rows_left * C + 8, H), F32),) * ways,
            1 + len(terms), 1, 1, [vm((ways, rows_left * C + 8, H), F32)],
        )(place, *terms)
        terms = [outs[0]] + [exchange(v, "mp", mp, o) for v, o in zip(outs[1:], offs)]
        seen *= ways
    for k, offs in enumerate(rounds[::-1]):
        got = [exchange(sums, "mp", mp, o) for o in offs]
        if k == len(rounds) - 1:
            g_pre, sums, terms[0] = lax.optimization_barrier((g_pre, sums, terms[0]))
            rows = by_channel(
                sums_kernel,
                shape((C, 40, B), F32),
                [chan(3 * N, 2 * B)] + [chan(N, B)] * 7 + [chan(B, 2 * B), whole(2, C, B)],
                chan(40, B),
                20,
                [],
                large,
                G,
            )(pin(u_rev), pin(lift), g_pre, p_blk, r_blk, rx_blk, pin(state), pin(state_x), pin(near_tab), jump)
            got, rows, terms = lax.optimization_barrier((got, rows, terms))
        sums = sum(got, sums)
    grad_tokens = call(partial(last_kernel, count=H), shape((C, L), F32), 5)(tokens, grad_out, gn, stat, sums)
    rows = call(join_kernel, shape((9, C, B), F32), 2)(plain, rows)
    others = sum_docs(rows, dp, 1) - rows if dp > 2 else partner(rows, dp)

    wsum = call(total_kernel, shape((C + 8, H), F32), len(terms))(*terms)
    wsum = sum_docs(wsum, dp, 2)
    across = partner(wsum, dp)
    thin, wide = shape((C, M), F32), shape((C, 2 * M), F32)
    line = shape((1, C), F32)
    (
        value_wgrad, gate_wgrad, vb, gb, step_grad, decay_grad, frequency_grad, readout_grad, liquid_grad,
        skip_grad, gain_grad, bias_grad,
    ) = call(
        partial(finish_kernel, M=M),
        (shape((C, H), F32), shape((C, H), F32), line, line, line, thin, thin, wide, wide, line, line, line),
        11, 1,
    )(
        place, rows, others, w_all, log_step[None], decay_log, frequency, readout, liquid_readout, wsum, across,
    )
    return (
        layer_out, grad_tokens, gain_grad[0], bias_grad[0], step_grad[0], decay_grad, frequency_grad, readout_grad,
        liquid_grad, skip_grad[0], value_wgrad.T, gate_wgrad.T, vb[0], gb[0],
    )


def solution(mesh):
    row, col, act = P("mp"), P(None, "mp"), P("mp", "dp")
    wide = P("mp", None)
    in_specs = (act, P("dp"), row, row, row, wide, wide, wide, wide, row, col, col, row, row, act)
    out_specs = (act, act, row, row, row, wide, wide, wide, wide, row, col, col, row, row)
    return jax.shard_map(
        partial(per_device, mesh.shape["mp"], mesh.shape["dp"]),
        mesh=mesh, in_specs=in_specs, out_specs=out_specs, check_vma=False,
    )
```

```python
from functools import partial

import jax
import jax.numpy as jnp
import numpy as np
from jax import lax
from jax.experimental import pallas as pl
from jax.experimental.pallas import tpu as pltpu
from jax.sharding import PartitionSpec as P

B = 128
TABLE_GROUP = 8
MIXER_GROUP = 16
F32 = jnp.float32
BF16 = jnp.bfloat16
NN = (((1,), (0,)), ((), ()))
NT = (((1,), (1,)), ((), ()))
TN = (((0,), (0,)), ((), ()))
EPS = 1e-05
SQUARE_SCALE = 65536.0
VMEM = pl.BlockSpec(memory_space=pltpu.VMEM)
SMEM = pl.BlockSpec(memory_space=pltpu.SMEM)


def params(mb):
    return pltpu.CompilerParams(vmem_limit_bytes=mb * 1024 * 1024)


def cost(us):
    return pl.CostEstimate(flops=int(us * 1e9), bytes_accessed=int(us * 1e6), transcendentals=0)


def dot(a, b, dims=NN):
    return lax.dot_general(a, b, dims, preferred_element_type=F32)


def split(v):
    hi = v.astype(BF16)
    return hi, (v - hi.astype(F32)).astype(BF16)


def sincos(x):
    k = jnp.floor(x * 0.6366197723675814 + 0.5)
    y = ((x - k * 1.5703125) - k * 4.837512969970703e-4) - k * 7.54978995489188e-8
    y2 = y * y
    s = y + y * y2 * (-1.6666654611e-1 + y2 * (8.3321608736e-3 - y2 * 1.9515295891e-4))
    c = 1.0 - 0.5 * y2 + y2 * y2 * (4.166664568298827e-2 + y2 * (-1.388731625493765e-3 + y2 * 2.443315711809948e-5))
    q = k.astype(jnp.int32)
    odd = (q & 1) == 1
    sin = jnp.where(odd, c, s)
    cos = jnp.where(odd, s, c)
    sin = jnp.where((q & 2) == 2, -sin, sin)
    cos = jnp.where(((q + 1) & 2) == 2, -cos, cos)
    return sin, cos


def row_iota(shape):
    return lax.broadcasted_iota(jnp.int32, shape, 0)


def lane_iota(shape):
    return lax.broadcasted_iota(jnp.int32, shape, 1)


def shift_token(x, k):
    n = x.shape[0]
    lanes = lane_iota(x.shape)
    rows = row_iota(x.shape)
    turned = pltpu.roll(x, k % B, 1)
    wrapped = pltpu.roll(turned, k % n, 0)
    if k > 0:
        wrapped = jnp.where(rows >= 1, wrapped, 0.0)
        return jnp.where(lanes == 0, wrapped, turned)
    wrapped = jnp.where(rows < n - 1, wrapped, 0.0)
    return jnp.where(lanes == B - 1, wrapped, turned)


def swap_halves(x):
    return pltpu.roll(x, B // 2, 1)


def scan_blocks(v_ref, out_ref, turned_ref, jump, N, backward):
    a_re, a_im = jump
    G = v_ref.shape[0] // N
    s = jnp.zeros((G, B), F32)
    t = s
    for k in range(N):
        n = N - 1 - k if backward else k
        out_ref[pl.ds(n, G, stride=N), :] = s
        turned_ref[pl.ds(n, G, stride=N), :] = t
        v = v_ref[pl.ds(n, G, stride=N), :]
        s, t = a_re * s + (a_im * t + v), a_re * t + (swap_halves(v) - a_im * s)


def start_kernel(
    place_ref, x_hbm, g_hbm, v_hbm, w_hbm, vb_hbm, gb_hbm, stat_ref, pay_ref, x_ref, g_ref, wt_ref, vb_ref, gb_ref, sems,
):
    C, L = x_ref.shape
    N = L // B
    mp, rows, nt = pay_ref.shape
    few = rows - 2 * C
    pairs = ((x_hbm, x_ref), (g_hbm, g_ref), (vb_hbm, vb_ref), (gb_hbm, gb_ref))
    moves = [pltpu.make_async_copy(src, dst, sems.at[1 + k]) for k, (src, dst) in enumerate(pairs)]
    for move in moves:
        move.start()
    for half, ref in enumerate((v_hbm, w_hbm)):

        @pl.when(place_ref[0] == half)
        def _():
            pltpu.make_async_copy(ref, wt_ref, sems.at[0]).start()

    moves[0].wait()
    for n in range(N):
        x = x_ref[:, n * B : (n + 1) * B].astype(F32)
        mean = jnp.sum(x, axis=0, keepdims=True) * (1.0 / C)
        dev = x - mean
        stat_ref[n : n + 1, :] = mean
        stat_ref[N + n : N + n + 1, :] = jnp.sum(dev * dev, axis=0, keepdims=True)
    own = row_iota((mp, B))
    moves[2].wait()
    moves[3].wait()
    bias = jnp.concatenate([vb_ref[...].astype(F32), gb_ref[...].astype(F32), jnp.zeros((1, B - 2 * C), F32)], axis=1)
    stat_ref[2 * N :, :] = jnp.where(own == place_ref[1], bias, 0.0)
    for j in range(mp):
        pay_ref[j, few : few + C, :] = x_ref[:, j * nt : (j + 1) * nt]
    moves[1].wait()
    for j in range(mp):
        pay_ref[j, few + C :, :] = g_ref[:, j * nt : (j + 1) * nt]
    pltpu.make_async_copy(v_hbm, wt_ref, sems.at[0]).wait()
    parts = wt_ref.shape[1] // B
    for j in range(mp):
        lanes = slice(j % parts * B, (j % parts + 1) * B)
        for q in range(nt // B):
            pay_ref[j, 0:few, q * B : (q + 1) * B] = wt_ref[q * few : (q + 1) * few, lanes]


def join_stats(parts, N, count):
    mean = sum(p[:N] for p in parts) * (1.0 / len(parts))
    spread = sum(p[N : 2 * N] for p in parts) + count * sum((p[:N] - mean) * (p[:N] - mean) for p in parts)
    return mean, spread, sum(p[2 * N :] for p in parts)


def columns(re, im, turn, w, cols, C):
    sin, cos = turn
    group = lane_iota(re.shape) // (B // 4)
    packed = jnp.where(group == 0, re, jnp.where(group == 1, im, jnp.where(group == 2, cos, sin)))
    pad = jnp.zeros((B - C, B), F32)
    for q, v in enumerate((packed, w)):
        cols[q] = jnp.concatenate([v, pad], axis=0).T


def channel_waves(cols, i, M, G):
    back = (B - i * G) % B
    pp = pltpu.roll(cols[0], back, 1)
    ww = 2.0 * pltpu.roll(cols[1], back, 1)
    place = lane_iota((M, B)).astype(F32)
    ahead = float(B) - place
    out = []
    for j in range(G):
        a, o, c, s = [jnp.broadcast_to(pp[q * M : (q + 1) * M, j : j + 1], (M, B)) for q in range(4)]
        w = [jnp.broadcast_to(ww[q * M : (q + 1) * M, j : j + 1], (M, B)) for q in range(4)]
        sin, cos = sincos(o * place)
        mag = jnp.exp(a * place)
        rest = jnp.exp(a * ahead)
        out.append(((mag * cos, mag * sin), (rest * (c * cos + s * sin), rest * (s * cos - c * sin)), w))
    return out


def toeplitz_rows(kern, start):
    return pltpu.roll(jnp.broadcast_to(kern, (B, B)), start, 1, stride=1, stride_axis=0)


def table_kernel(rates_ref, coef_ref, f_ref, again_ref, t_ref, jump_ref, wout_ref, cols, *, C, M):
    i = pl.program_id(0)
    G = f_ref.shape[0]

    @pl.when(i == 0)
    def _():
        step_size = jnp.exp(rates_ref[0])
        real_rate = -jnp.exp(rates_ref[1])
        freq = rates_ref[2]
        re = step_size * real_rate
        im = step_size * freq
        growth = jnp.exp(re)
        sin, cos = sincos(im)
        num_re = growth * cos - 1.0
        num_im = growth * sin
        den = real_rate * real_rate + freq * freq
        in_re = (num_re * real_rate + num_im * freq) / den
        in_im = (num_im * real_rate - num_re * freq) / den
        coef = coef_ref[...]
        first = lane_iota(coef.shape) < B // 2
        w = coef * in_re + swap_halves(coef) * jnp.where(first, -in_im, in_im)
        wout_ref[...] = w
        turn = sincos(im * float(B))
        mag = jnp.exp(re * float(B))
        jump_ref[0] = mag * turn[1]
        jump_ref[1] = mag * jnp.where(first, -turn[0], turn[0])
        columns(re, im, turn, w, cols, C)

    rows = row_iota((B, B))
    lanes = lane_iota((B, B))
    odd = (lanes & M) == M
    zero = jnp.zeros((B, B), BF16)
    every = range(G)
    waves = channel_waves(cols, i, M, G)
    feeds = [jnp.concatenate([f_re, f_re, f_im, f_im], axis=0).T for _, (f_re, f_im), _ in waves]
    kerns = []
    for j in every:
        (n_re, n_im), _, w = waves[j]
        for h in range(2):
            w_re, w_im = w[h], w[2 + h]
            e_re = w_re * n_re - w_im * n_im
            e_im = -(w_re * n_im + w_im * n_re)
            kerns.append(jnp.sum(e_re, axis=0, keepdims=True))
            for q, v in enumerate(split(e_re)):
                t_ref[j, 2 * B + h * M : 2 * B + (h + 1) * M, q * B : (q + 1) * B] = v
            for q, v in enumerate(split(e_im)):
                t_ref[j, 2 * B + (2 + h) * M : 2 * B + (3 + h) * M, q * B : (q + 1) * B] = v
    rolled = [toeplitz_rows(kern, 0) for kern in kerns]
    for j in every:
        parts = split(feeds[j])
        for h in range(2):
            for q, part in enumerate(parts):
                v = jnp.where(odd if h == 1 else ~odd, part, zero)
                f_ref[j, h * B : (h + 1) * B, q * B : (q + 1) * B] = v
                again_ref[j, h * B : (h + 1) * B, q * B : (q + 1) * B] = v
            toe = jnp.where(lanes >= rows, rolled[2 * j + h], 0.0)
            for q, v in enumerate(split(toe)):
                t_ref[j, h * B : (h + 1) * B, q * B : (q + 1) * B] = v


def back_table_kernel(rates_ref, w_ref, *refs, C, M, start):
    t_ref, near_ref, cols = refs[-3:]
    i = pl.program_id(0) + start
    G = t_ref.shape[0]

    @pl.when(i == start)
    def _():
        step_size = jnp.exp(rates_ref[0])
        im = step_size * rates_ref[2]
        columns(step_size * -jnp.exp(rates_ref[1]), im, sincos(im * float(B)), w_ref[...], cols, C)

    rows = row_iota((B, B))
    lanes = lane_iota((B, B))
    zero = jnp.zeros((M, B), BF16)
    every = range(G)
    waves = channel_waves(cols, i, M, G)
    turned = [jnp.concatenate([n_re, n_re, n_im, n_im], axis=0).T for (n_re, n_im), _, _ in waves]
    kerns, starts = [], []
    for j in every:
        (n_re, n_im), (f_re, f_im), w = waves[j]
        for h in range(2):
            w_re, w_im = w[h], w[2 + h]
            b_re = w_re * f_re - w_im * f_im
            b_im = -(w_re * f_im + w_im * f_re)
            kerns.append(jnp.sum(b_re, axis=0, keepdims=True))
            starts.append(jnp.sum(w_re * n_re - w_im * n_im, axis=0, keepdims=True)[:, 0:1])
            for part, v2 in ((0, b_re), (2, b_im)):
                for q, v in enumerate(split(v2)):
                    at = slice((2 * q + h) * B, (2 * q + h + 1) * B)
                    t_ref[j, B + part * M : B + (part + 1) * M, at] = v
                    t_ref[j, B + (part + 1) * M : B + (part + 2) * M, at] = zero
    rolled = [toeplitz_rows(kern, 0) for kern in kerns]
    for j in every:
        for q, v in enumerate(split(turned[j])):
            near_ref[j, :, q * B : (q + 1) * B] = v
        for h in range(2):
            start = jnp.broadcast_to(starts[2 * j + h], (B, B))
            toe = jnp.where(lanes < rows, rolled[2 * j + h], jnp.where(lanes == rows, start, 0.0))
            for q, v in enumerate(split(toe)):
                t_ref[j, 0:B, (2 * q + h) * B : (2 * q + h + 1) * B] = v


def token_stats(stat_ref, length, count):
    mean = stat_ref[0]
    inv = lax.rsqrt(stat_ref[1] * (1.0 / count) + EPS)
    place = row_iota(mean.shape) * B + lane_iota(mean.shape)
    return mean, inv, (place < length).astype(F32)


def mixer_kernel(len_ref, vec_ref, x_ref, *refs, count, parts):
    part_refs, refs = refs[:parts], refs[parts:]
    f_ref, t_ref, jump_ref = refs[:3]
    mixed_ref, slope_ref, state_ref, other_ref, stat_ref, bias_ref = refs[3:9]
    xs, ms, tok, us, ups, sts, ots = refs[9:]
    i = pl.program_id(0)
    G = f_ref.shape[0]
    C, L = x_ref.shape
    N = L // B
    nt = mixed_ref.shape[2]

    @pl.when(i == 0)
    def _():
        for n in range(N):
            xs[n * C : (n + 1) * C, :] = x_ref[:, n * B : (n + 1) * B].astype(F32)
        stat_ref[0], stat_ref[1], bias_ref[...] = join_stats([r[...] for r in part_refs], N, count / parts)
        mean, inv, mask = token_stats(stat_ref, len_ref[0], count)
        tok[0] = mean
        tok[1] = inv
        tok[2] = mask

    for j in range(G):
        ci = i * G + j
        normed = (xs[pl.ds(ci, N, stride=C), :] - tok[0]) * tok[1]
        sig = tok[2] * (normed * vec_ref[0, ci] + vec_ref[1, ci])
        liq = sig * shift_token(sig, 1)
        for q, v in enumerate((sig, liq)):
            hi, lo = split(v)
            us[j, 0:N, q * B : (q + 1) * B] = hi
            us[j, N:, q * B : (q + 1) * B] = lo
        slope_ref[j] = sig
    ups_all = [dot(us[j], f_ref[j]) for j in range(G)]
    for j, up in enumerate(ups_all):
        ups[j * N : (j + 1) * N, :] = up[:N, :B] + (up[:N, B:] + up[N:, :B])
    at = pl.ds(pl.multiple_of(i * G, G), G)
    scan_blocks(ups, sts, ots, (jump_ref[0, at, :], jump_ref[1, at, :]), N, False)
    left = []
    for j in range(G):
        state = sts[j * N : (j + 1) * N, :]
        state_ref[j] = state
        other_ref[j] = ots[j * N : (j + 1) * N, :]
        left.append(jnp.concatenate([us[j], jnp.concatenate(split(state), axis=0)], axis=1))
    outs = [dot(left[j], t_ref[j]) for j in range(G)]
    for j, out in enumerate(outs):
        ci = i * G + j
        mask = tok[2]
        y = out[:N, :B] + (out[:N, B:] + out[N:, :B]) + vec_ref[2, ci] * slope_ref[j]
        y2 = y * y
        th = jnp.tanh(0.7978845608028654 * (y + 0.044715 * (y * y2)))
        half = 0.5 * (1.0 + th)
        ms[pl.ds(pl.multiple_of(ci * N, N), N), :] = mask * (y * half)
        slope_ref[j] = mask * (half + 0.5 * y * (1.0 - th * th) * (0.7978845608028654 * (1.0 + 0.134145 * y2)))

    @pl.when(i == pl.num_programs(0) - 1)
    def _():
        per = nt // B
        for n in range(N):
            mixed_ref[n // per, :, (n % per) * B : (n % per + 1) * B] = ms[pl.ds(n, C, stride=N), :].astype(BF16)


def glu_kernel(place_ref, in_ref, first_ref, bias_ref, *refs, parts):
    own_refs, other_refs, refs = refs[:parts], refs[parts : 2 * parts], refs[2 * parts :]
    gm_ref, keep_ref, send_ref, gp, wt = refs
    mp, C, nt = in_ref.shape
    H = mp * C
    few = own_refs[0].shape[1]
    own = place_ref[0]
    mixed = in_ref[...].reshape(H, nt)
    for k in range(parts):
        lanes = pl.ds(pl.multiple_of((lax.rem(place_ref[1], parts) ^ k) * B, B), B)
        for q in range(nt // B):
            at = slice(q * few, (q + 1) * few)
            wt[own, :, at, lanes] = own_refs[k][:, :, q * B : (q + 1) * B]
            wt[1 - own, :, at, lanes] = other_refs[k][:, :, q * B : (q + 1) * B]
    step = B
    per = step // C
    bias = jnp.concatenate([bias_ref[...], jnp.zeros((B - mp, B), F32)], axis=0).T
    for s in range(mp // per):
        lo = s * step
        col_v = jnp.concatenate([bias[0:C, k : k + 1] for k in range(s * per, (s + 1) * per)], axis=0)
        col_g = jnp.concatenate([bias[C : 2 * C, k : k + 1] for k in range(s * per, (s + 1) * per)], axis=0)
        at = slice(s * per, (s + 1) * per)
        value = dot(wt[0, at].reshape(step, H), mixed) + col_v
        gate = dot(wt[1, at].reshape(step, H), mixed) + col_g
        sig = jax.nn.sigmoid(gate)
        x = first_ref[at, few : few + C, :].reshape(step, nt).astype(F32)
        g = first_ref[at, few + C :, :].reshape(step, nt).astype(F32)
        gm_ref[s * per : (s + 1) * per, C:, :] = (x + value * sig).astype(BF16).reshape(per, C, nt)
        gv = g * sig
        gp[0, lo : lo + step, :] = gv.astype(BF16)
        gp[1, lo : lo + step, :] = (gv * value * (1.0 - sig)).astype(BF16)
    for s in range(mp // per):
        at = slice(s * step, (s + 1) * step)
        gm = sum(dot(wt[h, :, :, at].reshape(H, step), gp[h], TN) for h in range(2))
        wide = gm * SQUARE_SCALE
        gm_ref[s * per : (s + 1) * per, 0:C, :] = (wide * jnp.abs(wide)).astype(BF16).reshape(per, C, nt)
    keep_ref[...] = gp[own]
    send_ref[...] = gp[1 - own]


def weight_kernel(place_ref, keep_ref, got_ref, mixed_ref, theirs_ref, *refs, C, mp):
    outs, wg = refs[:-1], refs[-1]
    nt = mixed_ref.shape[1]
    ways = len(outs)
    per = mp // ways
    total = dot(keep_ref[...], mixed_ref[...], NT) + dot(got_ref[...], theirs_ref[...], NT)
    for m in range(mp):
        at = (m // ways) * C
        wg[m % ways, at : at + C, :] = total[m * C : (m + 1) * C]
    ones = jnp.ones((8, nt), BF16)
    tail = dot(ones, keep_ref[...], NT) + dot(ones, got_ref[...], NT)
    for q in range(ways):
        wg[q, per * C :, :] = tail
    for k in range(ways):
        outs[k][...] = wg[lax.rem(place_ref[1], ways) ^ k]


def fold_kernel(place_ref, *refs, ways, got, C, seen):
    parts, outs, acc = refs[:got], refs[got:-1], refs[-1]
    total = parts[0][...]
    for p in parts[1:]:
        total = total + p[...]
    blocks = (total.shape[0] - 8) // C
    for z in range(blocks):
        at = (z // ways) * C
        acc[z % ways, at : at + C, :] = total[z * C : (z + 1) * C]
    for q in range(ways):
        acc[q, (blocks // ways) * C :, :] = total[blocks * C :]
    for k in range(ways):
        outs[k][...] = acc[lax.rem(lax.div(place_ref[1], seen), ways) ^ k]


def back_kernel(
    len_ref, vec_ref, x_ref, stat_ref, gm_ref, slope_hbm, t_ref, near_hbm, jump_ref,
    layer_ref, gn_ref, sum_ref, row_ref, g_ref, p_ref, r_ref, turned_ref, xs, gs, ns, tok, hs, ps, rs, rts, tab, near_ref, slope_ref, sem, *, count,
):
    i = pl.program_id(0)
    G = g_ref.shape[0]
    C, L = x_ref.shape
    N = L // B
    nt = gm_ref.shape[2]
    per = nt // B

    def fetch(q, k):
        src, dst = ((slope_hbm, slope_ref), (near_hbm, near_ref), (t_ref, tab))[q]
        at = pl.ds(k * G, G)
        return pltpu.make_async_copy(src.at[at], dst.at[at], sem.at[q, k])

    @pl.when(i == 0)
    def _():
        for k in range(C // G):
            for q in range(3):
                fetch(q, k).start()
        for n in range(N):
            xs[n * C : (n + 1) * C, :] = x_ref[:, n * B : (n + 1) * B].astype(F32)
            at = slice((n % per) * B, (n % per + 1) * B)
            square = gm_ref[n // per, 0:C, at].astype(F32)
            gs[n * C : (n + 1) * C, :] = square * (lax.rsqrt(jnp.maximum(jnp.abs(square), 1e-37)) * (1.0 / SQUARE_SCALE))
        mean, inv, mask = token_stats(stat_ref, len_ref[0], count)
        tok[0] = mean
        tok[1] = inv
        tok[2] = mask
        sum_ref[...] = jnp.zeros_like(sum_ref)
        for m in range(gm_ref.shape[0]):
            layer_ref[:, m * nt : (m + 1) * nt] = gm_ref[m, C:, :]

    fetch(0, i).wait()
    for j in range(G):
        ci = i * G + j
        g = gs[pl.ds(ci, N, stride=C), :] * slope_ref[ci]
        g_ref[j] = g
        hi, lo = split(g)
        hs[j, 0:N, :] = hi
        hs[j, N:, :] = lo
    fetch(1, i).wait()
    z_all = [dot(hs[j], near_ref[i * G + j]) for j in range(G)]
    for j, z in enumerate(z_all):
        p = z[:N, :B] + (z[:N, B:] + z[N:, :B])
        p_ref[j] = p
        ps[j * N : (j + 1) * N, :] = p
    at = pl.ds(pl.multiple_of(i * G, G), G)
    scan_blocks(ps, rs, rts, (jump_ref[0, at, :], jump_ref[1, at, :]), N, True)
    left = []
    for j in range(G):
        r = rs[j * N : (j + 1) * N, :]
        r_ref[j] = r
        turned_ref[j] = rts[j * N : (j + 1) * N, :]
        left.append(jnp.concatenate([hs[j], jnp.concatenate(split(r), axis=0)], axis=1))
    fetch(2, i).wait()
    both_all = [dot(left[j], tab[i * G + j]) for j in range(G)]
    for j, both in enumerate(both_all):
        ci = i * G + j
        mask = tok[2]
        normed = (xs[pl.ds(ci, N, stride=C), :] - tok[0]) * tok[1]
        sig = mask * (normed * vec_ref[0, ci] + vec_ref[1, ci])
        both = both[:N, : 2 * B] + (both[:N, 2 * B :] + both[N:, : 2 * B])
        gl = both[:, B:]
        grad = both[:, :B] + vec_ref[2, ci] * g_ref[j] + gl * shift_token(sig, 1) + shift_token(gl * sig, -1)
        masked = mask * grad
        gn = masked * vec_ref[0, ci]
        sum_ref[0] += gn
        sum_ref[1] += gn * normed
        ns[pl.ds(pl.multiple_of(ci * N, N), N), :] = gn
        for q, v in enumerate((g_ref[j] * sig, masked * normed, masked)):
            row_ref[j, q * 8 : (q + 1) * 8, :] = sum(v[8 * k : 8 * k + 8] for k in range(N // 8))

    @pl.when(i == pl.num_programs(0) - 1)
    def _():
        for n in range(N):
            gn_ref[:, n * B : (n + 1) * B] = ns[pl.ds(n, C, stride=N), :]


def lift_kernel(len_ref, vec_ref, x_ref, stat_ref, f_ref, u_ref, lift_ref, xs, tok, *, count):
    i = pl.program_id(0)
    G = f_ref.shape[0]
    C, L = x_ref.shape
    N = L // B

    @pl.when(i == 0)
    def _():
        for n in range(N):
            xs[n * C : (n + 1) * C, :] = x_ref[:, n * B : (n + 1) * B].astype(F32)
        tok[0], tok[1], tok[2] = token_stats(stat_ref, len_ref[0], count)

    ahead = float(B) - lane_iota((N, B)).astype(F32)
    flip = (lane_iota((B, B)) + row_iota((B, B)) == B - 1).astype(BF16)
    flat, left = [], []
    for j in range(G):
        ci = i * G + j
        normed = (xs[pl.ds(ci, N, stride=C), :] - tok[0]) * tok[1]
        sig = tok[2] * (normed * vec_ref[0, ci] + vec_ref[1, ci])
        liq = sig * shift_token(sig, 1)
        flat.append(jnp.concatenate(split(sig) + split(liq), axis=0))
        left.append(jnp.concatenate(split(jnp.concatenate([sig * ahead, liq * ahead], axis=1)), axis=0))
    turned_all = [dot(v, flip).astype(BF16) for v in flat]
    lifts = [dot(left[j], f_ref[j]) for j in range(G)]
    for j in range(G):
        turned, lift = turned_all[j], lifts[j]
        for q in range(2):
            at = slice(q * B, (q + 1) * B)
            u_ref[j, 0 : 2 * N, at] = turned[2 * q * N : (2 * q + 2) * N]
            u_ref[j, 2 * N :, at] = turned[2 * q * N : (2 * q + 1) * N]
        lift_ref[j] = lift[:N, :B] + (lift[:N, B:] + lift[N:, :B])


def sums_kernel(u_ref, lift_ref, g_ref, p_ref, r_ref, rx_ref, state_ref, sx_ref, near_ref, jump_ref, row_ref):
    i = pl.program_id(0)
    G = g_ref.shape[0]
    _, N, _ = g_ref.shape
    place = lane_iota((N, B)).astype(F32)
    rows2, lanes2 = row_iota((B, B)), lane_iota((B, B))
    inside = lanes2 + rows2 >= B - 1
    rows16 = row_iota((16, B))
    lag = lane_iota((16, B)).astype(F32)
    R = N + 16
    every = range(G)
    turned = []
    for j in every:
        g_hi, g_lo = split(g_ref[j])
        turned.append(jnp.concatenate([g_hi, g_hi, g_lo], axis=0).T)
    corr = [dot(turned[j], u_ref[j]) for j in every]
    left = []
    for j in every:
        lags = []
        for q in range(2):
            part = jnp.where(inside, corr[j][:, q * B : (q + 1) * B], 0.0)
            lags.append(jnp.sum(pltpu.roll(part, 1, 1, stride=1, stride_axis=0), axis=0, keepdims=True))
        pair = jnp.where((rows16 & 1) == 0, lags[0], lags[1])
        pair = jnp.where(rows16 < 2, pair, jnp.where(rows16 < 4, pair * lag, 0.0))
        left.append(jnp.concatenate(split(jnp.concatenate([g_ref[j] * place, pair], axis=0)), axis=0))
    both = [dot(left[j], near_ref[j]) for j in every]
    for j in every:
        ci = i * G + j
        z = both[j][:R, :B] + (both[j][:R, B:] + both[j][R:, :B])
        row_ref[j, 0:8, :] = z[N : N + 8]
        p, r, state, lift = p_ref[j], r_ref[j], state_ref[j], lift_ref[j]
        state_x, r_x = sx_ref[j], rx_ref[j]
        carry = z[:N] + float(B) * (r * jump_ref[0, pl.ds(ci, 1), :] + r_x * jump_ref[1, pl.ds(ci, 1), :])
        total = [p * state, p * state_x, carry * state + lift * r, carry * state_x + lift * r_x]
        for q, v in enumerate(total):
            row_ref[j, 8 + 8 * q : 16 + 8 * q, :] = sum(v[8 * k : 8 * k + 8] for k in range(N // 8))


def join_kernel(plain_ref, ref, out_ref):
    odd = (lane_iota((out_ref.shape[1], B)) & (B // 4)) != 0
    for q in range(2):
        out_ref[q] = jnp.where(odd, ref[:, 2 * q + 1, :], ref[:, 2 * q, :])
    for q in range(4):
        out_ref[2 + q] = jnp.sum(ref[:, 8 + 8 * q : 16 + 8 * q, :], axis=1)
    for q in range(3):
        out_ref[6 + q] = jnp.sum(plain_ref[:, 8 * q : 8 * q + 8, :], axis=1)


def finish_kernel(
    place_ref, mine_ref, theirs_ref, w_ref, step_ref, decay_ref, freq_ref, read_ref, liquid_ref, wsum_ref, across_ref,
    value_ref, gate_ref, vbias_ref, gbias_ref, step_out, decay_out, freq_out, read_out, liquid_out,
    skip_out, gain_out, bias_out, *, M,
):
    C = decay_ref.shape[0]
    half = B // 2

    def emit(first, second):
        value_ref[...] = first[0:C, :]
        gate_ref[...] = second[0:C, :]
        per = B // C
        group = place_ref[1] // per
        back = (B - (place_ref[1] % per) * C) % B
        for out, v in ((vbias_ref, first), (gbias_ref, second)):
            lanes = v[C : C + 8, pl.ds(pl.multiple_of(group * B, B), B)]
            out[...] = pltpu.roll(lanes, back, 1)[0:1, 0:C]

    @pl.when(place_ref[0] == 0)
    def _():
        emit(wsum_ref, across_ref)

    @pl.when(place_ref[0] == 1)
    def _():
        emit(across_ref, wsum_ref)

    rows = [mine_ref[q] + theirs_ref[q] for q in range(9)]

    def parts(a, b, c):
        return a[:, :half] - a[:, half:] + c[:, :half], b[:, :half] + b[:, half:] + c[:, half:]

    g_re, g_im = parts(rows[2], rows[3], rows[0])
    d_re, d_im = parts(rows[4], rows[5], rows[1])
    w = w_ref[...]
    w_re, w_im = w[:, :half], w[:, half:]
    l_re = w_re * d_re - w_im * d_im
    l_im = w_re * d_im + w_im * d_re
    cot = (
        2.0 * g_re[:, :M], -2.0 * g_im[:, :M], 2.0 * g_re[:, M:], -2.0 * g_im[:, M:],
        2.0 * (l_re[:, :M] + l_re[:, M:]), -2.0 * (l_im[:, :M] + l_im[:, M:]),
    )
    step = jnp.sum(jnp.where(row_iota((C, C)) == lane_iota((C, C)), step_ref[...], 0.0), axis=1, keepdims=True)
    _, back = jax.vjp(mode_terms, step, decay_ref[...], freq_ref[...], read_ref[...], liquid_ref[...])
    step_grad, decay_out[...], freq_out[...], read_out[...], liquid_out[...] = back(cot)
    lanes = lane_iota((B, B))
    pad = jnp.zeros((B - C, 1), F32)
    plain = jnp.zeros((B, B), F32)
    for q, v in enumerate([step_grad] + [jnp.sum(rows[6 + q], axis=1, keepdims=True) for q in range(3)]):
        plain = jnp.where(lanes == q, jnp.concatenate([v, pad], axis=0), plain)
    plain = plain.T
    for q, out in enumerate((step_out, skip_out, gain_out, bias_out)):
        out[...] = plain[q : q + 1, 0:C]


def last_kernel(x_ref, g_ref, gn_ref, stat_ref, sum_ref, out_ref, *, count):
    C, L = x_ref.shape
    for n in range(L // B):
        at = slice(n * B, (n + 1) * B)
        mean = stat_ref[0, n : n + 1, :]
        inv = lax.rsqrt(stat_ref[1, n : n + 1, :] * (1.0 / count) + EPS)
        first = sum_ref[0, n : n + 1, :] * (1.0 / count)
        second = sum_ref[1, n : n + 1, :] * (1.0 / count)
        normed = (x_ref[:, at].astype(F32) - mean) * inv
        out_ref[:, at] = inv * (gn_ref[:, at] - first - normed * second) + g_ref[:, at].astype(F32)


def total_kernel(*refs):
    total = refs[0][...]
    for p in refs[1:-1]:
        total = total + p[...]
    refs[-1][...] = total


def rounds_of(size):
    rounds, bit = [], 1
    while bit < size:
        if bit * 2 < size:
            rounds.append((bit, 2 * bit, 3 * bit))
            bit *= 4
        else:
            rounds.append((bit,))
            bit *= 2
    return rounds


def exchange(v, axis, size, off):
    return lax.ppermute(v, axis, [(k, k ^ off) for k in range(size)])


def all_sums(v, size):
    for offs in rounds_of(size):
        v = sum([exchange(v, "mp", size, o) for o in offs], v)
    return v


def sum_docs(v, size, stride):
    total = v
    for k in range(stride, size, stride):
        total = total + lax.ppermute(v, "dp", [(q, (q + k) % size) for q in range(size)])
    return total


def partner(v, size):
    return lax.ppermute(v, "dp", [(q, q ^ 1) for q in range(size)])


def mode_terms(log_step, decay_log, frequency, readout, liquid_readout):
    M = decay_log.shape[1]
    step_size = jnp.exp(log_step)
    real_rate = -jnp.exp(decay_log)
    real_step = step_size * real_rate
    imag_step = step_size * frequency
    growth = jnp.exp(real_step)
    num_real = growth * jnp.cos(imag_step) - 1.0
    num_imag = growth * jnp.sin(imag_step)
    denominator = real_rate * real_rate + frequency * frequency
    in_real = (num_real * real_rate + num_imag * frequency) / denominator
    in_imag = (num_imag * real_rate - num_real * frequency) / denominator

    def mix(coeffs):
        re, im = coeffs[:, :M], coeffs[:, M:]
        return re * in_real - im * in_imag, re * in_imag + im * in_real

    return mix(readout) + mix(liquid_readout) + (real_step, imag_step)


def per_device(
    mp, dp,
    tokens, lengths, norm_gain, norm_bias, log_step, decay_log, frequency, readout, liquid_readout,
    skip_gain, value_weight, gate_weight, value_bias, gate_bias, grad_out,
):
    C, L = tokens.shape
    H = value_weight.shape[0]
    M = decay_log.shape[1]
    N = L // B
    nt = L // mp
    few_rows = C * B // nt
    shape = jax.ShapeDtypeStruct

    place = jnp.stack([lax.axis_index("dp") & 1, lax.axis_index("mp")]).astype(jnp.int32)
    rounds = rounds_of(mp)
    small, large = 16, 32

    def pin(v):
        return pltpu.with_memory_space_constraint(v, pltpu.HBM)

    def call(kernel, out, n_in, smem=0, us=1, scratch=(), mb=small):
        return pl.pallas_call(
            kernel,
            out_shape=out,
            in_specs=[SMEM] * smem + [VMEM] * (n_in - smem),
            out_specs=jax.tree.map(lambda _: VMEM, out),
            scratch_shapes=list(scratch),
            compiler_params=params(mb),
            cost_estimate=cost(us),
        )

    def whole(*dims):
        return pl.BlockSpec(dims, lambda i: (0,) * len(dims))

    def chan_by(group):
        return lambda *dims: pl.BlockSpec((group,) + dims, lambda i: (i,) + (0,) * len(dims))

    def by_channel(kernel, out, in_specs, out_specs, us, scratch, mb=small, group=TABLE_GROUP):
        return pl.pallas_call(
            kernel,
            grid=(C // group,),
            out_shape=out,
            in_specs=in_specs,
            out_specs=out_specs,
            scratch_shapes=scratch,
            compiler_params=params(mb),
            cost_estimate=cost(us),
        )

    vm = pltpu.VMEM
    G = min(MIXER_GROUP, C)
    chan, few = chan_by(G), chan_by(TABLE_GROUP)
    blocks = shape((C, N, B), F32)
    far = pltpu.HBM
    far_blocks = far((C, N, B), F32)
    def pin(v):
        return pltpu.with_memory_space_constraint(v, far)

    hbm = pl.BlockSpec(memory_space=pltpu.HBM)
    stat, pay = pl.pallas_call(
        start_kernel,
        out_shape=(shape((2 * N + mp, B), F32), shape((mp, few_rows + 2 * C, nt), BF16)),
        in_specs=[SMEM] + [hbm] * 6,
        out_specs=(VMEM, VMEM),
        scratch_shapes=[
            pltpu.VMEM((C, L), BF16), pltpu.VMEM((C, L), BF16), pltpu.VMEM((C, H), BF16),
            pltpu.VMEM((1, C), BF16), pltpu.VMEM((1, C), BF16), pltpu.SemaphoreType.DMA((5,)),
        ],
        compiler_params=params(small),
        cost_estimate=cost(3),
    )(
        place, pin(tokens), pin(grad_out), pin(value_weight.T), pin(gate_weight.T), pin(value_bias[None]), pin(gate_bias[None])
    )
    first = lax.all_to_all(pay, "mp", split_axis=0, concat_axis=0, tiled=True)

    rates = jnp.stack(
        [jnp.broadcast_to(log_step[:, None], (C, 4 * M)), jnp.tile(decay_log, (1, 4)), jnp.tile(frequency, (1, 4))]
    )
    coef = jnp.concatenate([readout[:, :M], liquid_readout[:, :M], readout[:, M:], liquid_readout[:, M:]], axis=1)
    count = C
    for k, offs in enumerate(rounds[::-1]):
        parts = [stat] + [exchange(stat, "mp", mp, o) for o in offs]
        if k < len(rounds) - 1:
            stat = jnp.concatenate(join_stats(parts, N, float(count)), axis=0)
            count *= len(parts)
            stat, rates = lax.optimization_barrier((stat, rates))
    f_near, f_tab, t_tab, jump, w_all = by_channel(
        partial(table_kernel, C=C, M=M),
        (
            shape((C, 2 * B, 2 * B), BF16), far((C, 2 * B, 2 * B), BF16), shape((C, 3 * B, 2 * B), BF16),
            shape((2, C, B), F32), shape((C, B), F32),
        ),
        [whole(3, C, B), whole(C, B)],
        (few(2 * B, 2 * B), few(2 * B, 2 * B), few(3 * B, 2 * B), whole(2, C, B), whole(C, B)),
        6,
        [vm((2, B, B), F32)],
    )(rates, coef)
    parts, t_tab = lax.optimization_barrier((parts, t_tab))

    vecs = jnp.stack([norm_gain, norm_bias, skip_gain])
    mixed, slope, state, state_x, stat, bias = by_channel(
        partial(mixer_kernel, count=H, parts=len(parts)),
        (shape((mp, C, nt), BF16), far_blocks, far_blocks, far_blocks, far((2, N, B), F32), shape((mp, B), F32)),
        [SMEM, SMEM, whole(C, L)] + [whole(2 * N + mp, B)] * len(parts)
        + [chan(2 * B, 2 * B), chan(3 * B, 2 * B), whole(2, C, B)],
        (whole(mp, C, nt), chan(N, B), chan(N, B), chan(N, B), whole(2, N, B), whole(mp, B)),
        6,
        [
            vm((N * C, B), F32), vm((N * C, B), F32), vm((3, N, B), F32), vm((G, 2 * N, 2 * B), BF16),
            vm((G * N, B), F32), vm((G * N, B), F32), vm((G * N, B), F32),
        ],
        large,
        G,
    )(lengths, vecs, tokens, *parts, f_near, t_tab, jump)

    mixed, first, rates = lax.optimization_barrier((mixed, first, rates))
    own_w = [first[:, :few_rows, :]]
    own_w += [exchange(own_w[0], "mp", mp, o) for o in rounds[0]]
    other_w = [partner(v, dp) for v in own_w]
    mixed_tok = lax.all_to_all(mixed, "mp", split_axis=0, concat_axis=0, tiled=True)
    half_steps = C // TABLE_GROUP // 2

    def back_tables(held, start, steps):
        def block(*dims):
            return pl.BlockSpec((TABLE_GROUP,) + dims, lambda i: (i + start,) + (0,) * len(dims))

        return pl.pallas_call(
            partial(back_table_kernel, C=C, M=M, start=start),
            grid=(steps,),
            out_shape=(far((C, 2 * B, 4 * B), BF16), far((C, B, 2 * B), BF16)),
            in_specs=[whole(3, C, B), whole(C, B)] + [hbm] * len(held),
            out_specs=(block(2 * B, 4 * B), block(B, 2 * B)),
            scratch_shapes=[vm((2, B, B), F32)],
            input_output_aliases={2 + k: k for k in range(len(held))},
            compiler_params=params(small),
            cost_estimate=cost(4),
        )(rates, w_all, *[pin(v) for v in held])

    tables = back_tables([], 0, half_steps)
    mixed_tok, tables = lax.optimization_barrier((mixed_tok, tables))
    gm, keep, send = call(
        partial(glu_kernel, parts=len(own_w)),
        (shape((mp, 2 * C, nt), BF16),) + (shape((H, nt), BF16),) * 2,
        4 + 2 * len(own_w), 1, 2, [vm((2, H, nt), BF16), vm((2, mp, C, H), BF16)],
    )(place, mixed_tok, first, bias, *own_w, *other_w)
    mixed_tok = mixed_tok.reshape(H, nt)
    gm, f_tab, rates = lax.optimization_barrier((gm, f_tab, rates))
    gm = lax.all_to_all(gm, "mp", split_axis=0, concat_axis=0, tiled=True)
    u_rev, lift = by_channel(
        partial(lift_kernel, count=H),
        (far((C, 3 * N, 2 * B), BF16), far_blocks),
        [SMEM, SMEM, whole(C, L), whole(2, N, B), few(2 * B, 2 * B)],
        (few(3 * N, 2 * B), few(N, B)),
        3,
        [vm((N * C, B), F32), vm((3, N, B), F32)],
        56,
    )(lengths, vecs, tokens, stat, pin(f_tab))
    back_tab, near_tab = back_tables(tables, half_steps, half_steps)
    gm, lift, back_tab = lax.optimization_barrier((gm, lift, back_tab))

    ways = len(rounds[0]) + 1
    rows_left = mp // ways
    outs = call(
        partial(weight_kernel, C=C, mp=mp), (shape((rows_left * C + 8, H), F32),) * ways, 5, 1, 2,
        [vm((ways, rows_left * C + 8, H), F32)],
    )(place, keep, partner(send, dp), mixed_tok, partner(mixed_tok, dp))
    terms = [outs[0]] + [exchange(v, "mp", mp, o) for v, o in zip(outs[1:], rounds[0])]

    layer_out, gn, sums, plain, g_pre, p_blk, r_blk, rx_blk = by_channel(
        partial(back_kernel, count=H),
        (shape((C, L), BF16), shape((C, L), F32), shape((2, N, B), F32), shape((C, 24, B), F32)) + (blocks,) * 4,
        [
            SMEM, SMEM, VMEM, VMEM, VMEM, hbm, hbm, hbm, VMEM,
        ],
        (whole(C, L), whole(C, L), whole(2, N, B), chan(24, B)) + (chan(N, B),) * 4,
        7,
        [
            vm((N * C, B), F32), vm((N * C, B), F32), vm((N * C, B), F32), vm((3, N, B), F32),
            vm((G, 2 * N, B), BF16), vm((G * N, B), F32), vm((G * N, B), F32), vm((G * N, B), F32),
            vm((C, 2 * B, 4 * B), BF16), vm((C, B, 2 * B), BF16), vm((C, N, B), F32),
            pltpu.SemaphoreType.DMA((3, C // G)),
        ],
        large,
        G,
    )(lengths, vecs, tokens, stat, gm, pin(slope), pin(back_tab), pin(near_tab), jump)

    seen = ways
    terms[0], plain = lax.optimization_barrier((terms[0], plain))
    while seen < mp:
        ways, offs = 2, (seen,)
        rows_left //= ways
        outs = call(
            partial(fold_kernel, ways=ways, got=len(terms), C=C, seen=seen),
            (shape((rows_left * C + 8, H), F32),) * ways,
            1 + len(terms), 1, 1, [vm((ways, rows_left * C + 8, H), F32)],
        )(place, *terms)
        terms = [outs[0]] + [exchange(v, "mp", mp, o) for v, o in zip(outs[1:], offs)]
        seen *= ways
    for k, offs in enumerate(rounds[::-1]):
        got = [exchange(sums, "mp", mp, o) for o in offs]
        if k == len(rounds) - 1:
            g_pre, sums, terms[0] = lax.optimization_barrier((g_pre, sums, terms[0]))
            rows = by_channel(
                sums_kernel,
                shape((C, 40, B), F32),
                [chan(3 * N, 2 * B)] + [chan(N, B)] * 7 + [chan(B, 2 * B), whole(2, C, B)],
                chan(40, B),
                20,
                [],
                large,
                G,
            )(pin(u_rev), pin(lift), g_pre, p_blk, r_blk, rx_blk, pin(state), pin(state_x), pin(near_tab), jump)
            got, rows, terms = lax.optimization_barrier((got, rows, terms))
        sums = sum(got, sums)
    grad_tokens = call(partial(last_kernel, count=H), shape((C, L), F32), 5)(tokens, grad_out, gn, stat, sums)
    rows = call(join_kernel, shape((9, C, B), F32), 2)(plain, rows)
    others = sum_docs(rows, dp, 1) - rows if dp > 2 else partner(rows, dp)

    wsum = call(total_kernel, shape((C + 8, H), F32), len(terms))(*terms)
    wsum = sum_docs(wsum, dp, 2)
    across = partner(wsum, dp)
    thin, wide = shape((C, M), F32), shape((C, 2 * M), F32)
    line = shape((1, C), F32)
    (
        value_wgrad, gate_wgrad, vb, gb, step_grad, decay_grad, frequency_grad, readout_grad, liquid_grad,
        skip_grad, gain_grad, bias_grad,
    ) = call(
        partial(finish_kernel, M=M),
        (shape((C, H), F32), shape((C, H), F32), line, line, line, thin, thin, wide, wide, line, line, line),
        11, 1,
    )(
        place, rows, others, w_all, log_step[None], decay_log, frequency, readout, liquid_readout, wsum, across,
    )
    return (
        layer_out, grad_tokens, gain_grad[0], bias_grad[0], step_grad[0], decay_grad, frequency_grad, readout_grad,
        liquid_grad, skip_grad[0], value_wgrad.T, gate_wgrad.T, vb[0], gb[0],
    )


def solution(mesh):
    row, col, act = P("mp"), P(None, "mp"), P("mp", "dp")
    wide = P("mp", None)
    in_specs = (act, P("dp"), row, row, row, wide, wide, wide, wide, row, col, col, row, row, act)
    out_specs = (act, act, row, row, row, wide, wide, wide, wide, row, col, col, row, row)
    return jax.shard_map(
        partial(per_device, mesh.shape["mp"], mesh.shape["dp"]),
        mesh=mesh, in_specs=in_specs, out_specs=out_specs, check_vma=False,
    )
```

```python
from functools import partial

import jax
import jax.numpy as jnp
import numpy as np
from jax import lax
from jax.experimental import pallas as pl
from jax.experimental.pallas import tpu as pltpu
from jax.sharding import PartitionSpec as P

B = 128
TABLE_GROUP = 8
MIXER_GROUP = 16
F32 = jnp.float32
BF16 = jnp.bfloat16
NN = (((1,), (0,)), ((), ()))
NT = (((1,), (1,)), ((), ()))
TN = (((0,), (0,)), ((), ()))
EPS = 1e-05
SQUARE_SCALE = 65536.0
VMEM = pl.BlockSpec(memory_space=pltpu.VMEM)
SMEM = pl.BlockSpec(memory_space=pltpu.SMEM)


def params(mb):
    return pltpu.CompilerParams(vmem_limit_bytes=mb * 1024 * 1024)


def cost(us):
    return pl.CostEstimate(flops=int(us * 1e9), bytes_accessed=int(us * 1e6), transcendentals=0)


def dot(a, b, dims=NN):
    return lax.dot_general(a, b, dims, preferred_element_type=F32)


def split(v):
    hi = v.astype(BF16)
    return hi, (v - hi.astype(F32)).astype(BF16)


def sincos(x):
    k = jnp.floor(x * 0.6366197723675814 + 0.5)
    y = ((x - k * 1.5703125) - k * 4.837512969970703e-4) - k * 7.54978995489188e-8
    y2 = y * y
    s = y + y * y2 * (-1.6666654611e-1 + y2 * (8.3321608736e-3 - y2 * 1.9515295891e-4))
    c = 1.0 - 0.5 * y2 + y2 * y2 * (4.166664568298827e-2 + y2 * (-1.388731625493765e-3 + y2 * 2.443315711809948e-5))
    q = k.astype(jnp.int32)
    odd = (q & 1) == 1
    sin = jnp.where(odd, c, s)
    cos = jnp.where(odd, s, c)
    sin = jnp.where((q & 2) == 2, -sin, sin)
    cos = jnp.where(((q + 1) & 2) == 2, -cos, cos)
    return sin, cos


def row_iota(shape):
    return lax.broadcasted_iota(jnp.int32, shape, 0)


def lane_iota(shape):
    return lax.broadcasted_iota(jnp.int32, shape, 1)


def shift_token(x, k):
    n = x.shape[0]
    lanes = lane_iota(x.shape)
    rows = row_iota(x.shape)
    turned = pltpu.roll(x, k % B, 1)
    wrapped = pltpu.roll(turned, k % n, 0)
    if k > 0:
        wrapped = jnp.where(rows >= 1, wrapped, 0.0)
        return jnp.where(lanes == 0, wrapped, turned)
    wrapped = jnp.where(rows < n - 1, wrapped, 0.0)
    return jnp.where(lanes == B - 1, wrapped, turned)


def swap_halves(x):
    return pltpu.roll(x, B // 2, 1)


def scan_blocks(v_ref, out_ref, turned_ref, jump, N, backward):
    a_re, a_im = jump
    G = v_ref.shape[0] // N
    s = jnp.zeros((G, B), F32)
    t = s
    for k in range(N):
        n = N - 1 - k if backward else k
        out_ref[pl.ds(n, G, stride=N), :] = s
        turned_ref[pl.ds(n, G, stride=N), :] = t
        v = v_ref[pl.ds(n, G, stride=N), :]
        s, t = a_re * s + (a_im * t + v), a_re * t + (swap_halves(v) - a_im * s)


def start_kernel(place_ref, x_hbm, g_hbm, v_hbm, w_hbm, *refs):
    more, refs = refs[:2], refs[2:]
    stat_ref, pay_ref, x_ref, g_ref, wt_ref = refs[:5]
    held, sems = refs[5:7], refs[7]
    vb_ref, gb_ref = held
    C, L = x_ref.shape
    N = L // B
    mp, rows, nt = pay_ref.shape
    few = rows - 2 * C
    pairs = ((x_hbm, x_ref), (g_hbm, g_ref)) + tuple(zip(more, held))
    moves = [pltpu.make_async_copy(src, dst, sems.at[1 + k]) for k, (src, dst) in enumerate(pairs)]
    for move in moves:
        move.start()
    for half, ref in enumerate((v_hbm, w_hbm)):

        @pl.when(place_ref[0] == half)
        def _():
            pltpu.make_async_copy(ref, wt_ref, sems.at[0]).start()

    moves[0].wait()
    for n in range(N):
        x = x_ref[:, n * B : (n + 1) * B].astype(F32)
        mean = jnp.sum(x, axis=0, keepdims=True) * (1.0 / C)
        dev = x - mean
        stat_ref[n : n + 1, :] = mean
        stat_ref[N + n : N + n + 1, :] = jnp.sum(dev * dev, axis=0, keepdims=True)
    own = row_iota((mp, B))
    for move in moves[2:]:
        move.wait()
    bias = jnp.concatenate([vb_ref[...].astype(F32), gb_ref[...].astype(F32), jnp.zeros((1, B - 2 * C), F32)], axis=1)
    stat_ref[2 * N :, :] = jnp.where(own == place_ref[1], bias, 0.0)
    for j in range(mp):
        pay_ref[j, few : few + C, :] = x_ref[:, j * nt : (j + 1) * nt]
    moves[1].wait()
    for j in range(mp):
        pay_ref[j, few + C :, :] = g_ref[:, j * nt : (j + 1) * nt]
    pltpu.make_async_copy(v_hbm, wt_ref, sems.at[0]).wait()
    parts = wt_ref.shape[1] // B
    for j in range(mp):
        lanes = slice(j % parts * B, (j % parts + 1) * B)
        for q in range(nt // B):
            pay_ref[j, 0:few, q * B : (q + 1) * B] = wt_ref[q * few : (q + 1) * few, lanes]


def join_stats(parts, N, count):
    mean = sum(p[:N] for p in parts) * (1.0 / len(parts))
    spread = sum(p[N : 2 * N] for p in parts) + count * sum((p[:N] - mean) * (p[:N] - mean) for p in parts)
    return mean, spread, sum(p[2 * N :] for p in parts)


def mode_columns(log_step, decay, freq, coef):
    C = decay.shape[0]
    step_size = jnp.exp(log_step)
    real_rate = -jnp.exp(decay)
    re = step_size * real_rate
    im = step_size * freq
    growth = jnp.exp(re)
    sin, cos = sincos(im)
    num_re = growth * cos - 1.0
    num_im = growth * sin
    den = real_rate * real_rate + freq * freq
    in_re = (num_re * real_rate + num_im * freq) / den
    in_im = (num_im * real_rate - num_re * freq) / den
    first = lane_iota(coef.shape) < B // 2
    w = coef * in_re + swap_halves(coef) * jnp.where(first, -in_im, in_im)
    sin, cos = sincos(im * float(B))
    mag = jnp.exp(re * float(B))
    jump = mag * cos, mag * jnp.where(first, -sin, sin)
    group = lane_iota(re.shape) // (B // 4)
    packed = jnp.where(group == 0, re, jnp.where(group == 1, im, jnp.where(group == 2, cos, sin)))
    pad = jnp.zeros((B - C, B), F32)
    return w, jump, [jnp.concatenate([v, pad], axis=0).T for v in (packed, w)]


def mode_kernel(step_ref, decay_ref, freq_ref, read_ref, liquid_ref, cols_ref, jump_ref, w_all_ref):
    C, M = decay_ref.shape
    decay, freq, read, liquid = decay_ref[...], freq_ref[...], read_ref[...], liquid_ref[...]
    step = jnp.sum(jnp.where(row_iota((C, C)) == lane_iota((C, C)), step_ref[...], 0.0), axis=1, keepdims=True)
    coef = jnp.concatenate([read[:, :M], liquid[:, :M], read[:, M:], liquid[:, M:]], axis=1)
    w_all_ref[...], (jump_ref[0], jump_ref[1]), (cols_ref[0], cols_ref[1]) = mode_columns(
        step, jnp.concatenate([decay] * 4, axis=1), jnp.concatenate([freq] * 4, axis=1), coef
    )


def channel_waves(cols, i, M, G):
    back = (B - i * G) % B
    pp = pltpu.roll(cols[0], back, 1)
    ww = 2.0 * pltpu.roll(cols[1], back, 1)
    place = lane_iota((M, B)).astype(F32)
    ahead = float(B) - place
    out = []
    for j in range(G):
        a, o, c, s = [jnp.broadcast_to(pp[q * M : (q + 1) * M, j : j + 1], (M, B)) for q in range(4)]
        w = [jnp.broadcast_to(ww[q * M : (q + 1) * M, j : j + 1], (M, B)) for q in range(4)]
        sin, cos = sincos(o * place)
        mag = jnp.exp(a * place)
        rest = jnp.exp(a * ahead)
        out.append(((mag * cos, mag * sin), (rest * (c * cos + s * sin), rest * (s * cos - c * sin)), w))
    return out


def toeplitz_rows(kern, start):
    return pltpu.roll(jnp.broadcast_to(kern, (B, B)), start, 1, stride=1, stride_axis=0)


def table_kernel(cols, f_ref, again_ref, t_ref, *, M):
    i = pl.program_id(0)
    G = f_ref.shape[0]
    rows = row_iota((B, B))
    lanes = lane_iota((B, B))
    odd = (lanes & M) == M
    zero = jnp.zeros((B, B), BF16)
    every = range(G)
    waves = channel_waves(cols, i, M, G)
    feeds = [jnp.concatenate([f_re, f_re, f_im, f_im], axis=0).T for _, (f_re, f_im), _ in waves]
    kerns = []
    for j in every:
        (n_re, n_im), _, w = waves[j]
        for h in range(2):
            w_re, w_im = w[h], w[2 + h]
            e_re = w_re * n_re - w_im * n_im
            e_im = -(w_re * n_im + w_im * n_re)
            kerns.append(jnp.sum(e_re, axis=0, keepdims=True))
            for q, v in enumerate(split(e_re)):
                t_ref[j, 2 * B + h * M : 2 * B + (h + 1) * M, q * B : (q + 1) * B] = v
            for q, v in enumerate(split(e_im)):
                t_ref[j, 2 * B + (2 + h) * M : 2 * B + (3 + h) * M, q * B : (q + 1) * B] = v
    rolled = [toeplitz_rows(kern, 0) for kern in kerns]
    for j in every:
        parts = split(feeds[j])
        for h in range(2):
            for q, part in enumerate(parts):
                v = jnp.where(odd if h == 1 else ~odd, part, zero)
                f_ref[j, h * B : (h + 1) * B, q * B : (q + 1) * B] = v
                again_ref[j, h * B : (h + 1) * B, q * B : (q + 1) * B] = v
            toe = jnp.where(lanes >= rows, rolled[2 * j + h], 0.0)
            for q, v in enumerate(split(toe)):
                t_ref[j, h * B : (h + 1) * B, q * B : (q + 1) * B] = v


def back_table_kernel(cols, *refs, M, start):
    t_ref, near_ref = refs[-2:]
    i = pl.program_id(0) + start
    G = t_ref.shape[0]
    rows = row_iota((B, B))
    lanes = lane_iota((B, B))
    every = range(G)
    waves = channel_waves(cols, i, M, G)
    turned = [jnp.concatenate([n_re, n_re, n_im, n_im], axis=0).T for (n_re, n_im), _, _ in waves]
    kerns, starts = [], []
    for j in every:
        (n_re, n_im), (f_re, f_im), w = waves[j]
        for h in range(2):
            w_re, w_im = w[h], w[2 + h]
            b_re = w_re * f_re - w_im * f_im
            b_im = -(w_re * f_im + w_im * f_re)
            kerns.append(jnp.sum(b_re, axis=0, keepdims=True))
            starts.append(jnp.sum(w_re * n_re - w_im * n_im, axis=0, keepdims=True)[:, 0:1])
            for part, v2 in enumerate((b_re, b_im)):
                for q, v in enumerate(split(v2)):
                    at = slice((2 * q + h) * B, (2 * q + h + 1) * B)
                    t_ref[j, B + part * M : B + (part + 1) * M, at] = v
    rolled = [toeplitz_rows(kern, 0) for kern in kerns]
    for j in every:
        for q, v in enumerate(split(turned[j])):
            near_ref[j, :, q * B : (q + 1) * B] = v
        for h in range(2):
            start = jnp.broadcast_to(starts[2 * j + h], (B, B))
            toe = jnp.where(lanes < rows, rolled[2 * j + h], jnp.where(lanes == rows, start, 0.0))
            for q, v in enumerate(split(toe)):
                t_ref[j, 0:B, (2 * q + h) * B : (2 * q + h + 1) * B] = v


def token_stats(stat_ref, length, count):
    mean = stat_ref[0]
    inv = lax.rsqrt(stat_ref[1] * (1.0 / count) + EPS)
    place = row_iota(mean.shape) * B + lane_iota(mean.shape)
    return mean, inv, (place < length).astype(F32)


def mixer_kernel(len_ref, vec_ref, x_ref, *refs, count, parts):
    part_refs, refs = refs[:parts], refs[parts:]
    f_ref, t_ref, jump_ref = refs[:3]
    mixed_ref, slope_ref, state_ref, other_ref, stat_ref, bias_ref = refs[3:9]
    xs, ms, tok, us, ups, sts, ots = refs[9:]
    i = pl.program_id(0)
    G = f_ref.shape[0]
    C, L = x_ref.shape
    N = L // B
    nt = mixed_ref.shape[2]

    @pl.when(i == 0)
    def _():
        for n in range(N):
            xs[n * C : (n + 1) * C, :] = x_ref[:, n * B : (n + 1) * B].astype(F32)
        stat_ref[0], stat_ref[1], bias_ref[...] = join_stats([r[...] for r in part_refs], N, count / parts)
        mean, inv, mask = token_stats(stat_ref, len_ref[0], count)
        tok[0] = mean
        tok[1] = inv
        tok[2] = mask

    for j in range(G):
        ci = i * G + j
        normed = (xs[pl.ds(ci, N, stride=C), :] - tok[0]) * tok[1]
        sig = tok[2] * (normed * vec_ref[0, ci] + vec_ref[1, ci])
        liq = sig * shift_token(sig, 1)
        for q, v in enumerate((sig, liq)):
            hi, lo = split(v)
            us[j, 0:N, q * B : (q + 1) * B] = hi
            us[j, N:, q * B : (q + 1) * B] = lo
        slope_ref[j] = sig
    ups_all = [dot(us[j], f_ref[j]) for j in range(G)]
    for j, up in enumerate(ups_all):
        ups[j * N : (j + 1) * N, :] = up[:N, :B] + (up[:N, B:] + up[N:, :B])
    at = pl.ds(pl.multiple_of(i * G, G), G)
    scan_blocks(ups, sts, ots, (jump_ref[0, at, :], jump_ref[1, at, :]), N, False)
    left = []
    for j in range(G):
        state = sts[j * N : (j + 1) * N, :]
        state_ref[j] = state
        other_ref[j] = ots[j * N : (j + 1) * N, :]
        left.append(jnp.concatenate([us[j], jnp.concatenate(split(state), axis=0)], axis=1))
    outs = [dot(left[j], t_ref[j]) for j in range(G)]
    for j, out in enumerate(outs):
        ci = i * G + j
        mask = tok[2]
        y = out[:N, :B] + (out[:N, B:] + out[N:, :B]) + vec_ref[2, ci] * slope_ref[j]
        y2 = y * y
        th = jnp.tanh(0.7978845608028654 * (y + 0.044715 * (y * y2)))
        half = 0.5 * (1.0 + th)
        ms[pl.ds(pl.multiple_of(ci * N, N), N), :] = mask * (y * half)
        slope_ref[j] = mask * (half + 0.5 * y * (1.0 - th * th) * (0.7978845608028654 * (1.0 + 0.134145 * y2)))

    @pl.when(i == pl.num_programs(0) - 1)
    def _():
        per = nt // B
        for n in range(N):
            mixed_ref[n // per, :, (n % per) * B : (n % per + 1) * B] = ms[pl.ds(n, C, stride=N), :].astype(BF16)


def glu_kernel(place_ref, in_ref, first_ref, bias_ref, *refs, parts):
    own_refs, other_refs, refs = refs[:parts], refs[parts : 2 * parts], refs[2 * parts :]
    gm_ref, keep_ref, send_ref, gp, wt = refs
    mp, C, nt = in_ref.shape
    H = mp * C
    few = own_refs[0].shape[1]
    own = place_ref[0]
    mixed = in_ref[...].reshape(H, nt)
    for k in range(parts):
        lanes = pl.ds(pl.multiple_of((lax.rem(place_ref[1], parts) ^ k) * B, B), B)
        for q in range(nt // B):
            at = slice(q * few, (q + 1) * few)
            wt[own, :, at, lanes] = own_refs[k][:, :, q * B : (q + 1) * B]
            wt[1 - own, :, at, lanes] = other_refs[k][:, :, q * B : (q + 1) * B]
    step = B
    per = step // C
    bias = jnp.concatenate([bias_ref[...], jnp.zeros((B - mp, B), F32)], axis=0).T
    for s in range(mp // per):
        lo = s * step
        col_v = jnp.concatenate([bias[0:C, k : k + 1] for k in range(s * per, (s + 1) * per)], axis=0)
        col_g = jnp.concatenate([bias[C : 2 * C, k : k + 1] for k in range(s * per, (s + 1) * per)], axis=0)
        at = slice(s * per, (s + 1) * per)
        value = dot(wt[0, at].reshape(step, H), mixed) + col_v
        gate = dot(wt[1, at].reshape(step, H), mixed) + col_g
        sig = jax.nn.sigmoid(gate)
        x = first_ref[at, few : few + C, :].reshape(step, nt).astype(F32)
        g = first_ref[at, few + C :, :].reshape(step, nt).astype(F32)
        gm_ref[s * per : (s + 1) * per, C:, :] = (x + value * sig).astype(BF16).reshape(per, C, nt)
        gv = g * sig
        gp[0, lo : lo + step, :] = gv.astype(BF16)
        gp[1, lo : lo + step, :] = (gv * value * (1.0 - sig)).astype(BF16)
    for s in range(mp // per):
        at = slice(s * step, (s + 1) * step)
        gm = sum(dot(wt[h, :, :, at].reshape(H, step), gp[h], TN) for h in range(2))
        wide = gm * SQUARE_SCALE
        gm_ref[s * per : (s + 1) * per, 0:C, :] = (wide * jnp.abs(wide)).astype(BF16).reshape(per, C, nt)
    keep_ref[...] = gp[own]
    send_ref[...] = gp[1 - own]


def weight_kernel(place_ref, keep_ref, got_ref, mixed_ref, theirs_ref, *refs, C, mp):
    outs, wg = refs[:-1], refs[-1]
    nt = mixed_ref.shape[1]
    ways = len(outs)
    per = mp // ways
    total = dot(keep_ref[...], mixed_ref[...], NT) + dot(got_ref[...], theirs_ref[...], NT)
    for m in range(mp):
        at = (m // ways) * C
        wg[m % ways, at : at + C, :] = total[m * C : (m + 1) * C]
    ones = jnp.ones((8, nt), BF16)
    tail = dot(ones, keep_ref[...], NT) + dot(ones, got_ref[...], NT)
    for q in range(ways):
        wg[q, per * C :, :] = tail
    for k in range(ways):
        outs[k][...] = wg[lax.rem(place_ref[1], ways) ^ k]


def fold_kernel(place_ref, *refs, ways, got, C, seen):
    parts, outs, acc = refs[:got], refs[got:-1], refs[-1]
    total = parts[0][...]
    for p in parts[1:]:
        total = total + p[...]
    blocks = (total.shape[0] - 8) // C
    for z in range(blocks):
        at = (z // ways) * C
        acc[z % ways, at : at + C, :] = total[z * C : (z + 1) * C]
    for q in range(ways):
        acc[q, (blocks // ways) * C :, :] = total[blocks * C :]
    for k in range(ways):
        outs[k][...] = acc[lax.rem(lax.div(place_ref[1], seen), ways) ^ k]


def back_kernel(
    len_ref, vec_ref, x_ref, stat_ref, gm_ref, slope_hbm, t_ref, near_hbm, jump_ref,
    layer_ref, gn_ref, sum_ref, row_ref, g_ref, p_ref, r_ref, turned_ref, xs, gs, ns, tok, hs, ps, rs, rts, tab, near_ref, slope_ref, sem, *, count,
):
    i = pl.program_id(0)
    G = g_ref.shape[0]
    C, L = x_ref.shape
    N = L // B
    nt = gm_ref.shape[2]
    per = nt // B
    quarter = B // 4

    def fetch(q, k):
        at = pl.ds(k * G, G)
        src, dst = (
            (slope_hbm.at[at], slope_ref.at[at]),
            (near_hbm.at[at], near_ref.at[at]),
            (t_ref.at[at, 0:B, :], tab.at[at, 0:B, :]),
            (t_ref.at[at, B:, :], tab.at[at, B + quarter : B + 3 * quarter, :]),
        )[q]
        return pltpu.make_async_copy(src, dst, sem.at[q, k])

    @pl.when(i == 0)
    def _():
        for k in range(C // G):
            for q in range(4):
                fetch(q, k).start()
        tab[:, B : B + quarter, :] = jnp.zeros((C, quarter, 4 * B), BF16)
        tab[:, B + 3 * quarter :, :] = jnp.zeros((C, quarter, 4 * B), BF16)
        for n in range(N):
            xs[n * C : (n + 1) * C, :] = x_ref[:, n * B : (n + 1) * B].astype(F32)
            at = slice((n % per) * B, (n % per + 1) * B)
            square = gm_ref[n // per, 0:C, at].astype(F32)
            gs[n * C : (n + 1) * C, :] = square * (lax.rsqrt(jnp.maximum(jnp.abs(square), 1e-37)) * (1.0 / SQUARE_SCALE))
        mean, inv, mask = token_stats(stat_ref, len_ref[0], count)
        tok[0] = mean
        tok[1] = inv
        tok[2] = mask
        sum_ref[...] = jnp.zeros_like(sum_ref)
        for m in range(gm_ref.shape[0]):
            layer_ref[:, m * nt : (m + 1) * nt] = gm_ref[m, C:, :]

    fetch(0, i).wait()
    for j in range(G):
        ci = i * G + j
        g = gs[pl.ds(ci, N, stride=C), :] * slope_ref[ci]
        g_ref[j] = g
        hi, lo = split(g)
        hs[j, 0:N, :] = hi
        hs[j, N:, :] = lo
    fetch(1, i).wait()
    z_all = [dot(hs[j], near_ref[i * G + j]) for j in range(G)]
    for j, z in enumerate(z_all):
        p = z[:N, :B] + (z[:N, B:] + z[N:, :B])
        p_ref[j] = p
        ps[j * N : (j + 1) * N, :] = p
    at = pl.ds(pl.multiple_of(i * G, G), G)
    scan_blocks(ps, rs, rts, (jump_ref[0, at, :], jump_ref[1, at, :]), N, True)
    left = []
    for j in range(G):
        r = rs[j * N : (j + 1) * N, :]
        r_ref[j] = r
        turned_ref[j] = rts[j * N : (j + 1) * N, :]
        left.append(jnp.concatenate([hs[j], jnp.concatenate(split(r), axis=0)], axis=1))
    fetch(2, i).wait()
    fetch(3, i).wait()
    both_all = [dot(left[j], tab[i * G + j]) for j in range(G)]
    for j, both in enumerate(both_all):
        ci = i * G + j
        mask = tok[2]
        normed = (xs[pl.ds(ci, N, stride=C), :] - tok[0]) * tok[1]
        sig = mask * (normed * vec_ref[0, ci] + vec_ref[1, ci])
        both = both[:N, : 2 * B] + (both[:N, 2 * B :] + both[N:, : 2 * B])
        gl = both[:, B:]
        grad = both[:, :B] + vec_ref[2, ci] * g_ref[j] + gl * shift_token(sig, 1) + shift_token(gl * sig, -1)
        masked = mask * grad
        gn = masked * vec_ref[0, ci]
        sum_ref[0] += gn
        sum_ref[1] += gn * normed
        ns[pl.ds(pl.multiple_of(ci * N, N), N), :] = gn
        for q, v in enumerate((g_ref[j] * sig, masked * normed, masked)):
            row_ref[j, q * 8 : (q + 1) * 8, :] = sum(v[8 * k : 8 * k + 8] for k in range(N // 8))

    @pl.when(i == pl.num_programs(0) - 1)
    def _():
        for n in range(N):
            gn_ref[:, n * B : (n + 1) * B] = ns[pl.ds(n, C, stride=N), :]


def lift_kernel(len_ref, vec_ref, x_ref, stat_ref, f_ref, u_ref, lift_ref, xs, tok, *, count):
    i = pl.program_id(0)
    G = f_ref.shape[0]
    C, L = x_ref.shape
    N = L // B

    @pl.when(i == 0)
    def _():
        for n in range(N):
            xs[n * C : (n + 1) * C, :] = x_ref[:, n * B : (n + 1) * B].astype(F32)
        tok[0], tok[1], tok[2] = token_stats(stat_ref, len_ref[0], count)

    ahead = float(B) - lane_iota((N, B)).astype(F32)
    flip = (lane_iota((B, B)) + row_iota((B, B)) == B - 1).astype(BF16)
    flat, left = [], []
    for j in range(G):
        ci = i * G + j
        normed = (xs[pl.ds(ci, N, stride=C), :] - tok[0]) * tok[1]
        sig = tok[2] * (normed * vec_ref[0, ci] + vec_ref[1, ci])
        liq = sig * shift_token(sig, 1)
        flat.append(jnp.concatenate(split(sig) + split(liq), axis=0))
        left.append(jnp.concatenate(split(jnp.concatenate([sig * ahead, liq * ahead], axis=1)), axis=0))
    turned_all = [dot(v, flip).astype(BF16) for v in flat]
    lifts = [dot(left[j], f_ref[j]) for j in range(G)]
    for j in range(G):
        turned, lift = turned_all[j], lifts[j]
        for q in range(2):
            at = slice(q * B, (q + 1) * B)
            u_ref[j, 0 : 2 * N, at] = turned[2 * q * N : (2 * q + 2) * N]
            u_ref[j, 2 * N :, at] = turned[2 * q * N : (2 * q + 1) * N]
        lift_ref[j] = lift[:N, :B] + (lift[:N, B:] + lift[N:, :B])


def sums_kernel(u_ref, lift_ref, g_ref, p_ref, r_ref, rx_ref, state_ref, sx_ref, near_ref, jump_ref, row_ref):
    i = pl.program_id(0)
    G = g_ref.shape[0]
    _, N, _ = g_ref.shape
    place = lane_iota((N, B)).astype(F32)
    rows2, lanes2 = row_iota((B, B)), lane_iota((B, B))
    inside = lanes2 + rows2 >= B - 1
    rows16 = row_iota((16, B))
    lag = lane_iota((16, B)).astype(F32)
    R = N + 16
    every = range(G)
    turned = []
    for j in every:
        g_hi, g_lo = split(g_ref[j])
        turned.append(jnp.concatenate([g_hi, g_hi, g_lo], axis=0).T)
    corr = [dot(turned[j], u_ref[j]) for j in every]
    left = []
    for j in every:
        lags = []
        for q in range(2):
            part = jnp.where(inside, corr[j][:, q * B : (q + 1) * B], 0.0)
            lags.append(jnp.sum(pltpu.roll(part, 1, 1, stride=1, stride_axis=0), axis=0, keepdims=True))
        pair = jnp.where((rows16 & 1) == 0, lags[0], lags[1])
        pair = jnp.where(rows16 < 2, pair, jnp.where(rows16 < 4, pair * lag, 0.0))
        left.append(jnp.concatenate(split(jnp.concatenate([g_ref[j] * place, pair], axis=0)), axis=0))
    both = [dot(left[j], near_ref[j]) for j in every]
    for j in every:
        ci = i * G + j
        z = both[j][:R, :B] + (both[j][:R, B:] + both[j][R:, :B])
        row_ref[j, 0:8, :] = z[N : N + 8]
        p, r, state, lift = p_ref[j], r_ref[j], state_ref[j], lift_ref[j]
        state_x, r_x = sx_ref[j], rx_ref[j]
        carry = z[:N] + float(B) * (r * jump_ref[0, pl.ds(ci, 1), :] + r_x * jump_ref[1, pl.ds(ci, 1), :])
        total = [p * state, p * state_x, carry * state + lift * r, carry * state_x + lift * r_x]
        for q, v in enumerate(total):
            row_ref[j, 8 + 8 * q : 16 + 8 * q, :] = sum(v[8 * k : 8 * k + 8] for k in range(N // 8))


def join_kernel(plain_ref, ref, out_ref):
    odd = (lane_iota((out_ref.shape[1], B)) & (B // 4)) != 0
    for q in range(2):
        out_ref[q] = jnp.where(odd, ref[:, 2 * q + 1, :], ref[:, 2 * q, :])
    for q in range(4):
        out_ref[2 + q] = jnp.sum(ref[:, 8 + 8 * q : 16 + 8 * q, :], axis=1)
    for q in range(3):
        out_ref[6 + q] = jnp.sum(plain_ref[:, 8 * q : 8 * q + 8, :], axis=1)


def finish_kernel(
    place_ref, mine_ref, theirs_ref, w_ref, step_ref, decay_ref, freq_ref, read_ref, liquid_ref, wsum_ref, across_ref,
    value_ref, gate_ref, vbias_ref, gbias_ref, step_out, decay_out, freq_out, read_out, liquid_out,
    skip_out, gain_out, bias_out, *, M,
):
    C = decay_ref.shape[0]
    half = B // 2

    def emit(first, second):
        value_ref[...] = first[0:C, :]
        gate_ref[...] = second[0:C, :]
        per = B // C
        group = place_ref[1] // per
        back = (B - (place_ref[1] % per) * C) % B
        for out, v in ((vbias_ref, first), (gbias_ref, second)):
            lanes = v[C : C + 8, pl.ds(pl.multiple_of(group * B, B), B)]
            out[...] = pltpu.roll(lanes, back, 1)[0:1, 0:C]

    @pl.when(place_ref[0] == 0)
    def _():
        emit(wsum_ref, across_ref)

    @pl.when(place_ref[0] == 1)
    def _():
        emit(across_ref, wsum_ref)

    rows = [mine_ref[q] + theirs_ref[q] for q in range(9)]

    def parts(a, b, c):
        return a[:, :half] - a[:, half:] + c[:, :half], b[:, :half] + b[:, half:] + c[:, half:]

    g_re, g_im = parts(rows[2], rows[3], rows[0])
    d_re, d_im = parts(rows[4], rows[5], rows[1])
    w = w_ref[...]
    w_re, w_im = w[:, :half], w[:, half:]
    l_re = w_re * d_re - w_im * d_im
    l_im = w_re * d_im + w_im * d_re
    cot = (
        2.0 * g_re[:, :M], -2.0 * g_im[:, :M], 2.0 * g_re[:, M:], -2.0 * g_im[:, M:],
        2.0 * (l_re[:, :M] + l_re[:, M:]), -2.0 * (l_im[:, :M] + l_im[:, M:]),
    )
    step = jnp.sum(jnp.where(row_iota((C, C)) == lane_iota((C, C)), step_ref[...], 0.0), axis=1, keepdims=True)
    _, back = jax.vjp(mode_terms, step, decay_ref[...], freq_ref[...], read_ref[...], liquid_ref[...])
    step_grad, decay_out[...], freq_out[...], read_out[...], liquid_out[...] = back(cot)
    lanes = lane_iota((B, B))
    pad = jnp.zeros((B - C, 1), F32)
    plain = jnp.zeros((B, B), F32)
    for q, v in enumerate([step_grad] + [jnp.sum(rows[6 + q], axis=1, keepdims=True) for q in range(3)]):
        plain = jnp.where(lanes == q, jnp.concatenate([v, pad], axis=0), plain)
    plain = plain.T
    for q, out in enumerate((step_out, skip_out, gain_out, bias_out)):
        out[...] = plain[q : q + 1, 0:C]


def last_kernel(x_ref, g_ref, gn_ref, stat_ref, sum_ref, out_ref, *, count):
    C, L = x_ref.shape
    for n in range(L // B):
        at = slice(n * B, (n + 1) * B)
        mean = stat_ref[0, n : n + 1, :]
        inv = lax.rsqrt(stat_ref[1, n : n + 1, :] * (1.0 / count) + EPS)
        first = sum_ref[0, n : n + 1, :] * (1.0 / count)
        second = sum_ref[1, n : n + 1, :] * (1.0 / count)
        normed = (x_ref[:, at].astype(F32) - mean) * inv
        out_ref[:, at] = inv * (gn_ref[:, at] - first - normed * second) + g_ref[:, at].astype(F32)


def total_kernel(*refs):
    total = refs[0][...]
    for p in refs[1:-1]:
        total = total + p[...]
    refs[-1][...] = total


def rounds_of(size):
    rounds, bit = [], 1
    while bit < size:
        if bit * 2 < size:
            rounds.append((bit, 2 * bit, 3 * bit))
            bit *= 4
        else:
            rounds.append((bit,))
            bit *= 2
    return rounds


def exchange(v, axis, size, off):
    return lax.ppermute(v, axis, [(k, k ^ off) for k in range(size)])


def all_sums(v, size):
    for offs in rounds_of(size):
        v = sum([exchange(v, "mp", size, o) for o in offs], v)
    return v


def sum_docs(v, size, stride):
    total = v
    for k in range(stride, size, stride):
        total = total + lax.ppermute(v, "dp", [(q, (q + k) % size) for q in range(size)])
    return total


def partner(v, size):
    return lax.ppermute(v, "dp", [(q, q ^ 1) for q in range(size)])


def mode_terms(log_step, decay_log, frequency, readout, liquid_readout):
    M = decay_log.shape[1]
    step_size = jnp.exp(log_step)
    real_rate = -jnp.exp(decay_log)
    real_step = step_size * real_rate
    imag_step = step_size * frequency
    growth = jnp.exp(real_step)
    num_real = growth * jnp.cos(imag_step) - 1.0
    num_imag = growth * jnp.sin(imag_step)
    denominator = real_rate * real_rate + frequency * frequency
    in_real = (num_real * real_rate + num_imag * frequency) / denominator
    in_imag = (num_imag * real_rate - num_real * frequency) / denominator

    def mix(coeffs):
        re, im = coeffs[:, :M], coeffs[:, M:]
        return re * in_real - im * in_imag, re * in_imag + im * in_real

    return mix(readout) + mix(liquid_readout) + (real_step, imag_step)


def per_device(
    mp, dp,
    tokens, lengths, norm_gain, norm_bias, log_step, decay_log, frequency, readout, liquid_readout,
    skip_gain, value_weight, gate_weight, value_bias, gate_bias, grad_out,
):
    C, L = tokens.shape
    H = value_weight.shape[0]
    M = decay_log.shape[1]
    N = L // B
    nt = L // mp
    few_rows = C * B // nt
    shape = jax.ShapeDtypeStruct

    place = jnp.stack([lax.axis_index("dp") & 1, lax.axis_index("mp")]).astype(jnp.int32)
    rounds = rounds_of(mp)
    small, large = 16, 32

    def pin(v):
        return pltpu.with_memory_space_constraint(v, pltpu.HBM)

    def call(kernel, out, n_in, smem=0, us=1, scratch=(), mb=small):
        return pl.pallas_call(
            kernel,
            out_shape=out,
            in_specs=[SMEM] * smem + [VMEM] * (n_in - smem),
            out_specs=jax.tree.map(lambda _: VMEM, out),
            scratch_shapes=list(scratch),
            compiler_params=params(mb),
            cost_estimate=cost(us),
        )

    def whole(*dims):
        return pl.BlockSpec(dims, lambda i: (0,) * len(dims))

    def chan_by(group):
        return lambda *dims: pl.BlockSpec((group,) + dims, lambda i: (i,) + (0,) * len(dims))

    def by_channel(kernel, out, in_specs, out_specs, us, scratch, mb=small, group=TABLE_GROUP):
        return pl.pallas_call(
            kernel,
            grid=(C // group,),
            out_shape=out,
            in_specs=in_specs,
            out_specs=out_specs,
            scratch_shapes=scratch,
            compiler_params=params(mb),
            cost_estimate=cost(us),
        )

    vm = pltpu.VMEM
    G = min(MIXER_GROUP, C)
    chan, few = chan_by(G), chan_by(TABLE_GROUP)
    blocks = shape((C, N, B), F32)
    far = pltpu.HBM
    far_blocks = far((C, N, B), F32)
    def pin(v):
        return pltpu.with_memory_space_constraint(v, far)

    hbm = pl.BlockSpec(memory_space=pltpu.HBM)
    stat, pay = pl.pallas_call(
        start_kernel,
        out_shape=(shape((2 * N + mp, B), F32), shape((mp, few_rows + 2 * C, nt), BF16)),
        in_specs=[SMEM] + [hbm] * 6,
        out_specs=(VMEM, VMEM),
        scratch_shapes=[
            pltpu.VMEM((C, L), BF16), pltpu.VMEM((C, L), BF16), pltpu.VMEM((C, H), BF16),
            pltpu.VMEM((1, C), BF16), pltpu.VMEM((1, C), BF16), pltpu.SemaphoreType.DMA((5,)),
        ],
        compiler_params=params(small),
        cost_estimate=cost(3),
    )(
        place, pin(tokens), pin(grad_out), pin(value_weight.T), pin(gate_weight.T), pin(value_bias[None]), pin(gate_bias[None])
    )
    first = lax.all_to_all(pay, "mp", split_axis=0, concat_axis=0, tiled=True)

    count = C
    for k, offs in enumerate(rounds[::-1]):
        parts = [stat] + [exchange(stat, "mp", mp, o) for o in offs]
        if k < len(rounds) - 1:
            stat = jnp.concatenate(join_stats(parts, N, float(count)), axis=0)
            count *= len(parts)
            stat, rates = lax.optimization_barrier((stat, decay_log))
    cols, jump, w_all = call(
        mode_kernel, (shape((2, B, B), F32), shape((2, C, B), F32), shape((C, B), F32)), 5
    )(log_step[None], rates, frequency, readout, liquid_readout)
    f_near, f_tab, t_tab = by_channel(
        partial(table_kernel, M=M),
        (shape((C, 2 * B, 2 * B), BF16), far((C, 2 * B, 2 * B), BF16), shape((C, 3 * B, 2 * B), BF16)),
        [whole(2, B, B)],
        (few(2 * B, 2 * B), few(2 * B, 2 * B), few(3 * B, 2 * B)),
        6,
        [],
    )(cols)
    parts, t_tab = lax.optimization_barrier((parts, t_tab))

    vecs = jnp.stack([norm_gain, norm_bias, skip_gain])
    mixed, slope, state, state_x, stat, bias = by_channel(
        partial(mixer_kernel, count=H, parts=len(parts)),
        (shape((mp, C, nt), BF16), far_blocks, far_blocks, far_blocks, far((2, N, B), F32), shape((mp, B), F32)),
        [SMEM, SMEM, whole(C, L)] + [whole(2 * N + mp, B)] * len(parts)
        + [chan(2 * B, 2 * B), chan(3 * B, 2 * B), whole(2, C, B)],
        (whole(mp, C, nt), chan(N, B), chan(N, B), chan(N, B), whole(2, N, B), whole(mp, B)),
        6,
        [
            vm((N * C, B), F32), vm((N * C, B), F32), vm((3, N, B), F32), vm((G, 2 * N, 2 * B), BF16),
            vm((G * N, B), F32), vm((G * N, B), F32), vm((G * N, B), F32),
        ],
        large,
        G,
    )(lengths, vecs, tokens, *parts, f_near, t_tab, jump)

    mixed, first, cols = lax.optimization_barrier((mixed, first, cols))
    own_w = [first[:, :few_rows, :]]
    own_w += [exchange(own_w[0], "mp", mp, o) for o in rounds[0]]
    other_w = [partner(v, dp) for v in own_w]
    mixed_tok = lax.all_to_all(mixed, "mp", split_axis=0, concat_axis=0, tiled=True)
    half_steps = C // TABLE_GROUP // 2

    def back_tables(held, start, steps):
        def block(*dims):
            return pl.BlockSpec((TABLE_GROUP,) + dims, lambda i: (i + start,) + (0,) * len(dims))

        return pl.pallas_call(
            partial(back_table_kernel, M=M, start=start),
            grid=(steps,),
            out_shape=(far((C, B + 2 * M, 4 * B), BF16), far((C, B, 2 * B), BF16)),
            in_specs=[whole(2, B, B)] + [hbm] * len(held),
            out_specs=(block(B + 2 * M, 4 * B), block(B, 2 * B)),
            input_output_aliases={1 + k: k for k in range(len(held))},
            compiler_params=params(small),
            cost_estimate=cost(4),
        )(cols, *[pin(v) for v in held])

    tables = back_tables([], 0, half_steps)
    mixed_tok, tables = lax.optimization_barrier((mixed_tok, tables))
    gm, keep, send = call(
        partial(glu_kernel, parts=len(own_w)),
        (shape((mp, 2 * C, nt), BF16),) + (shape((H, nt), BF16),) * 2,
        4 + 2 * len(own_w), 1, 2, [vm((2, H, nt), BF16), vm((2, mp, C, H), BF16)],
    )(place, mixed_tok, first, bias, *own_w, *other_w)
    mixed_tok = mixed_tok.reshape(H, nt)
    gm, f_tab, cols = lax.optimization_barrier((gm, f_tab, cols))
    gm = lax.all_to_all(gm, "mp", split_axis=0, concat_axis=0, tiled=True)
    u_rev, lift = by_channel(
        partial(lift_kernel, count=H),
        (far((C, 3 * N, 2 * B), BF16), far_blocks),
        [SMEM, SMEM, whole(C, L), whole(2, N, B), few(2 * B, 2 * B)],
        (few(3 * N, 2 * B), few(N, B)),
        3,
        [vm((N * C, B), F32), vm((3, N, B), F32)],
        56,
    )(lengths, vecs, tokens, stat, pin(f_tab))
    back_tab, near_tab = back_tables(tables, half_steps, half_steps)
    gm, lift, back_tab = lax.optimization_barrier((gm, lift, back_tab))

    ways = len(rounds[0]) + 1
    rows_left = mp // ways
    outs = call(
        partial(weight_kernel, C=C, mp=mp), (shape((rows_left * C + 8, H), F32),) * ways, 5, 1, 2,
        [vm((ways, rows_left * C + 8, H), F32)],
    )(place, keep, partner(send, dp), mixed_tok, partner(mixed_tok, dp))
    terms = [outs[0]] + [exchange(v, "mp", mp, o) for v, o in zip(outs[1:], rounds[0])]

    layer_out, gn, sums, plain, g_pre, p_blk, r_blk, rx_blk = by_channel(
        partial(back_kernel, count=H),
        (shape((C, L), BF16), shape((C, L), F32), shape((2, N, B), F32), shape((C, 24, B), F32)) + (blocks,) * 4,
        [
            SMEM, SMEM, VMEM, VMEM, VMEM, hbm, hbm, hbm, VMEM,
        ],
        (whole(C, L), whole(C, L), whole(2, N, B), chan(24, B)) + (chan(N, B),) * 4,
        7,
        [
            vm((N * C, B), F32), vm((N * C, B), F32), vm((N * C, B), F32), vm((3, N, B), F32),
            vm((G, 2 * N, B), BF16), vm((G * N, B), F32), vm((G * N, B), F32), vm((G * N, B), F32),
            vm((C, 2 * B, 4 * B), BF16), vm((C, B, 2 * B), BF16), vm((C, N, B), F32),
            pltpu.SemaphoreType.DMA((4, C // G)),
        ],
        large,
        G,
    )(lengths, vecs, tokens, stat, gm, pin(slope), pin(back_tab), pin(near_tab), jump)

    seen = ways
    terms[0], plain = lax.optimization_barrier((terms[0], plain))
    while seen < mp:
        ways, offs = 2, (seen,)
        rows_left //= ways
        outs = call(
            partial(fold_kernel, ways=ways, got=len(terms), C=C, seen=seen),
            (shape((rows_left * C + 8, H), F32),) * ways,
            1 + len(terms), 1, 1, [vm((ways, rows_left * C + 8, H), F32)],
        )(place, *terms)
        terms = [outs[0]] + [exchange(v, "mp", mp, o) for v, o in zip(outs[1:], offs)]
        seen *= ways
    for k, offs in enumerate(rounds[::-1]):
        got = [exchange(sums, "mp", mp, o) for o in offs]
        if k == len(rounds) - 1:
            g_pre, sums, terms[0] = lax.optimization_barrier((g_pre, sums, terms[0]))
            rows = by_channel(
                sums_kernel,
                shape((C, 40, B), F32),
                [chan(3 * N, 2 * B)] + [chan(N, B)] * 7 + [chan(B, 2 * B), whole(2, C, B)],
                chan(40, B),
                20,
                [],
                large,
                G,
            )(pin(u_rev), pin(lift), g_pre, p_blk, r_blk, rx_blk, pin(state), pin(state_x), pin(near_tab), jump)
            got, rows, terms = lax.optimization_barrier((got, rows, terms))
        sums = sum(got, sums)
    grad_tokens = call(partial(last_kernel, count=H), shape((C, L), F32), 5)(tokens, grad_out, gn, stat, sums)
    rows = call(join_kernel, shape((9, C, B), F32), 2)(plain, rows)
    others = sum_docs(rows, dp, 1) - rows if dp > 2 else partner(rows, dp)

    wsum = call(total_kernel, shape((C + 8, H), F32), len(terms))(*terms)
    wsum = sum_docs(wsum, dp, 2)
    across = partner(wsum, dp)
    thin, wide = shape((C, M), F32), shape((C, 2 * M), F32)
    line = shape((1, C), F32)
    (
        value_wgrad, gate_wgrad, vb, gb, step_grad, decay_grad, frequency_grad, readout_grad, liquid_grad,
        skip_grad, gain_grad, bias_grad,
    ) = call(
        partial(finish_kernel, M=M),
        (shape((C, H), F32), shape((C, H), F32), line, line, line, thin, thin, wide, wide, line, line, line),
        11, 1,
    )(
        place, rows, others, w_all, log_step[None], decay_log, frequency, readout, liquid_readout, wsum, across,
    )
    return (
        layer_out, grad_tokens, gain_grad[0], bias_grad[0], step_grad[0], decay_grad, frequency_grad, readout_grad,
        liquid_grad, skip_grad[0], value_wgrad.T, gate_wgrad.T, vb[0], gb[0],
    )


def solution(mesh):
    row, col, act = P("mp"), P(None, "mp"), P("mp", "dp")
    wide = P("mp", None)
    in_specs = (act, P("dp"), row, row, row, wide, wide, wide, wide, row, col, col, row, row, act)
    out_specs = (act, act, row, row, row, wide, wide, wide, wide, row, col, col, row, row)
    return jax.shard_map(
        partial(per_device, mesh.shape["mp"], mesh.shape["dp"]),
        mesh=mesh, in_specs=in_specs, out_specs=out_specs, check_vma=False,
    )
```

```python
from functools import partial

import jax
import jax.numpy as jnp
import numpy as np
from jax import lax
from jax.experimental import pallas as pl
from jax.experimental.pallas import tpu as pltpu
from jax.sharding import PartitionSpec as P

B = 128
TABLE_GROUP = 8
MIXER_GROUP = 16
F32 = jnp.float32
BF16 = jnp.bfloat16
NN = (((1,), (0,)), ((), ()))
NT = (((1,), (1,)), ((), ()))
TN = (((0,), (0,)), ((), ()))
EPS = 1e-05
SQUARE_SCALE = 65536.0
VMEM = pl.BlockSpec(memory_space=pltpu.VMEM)
SMEM = pl.BlockSpec(memory_space=pltpu.SMEM)


def params(mb):
    return pltpu.CompilerParams(vmem_limit_bytes=mb * 1024 * 1024)


def cost(us):
    return pl.CostEstimate(flops=int(us * 1e9), bytes_accessed=int(us * 1e6), transcendentals=0)


def dot(a, b, dims=NN):
    return lax.dot_general(a, b, dims, preferred_element_type=F32)


def split(v):
    hi = v.astype(BF16)
    return hi, (v - hi.astype(F32)).astype(BF16)


def sincos(x):
    k = jnp.floor(x * 0.6366197723675814 + 0.5)
    y = ((x - k * 1.5703125) - k * 4.837512969970703e-4) - k * 7.54978995489188e-8
    y2 = y * y
    s = y + y * y2 * (-1.6666654611e-1 + y2 * (8.3321608736e-3 - y2 * 1.9515295891e-4))
    c = 1.0 - 0.5 * y2 + y2 * y2 * (4.166664568298827e-2 + y2 * (-1.388731625493765e-3 + y2 * 2.443315711809948e-5))
    q = k.astype(jnp.int32)
    odd = (q & 1) == 1
    sin = jnp.where(odd, c, s)
    cos = jnp.where(odd, s, c)
    sin = jnp.where((q & 2) == 2, -sin, sin)
    cos = jnp.where(((q + 1) & 2) == 2, -cos, cos)
    return sin, cos


def row_iota(shape):
    return lax.broadcasted_iota(jnp.int32, shape, 0)


def lane_iota(shape):
    return lax.broadcasted_iota(jnp.int32, shape, 1)


def shift_token(x, k):
    n = x.shape[0]
    lanes = lane_iota(x.shape)
    rows = row_iota(x.shape)
    turned = pltpu.roll(x, k % B, 1)
    wrapped = pltpu.roll(turned, k % n, 0)
    if k > 0:
        wrapped = jnp.where(rows >= 1, wrapped, 0.0)
        return jnp.where(lanes == 0, wrapped, turned)
    wrapped = jnp.where(rows < n - 1, wrapped, 0.0)
    return jnp.where(lanes == B - 1, wrapped, turned)


def swap_halves(x):
    return pltpu.roll(x, B // 2, 1)


def scan_blocks(v_ref, out_ref, turned_ref, jump, N, backward):
    a_re, a_im = jump
    G = v_ref.shape[0] // N
    s = jnp.zeros((G, B), F32)
    t = s
    for k in range(N):
        n = N - 1 - k if backward else k
        out_ref[pl.ds(n, G, stride=N), :] = s
        turned_ref[pl.ds(n, G, stride=N), :] = t
        v = v_ref[pl.ds(n, G, stride=N), :]
        s, t = a_re * s + (a_im * t + v), a_re * t + (swap_halves(v) - a_im * s)


def start_kernel(place_ref, x_hbm, g_hbm, v_hbm, w_hbm, *refs):
    more, refs = refs[:2], refs[2:]
    stat_ref, pay_ref, x_ref, g_ref, wt_ref = refs[:5]
    held, sems = refs[5:7], refs[7]
    vb_ref, gb_ref = held
    C, L = x_ref.shape
    N = L // B
    mp, rows, nt = pay_ref.shape
    few = rows - 2 * C
    pairs = ((x_hbm, x_ref), (g_hbm, g_ref)) + tuple(zip(more, held))
    moves = [pltpu.make_async_copy(src, dst, sems.at[1 + k]) for k, (src, dst) in enumerate(pairs)]
    for move in moves:
        move.start()
    for half, ref in enumerate((v_hbm, w_hbm)):

        @pl.when(place_ref[0] == half)
        def _():
            pltpu.make_async_copy(ref, wt_ref, sems.at[0]).start()

    moves[0].wait()
    for n in range(N):
        x = x_ref[:, n * B : (n + 1) * B].astype(F32)
        mean = jnp.sum(x, axis=0, keepdims=True) * (1.0 / C)
        dev = x - mean
        stat_ref[n : n + 1, :] = mean
        stat_ref[N + n : N + n + 1, :] = jnp.sum(dev * dev, axis=0, keepdims=True)
    own = row_iota((mp, B))
    for move in moves[2:]:
        move.wait()
    bias = jnp.concatenate([vb_ref[...].astype(F32), gb_ref[...].astype(F32), jnp.zeros((1, B - 2 * C), F32)], axis=1)
    stat_ref[2 * N :, :] = jnp.where(own == place_ref[1], bias, 0.0)
    for j in range(mp):
        pay_ref[j, few : few + C, :] = x_ref[:, j * nt : (j + 1) * nt]
    moves[1].wait()
    for j in range(mp):
        pay_ref[j, few + C :, :] = g_ref[:, j * nt : (j + 1) * nt]
    pltpu.make_async_copy(v_hbm, wt_ref, sems.at[0]).wait()
    parts = wt_ref.shape[1] // B
    for j in range(mp):
        lanes = slice(j % parts * B, (j % parts + 1) * B)
        for q in range(nt // B):
            pay_ref[j, 0:few, q * B : (q + 1) * B] = wt_ref[q * few : (q + 1) * few, lanes]


def join_stats(parts, N, count):
    mean = sum(p[:N] for p in parts) * (1.0 / len(parts))
    spread = sum(p[N : 2 * N] for p in parts) + count * sum((p[:N] - mean) * (p[:N] - mean) for p in parts)
    return mean, spread, sum(p[2 * N :] for p in parts)


def mode_columns(log_step, decay, freq, coef):
    C = decay.shape[0]
    step_size = jnp.exp(log_step)
    real_rate = -jnp.exp(decay)
    re = step_size * real_rate
    im = step_size * freq
    growth = jnp.exp(re)
    sin, cos = sincos(im)
    num_re = growth * cos - 1.0
    num_im = growth * sin
    den = real_rate * real_rate + freq * freq
    in_re = (num_re * real_rate + num_im * freq) / den
    in_im = (num_im * real_rate - num_re * freq) / den
    first = lane_iota(coef.shape) < B // 2
    w = coef * in_re + swap_halves(coef) * jnp.where(first, -in_im, in_im)
    sin, cos = sincos(im * float(B))
    mag = jnp.exp(re * float(B))
    jump = mag * cos, mag * jnp.where(first, -sin, sin)
    group = lane_iota(re.shape) // (B // 4)
    packed = jnp.where(group == 0, re, jnp.where(group == 1, im, jnp.where(group == 2, cos, sin)))
    pad = jnp.zeros((B - C, B), F32)
    return w, jump, [jnp.concatenate([v, pad], axis=0).T for v in (packed, w)]


def mode_kernel(step_ref, decay_ref, freq_ref, read_ref, liquid_ref, cols_ref, jump_ref, w_all_ref):
    C, M = decay_ref.shape
    decay, freq, read, liquid = decay_ref[...], freq_ref[...], read_ref[...], liquid_ref[...]
    step = jnp.sum(jnp.where(row_iota((C, C)) == lane_iota((C, C)), step_ref[...], 0.0), axis=1, keepdims=True)
    coef = jnp.concatenate([read[:, :M], liquid[:, :M], read[:, M:], liquid[:, M:]], axis=1)
    w_all_ref[...], (jump_ref[0], jump_ref[1]), (cols_ref[0], cols_ref[1]) = mode_columns(
        step, jnp.concatenate([decay] * 4, axis=1), jnp.concatenate([freq] * 4, axis=1), coef
    )


def channel_waves(cols, i, M, G):
    back = (B - i * G) % B
    pp = pltpu.roll(cols[0], back, 1)
    ww = 2.0 * pltpu.roll(cols[1], back, 1)
    place = lane_iota((M, B)).astype(F32)
    ahead = float(B) - place
    out = []
    for j in range(G):
        a, o, c, s = [jnp.broadcast_to(pp[q * M : (q + 1) * M, j : j + 1], (M, B)) for q in range(4)]
        w = [jnp.broadcast_to(ww[q * M : (q + 1) * M, j : j + 1], (M, B)) for q in range(4)]
        sin, cos = sincos(o * place)
        mag = jnp.exp(a * place)
        rest = jnp.exp(a * ahead)
        out.append(((mag * cos, mag * sin), (rest * (c * cos + s * sin), rest * (s * cos - c * sin)), w))
    return out


def toeplitz_rows(kern, start):
    return pltpu.roll(jnp.broadcast_to(kern, (B, B)), start, 1, stride=1, stride_axis=0)


def table_kernel(cols, f_ref, again_ref, t_ref, *, M):
    i = pl.program_id(0)
    G = f_ref.shape[0]
    rows = row_iota((B, B))
    lanes = lane_iota((B, B))
    odd = (lanes & M) == M
    zero = jnp.zeros((B, B), BF16)
    every = range(G)
    waves = channel_waves(cols, i, M, G)
    feeds = [jnp.concatenate([f_re, f_re, f_im, f_im], axis=0).T for _, (f_re, f_im), _ in waves]
    kerns = []
    for j in every:
        (n_re, n_im), _, w = waves[j]
        for h in range(2):
            w_re, w_im = w[h], w[2 + h]
            e_re = w_re * n_re - w_im * n_im
            e_im = -(w_re * n_im + w_im * n_re)
            kerns.append(jnp.sum(e_re, axis=0, keepdims=True))
            for q, v in enumerate(split(e_re)):
                t_ref[j, 2 * B + h * M : 2 * B + (h + 1) * M, q * B : (q + 1) * B] = v
            for q, v in enumerate(split(e_im)):
                t_ref[j, 2 * B + (2 + h) * M : 2 * B + (3 + h) * M, q * B : (q + 1) * B] = v
    rolled = [toeplitz_rows(kern, 0) for kern in kerns]
    for j in every:
        parts = split(feeds[j])
        for h in range(2):
            for q, part in enumerate(parts):
                v = jnp.where(odd if h == 1 else ~odd, part, zero)
                f_ref[j, h * B : (h + 1) * B, q * B : (q + 1) * B] = v
                again_ref[j, h * B : (h + 1) * B, q * B : (q + 1) * B] = v
            toe = jnp.where(lanes >= rows, rolled[2 * j + h], 0.0)
            for q, v in enumerate(split(toe)):
                t_ref[j, h * B : (h + 1) * B, q * B : (q + 1) * B] = v


def back_table_kernel(cols, *refs, M, start):
    t_ref, near_ref = refs[-2:]
    i = pl.program_id(0) + start
    G = t_ref.shape[0]
    rows = row_iota((B, B))
    lanes = lane_iota((B, B))
    every = range(G)
    waves = channel_waves(cols, i, M, G)
    turned = [jnp.concatenate([n_re, n_re, n_im, n_im], axis=0).T for (n_re, n_im), _, _ in waves]
    kerns, starts = [], []
    for j in every:
        (n_re, n_im), (f_re, f_im), w = waves[j]
        for h in range(2):
            w_re, w_im = w[h], w[2 + h]
            b_re = w_re * f_re - w_im * f_im
            b_im = -(w_re * f_im + w_im * f_re)
            kerns.append(jnp.sum(b_re, axis=0, keepdims=True))
            starts.append(jnp.sum(w_re * n_re - w_im * n_im, axis=0, keepdims=True)[:, 0:1])
            for part, v2 in enumerate((b_re, b_im)):
                for q, v in enumerate(split(v2)):
                    at = slice((2 * q + h) * B, (2 * q + h + 1) * B)
                    t_ref[j, B + part * M : B + (part + 1) * M, at] = v
    rolled = [toeplitz_rows(kern, 0) for kern in kerns]
    for j in every:
        for q, v in enumerate(split(turned[j])):
            near_ref[j, :, q * B : (q + 1) * B] = v
        for h in range(2):
            start = jnp.broadcast_to(starts[2 * j + h], (B, B))
            toe = jnp.where(lanes < rows, rolled[2 * j + h], jnp.where(lanes == rows, start, 0.0))
            for q, v in enumerate(split(toe)):
                t_ref[j, 0:B, (2 * q + h) * B : (2 * q + h + 1) * B] = v


def token_stats(stat_ref, length, count):
    mean = stat_ref[0]
    inv = lax.rsqrt(stat_ref[1] * (1.0 / count) + EPS)
    place = row_iota(mean.shape) * B + lane_iota(mean.shape)
    return mean, inv, (place < length).astype(F32)


def mixer_kernel(len_ref, vec_ref, x_ref, *refs, count, parts):
    part_refs, refs = refs[:parts], refs[parts:]
    f_ref, t_ref, jump_ref = refs[:3]
    mixed_ref, slope_ref, state_ref, other_ref, stat_ref, bias_ref = refs[3:9]
    xs, ms, tok, us, ups, sts, ots = refs[9:]
    i = pl.program_id(0)
    G = f_ref.shape[0]
    C, L = x_ref.shape
    N = L // B
    nt = mixed_ref.shape[2]

    @pl.when(i == 0)
    def _():
        for n in range(N):
            xs[n * C : (n + 1) * C, :] = x_ref[:, n * B : (n + 1) * B].astype(F32)
        stat_ref[0], stat_ref[1], bias_ref[...] = join_stats([r[...] for r in part_refs], N, count / parts)
        mean, inv, mask = token_stats(stat_ref, len_ref[0], count)
        tok[0] = mean
        tok[1] = inv
        tok[2] = mask

    for j in range(G):
        ci = i * G + j
        normed = (xs[pl.ds(ci, N, stride=C), :] - tok[0]) * tok[1]
        sig = tok[2] * (normed * vec_ref[0, ci] + vec_ref[1, ci])
        liq = sig * shift_token(sig, 1)
        for q, v in enumerate((sig, liq)):
            hi, lo = split(v)
            us[j, 0:N, q * B : (q + 1) * B] = hi
            us[j, N:, q * B : (q + 1) * B] = lo
        slope_ref[j] = sig
    ups_all = [dot(us[j], f_ref[j]) for j in range(G)]
    for j, up in enumerate(ups_all):
        ups[j * N : (j + 1) * N, :] = up[:N, :B] + (up[:N, B:] + up[N:, :B])
    at = pl.ds(pl.multiple_of(i * G, G), G)
    scan_blocks(ups, sts, ots, (jump_ref[0, at, :], jump_ref[1, at, :]), N, False)
    left = []
    for j in range(G):
        state = sts[j * N : (j + 1) * N, :]
        state_ref[j] = state
        other_ref[j] = ots[j * N : (j + 1) * N, :]
        left.append(jnp.concatenate([us[j], jnp.concatenate(split(state), axis=0)], axis=1))
    outs = [dot(left[j], t_ref[j]) for j in range(G)]
    for j, out in enumerate(outs):
        ci = i * G + j
        mask = tok[2]
        y = out[:N, :B] + (out[:N, B:] + out[N:, :B]) + vec_ref[2, ci] * slope_ref[j]
        y2 = y * y
        th = jnp.tanh(0.7978845608028654 * (y + 0.044715 * (y * y2)))
        half = 0.5 * (1.0 + th)
        ms[pl.ds(pl.multiple_of(ci * N, N), N), :] = mask * (y * half)
        slope_ref[j] = mask * (half + 0.5 * y * (1.0 - th * th) * (0.7978845608028654 * (1.0 + 0.134145 * y2)))

    @pl.when(i == pl.num_programs(0) - 1)
    def _():
        per = nt // B
        for n in range(N):
            mixed_ref[n // per, :, (n % per) * B : (n % per + 1) * B] = ms[pl.ds(n, C, stride=N), :].astype(BF16)


def glu_kernel(place_ref, in_ref, first_ref, bias_ref, *refs, parts):
    own_refs, other_refs, refs = refs[:parts], refs[parts : 2 * parts], refs[2 * parts :]
    gm_ref, keep_ref, send_ref, gp, wt = refs
    mp, C, nt = in_ref.shape
    H = mp * C
    few = own_refs[0].shape[1]
    own = place_ref[0]
    mixed = in_ref[...].reshape(H, nt)
    for k in range(parts):
        lanes = pl.ds(pl.multiple_of((lax.rem(place_ref[1], parts) ^ k) * B, B), B)
        for q in range(nt // B):
            at = slice(q * few, (q + 1) * few)
            wt[own, :, at, lanes] = own_refs[k][:, :, q * B : (q + 1) * B]
            wt[1 - own, :, at, lanes] = other_refs[k][:, :, q * B : (q + 1) * B]
    step = B
    per = step // C
    bias = jnp.concatenate([bias_ref[...], jnp.zeros((B - mp, B), F32)], axis=0).T
    for s in range(mp // per):
        lo = s * step
        col_v = jnp.concatenate([bias[0:C, k : k + 1] for k in range(s * per, (s + 1) * per)], axis=0)
        col_g = jnp.concatenate([bias[C : 2 * C, k : k + 1] for k in range(s * per, (s + 1) * per)], axis=0)
        at = slice(s * per, (s + 1) * per)
        value = dot(wt[0, at].reshape(step, H), mixed) + col_v
        gate = dot(wt[1, at].reshape(step, H), mixed) + col_g
        sig = jax.nn.sigmoid(gate)
        x = first_ref[at, few : few + C, :].reshape(step, nt).astype(F32)
        g = first_ref[at, few + C :, :].reshape(step, nt).astype(F32)
        gm_ref[s * per : (s + 1) * per, C:, :] = (x + value * sig).astype(BF16).reshape(per, C, nt)
        gv = g * sig
        gp[0, lo : lo + step, :] = gv.astype(BF16)
        gp[1, lo : lo + step, :] = (gv * value * (1.0 - sig)).astype(BF16)
    for s in range(mp // per):
        at = slice(s * step, (s + 1) * step)
        gm = sum(dot(wt[h, :, :, at].reshape(H, step), gp[h], TN) for h in range(2))
        wide = gm * SQUARE_SCALE
        gm_ref[s * per : (s + 1) * per, 0:C, :] = (wide * jnp.abs(wide)).astype(BF16).reshape(per, C, nt)
    keep_ref[...] = gp[own]
    send_ref[...] = gp[1 - own]


def weight_kernel(place_ref, keep_ref, got_ref, mixed_ref, theirs_ref, *refs, C, mp):
    outs, wg = refs[:-1], refs[-1]
    nt = mixed_ref.shape[1]
    ways = len(outs)
    per = mp // ways
    total = dot(keep_ref[...], mixed_ref[...], NT) + dot(got_ref[...], theirs_ref[...], NT)
    for m in range(mp):
        at = (m // ways) * C
        wg[m % ways, at : at + C, :] = total[m * C : (m + 1) * C]
    ones = jnp.ones((8, nt), BF16)
    tail = dot(ones, keep_ref[...], NT) + dot(ones, got_ref[...], NT)
    for q in range(ways):
        wg[q, per * C :, :] = tail
    for k in range(ways):
        outs[k][...] = wg[lax.rem(place_ref[1], ways) ^ k]


def fold_kernel(place_ref, *refs, ways, got, C, seen):
    parts, outs, acc = refs[:got], refs[got:-1], refs[-1]
    total = parts[0][...]
    for p in parts[1:]:
        total = total + p[...]
    blocks = (total.shape[0] - 8) // C
    for z in range(blocks):
        at = (z // ways) * C
        acc[z % ways, at : at + C, :] = total[z * C : (z + 1) * C]
    for q in range(ways):
        acc[q, (blocks // ways) * C :, :] = total[blocks * C :]
    for k in range(ways):
        outs[k][...] = acc[lax.rem(lax.div(place_ref[1], seen), ways) ^ k]


def back_kernel(
    len_ref, vec_ref, x_ref, stat_ref, gm_ref, slope_hbm, t_ref, near_hbm, jump_ref,
    layer_ref, gn_ref, sum_ref, row_ref, g_ref, p_ref, r_ref, turned_ref, xs, gs, ns, tok, hs, ps, rs, rts, tab, near_ref, slope_ref, sem, *, count,
):
    i = pl.program_id(0)
    G = g_ref.shape[0]
    C, L = x_ref.shape
    N = L // B
    nt = gm_ref.shape[2]
    per = nt // B
    quarter = B // 4

    def fetch(q, k):
        at = pl.ds(k * G, G)
        src, dst = (
            (slope_hbm.at[at], slope_ref.at[at]),
            (near_hbm.at[at], near_ref.at[at]),
            (t_ref.at[at, 0:B, :], tab.at[at, 0:B, :]),
            (t_ref.at[at, B:, :], tab.at[at, B + quarter : B + 3 * quarter, :]),
        )[q]
        return pltpu.make_async_copy(src, dst, sem.at[q, k])

    @pl.when(i == 0)
    def _():
        for k in range(C // G):
            for q in range(4):
                fetch(q, k).start()
        tab[:, B : B + quarter, :] = jnp.zeros((C, quarter, 4 * B), BF16)
        tab[:, B + 3 * quarter :, :] = jnp.zeros((C, quarter, 4 * B), BF16)
        for n in range(N):
            xs[n * C : (n + 1) * C, :] = x_ref[:, n * B : (n + 1) * B].astype(F32)
            at = slice((n % per) * B, (n % per + 1) * B)
            square = gm_ref[n // per, 0:C, at].astype(F32)
            gs[n * C : (n + 1) * C, :] = square * (lax.rsqrt(jnp.maximum(jnp.abs(square), 1e-37)) * (1.0 / SQUARE_SCALE))
        mean, inv, mask = token_stats(stat_ref, len_ref[0], count)
        tok[0] = mean
        tok[1] = inv
        tok[2] = mask
        sum_ref[...] = jnp.zeros_like(sum_ref)
        for m in range(gm_ref.shape[0]):
            layer_ref[:, m * nt : (m + 1) * nt] = gm_ref[m, C:, :]

    fetch(0, i).wait()
    for j in range(G):
        ci = i * G + j
        g = gs[pl.ds(ci, N, stride=C), :] * slope_ref[ci]
        g_ref[j] = g
        hi, lo = split(g)
        hs[j, 0:N, :] = hi
        hs[j, N:, :] = lo
    fetch(1, i).wait()
    z_all = [dot(hs[j], near_ref[i * G + j]) for j in range(G)]
    for j, z in enumerate(z_all):
        p = z[:N, :B] + (z[:N, B:] + z[N:, :B])
        p_ref[j] = p
        ps[j * N : (j + 1) * N, :] = p
    at = pl.ds(pl.multiple_of(i * G, G), G)
    scan_blocks(ps, rs, rts, (jump_ref[0, at, :], jump_ref[1, at, :]), N, True)
    left = []
    for j in range(G):
        r = rs[j * N : (j + 1) * N, :]
        r_ref[j] = r
        turned_ref[j] = rts[j * N : (j + 1) * N, :]
        left.append(jnp.concatenate([hs[j], jnp.concatenate(split(r), axis=0)], axis=1))
    fetch(2, i).wait()
    fetch(3, i).wait()
    both_all = [dot(left[j], tab[i * G + j]) for j in range(G)]
    for j, both in enumerate(both_all):
        ci = i * G + j
        mask = tok[2]
        normed = (xs[pl.ds(ci, N, stride=C), :] - tok[0]) * tok[1]
        sig = mask * (normed * vec_ref[0, ci] + vec_ref[1, ci])
        both = both[:N, : 2 * B] + (both[:N, 2 * B :] + both[N:, : 2 * B])
        gl = both[:, B:]
        grad = both[:, :B] + vec_ref[2, ci] * g_ref[j] + gl * shift_token(sig, 1) + shift_token(gl * sig, -1)
        masked = mask * grad
        gn = masked * vec_ref[0, ci]
        sum_ref[0] += gn
        sum_ref[1] += gn * normed
        ns[pl.ds(pl.multiple_of(ci * N, N), N), :] = gn
        for q, v in enumerate((g_ref[j] * sig, masked * normed, masked)):
            row_ref[j, q * 8 : (q + 1) * 8, :] = sum(v[8 * k : 8 * k + 8] for k in range(N // 8))

    @pl.when(i == pl.num_programs(0) - 1)
    def _():
        for n in range(N):
            gn_ref[:, n * B : (n + 1) * B] = ns[pl.ds(n, C, stride=N), :]


def lift_kernel(len_ref, vec_ref, x_ref, stat_ref, f_ref, u_ref, lift_ref, xs, tok, *, count):
    i = pl.program_id(0)
    G = f_ref.shape[0]
    C, L = x_ref.shape
    N = L // B

    @pl.when(i == 0)
    def _():
        for n in range(N):
            xs[n * C : (n + 1) * C, :] = x_ref[:, n * B : (n + 1) * B].astype(F32)
        tok[0], tok[1], tok[2] = token_stats(stat_ref, len_ref[0], count)

    ahead = float(B) - lane_iota((N, B)).astype(F32)
    flip = (lane_iota((B, B)) + row_iota((B, B)) == B - 1).astype(BF16)
    flat, left = [], []
    for j in range(G):
        ci = i * G + j
        normed = (xs[pl.ds(ci, N, stride=C), :] - tok[0]) * tok[1]
        sig = tok[2] * (normed * vec_ref[0, ci] + vec_ref[1, ci])
        liq = sig * shift_token(sig, 1)
        flat.append(jnp.concatenate(split(sig) + split(liq), axis=0))
        left.append(jnp.concatenate(split(jnp.concatenate([sig * ahead, liq * ahead], axis=1)), axis=0))
    turned_all = [dot(v, flip).astype(BF16) for v in flat]
    lifts = [dot(left[j], f_ref[j]) for j in range(G)]
    for j in range(G):
        turned, lift = turned_all[j], lifts[j]
        for q in range(2):
            at = slice(q * B, (q + 1) * B)
            u_ref[j, 0 : 2 * N, at] = turned[2 * q * N : (2 * q + 2) * N]
            u_ref[j, 2 * N :, at] = turned[2 * q * N : (2 * q + 1) * N]
        lift_ref[j] = lift[:N, :B] + (lift[:N, B:] + lift[N:, :B])


def sums_kernel(u_ref, lift_ref, g_ref, p_ref, r_ref, rx_ref, state_ref, sx_ref, near_ref, jump_ref, row_ref):
    i = pl.program_id(0)
    G = g_ref.shape[0]
    _, N, _ = g_ref.shape
    place = lane_iota((N, B)).astype(F32)
    rows2, lanes2 = row_iota((B, B)), lane_iota((B, B))
    inside = lanes2 + rows2 >= B - 1
    rows16 = row_iota((16, B))
    lag = lane_iota((16, B)).astype(F32)
    R = N + 16
    every = range(G)
    turned = []
    for j in every:
        g_hi, g_lo = split(g_ref[j])
        turned.append(jnp.concatenate([g_hi, g_hi, g_lo], axis=0).T)
    corr = [dot(turned[j], u_ref[j]) for j in every]
    left = []
    for j in every:
        lags = []
        for q in range(2):
            part = jnp.where(inside, corr[j][:, q * B : (q + 1) * B], 0.0)
            lags.append(jnp.sum(pltpu.roll(part, 1, 1, stride=1, stride_axis=0), axis=0, keepdims=True))
        pair = jnp.where((rows16 & 1) == 0, lags[0], lags[1])
        pair = jnp.where(rows16 < 2, pair, jnp.where(rows16 < 4, pair * lag, 0.0))
        left.append(jnp.concatenate(split(jnp.concatenate([g_ref[j] * place, pair], axis=0)), axis=0))
    both = [dot(left[j], near_ref[j]) for j in every]
    for j in every:
        ci = i * G + j
        z = both[j][:R, :B] + (both[j][:R, B:] + both[j][R:, :B])
        row_ref[j, 0:8, :] = z[N : N + 8]
        p, r, state, lift = p_ref[j], r_ref[j], state_ref[j], lift_ref[j]
        state_x, r_x = sx_ref[j], rx_ref[j]
        carry = z[:N] + float(B) * (r * jump_ref[0, pl.ds(ci, 1), :] + r_x * jump_ref[1, pl.ds(ci, 1), :])
        total = [p * state, p * state_x, carry * state + lift * r, carry * state_x + lift * r_x]
        for q, v in enumerate(total):
            row_ref[j, 8 + 8 * q : 16 + 8 * q, :] = sum(v[8 * k : 8 * k + 8] for k in range(N // 8))


def join_kernel(plain_ref, ref, out_ref):
    odd = (lane_iota((out_ref.shape[1], B)) & (B // 4)) != 0
    for q in range(2):
        out_ref[q] = jnp.where(odd, ref[:, 2 * q + 1, :], ref[:, 2 * q, :])
    for q in range(4):
        out_ref[2 + q] = jnp.sum(ref[:, 8 + 8 * q : 16 + 8 * q, :], axis=1)
    for q in range(3):
        out_ref[6 + q] = jnp.sum(plain_ref[:, 8 * q : 8 * q + 8, :], axis=1)


def finish_kernel(
    place_ref, mine_ref, theirs_ref, w_ref, step_ref, decay_ref, freq_ref, read_ref, liquid_ref, wsum_ref, across_ref,
    value_ref, gate_ref, vbias_ref, gbias_ref, step_out, decay_out, freq_out, read_out, liquid_out,
    skip_out, gain_out, bias_out, *, M,
):
    C = decay_ref.shape[0]
    half = B // 2

    def emit(first, second):
        value_ref[...] = first[0:C, :]
        gate_ref[...] = second[0:C, :]
        per = B // C
        group = place_ref[1] // per
        back = (B - (place_ref[1] % per) * C) % B
        for out, v in ((vbias_ref, first), (gbias_ref, second)):
            lanes = v[C : C + 8, pl.ds(pl.multiple_of(group * B, B), B)]
            out[...] = pltpu.roll(lanes, back, 1)[0:1, 0:C]

    @pl.when(place_ref[0] == 0)
    def _():
        emit(wsum_ref, across_ref)

    @pl.when(place_ref[0] == 1)
    def _():
        emit(across_ref, wsum_ref)

    rows = [mine_ref[q] + theirs_ref[q] for q in range(9)]

    def parts(a, b, c):
        return a[:, :half] - a[:, half:] + c[:, :half], b[:, :half] + b[:, half:] + c[:, half:]

    g_re, g_im = parts(rows[2], rows[3], rows[0])
    d_re, d_im = parts(rows[4], rows[5], rows[1])
    w = w_ref[...]
    w_re, w_im = w[:, :half], w[:, half:]
    l_re = w_re * d_re - w_im * d_im
    l_im = w_re * d_im + w_im * d_re
    cot = (
        2.0 * g_re[:, :M], -2.0 * g_im[:, :M], 2.0 * g_re[:, M:], -2.0 * g_im[:, M:],
        2.0 * (l_re[:, :M] + l_re[:, M:]), -2.0 * (l_im[:, :M] + l_im[:, M:]),
    )
    step = jnp.sum(jnp.where(row_iota((C, C)) == lane_iota((C, C)), step_ref[...], 0.0), axis=1, keepdims=True)
    _, back = jax.vjp(mode_terms, step, decay_ref[...], freq_ref[...], read_ref[...], liquid_ref[...])
    step_grad, decay_out[...], freq_out[...], read_out[...], liquid_out[...] = back(cot)
    lanes = lane_iota((B, B))
    pad = jnp.zeros((B - C, 1), F32)
    plain = jnp.zeros((B, B), F32)
    for q, v in enumerate([step_grad] + [jnp.sum(rows[6 + q], axis=1, keepdims=True) for q in range(3)]):
        plain = jnp.where(lanes == q, jnp.concatenate([v, pad], axis=0), plain)
    plain = plain.T
    for q, out in enumerate((step_out, skip_out, gain_out, bias_out)):
        out[...] = plain[q : q + 1, 0:C]


def last_kernel(x_ref, g_ref, gn_ref, stat_ref, sum_ref, out_ref, *, count):
    C, L = x_ref.shape
    for n in range(L // B):
        at = slice(n * B, (n + 1) * B)
        mean = stat_ref[0, n : n + 1, :]
        inv = lax.rsqrt(stat_ref[1, n : n + 1, :] * (1.0 / count) + EPS)
        first = sum_ref[0, n : n + 1, :] * (1.0 / count)
        second = sum_ref[1, n : n + 1, :] * (1.0 / count)
        normed = (x_ref[:, at].astype(F32) - mean) * inv
        out_ref[:, at] = inv * (gn_ref[:, at] - first - normed * second) + g_ref[:, at].astype(F32)


def total_kernel(*refs):
    total = refs[0][...]
    for p in refs[1:-1]:
        total = total + p[...]
    refs[-1][...] = total


def rounds_of(size):
    rounds, bit = [], 1
    while bit < size:
        if bit * 2 < size:
            rounds.append((bit, 2 * bit, 3 * bit))
            bit *= 4
        else:
            rounds.append((bit,))
            bit *= 2
    return rounds


def exchange(v, axis, size, off):
    return lax.ppermute(v, axis, [(k, k ^ off) for k in range(size)])


def all_sums(v, size):
    for offs in rounds_of(size):
        v = sum([exchange(v, "mp", size, o) for o in offs], v)
    return v


def sum_docs(v, size, stride):
    total = v
    for k in range(stride, size, stride):
        total = total + lax.ppermute(v, "dp", [(q, (q + k) % size) for q in range(size)])
    return total


def partner(v, size):
    return lax.ppermute(v, "dp", [(q, q ^ 1) for q in range(size)])


def mode_terms(log_step, decay_log, frequency, readout, liquid_readout):
    M = decay_log.shape[1]
    step_size = jnp.exp(log_step)
    real_rate = -jnp.exp(decay_log)
    real_step = step_size * real_rate
    imag_step = step_size * frequency
    growth = jnp.exp(real_step)
    num_real = growth * jnp.cos(imag_step) - 1.0
    num_imag = growth * jnp.sin(imag_step)
    denominator = real_rate * real_rate + frequency * frequency
    in_real = (num_real * real_rate + num_imag * frequency) / denominator
    in_imag = (num_imag * real_rate - num_real * frequency) / denominator

    def mix(coeffs):
        re, im = coeffs[:, :M], coeffs[:, M:]
        return re * in_real - im * in_imag, re * in_imag + im * in_real

    return mix(readout) + mix(liquid_readout) + (real_step, imag_step)


def per_device(
    mp, dp,
    tokens, lengths, norm_gain, norm_bias, log_step, decay_log, frequency, readout, liquid_readout,
    skip_gain, value_weight, gate_weight, value_bias, gate_bias, grad_out,
):
    C, L = tokens.shape
    H = value_weight.shape[0]
    M = decay_log.shape[1]
    N = L // B
    nt = L // mp
    few_rows = C * B // nt
    shape = jax.ShapeDtypeStruct

    place = jnp.stack([lax.axis_index("dp") & 1, lax.axis_index("mp")]).astype(jnp.int32)
    rounds = rounds_of(mp)
    small, large = 16, 32

    def pin(v):
        return pltpu.with_memory_space_constraint(v, pltpu.HBM)

    def call(kernel, out, n_in, smem=0, us=1, scratch=(), mb=small):
        return pl.pallas_call(
            kernel,
            out_shape=out,
            in_specs=[SMEM] * smem + [VMEM] * (n_in - smem),
            out_specs=jax.tree.map(lambda _: VMEM, out),
            scratch_shapes=list(scratch),
            compiler_params=params(mb),
            cost_estimate=cost(us),
        )

    def whole(*dims):
        return pl.BlockSpec(dims, lambda i: (0,) * len(dims))

    def chan_by(group):
        return lambda *dims: pl.BlockSpec((group,) + dims, lambda i: (i,) + (0,) * len(dims))

    def by_channel(kernel, out, in_specs, out_specs, us, scratch, mb=small, group=TABLE_GROUP):
        return pl.pallas_call(
            kernel,
            grid=(C // group,),
            out_shape=out,
            in_specs=in_specs,
            out_specs=out_specs,
            scratch_shapes=scratch,
            compiler_params=params(mb),
            cost_estimate=cost(us),
        )

    vm = pltpu.VMEM
    G = min(MIXER_GROUP, C)
    chan, few = chan_by(G), chan_by(TABLE_GROUP)
    blocks = shape((C, N, B), F32)
    far = pltpu.HBM
    far_blocks = far((C, N, B), F32)
    def pin(v):
        return pltpu.with_memory_space_constraint(v, far)

    hbm = pl.BlockSpec(memory_space=pltpu.HBM)
    stat, pay = pl.pallas_call(
        start_kernel,
        out_shape=(shape((2 * N + mp, B), F32), shape((mp, few_rows + 2 * C, nt), BF16)),
        in_specs=[SMEM] + [hbm] * 6,
        out_specs=(VMEM, VMEM),
        scratch_shapes=[
            pltpu.VMEM((C, L), BF16), pltpu.VMEM((C, L), BF16), pltpu.VMEM((C, H), BF16),
            pltpu.VMEM((1, C), BF16), pltpu.VMEM((1, C), BF16), pltpu.SemaphoreType.DMA((5,)),
        ],
        compiler_params=params(small),
        cost_estimate=cost(3),
    )(
        place, pin(tokens), pin(grad_out), pin(value_weight.T), pin(gate_weight.T), pin(value_bias[None]), pin(gate_bias[None])
    )
    first = lax.all_to_all(pay, "mp", split_axis=0, concat_axis=0, tiled=True)

    count = C
    for k, offs in enumerate(rounds[::-1]):
        parts = [stat] + [exchange(stat, "mp", mp, o) for o in offs]
        if k < len(rounds) - 1:
            stat = jnp.concatenate(join_stats(parts, N, float(count)), axis=0)
            count *= len(parts)
            stat, rates = lax.optimization_barrier((stat, decay_log))
    cols, jump, w_all = call(
        mode_kernel, (shape((2, B, B), F32), shape((2, C, B), F32), shape((C, B), F32)), 5
    )(log_step[None], rates, frequency, readout, liquid_readout)
    f_near, f_tab, t_tab = by_channel(
        partial(table_kernel, M=M),
        (shape((C, 2 * B, 2 * B), BF16), far((C, 2 * B, 2 * B), BF16), shape((C, 3 * B, 2 * B), BF16)),
        [whole(2, B, B)],
        (few(2 * B, 2 * B), few(2 * B, 2 * B), few(3 * B, 2 * B)),
        6,
        [],
    )(cols)
    parts, t_tab = lax.optimization_barrier((parts, t_tab))

    vecs = jnp.stack([norm_gain, norm_bias, skip_gain])
    mixed, slope, state, state_x, stat, bias = by_channel(
        partial(mixer_kernel, count=H, parts=len(parts)),
        (shape((mp, C, nt), BF16), far_blocks, far_blocks, far_blocks, far((2, N, B), F32), shape((mp, B), F32)),
        [SMEM, SMEM, whole(C, L)] + [whole(2 * N + mp, B)] * len(parts)
        + [chan(2 * B, 2 * B), chan(3 * B, 2 * B), whole(2, C, B)],
        (whole(mp, C, nt), chan(N, B), chan(N, B), chan(N, B), whole(2, N, B), whole(mp, B)),
        6,
        [
            vm((N * C, B), F32), vm((N * C, B), F32), vm((3, N, B), F32), vm((G, 2 * N, 2 * B), BF16),
            vm((G * N, B), F32), vm((G * N, B), F32), vm((G * N, B), F32),
        ],
        large,
        G,
    )(lengths, vecs, tokens, *parts, f_near, t_tab, jump)

    mixed, first, cols = lax.optimization_barrier((mixed, first, cols))
    own_w = [first[:, :few_rows, :]]
    own_w += [exchange(own_w[0], "mp", mp, o) for o in rounds[0]]
    other_w = [partner(v, dp) for v in own_w]
    mixed_tok = lax.all_to_all(mixed, "mp", split_axis=0, concat_axis=0, tiled=True)
    half_steps = C // TABLE_GROUP // 2

    def back_tables(held, start, steps):
        def block(*dims):
            return pl.BlockSpec((TABLE_GROUP,) + dims, lambda i: (i + start,) + (0,) * len(dims))

        return pl.pallas_call(
            partial(back_table_kernel, M=M, start=start),
            grid=(steps,),
            out_shape=(far((C, B + 2 * M, 4 * B), BF16), far((C, B, 2 * B), BF16)),
            in_specs=[whole(2, B, B)] + [hbm] * len(held),
            out_specs=(block(B + 2 * M, 4 * B), block(B, 2 * B)),
            input_output_aliases={1 + k: k for k in range(len(held))},
            compiler_params=params(small),
            cost_estimate=cost(4),
        )(cols, *[pin(v) for v in held])

    tables = back_tables([], 0, half_steps)
    mixed_tok, tables = lax.optimization_barrier((mixed_tok, tables))
    gm, keep, send = call(
        partial(glu_kernel, parts=len(own_w)),
        (shape((mp, 2 * C, nt), BF16),) + (shape((H, nt), BF16),) * 2,
        4 + 2 * len(own_w), 1, 2, [vm((2, H, nt), BF16), vm((2, mp, C, H), BF16)],
    )(place, mixed_tok, first, bias, *own_w, *other_w)
    mixed_tok = mixed_tok.reshape(H, nt)
    gm, f_tab, cols = lax.optimization_barrier((gm, f_tab, cols))
    gm = lax.all_to_all(gm, "mp", split_axis=0, concat_axis=0, tiled=True)
    u_rev, lift = by_channel(
        partial(lift_kernel, count=H),
        (far((C, 3 * N, 2 * B), BF16), far_blocks),
        [SMEM, SMEM, whole(C, L), whole(2, N, B), few(2 * B, 2 * B)],
        (few(3 * N, 2 * B), few(N, B)),
        3,
        [vm((N * C, B), F32), vm((3, N, B), F32)],
        56,
    )(lengths, vecs, tokens, stat, pin(f_tab))
    back_tab, near_tab = back_tables(tables, half_steps, half_steps)
    gm, lift, back_tab = lax.optimization_barrier((gm, lift, back_tab))

    ways = len(rounds[0]) + 1
    rows_left = mp // ways
    outs = call(
        partial(weight_kernel, C=C, mp=mp), (shape((rows_left * C + 8, H), F32),) * ways, 5, 1, 2,
        [vm((ways, rows_left * C + 8, H), F32)],
    )(place, keep, partner(send, dp), mixed_tok, partner(mixed_tok, dp))
    terms = [outs[0]] + [exchange(v, "mp", mp, o) for v, o in zip(outs[1:], rounds[0])]

    layer_out, gn, sums, plain, g_pre, p_blk, r_blk, rx_blk = by_channel(
        partial(back_kernel, count=H),
        (shape((C, L), BF16), shape((C, L), F32), shape((2, N, B), F32), shape((C, 24, B), F32)) + (blocks,) * 4,
        [
            SMEM, SMEM, VMEM, VMEM, VMEM, hbm, hbm, hbm, VMEM,
        ],
        (whole(C, L), whole(C, L), whole(2, N, B), chan(24, B)) + (chan(N, B),) * 4,
        7,
        [
            vm((N * C, B), F32), vm((N * C, B), F32), vm((N * C, B), F32), vm((3, N, B), F32),
            vm((G, 2 * N, B), BF16), vm((G * N, B), F32), vm((G * N, B), F32), vm((G * N, B), F32),
            vm((C, 2 * B, 4 * B), BF16), vm((C, B, 2 * B), BF16), vm((C, N, B), F32),
            pltpu.SemaphoreType.DMA((4, C // G)),
        ],
        large,
        G,
    )(lengths, vecs, tokens, stat, gm, pin(slope), pin(back_tab), pin(near_tab), jump)

    seen = ways
    terms[0], plain = lax.optimization_barrier((terms[0], plain))
    while seen < mp:
        ways, offs = 2, (seen,)
        rows_left //= ways
        outs = call(
            partial(fold_kernel, ways=ways, got=len(terms), C=C, seen=seen),
            (shape((rows_left * C + 8, H), F32),) * ways,
            1 + len(terms), 1, 1, [vm((ways, rows_left * C + 8, H), F32)],
        )(place, *terms)
        terms = [outs[0]] + [exchange(v, "mp", mp, o) for v, o in zip(outs[1:], offs)]
        seen *= ways
    for k, offs in enumerate(rounds[::-1]):
        got = [exchange(sums, "mp", mp, o) for o in offs]
        if k == len(rounds) - 1:
            g_pre, sums, terms[0] = lax.optimization_barrier((g_pre, sums, terms[0]))
            rows = by_channel(
                sums_kernel,
                shape((C, 40, B), F32),
                [chan(3 * N, 2 * B)] + [chan(N, B)] * 7 + [chan(B, 2 * B), whole(2, C, B)],
                chan(40, B),
                20,
                [],
                large,
                G,
            )(u_rev, lift, g_pre, p_blk, r_blk, rx_blk, state, state_x, near_tab, jump)
            got, rows, terms = lax.optimization_barrier((got, rows, terms))
        sums = sum(got, sums)
    grad_tokens = call(partial(last_kernel, count=H), shape((C, L), F32), 5)(tokens, grad_out, gn, stat, sums)
    rows = call(join_kernel, shape((9, C, B), F32), 2)(plain, rows)
    others = sum_docs(rows, dp, 1) - rows if dp > 2 else partner(rows, dp)

    wsum = call(total_kernel, shape((C + 8, H), F32), len(terms))(*terms)
    wsum = sum_docs(wsum, dp, 2)
    across = partner(wsum, dp)
    thin, wide = shape((C, M), F32), shape((C, 2 * M), F32)
    line = shape((1, C), F32)
    (
        value_wgrad, gate_wgrad, vb, gb, step_grad, decay_grad, frequency_grad, readout_grad, liquid_grad,
        skip_grad, gain_grad, bias_grad,
    ) = call(
        partial(finish_kernel, M=M),
        (shape((C, H), F32), shape((C, H), F32), line, line, line, thin, thin, wide, wide, line, line, line),
        11, 1,
    )(
        place, rows, others, w_all, log_step[None], decay_log, frequency, readout, liquid_readout, wsum, across,
    )
    return (
        layer_out, grad_tokens, gain_grad[0], bias_grad[0], step_grad[0], decay_grad, frequency_grad, readout_grad,
        liquid_grad, skip_grad[0], value_wgrad.T, gate_wgrad.T, vb[0], gb[0],
    )


def solution(mesh):
    row, col, act = P("mp"), P(None, "mp"), P("mp", "dp")
    wide = P("mp", None)
    in_specs = (act, P("dp"), row, row, row, wide, wide, wide, wide, row, col, col, row, row, act)
    out_specs = (act, act, row, row, row, wide, wide, wide, wide, row, col, col, row, row)
    return jax.shard_map(
        partial(per_device, mesh.shape["mp"], mesh.shape["dp"]),
        mesh=mesh, in_specs=in_specs, out_specs=out_specs, check_vma=False,
    )
```

```python
from functools import partial

import jax
import jax.numpy as jnp
import numpy as np
from jax import lax
from jax.experimental import pallas as pl
from jax.experimental.pallas import tpu as pltpu
from jax.sharding import PartitionSpec as P

B = 128
TABLE_GROUP = 8
MIXER_GROUP = 16
F32 = jnp.float32
BF16 = jnp.bfloat16
NN = (((1,), (0,)), ((), ()))
NT = (((1,), (1,)), ((), ()))
TN = (((0,), (0,)), ((), ()))
EPS = 1e-05
SQUARE_SCALE = 65536.0
VMEM = pl.BlockSpec(memory_space=pltpu.VMEM)
SMEM = pl.BlockSpec(memory_space=pltpu.SMEM)


def params(mb):
    return pltpu.CompilerParams(vmem_limit_bytes=mb * 1024 * 1024)


def cost(us):
    return pl.CostEstimate(flops=int(us * 1e9), bytes_accessed=int(us * 1e6), transcendentals=0)


def dot(a, b, dims=NN):
    return lax.dot_general(a, b, dims, preferred_element_type=F32)


def split(v):
    hi = v.astype(BF16)
    return hi, (v - hi.astype(F32)).astype(BF16)


def sincos(x):
    k = jnp.floor(x * 0.6366197723675814 + 0.5)
    y = ((x - k * 1.5703125) - k * 4.837512969970703e-4) - k * 7.54978995489188e-8
    y2 = y * y
    s = y + y * y2 * (-1.6666654611e-1 + y2 * (8.3321608736e-3 - y2 * 1.9515295891e-4))
    c = 1.0 - 0.5 * y2 + y2 * y2 * (4.166664568298827e-2 + y2 * (-1.388731625493765e-3 + y2 * 2.443315711809948e-5))
    q = k.astype(jnp.int32)
    odd = (q & 1) == 1
    sin = jnp.where(odd, c, s)
    cos = jnp.where(odd, s, c)
    sin = jnp.where((q & 2) == 2, -sin, sin)
    cos = jnp.where(((q + 1) & 2) == 2, -cos, cos)
    return sin, cos


def row_iota(shape):
    return lax.broadcasted_iota(jnp.int32, shape, 0)


def lane_iota(shape):
    return lax.broadcasted_iota(jnp.int32, shape, 1)


def shift_token(x, k):
    n = x.shape[0]
    lanes = lane_iota(x.shape)
    rows = row_iota(x.shape)
    turned = pltpu.roll(x, k % B, 1)
    wrapped = pltpu.roll(turned, k % n, 0)
    if k > 0:
        wrapped = jnp.where(rows >= 1, wrapped, 0.0)
        return jnp.where(lanes == 0, wrapped, turned)
    wrapped = jnp.where(rows < n - 1, wrapped, 0.0)
    return jnp.where(lanes == B - 1, wrapped, turned)


def swap_halves(x):
    return pltpu.roll(x, B // 2, 1)


def scan_blocks(v_ref, out_ref, turned_ref, jump, N, backward):
    a_re, a_im = jump
    G = v_ref.shape[0] // N
    s = jnp.zeros((G, B), F32)
    t = s
    for k in range(N):
        n = N - 1 - k if backward else k
        out_ref[pl.ds(n, G, stride=N), :] = s
        turned_ref[pl.ds(n, G, stride=N), :] = t
        v = v_ref[pl.ds(n, G, stride=N), :]
        s, t = a_re * s + (a_im * t + v), a_re * t + (swap_halves(v) - a_im * s)


def start_kernel(place_ref, x_hbm, g_hbm, v_hbm, w_hbm, *refs):
    more, refs = refs[:2], refs[2:]
    stat_ref, pay_ref, x_ref, g_ref, wt_ref = refs[:5]
    held, sems = refs[5:7], refs[7]
    vb_ref, gb_ref = held
    C, L = x_ref.shape
    N = L // B
    mp, rows, nt = pay_ref.shape
    few = rows - 2 * C
    pairs = ((x_hbm, x_ref), (g_hbm, g_ref)) + tuple(zip(more, held))
    moves = [pltpu.make_async_copy(src, dst, sems.at[1 + k]) for k, (src, dst) in enumerate(pairs)]
    for move in moves:
        move.start()
    for half, ref in enumerate((v_hbm, w_hbm)):

        @pl.when(place_ref[0] == half)
        def _():
            pltpu.make_async_copy(ref, wt_ref, sems.at[0]).start()

    moves[0].wait()
    for n in range(N):
        x = x_ref[:, n * B : (n + 1) * B].astype(F32)
        mean = jnp.sum(x, axis=0, keepdims=True) * (1.0 / C)
        dev = x - mean
        stat_ref[n : n + 1, :] = mean
        stat_ref[N + n : N + n + 1, :] = jnp.sum(dev * dev, axis=0, keepdims=True)
    own = row_iota((mp, B))
    for move in moves[2:]:
        move.wait()
    bias = jnp.concatenate([vb_ref[...].astype(F32), gb_ref[...].astype(F32), jnp.zeros((1, B - 2 * C), F32)], axis=1)
    stat_ref[2 * N :, :] = jnp.where(own == place_ref[1], bias, 0.0)
    for j in range(mp):
        pay_ref[j, few : few + C, :] = x_ref[:, j * nt : (j + 1) * nt]
    moves[1].wait()
    for j in range(mp):
        pay_ref[j, few + C :, :] = g_ref[:, j * nt : (j + 1) * nt]
    pltpu.make_async_copy(v_hbm, wt_ref, sems.at[0]).wait()
    parts = wt_ref.shape[1] // B
    for j in range(mp):
        lanes = slice(j % parts * B, (j % parts + 1) * B)
        for q in range(nt // B):
            pay_ref[j, 0:few, q * B : (q + 1) * B] = wt_ref[q * few : (q + 1) * few, lanes]


def join_stats(parts, N, count):
    mean = sum(p[:N] for p in parts) * (1.0 / len(parts))
    spread = sum(p[N : 2 * N] for p in parts) + count * sum((p[:N] - mean) * (p[:N] - mean) for p in parts)
    return mean, spread, sum(p[2 * N :] for p in parts)


def mode_columns(log_step, decay, freq, coef):
    C = decay.shape[0]
    step_size = jnp.exp(log_step)
    real_rate = -jnp.exp(decay)
    re = step_size * real_rate
    im = step_size * freq
    growth = jnp.exp(re)
    sin, cos = sincos(im)
    num_re = growth * cos - 1.0
    num_im = growth * sin
    den = real_rate * real_rate + freq * freq
    in_re = (num_re * real_rate + num_im * freq) / den
    in_im = (num_im * real_rate - num_re * freq) / den
    first = lane_iota(coef.shape) < B // 2
    w = coef * in_re + swap_halves(coef) * jnp.where(first, -in_im, in_im)
    sin, cos = sincos(im * float(B))
    mag = jnp.exp(re * float(B))
    jump = mag * cos, mag * jnp.where(first, -sin, sin)
    group = lane_iota(re.shape) // (B // 4)
    packed = jnp.where(group == 0, re, jnp.where(group == 1, im, jnp.where(group == 2, cos, sin)))
    pad = jnp.zeros((B - C, B), F32)
    return w, jump, [jnp.concatenate([v, pad], axis=0).T for v in (packed, w)]


def mode_kernel(step_ref, decay_ref, freq_ref, read_ref, liquid_ref, cols_ref, jump_ref, w_all_ref):
    C, M = decay_ref.shape
    decay, freq, read, liquid = decay_ref[...], freq_ref[...], read_ref[...], liquid_ref[...]
    step = jnp.sum(jnp.where(row_iota((C, C)) == lane_iota((C, C)), step_ref[...], 0.0), axis=1, keepdims=True)
    coef = jnp.concatenate([read[:, :M], liquid[:, :M], read[:, M:], liquid[:, M:]], axis=1)
    w_all_ref[...], (jump_ref[0], jump_ref[1]), (cols_ref[0], cols_ref[1]) = mode_columns(
        step, jnp.concatenate([decay] * 4, axis=1), jnp.concatenate([freq] * 4, axis=1), coef
    )


def channel_waves(cols, i, M, G):
    back = (B - i * G) % B
    pp = pltpu.roll(cols[0], back, 1)
    ww = 2.0 * pltpu.roll(cols[1], back, 1)
    place = lane_iota((M, B)).astype(F32)
    ahead = float(B) - place
    out = []
    for j in range(G):
        a, o, c, s = [jnp.broadcast_to(pp[q * M : (q + 1) * M, j : j + 1], (M, B)) for q in range(4)]
        w = [jnp.broadcast_to(ww[q * M : (q + 1) * M, j : j + 1], (M, B)) for q in range(4)]
        sin, cos = sincos(o * place)
        mag = jnp.exp(a * place)
        rest = jnp.exp(a * ahead)
        out.append(((mag * cos, mag * sin), (rest * (c * cos + s * sin), rest * (s * cos - c * sin)), w))
    return out


def toeplitz_rows(kern, start):
    return pltpu.roll(jnp.broadcast_to(kern, (B, B)), start, 1, stride=1, stride_axis=0)


def table_kernel(cols, f_ref, again_ref, t_ref, *, M):
    i = pl.program_id(0)
    G = f_ref.shape[0]
    rows = row_iota((B, B))
    lanes = lane_iota((B, B))
    odd = (lanes & M) == M
    zero = jnp.zeros((B, B), BF16)
    every = range(G)
    waves = channel_waves(cols, i, M, G)
    feeds = [jnp.concatenate([f_re, f_re, f_im, f_im], axis=0).T for _, (f_re, f_im), _ in waves]
    kerns = []
    for j in every:
        (n_re, n_im), _, w = waves[j]
        for h in range(2):
            w_re, w_im = w[h], w[2 + h]
            e_re = w_re * n_re - w_im * n_im
            e_im = -(w_re * n_im + w_im * n_re)
            kerns.append(jnp.sum(e_re, axis=0, keepdims=True))
            for q, v in enumerate(split(e_re)):
                t_ref[j, 2 * B + h * M : 2 * B + (h + 1) * M, q * B : (q + 1) * B] = v
            for q, v in enumerate(split(e_im)):
                t_ref[j, 2 * B + (2 + h) * M : 2 * B + (3 + h) * M, q * B : (q + 1) * B] = v
    rolled = [toeplitz_rows(kern, 0) for kern in kerns]
    for j in every:
        parts = split(feeds[j])
        for h in range(2):
            for q, part in enumerate(parts):
                v = jnp.where(odd if h == 1 else ~odd, part, zero)
                f_ref[j, h * B : (h + 1) * B, q * B : (q + 1) * B] = v
                again_ref[j, h * B : (h + 1) * B, q * B : (q + 1) * B] = v
            toe = jnp.where(lanes >= rows, rolled[2 * j + h], 0.0)
            for q, v in enumerate(split(toe)):
                t_ref[j, h * B : (h + 1) * B, q * B : (q + 1) * B] = v


def back_table_kernel(cols, *refs, M, start):
    t_ref, near_ref = refs[-2:]
    i = pl.program_id(0) + start
    G = t_ref.shape[0]
    rows = row_iota((B, B))
    lanes = lane_iota((B, B))
    every = range(G)
    waves = channel_waves(cols, i, M, G)
    turned = [jnp.concatenate([n_re, n_re, n_im, n_im], axis=0).T for (n_re, n_im), _, _ in waves]
    kerns, starts = [], []
    for j in every:
        (n_re, n_im), (f_re, f_im), w = waves[j]
        for h in range(2):
            w_re, w_im = w[h], w[2 + h]
            b_re = w_re * f_re - w_im * f_im
            b_im = -(w_re * f_im + w_im * f_re)
            kerns.append(jnp.sum(b_re, axis=0, keepdims=True))
            starts.append(jnp.sum(w_re * n_re - w_im * n_im, axis=0, keepdims=True)[:, 0:1])
            for part, v2 in enumerate((b_re, b_im)):
                for q, v in enumerate(split(v2)):
                    at = slice((2 * q + h) * B, (2 * q + h + 1) * B)
                    t_ref[j, B + part * M : B + (part + 1) * M, at] = v
    rolled = [toeplitz_rows(kern, 0) for kern in kerns]
    for j in every:
        for q, v in enumerate(split(turned[j])):
            near_ref[j, :, q * B : (q + 1) * B] = v
        for h in range(2):
            start = jnp.broadcast_to(starts[2 * j + h], (B, B))
            toe = jnp.where(lanes < rows, rolled[2 * j + h], jnp.where(lanes == rows, start, 0.0))
            for q, v in enumerate(split(toe)):
                t_ref[j, 0:B, (2 * q + h) * B : (2 * q + h + 1) * B] = v


def token_stats(stat_ref, length, count):
    mean = stat_ref[0]
    inv = lax.rsqrt(stat_ref[1] * (1.0 / count) + EPS)
    place = row_iota(mean.shape) * B + lane_iota(mean.shape)
    return mean, inv, (place < length).astype(F32)


def mixer_kernel(len_ref, vec_ref, x_ref, *refs, count, parts):
    part_refs, refs = refs[:parts], refs[parts:]
    f_ref, t_ref, jump_ref = refs[:3]
    mixed_ref, slope_ref, state_ref, other_ref, stat_ref, bias_ref = refs[3:9]
    xs, ms, tok, us, ups, sts, ots = refs[9:]
    i = pl.program_id(0)
    G = f_ref.shape[0]
    C, L = x_ref.shape
    N = L // B
    nt = mixed_ref.shape[2]

    @pl.when(i == 0)
    def _():
        for n in range(N):
            xs[n * C : (n + 1) * C, :] = x_ref[:, n * B : (n + 1) * B].astype(F32)
        stat_ref[0], stat_ref[1], bias_ref[...] = join_stats([r[...] for r in part_refs], N, count / parts)
        mean, inv, mask = token_stats(stat_ref, len_ref[0], count)
        tok[0] = mean
        tok[1] = inv
        tok[2] = mask

    for j in range(G):
        ci = i * G + j
        normed = (xs[pl.ds(ci, N, stride=C), :] - tok[0]) * tok[1]
        sig = tok[2] * (normed * vec_ref[0, ci] + vec_ref[1, ci])
        liq = sig * shift_token(sig, 1)
        for q, v in enumerate((sig, liq)):
            hi, lo = split(v)
            us[j, 0:N, q * B : (q + 1) * B] = hi
            us[j, N:, q * B : (q + 1) * B] = lo
        slope_ref[j] = sig
    ups_all = [dot(us[j], f_ref[j]) for j in range(G)]
    for j, up in enumerate(ups_all):
        ups[j * N : (j + 1) * N, :] = up[:N, :B] + (up[:N, B:] + up[N:, :B])
    at = pl.ds(pl.multiple_of(i * G, G), G)
    scan_blocks(ups, sts, ots, (jump_ref[0, at, :], jump_ref[1, at, :]), N, False)
    left = []
    for j in range(G):
        state = sts[j * N : (j + 1) * N, :]
        state_ref[j] = state
        other_ref[j] = ots[j * N : (j + 1) * N, :]
        left.append(jnp.concatenate([us[j], jnp.concatenate(split(state), axis=0)], axis=1))
    outs = [dot(left[j], t_ref[j]) for j in range(G)]
    for j, out in enumerate(outs):
        ci = i * G + j
        mask = tok[2]
        y = out[:N, :B] + (out[:N, B:] + out[N:, :B]) + vec_ref[2, ci] * slope_ref[j]
        y2 = y * y
        th = jnp.tanh(0.7978845608028654 * (y + 0.044715 * (y * y2)))
        half = 0.5 * (1.0 + th)
        ms[pl.ds(pl.multiple_of(ci * N, N), N), :] = mask * (y * half)
        slope_ref[j] = mask * (half + 0.5 * y * (1.0 - th * th) * (0.7978845608028654 * (1.0 + 0.134145 * y2)))

    @pl.when(i == pl.num_programs(0) - 1)
    def _():
        per = nt // B
        for n in range(N):
            mixed_ref[n // per, :, (n % per) * B : (n % per + 1) * B] = ms[pl.ds(n, C, stride=N), :].astype(BF16)


def glu_kernel(place_ref, in_ref, first_ref, bias_ref, *refs, parts):
    own_refs, other_refs, refs = refs[:parts], refs[parts : 2 * parts], refs[2 * parts :]
    gm_ref, keep_ref, send_ref, gp, wt = refs
    mp, C, nt = in_ref.shape
    H = mp * C
    few = own_refs[0].shape[1]
    own = place_ref[0]
    mixed = in_ref[...].reshape(H, nt)
    for k in range(parts):
        lanes = pl.ds(pl.multiple_of((lax.rem(place_ref[1], parts) ^ k) * B, B), B)
        for q in range(nt // B):
            at = slice(q * few, (q + 1) * few)
            wt[own, :, at, lanes] = own_refs[k][:, :, q * B : (q + 1) * B]
            wt[1 - own, :, at, lanes] = other_refs[k][:, :, q * B : (q + 1) * B]
    step = B
    per = step // C
    bias = jnp.concatenate([bias_ref[...], jnp.zeros((B - mp, B), F32)], axis=0).T
    for s in range(mp // per):
        lo = s * step
        col_v = jnp.concatenate([bias[0:C, k : k + 1] for k in range(s * per, (s + 1) * per)], axis=0)
        col_g = jnp.concatenate([bias[C : 2 * C, k : k + 1] for k in range(s * per, (s + 1) * per)], axis=0)
        at = slice(s * per, (s + 1) * per)
        value = dot(wt[0, at].reshape(step, H), mixed) + col_v
        gate = dot(wt[1, at].reshape(step, H), mixed) + col_g
        sig = jax.nn.sigmoid(gate)
        x = first_ref[at, few : few + C, :].reshape(step, nt).astype(F32)
        g = first_ref[at, few + C :, :].reshape(step, nt).astype(F32)
        gm_ref[s * per : (s + 1) * per, C:, :] = (x + value * sig).astype(BF16).reshape(per, C, nt)
        gv = g * sig
        gp[0, lo : lo + step, :] = gv.astype(BF16)
        gp[1, lo : lo + step, :] = (gv * value * (1.0 - sig)).astype(BF16)
    for s in range(mp // per):
        at = slice(s * step, (s + 1) * step)
        gm = sum(dot(wt[h, :, :, at].reshape(H, step), gp[h], TN) for h in range(2))
        wide = gm * SQUARE_SCALE
        gm_ref[s * per : (s + 1) * per, 0:C, :] = (wide * jnp.abs(wide)).astype(BF16).reshape(per, C, nt)
    keep_ref[...] = gp[own]
    send_ref[...] = gp[1 - own]


def weight_kernel(place_ref, keep_ref, got_ref, mixed_ref, theirs_ref, *refs, C, mp):
    outs, wg = refs[:-1], refs[-1]
    nt = mixed_ref.shape[1]
    ways = len(outs)
    per = mp // ways
    total = dot(keep_ref[...], mixed_ref[...], NT) + dot(got_ref[...], theirs_ref[...], NT)
    for m in range(mp):
        at = (m // ways) * C
        wg[m % ways, at : at + C, :] = total[m * C : (m + 1) * C]
    ones = jnp.ones((8, nt), BF16)
    tail = dot(ones, keep_ref[...], NT) + dot(ones, got_ref[...], NT)
    for q in range(ways):
        wg[q, per * C :, :] = tail
    for k in range(ways):
        outs[k][...] = wg[lax.rem(place_ref[1], ways) ^ k]


def fold_kernel(place_ref, *refs, ways, got, C, seen):
    parts, outs, acc = refs[:got], refs[got:-1], refs[-1]
    total = parts[0][...]
    for p in parts[1:]:
        total = total + p[...]
    blocks = (total.shape[0] - 8) // C
    for z in range(blocks):
        at = (z // ways) * C
        acc[z % ways, at : at + C, :] = total[z * C : (z + 1) * C]
    for q in range(ways):
        acc[q, (blocks // ways) * C :, :] = total[blocks * C :]
    for k in range(ways):
        outs[k][...] = acc[lax.rem(lax.div(place_ref[1], seen), ways) ^ k]


def back_kernel(
    len_ref, vec_ref, x_ref, stat_ref, gm_ref, slope_hbm, t_ref, near_hbm, jump_ref,
    layer_ref, gn_ref, sum_ref, row_ref, g_ref, p_ref, r_ref, turned_ref, xs, gs, ns, tok, hs, ps, rs, rts, tab, near_ref, slope_ref, sem, *, count,
):
    i = pl.program_id(0)
    G = g_ref.shape[0]
    C, L = x_ref.shape
    N = L // B
    nt = gm_ref.shape[2]
    per = nt // B
    quarter = B // 4

    def fetch(q, k):
        at = pl.ds(k * G, G)
        src, dst = (
            (slope_hbm.at[at], slope_ref.at[at]),
            (near_hbm.at[at], near_ref.at[at]),
            (t_ref.at[at, 0:B, :], tab.at[at, 0:B, :]),
            (t_ref.at[at, B:, :], tab.at[at, B + quarter : B + 3 * quarter, :]),
        )[q]
        return pltpu.make_async_copy(src, dst, sem.at[q, k])

    @pl.when(i == 0)
    def _():
        for k in range(C // G):
            for q in range(4):
                fetch(q, k).start()
        tab[:, B : B + quarter, :] = jnp.zeros((C, quarter, 4 * B), BF16)
        tab[:, B + 3 * quarter :, :] = jnp.zeros((C, quarter, 4 * B), BF16)
        for n in range(N):
            xs[n * C : (n + 1) * C, :] = x_ref[:, n * B : (n + 1) * B].astype(F32)
            at = slice((n % per) * B, (n % per + 1) * B)
            square = gm_ref[n // per, 0:C, at].astype(F32)
            gs[n * C : (n + 1) * C, :] = square * (lax.rsqrt(jnp.maximum(jnp.abs(square), 1e-37)) * (1.0 / SQUARE_SCALE))
        mean, inv, mask = token_stats(stat_ref, len_ref[0], count)
        tok[0] = mean
        tok[1] = inv
        tok[2] = mask
        sum_ref[...] = jnp.zeros_like(sum_ref)
        for m in range(gm_ref.shape[0]):
            layer_ref[:, m * nt : (m + 1) * nt] = gm_ref[m, C:, :]

    fetch(0, i).wait()
    for j in range(G):
        ci = i * G + j
        g = gs[pl.ds(ci, N, stride=C), :] * slope_ref[ci]
        g_ref[j] = g
        hi, lo = split(g)
        hs[j, 0:N, :] = hi
        hs[j, N:, :] = lo
    fetch(1, i).wait()
    z_all = [dot(hs[j], near_ref[i * G + j]) for j in range(G)]
    for j, z in enumerate(z_all):
        p = z[:N, :B] + (z[:N, B:] + z[N:, :B])
        p_ref[j] = p
        ps[j * N : (j + 1) * N, :] = p
    at = pl.ds(pl.multiple_of(i * G, G), G)
    scan_blocks(ps, rs, rts, (jump_ref[0, at, :], jump_ref[1, at, :]), N, True)
    left = []
    for j in range(G):
        r = rs[j * N : (j + 1) * N, :]
        r_ref[j] = r
        turned_ref[j] = rts[j * N : (j + 1) * N, :]
        left.append(jnp.concatenate([hs[j], jnp.concatenate(split(r), axis=0)], axis=1))
    fetch(2, i).wait()
    fetch(3, i).wait()
    both_all = [dot(left[j], tab[i * G + j]) for j in range(G)]
    for j, both in enumerate(both_all):
        ci = i * G + j
        mask = tok[2]
        normed = (xs[pl.ds(ci, N, stride=C), :] - tok[0]) * tok[1]
        sig = mask * (normed * vec_ref[0, ci] + vec_ref[1, ci])
        both = both[:N, : 2 * B] + (both[:N, 2 * B :] + both[N:, : 2 * B])
        gl = both[:, B:]
        grad = both[:, :B] + vec_ref[2, ci] * g_ref[j] + gl * shift_token(sig, 1) + shift_token(gl * sig, -1)
        masked = mask * grad
        gn = masked * vec_ref[0, ci]
        sum_ref[0] += gn
        sum_ref[1] += gn * normed
        ns[pl.ds(pl.multiple_of(ci * N, N), N), :] = gn
        for q, v in enumerate((g_ref[j] * sig, masked * normed, masked)):
            row_ref[j, q * 8 : (q + 1) * 8, :] = sum(v[8 * k : 8 * k + 8] for k in range(N // 8))

    @pl.when(i == pl.num_programs(0) - 1)
    def _():
        for n in range(N):
            gn_ref[:, n * B : (n + 1) * B] = ns[pl.ds(n, C, stride=N), :]


def lift_kernel(len_ref, vec_ref, x_ref, stat_ref, f_ref, u_ref, lift_ref, xs, tok, *, count):
    i = pl.program_id(0)
    G = f_ref.shape[0]
    C, L = x_ref.shape
    N = L // B

    @pl.when(i == 0)
    def _():
        for n in range(N):
            xs[n * C : (n + 1) * C, :] = x_ref[:, n * B : (n + 1) * B].astype(F32)
        tok[0], tok[1], tok[2] = token_stats(stat_ref, len_ref[0], count)

    ahead = float(B) - lane_iota((N, B)).astype(F32)
    flip = (lane_iota((B, B)) + row_iota((B, B)) == B - 1).astype(BF16)
    flat, left = [], []
    for j in range(G):
        ci = i * G + j
        normed = (xs[pl.ds(ci, N, stride=C), :] - tok[0]) * tok[1]
        sig = tok[2] * (normed * vec_ref[0, ci] + vec_ref[1, ci])
        liq = sig * shift_token(sig, 1)
        flat.append(jnp.concatenate(split(sig) + split(liq), axis=0))
        left.append(jnp.concatenate(split(jnp.concatenate([sig * ahead, liq * ahead], axis=1)), axis=0))
    turned_all = [dot(v, flip).astype(BF16) for v in flat]
    lifts = [dot(left[j], f_ref[j]) for j in range(G)]
    for j in range(G):
        turned, lift = turned_all[j], lifts[j]
        for q in range(2):
            at = slice(q * B, (q + 1) * B)
            u_ref[j, 0 : 2 * N, at] = turned[2 * q * N : (2 * q + 2) * N]
            u_ref[j, 2 * N :, at] = turned[2 * q * N : (2 * q + 1) * N]
        lift_ref[j] = lift[:N, :B] + (lift[:N, B:] + lift[N:, :B])


def sums_kernel(u_ref, lift_ref, g_ref, p_ref, r_ref, rx_ref, state_ref, sx_ref, near_ref, jump_ref, row_ref):
    i = pl.program_id(0)
    G = g_ref.shape[0]
    _, N, _ = g_ref.shape
    place = lane_iota((N, B)).astype(F32)
    rows2, lanes2 = row_iota((B, B)), lane_iota((B, B))
    inside = lanes2 + rows2 >= B - 1
    rows16 = row_iota((16, B))
    lag = lane_iota((16, B)).astype(F32)
    R = N + 16
    every = range(G)
    turned = []
    for j in every:
        g_hi, g_lo = split(g_ref[j])
        turned.append(jnp.concatenate([g_hi, g_hi, g_lo], axis=0).T)
    corr = [dot(turned[j], u_ref[j]) for j in every]
    left = []
    for j in every:
        lags = []
        for q in range(2):
            part = jnp.where(inside, corr[j][:, q * B : (q + 1) * B], 0.0)
            lags.append(jnp.sum(pltpu.roll(part, 1, 1, stride=1, stride_axis=0), axis=0, keepdims=True))
        pair = jnp.where((rows16 & 1) == 0, lags[0], lags[1])
        pair = jnp.where(rows16 < 2, pair, jnp.where(rows16 < 4, pair * lag, 0.0))
        left.append(jnp.concatenate(split(jnp.concatenate([g_ref[j] * place, pair], axis=0)), axis=0))
    both = [dot(left[j], near_ref[j]) for j in every]
    for j in every:
        ci = i * G + j
        z = both[j][:R, :B] + (both[j][:R, B:] + both[j][R:, :B])
        row_ref[j, 0:8, :] = z[N : N + 8]
        p, r, state, lift = p_ref[j], r_ref[j], state_ref[j], lift_ref[j]
        state_x, r_x = sx_ref[j], rx_ref[j]
        carry = z[:N] + float(B) * (r * jump_ref[0, pl.ds(ci, 1), :] + r_x * jump_ref[1, pl.ds(ci, 1), :])
        total = [p * state, p * state_x, carry * state + lift * r, carry * state_x + lift * r_x]
        for q, v in enumerate(total):
            row_ref[j, 8 + 8 * q : 16 + 8 * q, :] = sum(v[8 * k : 8 * k + 8] for k in range(N // 8))


def join_kernel(plain_ref, ref, out_ref):
    odd = (lane_iota((out_ref.shape[1], B)) & (B // 4)) != 0
    for q in range(2):
        out_ref[q] = jnp.where(odd, ref[:, 2 * q + 1, :], ref[:, 2 * q, :])
    for q in range(4):
        out_ref[2 + q] = jnp.sum(ref[:, 8 + 8 * q : 16 + 8 * q, :], axis=1)
    for q in range(3):
        out_ref[6 + q] = jnp.sum(plain_ref[:, 8 * q : 8 * q + 8, :], axis=1)


def finish_kernel(
    place_ref, mine_ref, theirs_ref, w_ref, step_ref, decay_ref, freq_ref, read_ref, liquid_ref, wsum_ref, across_ref,
    value_ref, gate_ref, vbias_ref, gbias_ref, step_out, decay_out, freq_out, read_out, liquid_out,
    skip_out, gain_out, bias_out, *, M,
):
    C = decay_ref.shape[0]
    half = B // 2

    def emit(first, second):
        value_ref[...] = first[0:C, :]
        gate_ref[...] = second[0:C, :]
        per = B // C
        group = place_ref[1] // per
        back = (B - (place_ref[1] % per) * C) % B
        for out, v in ((vbias_ref, first), (gbias_ref, second)):
            lanes = v[C : C + 8, pl.ds(pl.multiple_of(group * B, B), B)]
            out[...] = pltpu.roll(lanes, back, 1)[0:1, 0:C]

    @pl.when(place_ref[0] == 0)
    def _():
        emit(wsum_ref, across_ref)

    @pl.when(place_ref[0] == 1)
    def _():
        emit(across_ref, wsum_ref)

    rows = [mine_ref[q] + theirs_ref[q] for q in range(9)]

    def parts(a, b, c):
        return a[:, :half] - a[:, half:] + c[:, :half], b[:, :half] + b[:, half:] + c[:, half:]

    g_re, g_im = parts(rows[2], rows[3], rows[0])
    d_re, d_im = parts(rows[4], rows[5], rows[1])
    w = w_ref[...]
    w_re, w_im = w[:, :half], w[:, half:]
    l_re = w_re * d_re - w_im * d_im
    l_im = w_re * d_im + w_im * d_re
    cot = (
        2.0 * g_re[:, :M], -2.0 * g_im[:, :M], 2.0 * g_re[:, M:], -2.0 * g_im[:, M:],
        2.0 * (l_re[:, :M] + l_re[:, M:]), -2.0 * (l_im[:, :M] + l_im[:, M:]),
    )
    step = jnp.sum(jnp.where(row_iota((C, C)) == lane_iota((C, C)), step_ref[...], 0.0), axis=1, keepdims=True)
    _, back = jax.vjp(mode_terms, step, decay_ref[...], freq_ref[...], read_ref[...], liquid_ref[...])
    step_grad, decay_out[...], freq_out[...], read_out[...], liquid_out[...] = back(cot)
    lanes = lane_iota((B, B))
    pad = jnp.zeros((B - C, 1), F32)
    plain = jnp.zeros((B, B), F32)
    for q, v in enumerate([step_grad] + [jnp.sum(rows[6 + q], axis=1, keepdims=True) for q in range(3)]):
        plain = jnp.where(lanes == q, jnp.concatenate([v, pad], axis=0), plain)
    plain = plain.T
    for q, out in enumerate((step_out, skip_out, gain_out, bias_out)):
        out[...] = plain[q : q + 1, 0:C]


def last_kernel(x_ref, g_ref, gn_ref, stat_ref, sum_ref, out_ref, *, count):
    C, L = x_ref.shape
    for n in range(L // B):
        at = slice(n * B, (n + 1) * B)
        mean = stat_ref[0, n : n + 1, :]
        inv = lax.rsqrt(stat_ref[1, n : n + 1, :] * (1.0 / count) + EPS)
        first = sum_ref[0, n : n + 1, :] * (1.0 / count)
        second = sum_ref[1, n : n + 1, :] * (1.0 / count)
        normed = (x_ref[:, at].astype(F32) - mean) * inv
        out_ref[:, at] = inv * (gn_ref[:, at] - first - normed * second) + g_ref[:, at].astype(F32)


def total_kernel(*refs):
    total = refs[0][...]
    for p in refs[1:-1]:
        total = total + p[...]
    refs[-1][...] = total


def rounds_of(size):
    rounds, bit = [], 1
    while bit < size:
        if bit * 2 < size:
            rounds.append((bit, 2 * bit, 3 * bit))
            bit *= 4
        else:
            rounds.append((bit,))
            bit *= 2
    return rounds


def exchange(v, axis, size, off):
    return lax.ppermute(v, axis, [(k, k ^ off) for k in range(size)])


def all_sums(v, size):
    for offs in rounds_of(size):
        v = sum([exchange(v, "mp", size, o) for o in offs], v)
    return v


def sum_docs(v, size, stride):
    total = v
    for k in range(stride, size, stride):
        total = total + lax.ppermute(v, "dp", [(q, (q + k) % size) for q in range(size)])
    return total


def partner(v, size):
    return lax.ppermute(v, "dp", [(q, q ^ 1) for q in range(size)])


def mode_terms(log_step, decay_log, frequency, readout, liquid_readout):
    M = decay_log.shape[1]
    step_size = jnp.exp(log_step)
    real_rate = -jnp.exp(decay_log)
    real_step = step_size * real_rate
    imag_step = step_size * frequency
    growth = jnp.exp(real_step)
    num_real = growth * jnp.cos(imag_step) - 1.0
    num_imag = growth * jnp.sin(imag_step)
    denominator = real_rate * real_rate + frequency * frequency
    in_real = (num_real * real_rate + num_imag * frequency) / denominator
    in_imag = (num_imag * real_rate - num_real * frequency) / denominator

    def mix(coeffs):
        re, im = coeffs[:, :M], coeffs[:, M:]
        return re * in_real - im * in_imag, re * in_imag + im * in_real

    return mix(readout) + mix(liquid_readout) + (real_step, imag_step)


def per_device(
    mp, dp,
    tokens, lengths, norm_gain, norm_bias, log_step, decay_log, frequency, readout, liquid_readout,
    skip_gain, value_weight, gate_weight, value_bias, gate_bias, grad_out,
):
    C, L = tokens.shape
    H = value_weight.shape[0]
    M = decay_log.shape[1]
    N = L // B
    nt = L // mp
    few_rows = C * B // nt
    shape = jax.ShapeDtypeStruct

    place = jnp.stack([lax.axis_index("dp") & 1, lax.axis_index("mp")]).astype(jnp.int32)
    rounds = rounds_of(mp)
    small, large = 16, 32

    def pin(v):
        return pltpu.with_memory_space_constraint(v, pltpu.HBM)

    def call(kernel, out, n_in, smem=0, us=1, scratch=(), mb=small):
        return pl.pallas_call(
            kernel,
            out_shape=out,
            in_specs=[SMEM] * smem + [VMEM] * (n_in - smem),
            out_specs=jax.tree.map(lambda _: VMEM, out),
            scratch_shapes=list(scratch),
            compiler_params=params(mb),
            cost_estimate=cost(us),
        )

    def whole(*dims):
        return pl.BlockSpec(dims, lambda i: (0,) * len(dims))

    def chan_by(group):
        return lambda *dims: pl.BlockSpec((group,) + dims, lambda i: (i,) + (0,) * len(dims))

    def by_channel(kernel, out, in_specs, out_specs, us, scratch, mb=small, group=TABLE_GROUP):
        return pl.pallas_call(
            kernel,
            grid=(C // group,),
            out_shape=out,
            in_specs=in_specs,
            out_specs=out_specs,
            scratch_shapes=scratch,
            compiler_params=params(mb),
            cost_estimate=cost(us),
        )

    vm = pltpu.VMEM
    G = min(MIXER_GROUP, C)
    chan, few = chan_by(G), chan_by(TABLE_GROUP)
    blocks = shape((C, N, B), F32)
    far = pltpu.HBM
    far_blocks = far((C, N, B), F32)
    def pin(v):
        return pltpu.with_memory_space_constraint(v, far)

    hbm = pl.BlockSpec(memory_space=pltpu.HBM)
    stat, pay = pl.pallas_call(
        start_kernel,
        out_shape=(shape((2 * N + mp, B), F32), shape((mp, few_rows + 2 * C, nt), BF16)),
        in_specs=[SMEM] + [hbm] * 6,
        out_specs=(VMEM, VMEM),
        scratch_shapes=[
            pltpu.VMEM((C, L), BF16), pltpu.VMEM((C, L), BF16), pltpu.VMEM((C, H), BF16),
            pltpu.VMEM((1, C), BF16), pltpu.VMEM((1, C), BF16), pltpu.SemaphoreType.DMA((5,)),
        ],
        compiler_params=params(small),
        cost_estimate=cost(3),
    )(
        place, pin(tokens), pin(grad_out), pin(value_weight.T), pin(gate_weight.T), pin(value_bias[None]), pin(gate_bias[None])
    )
    first = lax.all_to_all(pay, "mp", split_axis=0, concat_axis=0, tiled=True)

    count = C
    for k, offs in enumerate(rounds[::-1]):
        parts = [stat] + [exchange(stat, "mp", mp, o) for o in offs]
        if k < len(rounds) - 1:
            stat = jnp.concatenate(join_stats(parts, N, float(count)), axis=0)
            count *= len(parts)
            stat, rates = lax.optimization_barrier((stat, decay_log))
    cols, jump, w_all = call(
        mode_kernel, (shape((2, B, B), F32), shape((2, C, B), F32), shape((C, B), F32)), 5
    )(log_step[None], rates, frequency, readout, liquid_readout)
    f_near, f_tab, t_tab = by_channel(
        partial(table_kernel, M=M),
        (shape((C, 2 * B, 2 * B), BF16), far((C, 2 * B, 2 * B), BF16), shape((C, 3 * B, 2 * B), BF16)),
        [whole(2, B, B)],
        (few(2 * B, 2 * B), few(2 * B, 2 * B), few(3 * B, 2 * B)),
        6,
        [],
    )(cols)
    parts, t_tab = lax.optimization_barrier((parts, t_tab))

    vecs = jnp.stack([norm_gain, norm_bias, skip_gain])
    mixed, slope, state, state_x, stat, bias = by_channel(
        partial(mixer_kernel, count=H, parts=len(parts)),
        (shape((mp, C, nt), BF16), far_blocks, far_blocks, far_blocks, far((2, N, B), F32), shape((mp, B), F32)),
        [SMEM, SMEM, whole(C, L)] + [whole(2 * N + mp, B)] * len(parts)
        + [chan(2 * B, 2 * B), chan(3 * B, 2 * B), whole(2, C, B)],
        (whole(mp, C, nt), chan(N, B), chan(N, B), chan(N, B), whole(2, N, B), whole(mp, B)),
        6,
        [
            vm((N * C, B), F32), vm((N * C, B), F32), vm((3, N, B), F32), vm((G, 2 * N, 2 * B), BF16),
            vm((G * N, B), F32), vm((G * N, B), F32), vm((G * N, B), F32),
        ],
        large,
        G,
    )(lengths, vecs, tokens, *parts, f_near, t_tab, jump)

    mixed, first, cols = lax.optimization_barrier((mixed, first, cols))
    own_w = [first[:, :few_rows, :]]
    own_w += [exchange(own_w[0], "mp", mp, o) for o in rounds[0]]
    other_w = [partner(v, dp) for v in own_w]
    mixed_tok = lax.all_to_all(mixed, "mp", split_axis=0, concat_axis=0, tiled=True)
    half_steps = C // TABLE_GROUP // 2

    def back_tables(held, start, steps):
        def block(*dims):
            return pl.BlockSpec((TABLE_GROUP,) + dims, lambda i: (i + start,) + (0,) * len(dims))

        return pl.pallas_call(
            partial(back_table_kernel, M=M, start=start),
            grid=(steps,),
            out_shape=(far((C, B + 2 * M, 4 * B), BF16), far((C, B, 2 * B), BF16)),
            in_specs=[whole(2, B, B)] + [hbm] * len(held),
            out_specs=(block(B + 2 * M, 4 * B), block(B, 2 * B)),
            input_output_aliases={1 + k: k for k in range(len(held))},
            compiler_params=params(small),
            cost_estimate=cost(4),
        )(cols, *[pin(v) for v in held])

    tables = back_tables([], 0, half_steps)
    mixed_tok, tables = lax.optimization_barrier((mixed_tok, tables))
    gm, keep, send = call(
        partial(glu_kernel, parts=len(own_w)),
        (shape((mp, 2 * C, nt), BF16),) + (shape((H, nt), BF16),) * 2,
        4 + 2 * len(own_w), 1, 2, [vm((2, H, nt), BF16), vm((2, mp, C, H), BF16)],
    )(place, mixed_tok, first, bias, *own_w, *other_w)
    mixed_tok = mixed_tok.reshape(H, nt)
    gm, f_tab, cols = lax.optimization_barrier((gm, f_tab, cols))
    gm = lax.all_to_all(gm, "mp", split_axis=0, concat_axis=0, tiled=True)
    u_rev, lift = by_channel(
        partial(lift_kernel, count=H),
        (far((C, 3 * N, 2 * B), BF16), far_blocks),
        [SMEM, SMEM, whole(C, L), whole(2, N, B), few(2 * B, 2 * B)],
        (few(3 * N, 2 * B), few(N, B)),
        3,
        [vm((N * C, B), F32), vm((3, N, B), F32)],
        56,
    )(lengths, vecs, tokens, stat, pin(f_tab))
    back_tab, near_tab = back_tables(tables, half_steps, half_steps)
    gm, lift, back_tab = lax.optimization_barrier((gm, lift, back_tab))

    ways = len(rounds[0]) + 1
    rows_left = mp // ways
    outs = call(
        partial(weight_kernel, C=C, mp=mp), (shape((rows_left * C + 8, H), F32),) * ways, 5, 1, 2,
        [vm((ways, rows_left * C + 8, H), F32)],
    )(place, keep, partner(send, dp), mixed_tok, partner(mixed_tok, dp))
    terms = [outs[0]] + [exchange(v, "mp", mp, o) for v, o in zip(outs[1:], rounds[0])]

    layer_out, gn, sums, plain, g_pre, p_blk, r_blk, rx_blk = by_channel(
        partial(back_kernel, count=H),
        (shape((C, L), BF16), shape((C, L), F32), shape((2, N, B), F32), shape((C, 24, B), F32)) + (blocks,) * 4,
        [
            SMEM, SMEM, VMEM, VMEM, VMEM, hbm, hbm, hbm, VMEM,
        ],
        (whole(C, L), whole(C, L), whole(2, N, B), chan(24, B)) + (chan(N, B),) * 4,
        7,
        [
            vm((N * C, B), F32), vm((N * C, B), F32), vm((N * C, B), F32), vm((3, N, B), F32),
            vm((G, 2 * N, B), BF16), vm((G * N, B), F32), vm((G * N, B), F32), vm((G * N, B), F32),
            vm((C, 2 * B, 4 * B), BF16), vm((C, B, 2 * B), BF16), vm((C, N, B), F32),
            pltpu.SemaphoreType.DMA((4, C // G)),
        ],
        large,
        G,
    )(lengths, vecs, tokens, stat, gm, pin(slope), pin(back_tab), pin(near_tab), jump)

    seen = ways
    terms[0], plain = lax.optimization_barrier((terms[0], plain))
    while seen < mp:
        ways, offs = 2, (seen,)
        rows_left //= ways
        outs = call(
            partial(fold_kernel, ways=ways, got=len(terms), C=C, seen=seen),
            (shape((rows_left * C + 8, H), F32),) * ways,
            1 + len(terms), 1, 1, [vm((ways, rows_left * C + 8, H), F32)],
        )(place, *terms)
        terms = [outs[0]] + [exchange(v, "mp", mp, o) for v, o in zip(outs[1:], offs)]
        seen *= ways
    for k, offs in enumerate(rounds[::-1]):
        got = [exchange(sums, "mp", mp, o) for o in offs]
        if k == len(rounds) - 1:
            g_pre, sums, terms[0] = lax.optimization_barrier((g_pre, sums, terms[0]))
            rows = by_channel(
                sums_kernel,
                shape((C, 40, B), F32),
                [chan(3 * N, 2 * B)] + [chan(N, B)] * 7 + [chan(B, 2 * B), whole(2, C, B)],
                chan(40, B),
                20,
                [],
                large,
                G,
            )(u_rev, lift, g_pre, p_blk, r_blk, rx_blk, state, state_x, near_tab, jump)
            got, rows, terms = lax.optimization_barrier((got, rows, terms))
        sums = sum(got, sums)
    cut = 2
    wide_block = pl.BlockSpec((C, L // cut), lambda i: (0, i))
    tall_block = pl.BlockSpec((2, N // cut, B), lambda i: (0, i, 0))
    grad_tokens = pl.pallas_call(
        partial(last_kernel, count=H),
        grid=(cut,),
        out_shape=shape((C, L), F32),
        in_specs=[wide_block] * 3 + [tall_block] * 2,
        out_specs=wide_block,
        compiler_params=params(small),
        cost_estimate=cost(1),
    )(tokens, grad_out, gn, stat, sums)
    rows = call(join_kernel, shape((9, C, B), F32), 2)(plain, rows)
    others = sum_docs(rows, dp, 1) - rows if dp > 2 else partner(rows, dp)

    wsum = call(total_kernel, shape((C + 8, H), F32), len(terms))(*terms)
    wsum = sum_docs(wsum, dp, 2)
    across = partner(wsum, dp)
    thin, wide = shape((C, M), F32), shape((C, 2 * M), F32)
    line = shape((1, C), F32)
    (
        value_wgrad, gate_wgrad, vb, gb, step_grad, decay_grad, frequency_grad, readout_grad, liquid_grad,
        skip_grad, gain_grad, bias_grad,
    ) = call(
        partial(finish_kernel, M=M),
        (shape((C, H), F32), shape((C, H), F32), line, line, line, thin, thin, wide, wide, line, line, line),
        11, 1,
    )(
        place, rows, others, w_all, log_step[None], decay_log, frequency, readout, liquid_readout, wsum, across,
    )
    return (
        layer_out, grad_tokens, gain_grad[0], bias_grad[0], step_grad[0], decay_grad, frequency_grad, readout_grad,
        liquid_grad, skip_grad[0], value_wgrad.T, gate_wgrad.T, vb[0], gb[0],
    )


def solution(mesh):
    row, col, act = P("mp"), P(None, "mp"), P("mp", "dp")
    wide = P("mp", None)
    in_specs = (act, P("dp"), row, row, row, wide, wide, wide, wide, row, col, col, row, row, act)
    out_specs = (act, act, row, row, row, wide, wide, wide, wide, row, col, col, row, row)
    return jax.shard_map(
        partial(per_device, mesh.shape["mp"], mesh.shape["dp"]),
        mesh=mesh, in_specs=in_specs, out_specs=out_specs, check_vma=False,
    )
```
